32 devices in a mesh: batch: 4 (over y, core), res: 8 (over z, x).
Axes of the slice: x: 2, y: 2, z: 4, core: 2. Of those that a mesh axis runs over, the one named last changes fastest.
Arguments:
- node_states: bfloat16 [4, 512, 512], P('batch', 'res'), may hold values from -6 to 6
- edge_states: bfloat16 [4, 512, 60, 192], P('batch', 'res'), may hold values from -6 to 6
- neighbour_index: int32 [4, 512, 60], P('batch', 'res'), may hold values from 0 to 511, as said below
- edge_mask: int32 [4, 512, 60], P('batch', 'res'), may hold values from 0 to 1, as said below
- node_cotangent: bfloat16 [4, 512, 512], P('batch', 'res'), may hold values from -6 to 6
- edge_cotangent: bfloat16 [4, 512, 60, 192], P('batch', 'res'), may hold values from -6 to 6
- message_weight1: bfloat16 [1216, 512], replicated, may hold values from -0.15625 to 0.15625
- message_bias1: bfloat16 [512], replicated, may hold values from -2 to 2
- message_weight2: bfloat16 [512, 512], replicated, may hold values from -0.25 to 0.25
- message_bias2: bfloat16 [512], replicated, may hold values from -2 to 2
- message_weight3: bfloat16 [512, 512], replicated, may hold values from -0.25 to 0.25
- message_bias3: bfloat16 [512], replicated, may hold values from -2 to 2
- norm1_gain: bfloat16 [512], replicated, may hold values from 0.5 to 1.5
- norm1_shift: bfloat16 [512], replicated, may hold values from -2 to 2
- expand_weight: bfloat16 [512, 2048], replicated, may hold values from -0.25 to 0.25
- expand_bias: bfloat16 [2048], replicated, may hold values from -2 to 2
- contract_weight: bfloat16 [2048, 512], replicated, may hold values from -0.125 to 0.125
- contract_bias: bfloat16 [512], replicated, may hold values from -2 to 2
- norm2_gain: bfloat16 [512], replicated, may hold values from 0.5 to 1.5
- norm2_shift: bfloat16 [512], replicated, may hold values from -2 to 2
- edge_weight1: bfloat16 [1216, 192], replicated, may hold values from -0.15625 to 0.15625
- edge_bias1: bfloat16 [192], replicated, may hold values from -2 to 2
- edge_weight2: bfloat16 [192, 192], replicated, may hold values from -0.4375 to 0.4375
- edge_bias2: bfloat16 [192], replicated, may hold values from -2 to 2
- edge_weight3: bfloat16 [192, 192], replicated, may hold values from -0.4375 to 0.4375
- edge_bias3: bfloat16 [192], replicated, may hold values from -2 to 2
- norm3_gain: bfloat16 [192], replicated, may hold values from 0.5 to 1.5
- norm3_shift: bfloat16 [192], replicated, may hold values from -2 to 2
Outputs:
- node_output: bfloat16 [4, 512, 512], P('batch', 'res')
- edge_output: bfloat16 [4, 512, 60, 192], P('batch', 'res')
- node_grad: float32 [4, 512, 512], P('batch', 'res')
- edge_grad: float32 [4, 512, 60, 192], P('batch', 'res')
- grad_message_weight1: float32 [1216, 512], replicated
- grad_message_bias1: float32 [512], replicated
- grad_message_weight2: float32 [512, 512], replicated
- grad_message_bias2: float32 [512], replicated
- grad_message_weight3: float32 [512, 512], replicated
- grad_message_bias3: float32 [512], replicated
- grad_norm1_gain: float32 [512], replicated
- grad_norm1_shift: float32 [512], replicated
- grad_expand_weight: float32 [512, 2048], replicated
- grad_expand_bias: float32 [2048], replicated
- grad_contract_weight: float32 [2048, 512], replicated
- grad_contract_bias: float32 [512], replicated
- grad_norm2_gain: float32 [512], replicated
- grad_norm2_shift: float32 [512], replicated
- grad_edge_weight1: float32 [1216, 192], replicated
- grad_edge_bias1: float32 [192], replicated
- grad_edge_weight2: float32 [192, 192], replicated
- grad_edge_bias2: float32 [192], replicated
- grad_edge_weight3: float32 [192, 192], replicated
- grad_edge_bias3: float32 [192], replicated
- grad_norm3_gain: float32 [192], replicated
- grad_norm3_shift: float32 [192], replicated
The draws below stay inside these ranges and needn't reach their ends.
Inputs may be any that keep to these rules, and one draw needn't show every extreme that they name: `neighbour_index`: entries name residues of the same complex. Slots at or beyond a residue's valid count name the residue itself. Over the valid slots of one block of 64 consecutive residues (starting at a multiple of 64), at most 8 distinct residues of any other such block are named, and in every draw some block names exactly 8 residues of another block. `edge_mask`: in each residue the first 30 to 60 slots are 1 and the rest 0.
All inputs are finite; a program needn't handle non-finite values.
Results may differ from the reference program's by a relative error of at most 0.014.
Values may be sent and summed in bfloat16 or wider, within the bound.
No kernel may reach another device: no remote copies, remote signals or barrier semaphores. Data moves between devices by JAX's collectives and lax.ppermute only.
A program may use at most 192 MiB of HBM per device.

```python
import math
import jax
import jax.numpy as jnp
from jax import lax

D = 512
DE = 192
FF = 2048
MSG_IN = 1216
SLOTS = 60
ROW_CAP = 8
RES_DEV = 64
CPLX_LEN = 512
COMPLEXES = 4


def graph_tables(key):
    block_count = CPLX_LEN // RES_DEV
    least_long = (block_count * ROW_CAP + RES_DEV - 1) // RES_DEV

    def one_complex(complex_key):
        key_list = jax.random.split(complex_key, 8)
        owner_ids = jnp.arange(block_count, dtype=jnp.int32)
        residue_ids = jnp.arange(RES_DEV, dtype=jnp.int32)
        scores = jax.random.randint(key_list[0], (block_count, block_count, RES_DEV), 0, 2 ** 20) * RES_DEV + residue_ids
        shuffled = jnp.argsort(scores, axis=-1).astype(jnp.int32)
        candidates = owner_ids[None, :, None] * RES_DEV + shuffled[:, :, :ROW_CAP]
        used_count = jax.random.randint(key_list[1], (block_count, block_count), 1, ROW_CAP + 1)
        full_owner = (owner_ids + jax.random.randint(key_list[2], (block_count,), 1, block_count)) % block_count
        is_full = owner_ids[None, :] == full_owner[:, None]
        used_count = jnp.where(is_full, ROW_CAP, used_count)
        slot_ids = jnp.arange(ROW_CAP, dtype=jnp.int32)
        remote = owner_ids[None, :] != owner_ids[:, None]
        used_slot = remote[:, :, None] & (slot_ids[None, None, :] < used_count[:, :, None])
        distance = (owner_ids[None, :] - owner_ids[:, None]) % block_count
        order_key = (1 - used_slot.astype(jnp.int32)) * (2 * block_count * ROW_CAP) + (1 - is_full.astype(jnp.int32))[:, :, None] * (block_count * ROW_CAP) + distance[:, :, None] * ROW_CAP + slot_ids[None, None, :]
        ordering = jnp.argsort(order_key.reshape(block_count, block_count * ROW_CAP), axis=-1)
        row_pool = jnp.take_along_axis(candidates.reshape(block_count, block_count * ROW_CAP), ordering, axis=-1)
        pool_size = jnp.sum(used_slot.reshape(block_count, -1).astype(jnp.int32), axis=-1)
        most_long = jax.random.randint(key_list[3], (block_count, 1), least_long, 26)
        long_count = jax.random.randint(key_list[4], (block_count, RES_DEV), least_long, most_long + 1)
        lowest_valid = jax.random.randint(key_list[5], (block_count, 1), 30, 61)
        valid_count = jax.random.randint(key_list[6], (block_count, RES_DEV), lowest_valid, 61)
        slot_range = jnp.arange(SLOTS, dtype=jnp.int32)
        is_long = slot_range[None, None, :] < long_count[:, :, None]
        is_valid = slot_range[None, None, :] < valid_count[:, :, None]
        long_rank = jnp.cumsum(is_long.reshape(block_count, -1).astype(jnp.int32), axis=-1) - 1
        picked = jnp.take_along_axis(row_pool, jnp.maximum(long_rank, 0) % pool_size[:, None], axis=-1)
        picked = picked.reshape(block_count, RES_DEV, SLOTS)
        local_pick = owner_ids[:, None, None] * RES_DEV + jax.random.randint(key_list[7], (block_count, RES_DEV, SLOTS), 0, RES_DEV)
        self_ids = (owner_ids[:, None] * RES_DEV + residue_ids[None, :])[:, :, None]
        neighbours = jnp.where(is_long, picked, jnp.where(is_valid, local_pick, self_ids))
        return (neighbours.reshape(CPLX_LEN, SLOTS).astype(jnp.int32), is_valid.reshape(CPLX_LEN, SLOTS).astype(jnp.int32))
    return jax.vmap(one_complex)(jax.random.split(key, COMPLEXES))


def draw_neighbour_index(key, part):
    tables = graph_tables(key)
    return tables[0]


def draw_edge_mask(key, part):
    tables = graph_tables(key)
    return tables[1]


def level_of(rng, shape, shards, low, largest):
    level = 1.0
    for dim, blocks in shards:
        draws = jax.random.uniform(jax.random.fold_in(jax.random.fold_in(rng, 6), dim), (blocks,), jnp.float32, low / len(shards), largest / len(shards))
        level = level * jnp.repeat(jnp.exp(draws), shape[dim] // blocks).reshape((-1,) + (1,) * (len(shape) - 1 - dim))
    return level


def gaussian(own_key, extent, scale, reach, cuts=(), kind=jnp.bfloat16):
    entries = jax.random.normal(own_key, extent, jnp.float32) * scale
    if len(cuts) > 0:
        entries = level_of(own_key, extent, cuts, -0.22, 0.18) * entries
    return jnp.clip(entries, min=-reach, max=reach).astype(kind)


def setup_inputs(seed: int = 0) -> dict:
    keys = jax.random.split(jax.random.key(seed), 29)
    return {
        "node_states": gaussian(keys[0], (COMPLEXES, CPLX_LEN, D), 1.0, 6.0, ((0, 4), (1, 8))),
        "edge_states": gaussian(keys[1], (COMPLEXES, CPLX_LEN, SLOTS, DE), 1.0, 6.0, ((0, 4), (1, 8))),
        "neighbour_index": draw_neighbour_index(jax.random.fold_in(keys[28], 71), 0),
        "edge_mask": draw_edge_mask(jax.random.fold_in(keys[28], 71), 0),
        "node_cotangent": gaussian(keys[4], (COMPLEXES, CPLX_LEN, D), 1.0, 6.0, ((0, 4), (1, 8))),
        "edge_cotangent": gaussian(keys[5], (COMPLEXES, CPLX_LEN, SLOTS, DE), 1.0, 6.0, ((0, 4), (1, 8))),
        "message_weight1": gaussian(keys[6], (MSG_IN, D), MSG_IN ** -0.5, 0.15625),
        "message_bias1": gaussian(keys[7], (D,), 0.3, 2.0),
        "message_weight2": gaussian(keys[8], (D, D), D ** -0.5, 0.25),
        "message_bias2": gaussian(keys[9], (D,), 0.3, 2.0),
        "message_weight3": gaussian(keys[10], (D, D), D ** -0.5, 0.25),
        "message_bias3": gaussian(keys[11], (D,), 0.3, 2.0),
        "norm1_gain": jnp.clip(1.0 + 0.1 * jax.random.normal(keys[12], (D,), jnp.float32), 0.5, 1.5).astype(jnp.bfloat16),
        "norm1_shift": gaussian(keys[13], (D,), 0.3, 2.0),
        "expand_weight": gaussian(keys[14], (D, FF), D ** -0.5, 0.25),
        "expand_bias": gaussian(keys[15], (FF,), 0.3, 2.0),
        "contract_weight": gaussian(keys[16], (FF, D), FF ** -0.5, 0.125),
        "contract_bias": gaussian(keys[17], (D,), 0.3, 2.0),
        "norm2_gain": jnp.clip(1.0 + 0.1 * jax.random.normal(keys[18], (D,), jnp.float32), 0.5, 1.5).astype(jnp.bfloat16),
        "norm2_shift": gaussian(keys[19], (D,), 0.3, 2.0),
        "edge_weight1": gaussian(keys[20], (MSG_IN, DE), MSG_IN ** -0.5, 0.15625),
        "edge_bias1": gaussian(keys[21], (DE,), 0.3, 2.0),
        "edge_weight2": gaussian(keys[22], (DE, DE), DE ** -0.5, 0.4375),
        "edge_bias2": gaussian(keys[23], (DE,), 0.3, 2.0),
        "edge_weight3": gaussian(keys[24], (DE, DE), DE ** -0.5, 0.4375),
        "edge_bias3": gaussian(keys[25], (DE,), 0.3, 2.0),
        "norm3_gain": jnp.clip(1.0 + 0.1 * jax.random.normal(keys[26], (DE,), jnp.float32), 0.5, 1.5).astype(jnp.bfloat16),
        "norm3_shift": gaussian(keys[27], (DE,), 0.3, 2.0),
    }


@jax.custom_vjp
def low(v):
    return lax.optimization_barrier(v.astype(jnp.bfloat16)).astype(jnp.float32)

@jax.custom_vjp
def low_back(v):
    return v

def low_keep(v):
    return (low(v), None)

def low_pass(kept, grad):
    return (grad,)

def back_keep(v):
    return (v, None)

def back_low(kept, grad):
    return (low(grad),)
low.defvjp(low_keep, low_pass)
low_back.defvjp(back_keep, back_low)
EPSILON = 1e-05
HIGHEST = lax.Precision.HIGHEST

def layer_norm(values, norm_gain, norm_shift):
    average = lax.optimization_barrier(jnp.mean(values, axis=-1, keepdims=True))
    centred = values - average
    variance = lax.optimization_barrier(jnp.mean(centred * centred, axis=-1, keepdims=True))
    return centred * lax.rsqrt(variance + EPSILON) * norm_gain + norm_shift

def gelu_exact(values):
    return jax.nn.gelu(values, approximate=False)

def affine(values, weight, bias):
    return jnp.dot(values, weight, precision=HIGHEST) + bias

def graph_layer(node_in, edge_in, neighbour_rows, validity, weight_set):
    message_weight1, message_bias1, message_weight2, message_bias2, message_weight3, message_bias3, norm1_gain, norm1_shift, expand_weight, expand_bias, contract_weight, contract_bias, norm2_gain, norm2_shift, edge_weight1, edge_bias1, edge_weight2, edge_bias2, edge_weight3, edge_bias3, norm3_gain, norm3_shift = weight_set
    length = node_in.shape[0]
    node_width = node_in.shape[1]
    block_rows = math.gcd(length, 128)
    blocks = length // block_rows
    counts = lax.optimization_barrier(jnp.sum(validity, axis=1))

    def blocked(values):
        return values.reshape((blocks, block_rows) + values.shape[1:])

    def message_block(pieces):
        self_rows, index_rows, edge_rows, valid_rows = pieces
        neighbours = node_in[index_rows]
        joined = jnp.concatenate([jnp.broadcast_to(self_rows[:, None, :], neighbours.shape), neighbours, edge_rows], axis=-1)
        pre_first = low_back(affine(joined, message_weight1, message_bias1))
        act_first = low(gelu_exact(pre_first))
        pre_second = low_back(affine(act_first, message_weight2, message_bias2))
        act_second = low(gelu_exact(pre_second))
        message = low_back(affine(act_second, message_weight3, message_bias3))
        return lax.optimization_barrier(jnp.sum(message * valid_rows[:, :, None], axis=1))
    summed = lax.map(jax.checkpoint(message_block), (blocked(node_in), blocked(neighbour_rows), blocked(edge_in), blocked(validity)))
    summed = summed.reshape(length, node_width)
    mixed_rows = node_in + summed / counts[:, None]
    updated = layer_norm(mixed_rows, norm1_gain, norm1_shift)
    expanded = low(gelu_exact(low_back(affine(low(updated), expand_weight, expand_bias))))
    contracted = low_back(affine(expanded, contract_weight, contract_bias))
    node_out = low(layer_norm(updated + contracted, norm2_gain, norm2_shift))

    def edge_block(pieces):
        self_rows, index_rows, edge_rows, valid_rows = pieces
        neighbours = node_out[index_rows]
        joined = jnp.concatenate([jnp.broadcast_to(self_rows[:, None, :], neighbours.shape), neighbours, edge_rows], axis=-1)
        pre_first = low_back(affine(joined, edge_weight1, edge_bias1))
        act_first = low(gelu_exact(pre_first))
        pre_second = low_back(affine(act_first, edge_weight2, edge_bias2))
        act_second = low(gelu_exact(pre_second))
        edge_delta = low_back(affine(act_second, edge_weight3, edge_bias3))
        return layer_norm(edge_rows + edge_delta, norm3_gain, norm3_shift) * valid_rows[:, :, None]
    edge_out = lax.map(jax.checkpoint(edge_block), (blocked(node_out), blocked(neighbour_rows), blocked(edge_in), blocked(validity)))
    return (node_out, edge_out.reshape(edge_in.shape))

def reference(node_states, edge_states, neighbour_index, edge_mask, node_cotangent, edge_cotangent, message_weight1, message_bias1, message_weight2, message_bias2, message_weight3, message_bias3, norm1_gain, norm1_shift, expand_weight, expand_bias, contract_weight, contract_bias, norm2_gain, norm2_shift, edge_weight1, edge_bias1, edge_weight2, edge_bias2, edge_weight3, edge_bias3, norm3_gain, norm3_shift):
    weights = tuple((weight.astype(jnp.float32) for weight in (message_weight1, message_bias1, message_weight2, message_bias2, message_weight3, message_bias3, norm1_gain, norm1_shift, expand_weight, expand_bias, contract_weight, contract_bias, norm2_gain, norm2_shift, edge_weight1, edge_bias1, edge_weight2, edge_bias2, edge_weight3, edge_bias3, norm3_gain, norm3_shift)))

    def one_complex(running, pieces):
        node_piece, edge_piece, index_piece, mask_piece, node_cot_piece, edge_cot_piece = pieces
        validity = mask_piece.astype(jnp.float32)

        def forward(node_in, edge_in, weight_set):
            return graph_layer(node_in, edge_in, index_piece, validity, weight_set)
        outputs, backward = jax.vjp(forward, node_piece.astype(jnp.float32), edge_piece.astype(jnp.float32), weights)
        grad_nodes, grad_edges, grad_weights = backward((node_cot_piece.astype(jnp.float32), edge_cot_piece.astype(jnp.float32)))
        running = tuple((total + extra for total, extra in zip(running, grad_weights)))
        return (running, (outputs[0], outputs[1], grad_nodes, grad_edges))
    zero_grads = tuple((jnp.zeros_like(weight) for weight in weights))
    totals, stacked = lax.scan(one_complex, zero_grads, (node_states, edge_states, neighbour_index, edge_mask, node_cotangent, edge_cotangent))
    node_out, edge_out, node_grad, edge_grad = stacked
    grad_mw1, grad_mb1, grad_mw2, grad_mb2, grad_mw3, grad_mb3, grad_n1g, grad_n1s, grad_ew, grad_eb, grad_cw, grad_cb, grad_n2g, grad_n2s, grad_ew1, grad_eb1, grad_ew2, grad_eb2, grad_ew3, grad_eb3, grad_n3g, grad_n3s = totals
    return (node_out.astype(jnp.bfloat16), edge_out.astype(jnp.bfloat16), node_grad, edge_grad, grad_mw1, grad_mb1, grad_mw2, grad_mb2, grad_mw3, grad_mb3, grad_n1g, grad_n1s, grad_ew, grad_eb, grad_cw, grad_cb, grad_n2g, grad_n2s, grad_ew1, grad_eb1, grad_ew2, grad_eb2, grad_ew3, grad_eb3, grad_n3g, grad_n3s)
```

```python
import functools
import math

import jax
import jax.numpy as jnp
from jax import lax
from jax.experimental import pallas as pl
from jax.experimental.pallas import tpu as pltpu
from jax.sharding import PartitionSpec as P

ROW_CAP = 8
EPSILON = 1e-05
LANES = 128
VMEM_BYTES = 56 * 1024 * 1024
F32 = jnp.float32
BF16 = jnp.bfloat16

V_MB1, V_MB2, V_MB3, V_N1G, V_N1S, V_CB, V_N2G, V_N2S, V_EB = range(9)
V_EDGE = 12
V_ROWS = 24


def dot_nn(left, right):
    return lax.dot_general(left, right, (((1,), (0,)), ((), ())), preferred_element_type=F32)


def dot_nt(left, right):
    return lax.dot_general(left, right, (((1,), (1,)), ((), ())), preferred_element_type=F32)


def dot_tn(left, right):
    return lax.dot_general(left, right, (((0,), (0,)), ((), ())), preferred_element_type=F32)


def split_low(values):
    high = values.astype(BF16)
    return high, (values - high.astype(F32)).astype(BF16)


def dot_split(dot, left, right):
    high, rest = split_low(left)
    return dot(high, right) + dot(rest, right)


def dot_split_right(dot, left, right):
    high, rest = split_low(right)
    return dot(left, high) + dot(left, rest)


def gelu_pair(v):
    size = jnp.abs(v)
    den = 1.0 + (0.3275911 / math.sqrt(2.0)) * size
    t = pl.reciprocal(den, approx=True)
    t = t * (2.0 - den * t)
    e = jnp.exp2((v * v) * (-0.5 * math.log2(math.e)))
    poly = 0.5 * 1.061405429
    poly = poly * t + 0.5 * -1.453152027
    poly = poly * t + 0.5 * 1.421413741
    poly = poly * t + 0.5 * -0.284496736
    poly = poly * t + 0.5 * 0.254829592
    tail = poly * t * e
    phi_sum = jnp.where(v < 0, tail, 1.0 - tail)
    return v * phi_sum, phi_sum + (v * (1.0 / math.sqrt(2.0 * math.pi))) * e


def norm_parts(values):
    average = jnp.mean(values, axis=-1, keepdims=True)
    centred = values - average
    variance = jnp.mean(centred * centred, axis=-1, keepdims=True)
    scale = lax.rsqrt(variance + EPSILON)
    return centred * scale, scale


def norm_back(xhat, scale, gain, upstream):
    w = upstream * gain
    mean_w = jnp.mean(w, axis=-1, keepdims=True)
    mean_wx = jnp.mean(w * xhat, axis=-1, keepdims=True)
    return (w - mean_w - xhat * mean_wx) * scale


def edge_onehot(pos_ref, table_rows):
    pairs = pos_ref.shape[2]
    lane = lax.broadcasted_iota(jnp.int32, (LANES, table_rows), 1)
    return jnp.concatenate(
        [(pos_ref[0, :, p : p + 1] == lane).astype(F32).astype(BF16) for p in range(pairs)], axis=0
    )


def index_kernel(me_ref, idx_ref, pos_ref, select_ref, ids_ref, *, rows, parts, cap, steps):
    total = rows * parts
    table = rows + parts * cap
    me = me_ref[0]
    pair_rows = idx_ref.shape[0]
    residue = lax.broadcasted_iota(jnp.int32, (total, LANES), 0)
    hits = jnp.zeros((total, LANES), F32)
    for j in range(pair_rows):
        hits = jnp.where(idx_ref[j : j + 1, :] == residue, 1.0, hits)
    hit = jnp.max(hits, axis=1, keepdims=True)
    owner = residue // rows
    within = residue - owner * rows
    own = owner == me
    wanted = jnp.where(own, 0.0, jnp.broadcast_to(hit, (total, LANES)))
    low_row = lax.broadcasted_iota(jnp.int32, (rows, rows), 0)
    low_col = lax.broadcasted_iota(jnp.int32, (rows, rows), 1)
    lower = (low_col <= low_row).astype(F32).astype(BF16)
    wanted_low = wanted.astype(BF16)
    place = jnp.concatenate(
        [dot_nn(lower, wanted_low[o * rows : (o + 1) * rows]) for o in range(parts)], axis=0
    )
    place = jnp.clip(place - 1.0, 0.0, cap - 1.0)
    pos = jnp.where(
        own, within.astype(F32), (rows + owner * cap).astype(F32) + place
    )
    picked = [
        jnp.sum(jnp.where(idx_ref[j : j + 1, :] == residue, pos, 0.0), axis=0, keepdims=True)
        for j in range(pair_rows)
    ]
    picked.append(jnp.zeros((LANES - pair_rows, LANES), F32))
    turned = jnp.concatenate(picked, axis=0).T.astype(jnp.int32)
    per = pair_rows // steps
    for s in range(steps):
        pos_ref[s] = turned[:, s * per : (s + 1) * per]
    lane = lax.broadcasted_iota(jnp.int32, (total, table), 1).astype(F32)
    live = jnp.where(own, 1.0, wanted)
    chosen = jnp.where(lane == pos[:, :1], jnp.broadcast_to(live[:, :1], (total, table)), 0.0)
    select_ref[...] = chosen.astype(BF16)
    within_wide = jnp.broadcast_to(within[:, :1].astype(F32), (total, table))
    ids_ref[...] = jnp.sum(chosen * within_wide, axis=0, keepdims=True).astype(jnp.int32)


def node_kernel(
    edge_ref,
    pos_ref,
    all_ref,
    select_ref,
    self_ref,
    count_ref,
    asked_ref,
    vec_ref,
    w1_ref,
    w2_ref,
    w3_ref,
    expand_hbm,
    contract_hbm,
    act1_ref,
    slope1_ref,
    slope2_ref,
    fresh_ref,
    outgoing_ref,
    table_ref,
    mixed1_ref,
    mixed2_ref,
    low_ref,
    expanded_ref,
    slope_e_ref,
    act_sum_ref,
    proj_ref,
    self_pre_ref,
    expand_ref,
    contract_ref,
    sems,
):
    step = pl.program_id(0)
    last = pl.num_programs(0) - 1
    rows, width = self_ref.shape
    slots = edge_ref.shape[0]
    edge_width = edge_ref.shape[2]
    table_rows = table_ref.shape[0]
    expand_copy = pltpu.make_async_copy(expand_hbm, expand_ref, sems.at[0])
    contract_copy = pltpu.make_async_copy(contract_hbm, contract_ref, sems.at[1])

    @pl.when(step == 0)
    def _():
        expand_copy.start()
        contract_copy.start()
        table = dot_tn(select_ref[...], all_ref[...]).astype(BF16)
        table_ref[...] = table
        proj_ref[...] = dot_nn(table, w1_ref[width : 2 * width]).astype(BF16)
        self_pre_ref[...] = (
            dot_nn(self_ref[...], w1_ref[:width]) + vec_ref[V_MB1 : V_MB1 + 1, :]
        )
        act_sum_ref[...] = jnp.zeros_like(act_sum_ref)

    onehot = edge_onehot(pos_ref, table_rows)
    features = edge_ref[...].reshape(slots * rows, edge_width)
    pre1 = dot_nn(features, w1_ref[2 * width :]) + dot_nn(onehot, proj_ref[...])
    self_pre = self_pre_ref[...]
    act1 = []
    for k in range(slots):
        part = pl.ds(k * rows, rows)
        act, slope = gelu_pair(pre1[k * rows : (k + 1) * rows] + self_pre)
        act = act.astype(BF16)
        act1.append(act)
        act1_ref[part, :] = act
        slope1_ref[part, :] = slope.astype(BF16)
    pre2 = dot_nn(jnp.concatenate(act1, axis=0), w2_ref[...])
    bias2 = vec_ref[V_MB2 : V_MB2 + 1, :]
    act_sum = act_sum_ref[...]
    counts = count_ref[...]
    for k in range(slots):
        act, slope = gelu_pair(pre2[k * rows : (k + 1) * rows] + bias2)
        valid = counts > (step * slots + k).astype(F32)
        act_sum = act_sum + jnp.where(valid, act.astype(BF16).astype(F32), 0.0)
        slope2_ref[pl.ds(k * rows, rows), :] = jnp.where(valid, slope, 0.0).astype(BF16)
    act_sum_ref[...] = act_sum

    @pl.when(step == last)
    def _():
        summed = dot_split(dot_nn, act_sum_ref[...], w3_ref[...])
        summed = summed + counts * vec_ref[V_MB3 : V_MB3 + 1, :]
        mixed1 = self_ref[...].astype(F32) + summed / counts
        mixed1_ref[...] = mixed1
        xhat1, _ = norm_parts(mixed1)
        updated = xhat1 * vec_ref[V_N1G : V_N1G + 1, :] + vec_ref[V_N1S : V_N1S + 1, :]
        low = updated.astype(BF16)
        low_ref[...] = low
        expand_copy.wait()
        contract_copy.wait()
        mixed2 = updated + vec_ref[V_CB : V_CB + 1, :]
        for c in range(expand_ref.shape[1] // width):
            cols = slice(c * width, (c + 1) * width)
            pre = dot_nn(low, expand_ref[:, cols]) + vec_ref[V_EB + c : V_EB + c + 1, :]
            act, slope = gelu_pair(pre)
            act = act.astype(BF16)
            expanded_ref[:, cols] = act
            slope_e_ref[:, cols] = slope
            mixed2 = mixed2 + dot_nn(act, contract_ref[cols, :])
        mixed2_ref[...] = mixed2
        xhat2, _ = norm_parts(mixed2)
        fresh = (xhat2 * vec_ref[V_N2G : V_N2G + 1, :] + vec_ref[V_N2S : V_N2S + 1, :]).astype(BF16)
        fresh_ref[...] = fresh
        asked = asked_onehot(asked_ref, rows)
        outgoing_ref[...] = dot_tn(asked, fresh).astype(BF16)


def asked_onehot(asked_ref, rows):
    row = lax.broadcasted_iota(jnp.int32, (rows, asked_ref.shape[1]), 0)
    return (asked_ref[...] == row).astype(F32).astype(BF16)


def edge_kernel(
    edge_ref,
    cot_ref,
    pos_ref,
    fresh_ref,
    incoming_ref,
    count_ref,
    vec_ref,
    w1t_ref,
    w2_ref,
    w3_ref,
    out_ref,
    grad_ref,
    first_ref,
    own_ref,
    away_ref,
    pack_ref,
    vec_out_ref,
    table_ref,
    proj_ref,
    self_pre_ref,
    back_ref,
    dw3_ref,
    dw2_ref,
    dw1_ref,
    sums_ref,
):
    step = pl.program_id(0)
    last = pl.num_programs(0) - 1
    rows, width = fresh_ref.shape
    slots, _, edge_width = edge_ref.shape
    block = slots * rows
    table_rows = table_ref.shape[0]
    own_t = w1t_ref[:, :width]
    nbr_t = w1t_ref[:, width : 2 * width]
    feat_t = w1t_ref[:, 2 * width :]

    def vector(i):
        return vec_ref[V_EDGE + i : V_EDGE + i + 1, :edge_width]

    @pl.when(step == 0)
    def _():
        table_ref[:rows] = fresh_ref[...]
        table_ref[rows:] = incoming_ref[...]
        proj_ref[...] = dot_nt(table_ref[...], nbr_t).astype(BF16)
        self_pre_ref[...] = dot_nt(fresh_ref[...], own_t) + vector(0)
        for ref in (back_ref, dw3_ref, dw2_ref, dw1_ref, sums_ref, first_ref):
            ref[...] = jnp.zeros_like(ref)

    def flat(values):
        return values.reshape(block, edge_width)

    def deep(values):
        return values.reshape(slots, rows, edge_width)

    onehot = edge_onehot(pos_ref, table_rows)
    features = flat(edge_ref[...])
    pre1 = dot_nt(features, feat_t) + dot_nn(onehot, proj_ref[...])
    pre1 = deep(pre1) + self_pre_ref[...][None]
    act1, slope1 = gelu_pair(flat(pre1))
    act1 = act1.astype(BF16)
    pre2 = dot_nn(act1, w2_ref[...]) + vector(1)
    act2, slope2 = gelu_pair(pre2)
    act2 = act2.astype(BF16)
    mixed3 = features.astype(F32) + (dot_nn(act2, w3_ref[...]) + vector(2))
    xhat, scale = norm_parts(mixed3)
    gain = vector(3)
    slot = lax.broadcasted_iota(jnp.int32, (slots, rows, edge_width), 0) + step * slots
    valid = count_ref[...][None, :, :edge_width] > slot.astype(F32)
    out_ref[...] = jnp.where(valid, deep(xhat * gain + vector(4)), 0.0).astype(BF16)
    upstream = flat(jnp.where(valid, cot_ref[...].astype(F32), 0.0))
    sums_ref[3] += jnp.sum(deep(upstream * xhat), axis=0)
    sums_ref[4] += jnp.sum(deep(upstream), axis=0)
    grad_mixed = norm_back(xhat, scale, gain, upstream)
    grad_delta = grad_mixed.astype(BF16)
    dw3_ref[...] += dot_tn(act2, grad_delta)
    sums_ref[2] += jnp.sum(deep(grad_delta.astype(F32)), axis=0)
    grad2 = (dot_nt(grad_delta, w3_ref[...]) * slope2).astype(BF16)
    dw2_ref[...] += dot_tn(act1, grad2)
    sums_ref[1] += jnp.sum(deep(grad2.astype(F32)), axis=0)
    grad1 = (dot_nt(grad2, w2_ref[...]) * slope1).astype(BF16)
    dw1_ref[...] += dot_tn(grad1, features)
    first_ref[...] += jnp.sum(deep(grad1.astype(F32)), axis=0)
    back_ref[...] += dot_tn(onehot, grad1)
    grad_ref[...] = deep(grad_mixed + dot_nn(grad1, feat_t))

    @pl.when(step == last)
    def _():
        first = first_ref[...]
        back = back_ref[...]
        own_ref[...] = back[:rows]
        away_ref[...] = back[rows:].astype(BF16)
        first_high, first_rest = split_low(first)
        back_high, back_rest = split_low(back)
        own_grad = dot_tn(first_high, fresh_ref[...]) + dot_tn(first_rest, fresh_ref[...])
        nbr_grad = dot_tn(back_high, table_ref[...]) + dot_tn(back_rest, table_ref[...])
        pack_ref[:edge_width, :] = own_grad.astype(BF16)
        pack_ref[edge_width : 2 * edge_width, :] = nbr_grad.astype(BF16)
        pad = jnp.zeros((edge_width, width // 2 - edge_width), BF16)
        third = [dw1_ref[...].astype(BF16), pad, dw2_ref[...].astype(BF16), pad]
        pack_ref[2 * edge_width : 3 * edge_width, :] = jnp.concatenate(third, axis=1)
        fourth = [dw3_ref[...].astype(BF16), pad, jnp.zeros((edge_width, width // 2), BF16)]
        pack_ref[3 * edge_width :, :] = jnp.concatenate(fourth, axis=1)
        vec_out_ref[...] = jnp.zeros_like(vec_out_ref)
        vec_out_ref[0:1, :edge_width] = jnp.sum(first, axis=0, keepdims=True)
        for i in range(1, 5):
            vec_out_ref[i : i + 1, :edge_width] = jnp.sum(sums_ref[i], axis=0, keepdims=True)


def feed_kernel(
    cot_ref,
    first_ref,
    own_ref,
    arrived_ref,
    asked_ref,
    count_ref,
    vec_ref,
    w1t_ref,
    mixed1_ref,
    mixed2_ref,
    low_ref,
    expanded_ref,
    slope_ref,
    act_sum_ref,
    expand_ref,
    contract_ref,
    w3_ref,
    edge_pack_ref,
    edge_vec_ref,
    pack_ref,
    spread_ref,
    grad_mixed1_ref,
):
    rows, width = cot_ref.shape
    hidden = expand_ref.shape[1]
    edge_rows = edge_pack_ref.shape[0]
    own_t = w1t_ref[:, :width]
    nbr_t = w1t_ref[:, width : 2 * width]
    counts = count_ref[...]

    def vector(i):
        return vec_ref[i : i + 1, :]

    def total(values):
        return jnp.sum(values.astype(F32), axis=0, keepdims=True)

    back = own_ref[...] + dot_nn(asked_onehot(asked_ref, rows), arrived_ref[...])
    grad_fresh = (
        cot_ref[...].astype(F32)
        + dot_split(dot_nn, first_ref[...], own_t)
        + dot_split(dot_nn, back, nbr_t)
    )
    xhat2, scale2 = norm_parts(mixed2_ref[...])
    grad_mixed2 = norm_back(xhat2, scale2, vector(V_N2G), grad_fresh)
    grad_contracted = grad_mixed2.astype(BF16)
    grad_updated = grad_mixed2
    base = 0
    expand_bias = []
    for c in range(hidden // width):
        cols = slice(c * width, (c + 1) * width)
        pre = dot_nt(grad_contracted, contract_ref[cols, :]) * slope_ref[:, cols]
        pre = pre.astype(BF16)
        expand_bias.append(total(pre))
        grad_updated = grad_updated + dot_nt(pre, expand_ref[:, cols])
        pack_ref[base + c * width : base + (c + 1) * width, :] = dot_tn(
            low_ref[...], pre
        ).astype(BF16)
        pack_ref[hidden + c * width : hidden + (c + 1) * width, :] = dot_tn(
            expanded_ref[:, cols], grad_contracted
        ).astype(BF16)
    base = 2 * hidden
    pack_ref[base : base + edge_rows, :] = edge_pack_ref[...]
    base = base + edge_rows
    xhat1, scale1 = norm_parts(mixed1_ref[...])
    grad_mixed1 = norm_back(xhat1, scale1, vector(V_N1G), grad_updated)
    grad_mixed1_ref[...] = grad_mixed1
    grad_message = (grad_mixed1 / counts).astype(BF16)
    spread_ref[...] = dot_nt(grad_message, w3_ref[...])
    pack_ref[base : base + width, :] = dot_split(
        dot_tn, act_sum_ref[...], grad_message
    ).astype(BF16)
    base = base + width
    vectors = [
        total(counts * grad_message.astype(F32)),
        total(grad_updated * xhat1),
        total(grad_updated),
        *expand_bias,
        total(grad_contracted),
        total(grad_fresh * xhat2),
        total(grad_fresh),
        edge_vec_ref[...],
    ]
    vectors = jnp.concatenate(vectors, axis=0)
    vectors = jnp.concatenate(
        [vectors, jnp.zeros((pack_ref.shape[0] - base - vectors.shape[0], width), F32)], axis=0
    )
    pack_ref[base:, :] = vectors.astype(BF16)


def message_kernel(
    edge_ref,
    pos_ref,
    act1_ref,
    slope1_ref,
    slope2_ref,
    partial_ref,
    spread_ref,
    table_ref,
    w1_ref,
    w2_ref,
    grad_ref,
    first_ref,
    own_ref,
    away_ref,
    pack_ref,
    back_ref,
    dw2_ref,
    dw1_ref,
    bias2_ref,
):
    step = pl.program_id(0)
    last = pl.num_programs(0) - 1
    slots, rows, edge_width = edge_ref.shape
    width = act1_ref.shape[1]
    block = slots * rows
    table_rows = table_ref.shape[0]

    @pl.when(step == 0)
    def _():
        for ref in (back_ref, dw2_ref, dw1_ref, bias2_ref, first_ref):
            ref[...] = jnp.zeros_like(ref)

    spread = spread_ref[...]
    grad2 = []
    bias2 = bias2_ref[...]
    for k in range(slots):
        part = (spread * slope2_ref[pl.ds(k * rows, rows), :].astype(F32)).astype(BF16)
        bias2 = bias2 + part.astype(F32)
        grad2.append(part)
    bias2_ref[...] = bias2
    grad2 = jnp.concatenate(grad2, axis=0)
    dw2_ref[...] += dot_tn(act1_ref[...], grad2)
    grad1 = (dot_nt(grad2, w2_ref[...]) * slope1_ref[...].astype(F32)).astype(BF16)
    first_ref[...] += jnp.sum(grad1.astype(F32).reshape(slots, rows, width), axis=0)
    onehot = edge_onehot(pos_ref, table_rows)
    back_ref[...] += dot_tn(onehot, grad1)
    features = edge_ref[...].reshape(block, edge_width)
    dw1_ref[...] += dot_tn(features, grad1)
    grad_ref[...] = partial_ref[...] + dot_nt(grad1, w1_ref[2 * width :]).reshape(
        slots, rows, edge_width
    )

    @pl.when(step == last)
    def _():
        first = first_ref[...]
        back = back_ref[...]
        own_ref[...] = back[:rows]
        away_ref[...] = back[rows:].astype(BF16)
        pack_ref[:width, :] = dot_split_right(dot_tn, table_ref[:rows], first).astype(BF16)
        pack_ref[width : 2 * width, :] = dot_split_right(dot_tn, table_ref[...], back).astype(BF16)
        base = 2 * width
        pack_ref[base : base + edge_width, :] = dw1_ref[...].astype(BF16)
        base = base + edge_width
        pack_ref[base : base + width, :] = dw2_ref[...].astype(BF16)
        base = base + width
        vectors = jnp.concatenate(
            [
                jnp.sum(first, axis=0, keepdims=True),
                jnp.sum(bias2_ref[...], axis=0, keepdims=True),
                jnp.zeros((pack_ref.shape[0] - base - 2, width), F32),
            ],
            axis=0,
        )
        pack_ref[base:, :] = vectors.astype(BF16)


def node_grad_kernel(grad_ref, first_ref, own_ref, arrived_ref, asked_ref, w1_ref, out_ref):
    rows, width = grad_ref.shape
    back = own_ref[...] + dot_nn(asked_onehot(asked_ref, rows), arrived_ref[...])
    out_ref[...] = (
        grad_ref[...]
        + dot_split(dot_nt, first_ref[...], w1_ref[:width])
        + dot_split(dot_nt, back, w1_ref[width : 2 * width])
    )


def whole(shape):
    return pl.BlockSpec(shape, lambda i: (0,) * len(shape))


def params():
    return pltpu.CompilerParams(vmem_limit_bytes=VMEM_BYTES)


def body(
    node_states,
    edge_states,
    neighbour_index,
    edge_mask,
    node_cotangent,
    edge_cotangent,
    message_weight1,
    message_bias1,
    message_weight2,
    message_bias2,
    message_weight3,
    message_bias3,
    norm1_gain,
    norm1_shift,
    expand_weight,
    expand_bias,
    contract_weight,
    contract_bias,
    norm2_gain,
    norm2_shift,
    edge_weight1,
    edge_bias1,
    edge_weight2,
    edge_bias2,
    edge_weight3,
    edge_bias3,
    norm3_gain,
    norm3_shift,
):
    self_rows = node_states[0]
    rows, width = self_rows.shape
    slots = neighbour_index.shape[2]
    edge_width = edge_states.shape[3]
    hidden = expand_weight.shape[1]
    edges = rows * slots
    parts = lax.axis_size("res")
    cap = ROW_CAP
    table_rows = rows + parts * cap
    steps = 5
    block_slots = slots // steps
    block = block_slots * rows
    pairs = block // LANES

    me = lax.axis_index("res").astype(jnp.int32).reshape(1)
    everyone = lax.all_gather(self_rows, "res", axis=0, tiled=True)
    edge_rows = edge_states[0].transpose(1, 0, 2)
    edge_cot = edge_cotangent[0].transpose(1, 0, 2)
    idx_rows = neighbour_index[0].T.reshape(edges // LANES, LANES)
    counts = jnp.sum(edge_mask[0], axis=1).astype(F32)
    counts = jnp.broadcast_to(counts[:, None], (rows, width))
    edge_w1t = edge_weight1.T
    pad = jnp.zeros((width - edge_width,), BF16)
    vectors = [
        message_bias1,
        message_bias2,
        message_bias3,
        norm1_gain,
        norm1_shift,
        contract_bias,
        norm2_gain,
        norm2_shift,
        expand_bias,
    ]
    for v in (edge_bias1, edge_bias2, edge_bias3, norm3_gain, norm3_shift):
        vectors += [v, pad]
    vectors = jnp.concatenate(vectors).astype(F32).reshape(-1, width)
    vectors = jnp.pad(vectors, ((0, V_ROWS - vectors.shape[0]), (0, 0)))

    pos, select, ids = pl.pallas_call(
        functools.partial(index_kernel, rows=rows, parts=parts, cap=cap, steps=steps),
        out_shape=(
            jax.ShapeDtypeStruct((steps, LANES, pairs), jnp.int32),
            jax.ShapeDtypeStruct((parts * rows, table_rows), BF16),
            jax.ShapeDtypeStruct((1, table_rows), jnp.int32),
        ),
        in_specs=[
            pl.BlockSpec(memory_space=pltpu.SMEM),
            pl.BlockSpec(memory_space=pltpu.VMEM),
        ],
        out_specs=(pl.BlockSpec(memory_space=pltpu.VMEM),) * 3,
        compiler_params=params(),
        name="index_tables",
    )(me, idx_rows)
    asked = lax.all_to_all(
        ids[0, rows:].reshape(parts, cap), "res", split_axis=0, concat_axis=0, tiled=True
    ).reshape(1, parts * cap)

    edge_spec = pl.BlockSpec((block_slots, rows, edge_width), lambda i: (i, 0, 0))
    flat_spec = pl.BlockSpec((block, width), lambda i: (i, 0))
    pos_spec = pl.BlockSpec((1, LANES, pairs), lambda i: (i, 0, 0))
    any_spec = pl.BlockSpec(memory_space=pl.ANY)

    def shape(dims, kind):
        return jax.ShapeDtypeStruct(dims, kind)

    (
        act1,
        slope1,
        slope2,
        fresh,
        outgoing,
        table,
        mixed1,
        mixed2,
        low,
        expanded,
        slope_e,
        act_sum,
    ) = pl.pallas_call(
        node_kernel,
        grid=(steps,),
        in_specs=[
            edge_spec,
            pos_spec,
            whole((parts * rows, width)),
            whole((parts * rows, table_rows)),
            whole((rows, width)),
            whole((rows, width)),
            whole((1, parts * cap)),
            whole((V_ROWS, width)),
            whole(message_weight1.shape),
            whole((width, width)),
            whole((width, width)),
            any_spec,
            any_spec,
        ],
        out_specs=[
            flat_spec,
            flat_spec,
            flat_spec,
            whole((rows, width)),
            whole((parts * cap, width)),
            whole((table_rows, width)),
            whole((rows, width)),
            whole((rows, width)),
            whole((rows, width)),
            whole((rows, hidden)),
            whole((rows, hidden)),
            whole((rows, width)),
        ],
        out_shape=[
            shape((edges, width), BF16),
            shape((edges, width), BF16),
            shape((edges, width), BF16),
            shape((rows, width), BF16),
            shape((parts * cap, width), BF16),
            shape((table_rows, width), BF16),
            shape((rows, width), F32),
            shape((rows, width), F32),
            shape((rows, width), BF16),
            shape((rows, hidden), BF16),
            shape((rows, hidden), F32),
            shape((rows, width), F32),
        ],
        scratch_shapes=[
            pltpu.VMEM((table_rows, width), BF16),
            pltpu.VMEM((rows, width), F32),
            pltpu.VMEM((width, hidden), BF16),
            pltpu.VMEM((hidden, width), BF16),
            pltpu.SemaphoreType.DMA((2,)),
        ],
        compiler_params=params(),
        name="node_forward",
    )(
        edge_rows,
        pos,
        everyone,
        select,
        self_rows,
        counts,
        asked,
        vectors,
        message_weight1,
        message_weight2,
        message_weight3,
        expand_weight,
        contract_weight,
    )

    def exchange(values):
        arrived = lax.all_to_all(
            values.reshape(parts, cap, values.shape[1]),
            "res",
            split_axis=0,
            concat_axis=0,
            tiled=True,
        )
        return arrived.reshape(values.shape)

    incoming = exchange(outgoing)

    edge_pack_rows = 4 * edge_width
    edge_out, grad_partial, edge_first, edge_own, edge_away, edge_pack, edge_vec = pl.pallas_call(
        edge_kernel,
        grid=(steps,),
        in_specs=[
            edge_spec,
            edge_spec,
            pos_spec,
            whole((rows, width)),
            whole((parts * cap, width)),
            whole((rows, width)),
            whole((V_ROWS, width)),
            whole(edge_w1t.shape),
            whole((edge_width, edge_width)),
            whole((edge_width, edge_width)),
        ],
        out_specs=[
            edge_spec,
            edge_spec,
            whole((rows, edge_width)),
            whole((rows, edge_width)),
            whole((parts * cap, edge_width)),
            whole((edge_pack_rows, width)),
            whole((8, width)),
        ],
        out_shape=[
            shape((slots, rows, edge_width), BF16),
            shape((slots, rows, edge_width), F32),
            shape((rows, edge_width), F32),
            shape((rows, edge_width), F32),
            shape((parts * cap, edge_width), BF16),
            shape((edge_pack_rows, width), BF16),
            shape((8, width), F32),
        ],
        scratch_shapes=[
            pltpu.VMEM((table_rows, width), BF16),
            pltpu.VMEM((table_rows, edge_width), BF16),
            pltpu.VMEM((rows, edge_width), F32),
            pltpu.VMEM((table_rows, edge_width), F32),
            pltpu.VMEM((edge_width, edge_width), F32),
            pltpu.VMEM((edge_width, edge_width), F32),
            pltpu.VMEM((edge_width, edge_width), F32),
            pltpu.VMEM((5, rows, edge_width), F32),
        ],
        compiler_params=params(),
        name="edge_both",
    )(
        edge_rows,
        edge_cot,
        pos,
        fresh,
        incoming,
        counts,
        vectors,
        edge_w1t,
        edge_weight2,
        edge_weight3,
    )

    edge_arrived = exchange(edge_away)

    early_rows = 2 * hidden + edge_pack_rows + width + 32
    vmem = pl.BlockSpec(memory_space=pltpu.VMEM)
    early, spread, grad_mixed1 = pl.pallas_call(
        feed_kernel,
        in_specs=[vmem] * 19,
        out_specs=[vmem] * 3,
        out_shape=[
            shape((early_rows, width), BF16),
            shape((rows, width), F32),
            shape((rows, width), F32),
        ],
        compiler_params=params(),
        name="feed_backward",
    )(
        node_cotangent[0],
        edge_first,
        edge_own,
        edge_arrived,
        asked,
        counts,
        vectors,
        edge_w1t,
        mixed1,
        mixed2,
        low,
        expanded,
        slope_e,
        act_sum,
        expand_weight,
        contract_weight,
        message_weight3,
        edge_pack,
        edge_vec,
    )
    early = lax.psum(early, ("batch", "res"))

    late_rows = 2 * width + edge_width + width + 32
    edge_grad, first, own, away, late = pl.pallas_call(
        message_kernel,
        grid=(steps,),
        in_specs=[
            edge_spec,
            pos_spec,
            flat_spec,
            flat_spec,
            flat_spec,
            edge_spec,
            whole((rows, width)),
            whole((table_rows, width)),
            whole(message_weight1.shape),
            whole((width, width)),
        ],
        out_specs=[
            edge_spec,
            whole((rows, width)),
            whole((rows, width)),
            whole((parts * cap, width)),
            whole((late_rows, width)),
        ],
        out_shape=[
            shape((slots, rows, edge_width), F32),
            shape((rows, width), F32),
            shape((rows, width), F32),
            shape((parts * cap, width), BF16),
            shape((late_rows, width), BF16),
        ],
        scratch_shapes=[
            pltpu.VMEM((table_rows, width), F32),
            pltpu.VMEM((width, width), F32),
            pltpu.VMEM((edge_width, width), F32),
            pltpu.VMEM((rows, width), F32),
        ],
        compiler_params=params(),
        name="message_backward",
    )(
        edge_rows,
        pos,
        act1,
        slope1,
        slope2,
        grad_partial,
        spread,
        table,
        message_weight1,
        message_weight2,
    )
    late = lax.psum(late, ("batch", "res"))
    arrived = exchange(away)
    node_grad = pl.pallas_call(
        node_grad_kernel,
        in_specs=[vmem] * 6,
        out_specs=vmem,
        out_shape=shape((rows, width), F32),
        compiler_params=params(),
        name="node_gradient",
    )(grad_mixed1, first, own, arrived, asked, message_weight1)

    early = early.astype(F32)
    late = late.astype(F32)
    base = 0
    grad_expand = jnp.concatenate(
        [early[c * width : (c + 1) * width] for c in range(hidden // width)], axis=1
    )
    grad_contract = early[hidden : 2 * hidden]
    base = 2 * hidden
    half = width // 2
    edge_part = early[base : base + edge_pack_rows]
    grad_edge1 = jnp.concatenate(
        [
            edge_part[:edge_width],
            edge_part[edge_width : 2 * edge_width],
            edge_part[2 * edge_width : 3 * edge_width, :edge_width],
        ],
        axis=1,
    ).T
    grad_edge2 = edge_part[2 * edge_width : 3 * edge_width, half : half + edge_width]
    grad_edge3 = edge_part[3 * edge_width :, :edge_width]
    base = base + edge_pack_rows
    grad_message3 = early[base : base + width]
    vec = early[base + width :]
    chunks = hidden // width
    grad_mb3, grad_n1g, grad_n1s = vec[0], vec[1], vec[2]
    grad_eb = vec[3 : 3 + chunks].reshape(hidden)
    grad_cb, grad_n2g, grad_n2s = vec[3 + chunks], vec[4 + chunks], vec[5 + chunks]
    edge_vecs = vec[6 + chunks : 11 + chunks, :edge_width]
    grad_message1 = late[: 2 * width + edge_width]
    grad_message2 = late[2 * width + edge_width : 3 * width + edge_width]
    late_vec = late[3 * width + edge_width :]
    return (
        fresh[None],
        edge_out.transpose(1, 0, 2)[None],
        node_grad[None],
        edge_grad.transpose(1, 0, 2)[None],
        grad_message1,
        late_vec[0],
        grad_message2,
        late_vec[1],
        grad_message3,
        grad_mb3,
        grad_n1g,
        grad_n1s,
        grad_expand,
        grad_eb,
        grad_contract,
        grad_cb,
        grad_n2g,
        grad_n2s,
        grad_edge1,
        edge_vecs[0],
        grad_edge2,
        edge_vecs[1],
        grad_edge3,
        edge_vecs[2],
        edge_vecs[3],
        edge_vecs[4],
    )


def solution(mesh):
    row_spec = P("batch", "res", None)
    edge_spec = P("batch", "res", None, None)
    return jax.shard_map(
        body,
        mesh=mesh,
        in_specs=(row_spec, edge_spec, row_spec, row_spec, row_spec, edge_spec) + (P(),) * 22,
        out_specs=(row_spec, edge_spec, row_spec, edge_spec) + (P(),) * 22,
        check_vma=False,
    )
```

```python
import functools
import math

import jax
import jax.numpy as jnp
from jax import lax
from jax.experimental import pallas as pl
from jax.experimental.pallas import tpu as pltpu
from jax.sharding import PartitionSpec as P

ROW_CAP = 8
EPSILON = 1e-05
LANES = 128
VMEM_BYTES = 56 * 1024 * 1024
F32 = jnp.float32
BF16 = jnp.bfloat16

V_MB1, V_MB2, V_MB3, V_N1G, V_N1S, V_CB, V_N2G, V_N2S, V_EB = range(9)
V_EDGE = 12
V_ROWS = 24


def dot_nn(left, right):
    return lax.dot_general(left, right, (((1,), (0,)), ((), ())), preferred_element_type=F32)


def dot_nt(left, right):
    return lax.dot_general(left, right, (((1,), (1,)), ((), ())), preferred_element_type=F32)


def dot_tn(left, right):
    return lax.dot_general(left, right, (((0,), (0,)), ((), ())), preferred_element_type=F32)


def split_low(values):
    high = values.astype(BF16)
    return high, (values - high.astype(F32)).astype(BF16)


def dot_split(dot, left, right):
    high, rest = split_low(left)
    return dot(high, right) + dot(rest, right)


def dot_split_right(dot, left, right):
    high, rest = split_low(right)
    return dot(left, high) + dot(left, rest)


def gelu_pair(v):
    size = jnp.abs(v)
    den = 1.0 + (0.3275911 / math.sqrt(2.0)) * size
    t = pl.reciprocal(den, approx=True)
    t = t * (2.0 - den * t)
    e = jnp.exp2((v * v) * (-0.5 * math.log2(math.e)))
    poly = 0.5 * 1.061405429
    poly = poly * t + 0.5 * -1.453152027
    poly = poly * t + 0.5 * 1.421413741
    poly = poly * t + 0.5 * -0.284496736
    poly = poly * t + 0.5 * 0.254829592
    tail = poly * t * e
    phi_sum = jnp.where(v < 0, tail, 1.0 - tail)
    return v * phi_sum, phi_sum + (v * (1.0 / math.sqrt(2.0 * math.pi))) * e


def norm_parts(values):
    average = jnp.mean(values, axis=-1, keepdims=True)
    centred = values - average
    variance = jnp.mean(centred * centred, axis=-1, keepdims=True)
    scale = lax.rsqrt(variance + EPSILON)
    return centred * scale, scale


def norm_back(xhat, scale, gain, upstream):
    w = upstream * gain
    mean_w = jnp.mean(w, axis=-1, keepdims=True)
    mean_wx = jnp.mean(w * xhat, axis=-1, keepdims=True)
    return (w - mean_w - xhat * mean_wx) * scale


def edge_onehot(pos_ref, table_rows):
    pairs = pos_ref.shape[2]
    lane = lax.broadcasted_iota(jnp.int32, (LANES, table_rows), 1)
    return jnp.concatenate(
        [(pos_ref[0, :, p : p + 1] == lane).astype(F32).astype(BF16) for p in range(pairs)], axis=0
    )


def prepare_kernel(me_ref, idx_ref, mask_ref, *refs, parts, cap, steps, wide, narrow):
    wide_refs = refs[:wide]
    narrow_refs = refs[wide : wide + narrow]
    pos_ref, select_ref, ids_ref, count_ref, vec_ref = refs[wide + narrow :]
    rows, width = count_ref.shape
    total = rows * parts
    table = rows + parts * cap
    me = me_ref[0]
    pair_rows = idx_ref.shape[0]
    row = lax.broadcasted_iota(jnp.int32, (total, LANES), 0)
    distance = row // rows
    within = row - distance * rows
    owner = jnp.where(distance > me, me - distance + parts, me - distance)
    residue = owner * rows + within
    hits = jnp.zeros((total, LANES), F32)
    for j in range(pair_rows):
        hits = jnp.where(idx_ref[j : j + 1, :] == residue, 1.0, hits)
    hit = jnp.max(hits, axis=1, keepdims=True)
    own = distance == 0
    wanted = jnp.where(own, 0.0, jnp.broadcast_to(hit, (total, LANES)))
    low_row = lax.broadcasted_iota(jnp.int32, (rows, rows), 0)
    low_col = lax.broadcasted_iota(jnp.int32, (rows, rows), 1)
    lower = (low_col <= low_row).astype(F32).astype(BF16)
    wanted_low = wanted.astype(BF16)
    place = jnp.concatenate(
        [dot_nn(lower, wanted_low[o * rows : (o + 1) * rows]) for o in range(parts)], axis=0
    )
    place = jnp.clip(place - 1.0, 0.0, cap - 1.0)
    pos = jnp.where(own, within.astype(F32), (rows + distance * cap).astype(F32) + place)
    picked = [
        jnp.sum(jnp.where(idx_ref[j : j + 1, :] == residue, pos, 0.0), axis=0, keepdims=True)
        for j in range(pair_rows)
    ]
    picked.append(jnp.zeros((LANES - pair_rows, LANES), F32))
    turned = jnp.concatenate(picked, axis=0).T.astype(jnp.int32)
    per = pair_rows // steps
    for s in range(steps):
        pos_ref[s] = turned[:, s * per : (s + 1) * per]
    lane = lax.broadcasted_iota(jnp.int32, (total, table), 1).astype(F32)
    live = jnp.where(own, 1.0, wanted)
    chosen = jnp.where(lane == pos[:, :1], jnp.broadcast_to(live[:, :1], (total, table)), 0.0)
    select_ref[...] = chosen.astype(BF16)
    asked_place = (owner * cap).astype(F32) + place
    lane = lax.broadcasted_iota(jnp.int32, (total, parts * cap), 1).astype(F32)
    asked_row = (wanted * within.astype(F32))[:, :1]
    ids = jnp.where(lane == asked_place[:, :1], asked_row, 0.0)
    ids_ref[...] = jnp.sum(ids, axis=0, keepdims=True).astype(jnp.int32)
    ones = jnp.ones((mask_ref.shape[0], width), F32).astype(BF16)
    count_ref[...] = dot_tn(mask_ref[...].astype(F32).astype(BF16), ones)
    vec_ref[...] = jnp.zeros_like(vec_ref)
    at = 0
    for ref in wide_refs:
        for c in range(ref.shape[0] // width):
            part = ref[c * width : (c + 1) * width]
            vec_ref[at : at + 1, :] = part.astype(F32).reshape(1, width)
            at += 1
    for ref in narrow_refs:
        vec_ref[at : at + 1, : ref.shape[0]] = ref[...].astype(F32).reshape(1, ref.shape[0])
        at += 1


def stack_pieces(refs, cap):
    pieces = [jnp.zeros((cap, refs[0].shape[1]), F32)] + [ref[...].astype(F32) for ref in refs]
    return jnp.concatenate(pieces, axis=0)


def store_pieces(refs, values, cap):
    for d, ref in enumerate(refs, start=1):
        ref[...] = values[d * cap : (d + 1) * cap].astype(BF16)


def node_kernel(edge_ref, pos_ref, select_ref, self_ref, count_ref, asked_ref, vec_ref, *refs, parts):
    others = parts - 1
    away_refs = refs[:others]
    w1_ref, w2_ref, w3_ref, expand_hbm, contract_hbm = refs[others : others + 5]
    outgoing_refs = refs[others + 5 : 2 * others + 5]
    (
        act1_ref,
        slope1_ref,
        slope2_ref,
        fresh_ref,
        table_ref,
        mixed1_ref,
        mixed2_ref,
        low_ref,
        slope_e_ref,
        act_sum_ref,
        proj_ref,
        self_pre_ref,
        expand_ref,
        contract_ref,
        sems,
    ) = refs[2 * others + 5 :]
    step = pl.program_id(0)
    last = pl.num_programs(0) - 1
    rows, width = self_ref.shape
    slots = edge_ref.shape[0]
    edge_width = edge_ref.shape[2]
    table_rows = table_ref.shape[0]
    expand_copy = pltpu.make_async_copy(expand_hbm, expand_ref, sems.at[0])
    contract_copy = pltpu.make_async_copy(contract_hbm, contract_ref, sems.at[1])

    @pl.when(step == 0)
    def _():
        expand_copy.start()
        contract_copy.start()
        table = dot_tn(select_ref[:rows], self_ref[...])
        for d, ref in enumerate(away_refs, start=1):
            table = table + dot_tn(select_ref[d * rows : (d + 1) * rows], ref[...])
        table = table.astype(BF16)
        table_ref[...] = table
        proj_ref[...] = dot_nn(table, w1_ref[width : 2 * width]).astype(BF16)
        self_pre_ref[...] = (
            dot_nn(self_ref[...], w1_ref[:width]) + vec_ref[V_MB1 : V_MB1 + 1, :]
        )
        act_sum_ref[...] = jnp.zeros_like(act_sum_ref)

    onehot = edge_onehot(pos_ref, table_rows)
    features = edge_ref[...].reshape(slots * rows, edge_width)
    pre1 = dot_nn(features, w1_ref[2 * width :]) + dot_nn(onehot, proj_ref[...])
    self_pre = self_pre_ref[...]
    act1 = []
    for k in range(slots):
        part = pl.ds(k * rows, rows)
        act, slope = gelu_pair(pre1[k * rows : (k + 1) * rows] + self_pre)
        act = act.astype(BF16)
        act1.append(act)
        act1_ref[part, :] = act
        slope1_ref[part, :] = slope.astype(BF16)
    pre2 = dot_nn(jnp.concatenate(act1, axis=0), w2_ref[...])
    bias2 = vec_ref[V_MB2 : V_MB2 + 1, :]
    act_sum = act_sum_ref[...]
    counts = count_ref[...]
    for k in range(slots):
        act, slope = gelu_pair(pre2[k * rows : (k + 1) * rows] + bias2)
        valid = counts > (step * slots + k).astype(F32)
        act_sum = act_sum + jnp.where(valid, act.astype(BF16).astype(F32), 0.0)
        slope2_ref[pl.ds(k * rows, rows), :] = jnp.where(valid, slope, 0.0).astype(BF16)
    act_sum_ref[...] = act_sum

    @pl.when(step == last)
    def _():
        summed = dot_split(dot_nn, act_sum_ref[...], w3_ref[...])
        summed = summed + counts * vec_ref[V_MB3 : V_MB3 + 1, :]
        mixed1 = self_ref[...].astype(F32) + summed / counts
        mixed1_ref[...] = mixed1
        xhat1, _ = norm_parts(mixed1)
        updated = xhat1 * vec_ref[V_N1G : V_N1G + 1, :] + vec_ref[V_N1S : V_N1S + 1, :]
        low = updated.astype(BF16)
        low_ref[...] = low
        expand_copy.wait()
        contract_copy.wait()
        mixed2 = updated + vec_ref[V_CB : V_CB + 1, :]
        for c in range(expand_ref.shape[1] // width):
            cols = slice(c * width, (c + 1) * width)
            pre = dot_nn(low, expand_ref[:, cols]) + vec_ref[V_EB + c : V_EB + c + 1, :]
            act, slope = gelu_pair(pre)
            act = act.astype(BF16)
            slope_e_ref[:, cols] = slope
            mixed2 = mixed2 + dot_nn(act, contract_ref[cols, :])
        mixed2_ref[...] = mixed2
        xhat2, _ = norm_parts(mixed2)
        fresh = (xhat2 * vec_ref[V_N2G : V_N2G + 1, :] + vec_ref[V_N2S : V_N2S + 1, :]).astype(BF16)
        fresh_ref[...] = fresh
        asked = asked_onehot(asked_ref, rows)
        store_pieces(outgoing_refs, dot_tn(asked, fresh), ROW_CAP)


def asked_onehot(asked_ref, rows):
    row = lax.broadcasted_iota(jnp.int32, (rows, asked_ref.shape[1]), 0)
    return (asked_ref[...] == row).astype(F32).astype(BF16)


def edge_kernel(edge_ref, cot_ref, pos_ref, fresh_ref, count_ref, vec_ref, *refs, parts):
    others = parts - 1
    incoming_refs = refs[:others]
    w1t_ref, w2_ref, w3_ref = refs[others : others + 3]
    away_refs = refs[others + 3 : 2 * others + 3]
    (
        out_ref,
        grad_ref,
        first_ref,
        own_ref,
        pack_ref,
        vec_out_ref,
        table_ref,
        proj_ref,
        self_pre_ref,
        back_ref,
        dw3_ref,
        dw2_ref,
        dw1_ref,
        sums_ref,
    ) = refs[2 * others + 3 :]
    step = pl.program_id(0)
    last = pl.num_programs(0) - 1
    rows, width = fresh_ref.shape
    slots, _, edge_width = edge_ref.shape
    block = slots * rows
    table_rows = table_ref.shape[0]
    own_t = w1t_ref[:, :width]
    nbr_t = w1t_ref[:, width : 2 * width]
    feat_t = w1t_ref[:, 2 * width :]

    def vector(i):
        return vec_ref[V_EDGE + i : V_EDGE + i + 1, :edge_width]

    @pl.when(step == 0)
    def _():
        table_ref[:rows] = fresh_ref[...]
        table_ref[rows:] = stack_pieces(incoming_refs, ROW_CAP).astype(BF16)
        proj_ref[...] = dot_nt(table_ref[...], nbr_t).astype(BF16)
        self_pre_ref[...] = dot_nt(fresh_ref[...], own_t) + vector(0)
        for ref in (back_ref, dw3_ref, dw2_ref, dw1_ref, sums_ref, first_ref):
            ref[...] = jnp.zeros_like(ref)

    def flat(values):
        return values.reshape(block, edge_width)

    def deep(values):
        return values.reshape(slots, rows, edge_width)

    onehot = edge_onehot(pos_ref, table_rows)
    features = flat(edge_ref[...])
    pre1 = dot_nt(features, feat_t) + dot_nn(onehot, proj_ref[...])
    pre1 = deep(pre1) + self_pre_ref[...][None]
    act1, slope1 = gelu_pair(flat(pre1))
    act1 = act1.astype(BF16)
    pre2 = dot_nn(act1, w2_ref[...]) + vector(1)
    act2, slope2 = gelu_pair(pre2)
    act2 = act2.astype(BF16)
    mixed3 = features.astype(F32) + (dot_nn(act2, w3_ref[...]) + vector(2))
    xhat, scale = norm_parts(mixed3)
    gain = vector(3)
    slot = lax.broadcasted_iota(jnp.int32, (slots, rows, edge_width), 0) + step * slots
    valid = count_ref[...][None, :, :edge_width] > slot.astype(F32)
    out_ref[...] = jnp.where(valid, deep(xhat * gain + vector(4)), 0.0).astype(BF16)
    upstream = flat(jnp.where(valid, cot_ref[...].astype(F32), 0.0))
    sums_ref[3] += jnp.sum(deep(upstream * xhat), axis=0)
    sums_ref[4] += jnp.sum(deep(upstream), axis=0)
    grad_mixed = norm_back(xhat, scale, gain, upstream)
    grad_delta = grad_mixed.astype(BF16)
    dw3_ref[...] += dot_tn(act2, grad_delta)
    sums_ref[2] += jnp.sum(deep(grad_delta.astype(F32)), axis=0)
    grad2 = (dot_nt(grad_delta, w3_ref[...]) * slope2).astype(BF16)
    dw2_ref[...] += dot_tn(act1, grad2)
    sums_ref[1] += jnp.sum(deep(grad2.astype(F32)), axis=0)
    grad1 = (dot_nt(grad2, w2_ref[...]) * slope1).astype(BF16)
    dw1_ref[...] += dot_tn(grad1, features)
    first_ref[...] += jnp.sum(deep(grad1.astype(F32)), axis=0)
    back_ref[...] += dot_tn(onehot, grad1)
    grad_ref[...] = deep(grad_mixed + dot_nn(grad1, feat_t))

    @pl.when(step == last)
    def _():
        first = first_ref[...]
        back = back_ref[...]
        own_ref[...] = back[:rows]
        store_pieces(away_refs, back[rows:], ROW_CAP)
        first_high, first_rest = split_low(first)
        back_high, back_rest = split_low(back)
        own_grad = dot_tn(first_high, fresh_ref[...]) + dot_tn(first_rest, fresh_ref[...])
        nbr_grad = dot_tn(back_high, table_ref[...]) + dot_tn(back_rest, table_ref[...])
        pack_ref[:edge_width, :] = own_grad.astype(BF16)
        pack_ref[edge_width : 2 * edge_width, :] = nbr_grad.astype(BF16)
        pad = jnp.zeros((edge_width, width // 2 - edge_width), BF16)
        third = [dw1_ref[...].astype(BF16), pad, dw2_ref[...].astype(BF16), pad]
        pack_ref[2 * edge_width : 3 * edge_width, :] = jnp.concatenate(third, axis=1)
        fourth = [dw3_ref[...].astype(BF16), pad, jnp.zeros((edge_width, width // 2), BF16)]
        pack_ref[3 * edge_width :, :] = jnp.concatenate(fourth, axis=1)
        vec_out_ref[...] = jnp.zeros_like(vec_out_ref)
        vec_out_ref[0:1, :edge_width] = jnp.sum(first, axis=0, keepdims=True)
        for i in range(1, 5):
            vec_out_ref[i : i + 1, :edge_width] = jnp.sum(sums_ref[i], axis=0, keepdims=True)


def feed_kernel(
    cot_ref,
    first_ref,
    own_ref,
    asked_ref,
    count_ref,
    vec_ref,
    w1t_ref,
    mixed1_ref,
    mixed2_ref,
    slope_ref,
    act_sum_ref,
    expand_ref,
    contract_ref,
    w3_ref,
    edge_vec_ref,
    *refs,
    parts,
):
    arrived_refs = refs[: parts - 1]
    pack_ref, contracted_ref, spread_ref, grad_mixed1_ref = refs[parts - 1 :]
    rows, width = cot_ref.shape
    hidden = expand_ref.shape[1]
    own_t = w1t_ref[:, :width]
    nbr_t = w1t_ref[:, width : 2 * width]
    counts = count_ref[...]

    def vector(i):
        return vec_ref[i : i + 1, :]

    def total(values):
        return jnp.sum(values.astype(F32), axis=0, keepdims=True)

    arrived = stack_pieces(arrived_refs, ROW_CAP).astype(BF16)
    back = own_ref[...] + dot_nn(asked_onehot(asked_ref, rows), arrived)
    grad_fresh = (
        cot_ref[...].astype(F32)
        + dot_split(dot_nn, first_ref[...], own_t)
        + dot_split(dot_nn, back, nbr_t)
    )
    xhat2, scale2 = norm_parts(mixed2_ref[...])
    grad_mixed2 = norm_back(xhat2, scale2, vector(V_N2G), grad_fresh)
    grad_contracted = grad_mixed2.astype(BF16)
    contracted_ref[...] = grad_contracted
    grad_updated = grad_mixed2
    for c in range(hidden // width):
        cols = slice(c * width, (c + 1) * width)
        pre = dot_nt(grad_contracted, contract_ref[cols, :]) * slope_ref[:, cols]
        grad_updated = grad_updated + dot_nt(pre.astype(BF16), expand_ref[:, cols])
    xhat1, scale1 = norm_parts(mixed1_ref[...])
    grad_mixed1 = norm_back(xhat1, scale1, vector(V_N1G), grad_updated)
    grad_mixed1_ref[...] = grad_mixed1
    grad_message = (grad_mixed1 / counts).astype(BF16)
    spread_ref[...] = dot_nt(grad_message, w3_ref[...])
    pack_ref[:width, :] = dot_split(dot_tn, act_sum_ref[...], grad_message).astype(BF16)
    vectors = [
        total(counts * grad_message.astype(F32)),
        total(grad_updated * xhat1),
        total(grad_updated),
        total(grad_fresh * xhat2),
        total(grad_fresh),
        edge_vec_ref[...],
    ]
    vectors = jnp.concatenate(vectors, axis=0)
    vectors = jnp.concatenate(
        [vectors, jnp.zeros((pack_ref.shape[0] - width - vectors.shape[0], width), F32)], axis=0
    )
    pack_ref[width:, :] = vectors.astype(BF16)


def feed_weight_kernel(
    low_a_ref,
    low_b_ref,
    grad_a_ref,
    grad_b_ref,
    expand_ref,
    bias_ref,
    contract_ref,
    expand_out_ref,
    contract_out_ref,
    bias_out_ref,
    last_bias_ref,
    turned_ref,
):
    chunk = pl.program_id(0)
    step = pl.program_id(1)
    units = expand_ref.shape[1]
    weight_t = expand_ref[...].T
    bias = jnp.broadcast_to(bias_ref[0:1, :], (8, units)).T[:, :1]
    turned = jnp.zeros((units, low_a_ref.shape[1]), F32)
    contracted = jnp.zeros((units, low_a_ref.shape[1]), F32)
    sums = jnp.zeros((8, units), F32)
    ones = jnp.ones((8, low_a_ref.shape[0]), F32).astype(BF16)
    for low_ref, grad_ref in ((low_a_ref, grad_a_ref), (low_b_ref, grad_b_ref)):
        act, slope = gelu_pair(dot_nt(weight_t, low_ref[...]) + bias)
        contracted = contracted + dot_nn(act.astype(BF16), grad_ref[...])
        pre = (dot_nt(contract_ref[...], grad_ref[...]) * slope).astype(BF16)
        turned = turned + dot_nn(pre, low_ref[...])
        sums = sums + dot_nt(ones, pre)

    @pl.when(step == 0)
    def _():
        turned_ref[...] = turned
        contract_out_ref[...] = contracted
        bias_out_ref[...] = sums

    @pl.when(step > 0)
    def _():
        turned_ref[...] += turned
        contract_out_ref[...] += contracted
        bias_out_ref[...] += sums

    @pl.when(step == pl.num_programs(1) - 1)
    def _():
        expand_out_ref[...] = turned_ref[...].T

    @pl.when((chunk == 0) & (step == 0))
    def _():
        last_bias_ref[...] = jnp.zeros_like(last_bias_ref)

    @pl.when(chunk == 0)
    def _():
        last_bias_ref[...] += dot_nn(ones, grad_a_ref[...]) + dot_nn(ones, grad_b_ref[...])


def message_kernel(
    edge_ref,
    pos_ref,
    act1_ref,
    slope1_ref,
    slope2_ref,
    partial_ref,
    spread_ref,
    table_ref,
    w1_ref,
    w2_ref,
    *refs,
    parts,
):
    away_refs = refs[: parts - 1]
    (
        grad_ref,
        first_ref,
        own_ref,
        pack_ref,
        back_ref,
        dw2_ref,
        dw1_ref,
        bias2_ref,
    ) = refs[parts - 1 :]
    step = pl.program_id(0)
    last = pl.num_programs(0) - 1
    slots, rows, edge_width = edge_ref.shape
    width = act1_ref.shape[1]
    block = slots * rows
    table_rows = table_ref.shape[0]

    @pl.when(step == 0)
    def _():
        for ref in (back_ref, dw2_ref, dw1_ref, bias2_ref, first_ref):
            ref[...] = jnp.zeros_like(ref)

    spread = spread_ref[...]
    grad2 = []
    bias2 = bias2_ref[...]
    for k in range(slots):
        part = (spread * slope2_ref[pl.ds(k * rows, rows), :].astype(F32)).astype(BF16)
        bias2 = bias2 + part.astype(F32)
        grad2.append(part)
    bias2_ref[...] = bias2
    grad2 = jnp.concatenate(grad2, axis=0)
    dw2_ref[...] += dot_tn(act1_ref[...], grad2)
    grad1 = (dot_nt(grad2, w2_ref[...]) * slope1_ref[...].astype(F32)).astype(BF16)
    first_ref[...] += jnp.sum(grad1.astype(F32).reshape(slots, rows, width), axis=0)
    onehot = edge_onehot(pos_ref, table_rows)
    back_ref[...] += dot_tn(onehot, grad1)
    features = edge_ref[...].reshape(block, edge_width)
    dw1_ref[...] += dot_tn(features, grad1)
    grad_ref[...] = partial_ref[...] + dot_nt(grad1, w1_ref[2 * width :]).reshape(
        slots, rows, edge_width
    )

    @pl.when(step == last)
    def _():
        first = first_ref[...]
        back = back_ref[...]
        own_ref[...] = back[:rows]
        store_pieces(away_refs, back[rows:], ROW_CAP)
        pack_ref[:width, :] = dot_split_right(dot_tn, table_ref[:rows], first).astype(BF16)
        pack_ref[width : 2 * width, :] = dot_split_right(dot_tn, table_ref[...], back).astype(BF16)
        base = 2 * width
        pack_ref[base : base + edge_width, :] = dw1_ref[...].astype(BF16)
        base = base + edge_width
        pack_ref[base : base + width, :] = dw2_ref[...].astype(BF16)
        base = base + width
        vectors = jnp.concatenate(
            [
                jnp.sum(first, axis=0, keepdims=True),
                jnp.sum(bias2_ref[...], axis=0, keepdims=True),
                jnp.zeros((pack_ref.shape[0] - base - 2, width), F32),
            ],
            axis=0,
        )
        pack_ref[base:, :] = vectors.astype(BF16)


def node_grad_kernel(grad_ref, first_ref, own_ref, asked_ref, w1_ref, *refs):
    arrived_refs, out_ref = refs[:-1], refs[-1]
    rows, width = grad_ref.shape
    arrived = stack_pieces(arrived_refs, ROW_CAP).astype(BF16)
    back = own_ref[...] + dot_nn(asked_onehot(asked_ref, rows), arrived)
    out_ref[...] = (
        grad_ref[...]
        + dot_split(dot_nt, first_ref[...], w1_ref[:width])
        + dot_split(dot_nt, back, w1_ref[width : 2 * width])
    )


def unpack_kernel(edge_ref, feed_ref, late_ref, bias_ref, last_bias_ref, *refs):
    (
        message1_ref,
        message1_bias_ref,
        message2_ref,
        message2_bias_ref,
        message3_ref,
        message3_bias_ref,
        gain1_ref,
        shift1_ref,
        expand_bias_ref,
        contract_bias_ref,
        gain2_ref,
        shift2_ref,
        edge1_ref,
        edge1_bias_ref,
        edge2_ref,
        edge2_bias_ref,
        edge3_ref,
        edge3_bias_ref,
        gain3_ref,
        shift3_ref,
    ) = refs
    width = late_ref.shape[1]
    edge_width = edge2_ref.shape[0]
    half = width // 2
    first_rows = message1_ref.shape[0]
    message1_ref[...] = late_ref[:first_rows].astype(F32)
    message2_ref[...] = late_ref[first_rows : first_rows + width].astype(F32)
    late_vectors = late_ref[first_rows + width :].astype(F32)
    message1_bias_ref[...] = late_vectors[0]
    message2_bias_ref[...] = late_vectors[1]
    message3_ref[...] = feed_ref[:width].astype(F32)
    vectors = feed_ref[width:].astype(F32)
    targets = (message3_bias_ref, gain1_ref, shift1_ref, gain2_ref, shift2_ref)
    for i, ref in enumerate(targets):
        ref[...] = vectors[i]
    targets = (edge1_bias_ref, edge2_bias_ref, edge3_bias_ref, gain3_ref, shift3_ref)
    for i, ref in enumerate(targets):
        ref[...] = vectors[5 + i, :edge_width]
    edge1_ref[:, :width] = edge_ref[:edge_width].astype(F32)
    edge1_ref[:, width : 2 * width] = edge_ref[edge_width : 2 * edge_width].astype(F32)
    third = edge_ref[2 * edge_width : 3 * edge_width].astype(F32)
    edge1_ref[:, 2 * width :] = third[:, :edge_width]
    edge2_ref[...] = third[:, half : half + edge_width]
    edge3_ref[...] = edge_ref[3 * edge_width :, :edge_width].astype(F32)
    expand_bias_ref[...] = bias_ref[0]
    contract_bias_ref[...] = last_bias_ref[0]


class Places:
    def __init__(self):
        self.batch = lax.axis_size("batch")
        self.res = lax.axis_size("res")
        self.cores = 2
        self.y = self.batch // self.cores
        self.x = 1 << ((self.res.bit_length() - 1) // 2)
        self.z = self.res // self.x

    def shifted(self, dy=0, dcore=0, dz=0, dx=0):
        pairs = []
        for b in range(self.batch):
            for r in range(self.res):
                y, core = divmod(b, self.cores)
                z, x = divmod(r, self.x)
                other_b = (y + dy) % self.y * self.cores + (core + dcore) % self.cores
                other_r = (z + dz) % self.z * self.x + (x + dx) % self.x
                pairs.append((b * self.res + r, other_b * self.res + other_r))
        return pairs

    def move(self, values, **shift):
        return lax.ppermute(values, ("batch", "res"), self.shifted(**shift))

    def ring(self, values, distance):
        pairs = [(i, (i + distance) % self.res) for i in range(self.res)]
        return lax.ppermute(values, "res", pairs)

    def gather(self, values):
        parts = [values] + [self.move(values, dz=d) for d in range(1, self.z)]
        column = jnp.concatenate(parts, axis=0)
        parts = [column]
        for dy in range(self.y):
            for dx in range(self.x):
                if dy or dx:
                    parts.append(self.move(column, dy=dy, dx=dx))
        side = jnp.concatenate(parts, axis=0)
        return side, self.move(side, dcore=1)


def whole(shape):
    return pl.BlockSpec(shape, lambda *_: (0,) * len(shape))


def params():
    return pltpu.CompilerParams(vmem_limit_bytes=VMEM_BYTES)


def cost(microseconds):
    return pl.CostEstimate(
        flops=int(microseconds * 1.15e9),
        bytes_accessed=int(microseconds * 3.69e6),
        transcendentals=0,
    )


def body(
    node_states,
    edge_states,
    neighbour_index,
    edge_mask,
    node_cotangent,
    edge_cotangent,
    message_weight1,
    message_bias1,
    message_weight2,
    message_bias2,
    message_weight3,
    message_bias3,
    norm1_gain,
    norm1_shift,
    expand_weight,
    expand_bias,
    contract_weight,
    contract_bias,
    norm2_gain,
    norm2_shift,
    edge_weight1,
    edge_bias1,
    edge_weight2,
    edge_bias2,
    edge_weight3,
    edge_bias3,
    norm3_gain,
    norm3_shift,
):
    self_rows = node_states[0]
    rows, width = self_rows.shape
    slots = neighbour_index.shape[2]
    edge_width = edge_states.shape[3]
    hidden = expand_weight.shape[1]
    edges = rows * slots
    parts = lax.axis_size("res")
    cap = ROW_CAP
    table_rows = rows + parts * cap
    steps = 5
    block_slots = slots // steps
    block = block_slots * rows
    pairs = block // LANES

    places = Places()
    others = range(1, parts)
    everyone = [places.ring(self_rows, d) for d in others]
    me = lax.axis_index("res").astype(jnp.int32).reshape(1)
    edge_rows = edge_states[0].transpose(1, 0, 2)
    edge_cot = edge_cotangent[0].transpose(1, 0, 2)
    idx_rows = neighbour_index[0].T.reshape(edges // LANES, LANES)
    edge_w1t = edge_weight1.T
    wide = (
        message_bias1,
        message_bias2,
        message_bias3,
        norm1_gain,
        norm1_shift,
        contract_bias,
        norm2_gain,
        norm2_shift,
        expand_bias,
    )
    narrow = (edge_bias1, edge_bias2, edge_bias3, norm3_gain, norm3_shift)
    vmem = pl.BlockSpec(memory_space=pltpu.VMEM)

    def shape(dims, kind):
        return jax.ShapeDtypeStruct(dims, kind)

    pos, select, ids, counts, vectors = pl.pallas_call(
        functools.partial(
            prepare_kernel, parts=parts, cap=cap, steps=steps, wide=len(wide), narrow=len(narrow)
        ),
        out_shape=(
            shape((steps, LANES, pairs), jnp.int32),
            shape((parts * rows, table_rows), BF16),
            shape((1, parts * cap), jnp.int32),
            shape((rows, width), F32),
            shape((V_ROWS, width), F32),
        ),
        in_specs=[pl.BlockSpec(memory_space=pltpu.SMEM)] + [vmem] * (2 + len(wide) + len(narrow)),
        out_specs=(vmem,) * 5,
        compiler_params=params(),
        cost_estimate=cost(6),
        name="prepare",
    )(me, idx_rows, edge_mask[0].T, *wide, *narrow)
    asked = lax.all_to_all(
        ids.reshape(parts, cap), "res", split_axis=0, concat_axis=0, tiled=True
    )
    asked = lax.dynamic_slice_in_dim(jnp.concatenate([asked, asked], axis=0), me[0], parts, axis=0)
    asked = asked.reshape(1, parts * cap)

    edge_spec = pl.BlockSpec((block_slots, rows, edge_width), lambda i: (i, 0, 0))
    flat_spec = pl.BlockSpec((block, width), lambda i: (i, 0))
    pos_spec = pl.BlockSpec((1, LANES, pairs), lambda i: (i, 0, 0))
    any_spec = pl.BlockSpec(memory_space=pl.ANY)
    node_spec = whole((rows, width))
    piece_specs = [whole((cap, width))] * (parts - 1)
    piece_shapes = [shape((cap, width), BF16)] * (parts - 1)
    thin_specs = [whole((cap, edge_width))] * (parts - 1)
    thin_shapes = [shape((cap, edge_width), BF16)] * (parts - 1)

    results = pl.pallas_call(
        functools.partial(node_kernel, parts=parts),
        grid=(steps,),
        in_specs=[
            edge_spec,
            pos_spec,
            whole((parts * rows, table_rows)),
            node_spec,
            node_spec,
            whole((1, parts * cap)),
            whole((V_ROWS, width)),
            *[node_spec] * (parts - 1),
            whole(message_weight1.shape),
            whole((width, width)),
            whole((width, width)),
            any_spec,
            any_spec,
        ],
        out_specs=[
            *piece_specs,
            flat_spec,
            flat_spec,
            flat_spec,
            node_spec,
            whole((table_rows, width)),
            node_spec,
            node_spec,
            node_spec,
            whole((rows, hidden)),
            node_spec,
        ],
        out_shape=[
            *piece_shapes,
            shape((edges, width), BF16),
            shape((edges, width), BF16),
            shape((edges, width), BF16),
            shape((rows, width), BF16),
            shape((table_rows, width), BF16),
            shape((rows, width), F32),
            shape((rows, width), F32),
            shape((rows, width), BF16),
            shape((rows, hidden), F32),
            shape((rows, width), F32),
        ],
        scratch_shapes=[
            pltpu.VMEM((table_rows, width), BF16),
            pltpu.VMEM((rows, width), F32),
            pltpu.VMEM((width, hidden), BF16),
            pltpu.VMEM((hidden, width), BF16),
            pltpu.SemaphoreType.DMA((2,)),
        ],
        compiler_params=params(),
        cost_estimate=cost(26),
        name="node_forward",
    )(
        edge_rows,
        pos,
        select,
        self_rows,
        counts,
        asked,
        vectors,
        *everyone,
        message_weight1,
        message_weight2,
        message_weight3,
        expand_weight,
        contract_weight,
    )
    outgoing = results[: parts - 1]
    act1, slope1, slope2, fresh, table, mixed1, mixed2, low, slope_e, act_sum = results[parts - 1 :]
    incoming = [places.ring(outgoing[d - 1], d) for d in others]
    low_a, low_b = places.gather(low)

    edge_pack_rows = 4 * edge_width
    results = pl.pallas_call(
        functools.partial(edge_kernel, parts=parts),
        grid=(steps,),
        in_specs=[
            edge_spec,
            edge_spec,
            pos_spec,
            node_spec,
            node_spec,
            whole((V_ROWS, width)),
            *piece_specs,
            whole(edge_w1t.shape),
            whole((edge_width, edge_width)),
            whole((edge_width, edge_width)),
        ],
        out_specs=[
            *thin_specs,
            edge_spec,
            edge_spec,
            whole((rows, edge_width)),
            whole((rows, edge_width)),
            whole((edge_pack_rows, width)),
            whole((8, width)),
        ],
        out_shape=[
            *thin_shapes,
            shape((slots, rows, edge_width), BF16),
            shape((slots, rows, edge_width), F32),
            shape((rows, edge_width), F32),
            shape((rows, edge_width), F32),
            shape((edge_pack_rows, width), BF16),
            shape((8, width), F32),
        ],
        scratch_shapes=[
            pltpu.VMEM((table_rows, width), BF16),
            pltpu.VMEM((table_rows, edge_width), BF16),
            pltpu.VMEM((rows, edge_width), F32),
            pltpu.VMEM((table_rows, edge_width), F32),
            pltpu.VMEM((edge_width, edge_width), F32),
            pltpu.VMEM((edge_width, edge_width), F32),
            pltpu.VMEM((edge_width, edge_width), F32),
            pltpu.VMEM((5, rows, edge_width), F32),
        ],
        compiler_params=params(),
        cost_estimate=cost(21),
        name="edge_both",
    )(
        edge_rows,
        edge_cot,
        pos,
        fresh,
        counts,
        vectors,
        *incoming,
        edge_w1t,
        edge_weight2,
        edge_weight3,
    )
    edge_away = results[: parts - 1]
    edge_out, grad_partial, edge_first, edge_own, edge_pack, edge_vec = results[parts - 1 :]
    edge_arrived = [places.ring(edge_away[d - 1], -d) for d in others]

    feed_rows = width + 16
    feed_pack, grad_contracted, spread, grad_mixed1 = pl.pallas_call(
        functools.partial(feed_kernel, parts=parts),
        in_specs=[vmem] * (15 + parts - 1),
        out_specs=[vmem] * 4,
        out_shape=[
            shape((feed_rows, width), BF16),
            shape((rows, width), BF16),
            shape((rows, width), F32),
            shape((rows, width), F32),
        ],
        compiler_params=params(),
        cost_estimate=cost(7),
        name="feed_backward",
    )(
        node_cotangent[0],
        edge_first,
        edge_own,
        asked,
        counts,
        vectors,
        edge_w1t,
        mixed1,
        mixed2,
        slope_e,
        act_sum,
        expand_weight,
        contract_weight,
        message_weight3,
        edge_vec,
        *edge_arrived,
    )
    grad_a, grad_b = places.gather(grad_contracted)

    late_rows = 2 * width + edge_width + width + 32
    results = pl.pallas_call(
        functools.partial(message_kernel, parts=parts),
        grid=(steps,),
        in_specs=[
            edge_spec,
            pos_spec,
            flat_spec,
            flat_spec,
            flat_spec,
            edge_spec,
            node_spec,
            whole((table_rows, width)),
            whole(message_weight1.shape),
            whole((width, width)),
        ],
        out_specs=[
            *piece_specs,
            edge_spec,
            node_spec,
            node_spec,
            whole((late_rows, width)),
        ],
        out_shape=[
            *piece_shapes,
            shape((slots, rows, edge_width), F32),
            shape((rows, width), F32),
            shape((rows, width), F32),
            shape((late_rows, width), BF16),
        ],
        scratch_shapes=[
            pltpu.VMEM((table_rows, width), F32),
            pltpu.VMEM((width, width), F32),
            pltpu.VMEM((edge_width, width), F32),
            pltpu.VMEM((rows, width), F32),
        ],
        compiler_params=params(),
        cost_estimate=cost(14),
        name="message_backward",
    )(
        edge_rows,
        pos,
        act1,
        slope1,
        slope2,
        grad_partial,
        spread,
        table,
        message_weight1,
        message_weight2,
    )
    away = results[: parts - 1]
    edge_grad, first, own, late = results[parts - 1 :]
    edge_sum, feed_sum, late_sum = lax.psum((edge_pack, feed_pack, late), ("batch", "res"))
    arrived = [places.ring(away[d - 1], -d) for d in others]
    node_grad = pl.pallas_call(
        node_grad_kernel,
        in_specs=[vmem] * (5 + parts - 1),
        out_specs=vmem,
        out_shape=shape((rows, width), F32),
        compiler_params=params(),
        cost_estimate=cost(3),
        name="node_gradient",
    )(grad_mixed1, first, own, asked, message_weight1, *arrived)

    units = 256
    half_rows = low_a.shape[0]
    row_block = min(half_rows, 1024)
    low_spec = pl.BlockSpec((row_block, width), lambda c, r: (r, 0))
    bias_row = vectors[V_EB : V_EB + hidden // width].reshape(1, hidden)
    grad_expand, grad_contract, expand_bias_sum, contract_bias_sum = pl.pallas_call(
        feed_weight_kernel,
        grid=(hidden // units, half_rows // row_block),
        in_specs=[
            low_spec,
            low_spec,
            low_spec,
            low_spec,
            pl.BlockSpec((width, units), lambda c, r: (0, c)),
            pl.BlockSpec((1, units), lambda c, r: (0, c)),
            pl.BlockSpec((units, width), lambda c, r: (c, 0)),
        ],
        out_specs=[
            pl.BlockSpec((width, units), lambda c, r: (0, c)),
            pl.BlockSpec((units, width), lambda c, r: (c, 0)),
            pl.BlockSpec((8, units), lambda c, r: (0, c)),
            whole((8, width)),
        ],
        out_shape=[
            shape((width, hidden), F32),
            shape((hidden, width), F32),
            shape((8, hidden), F32),
            shape((8, width), F32),
        ],
        scratch_shapes=[pltpu.VMEM((units, width), F32)],
        compiler_params=params(),
        cost_estimate=cost(25),
        name="feed_weights",
    )(low_a, low_b, grad_a, grad_b, expand_weight, bias_row, contract_weight)

    vec = shape((width,), F32)
    thin = shape((edge_width,), F32)
    square = shape((width, width), F32)
    small = shape((edge_width, edge_width), F32)
    (
        grad_message1,
        grad_mb1,
        grad_message2,
        grad_mb2,
        grad_message3,
        grad_mb3,
        grad_n1g,
        grad_n1s,
        grad_eb,
        grad_cb,
        grad_n2g,
        grad_n2s,
        grad_edge1_t,
        grad_eb1,
        grad_edge2,
        grad_eb2,
        grad_edge3,
        grad_eb3,
        grad_n3g,
        grad_n3s,
    ) = pl.pallas_call(
        unpack_kernel,
        in_specs=[vmem] * 5,
        out_specs=[vmem] * 20,
        out_shape=[
            shape(message_weight1.shape, F32),
            vec,
            square,
            vec,
            square,
            vec,
            vec,
            vec,
            shape((hidden,), F32),
            vec,
            vec,
            vec,
            shape(edge_w1t.shape, F32),
            thin,
            small,
            thin,
            small,
            thin,
            thin,
            thin,
        ],
        compiler_params=params(),
        cost_estimate=cost(4),
        name="unpack",
    )(edge_sum, feed_sum, late_sum, expand_bias_sum, contract_bias_sum)
    return (
        fresh[None],
        edge_out.transpose(1, 0, 2)[None],
        node_grad[None],
        edge_grad.transpose(1, 0, 2)[None],
        grad_message1,
        grad_mb1,
        grad_message2,
        grad_mb2,
        grad_message3,
        grad_mb3,
        grad_n1g,
        grad_n1s,
        grad_expand,
        grad_eb,
        grad_contract,
        grad_cb,
        grad_n2g,
        grad_n2s,
        grad_edge1_t.T,
        grad_eb1,
        grad_edge2,
        grad_eb2,
        grad_edge3,
        grad_eb3,
        grad_n3g,
        grad_n3s,
    )


def solution(mesh):
    row_spec = P("batch", "res", None)
    edge_spec = P("batch", "res", None, None)
    return jax.shard_map(
        body,
        mesh=mesh,
        in_specs=(row_spec, edge_spec, row_spec, row_spec, row_spec, edge_spec) + (P(),) * 22,
        out_specs=(row_spec, edge_spec, row_spec, edge_spec) + (P(),) * 22,
        check_vma=False,
    )
```

```python
import functools
import math

import jax
import jax.numpy as jnp
from jax import lax
from jax.experimental import pallas as pl
from jax.experimental.pallas import tpu as pltpu
from jax.sharding import PartitionSpec as P

ROW_CAP = 8
CORES = 2
RES = ("z", "x")
SIDE = ("y", "z", "x")
ALL = ("y", "core", "z", "x")
EPSILON = 1e-05
LANES = 128
VMEM_BYTES = 56 * 1024 * 1024
F32 = jnp.float32
BF16 = jnp.bfloat16

V_MB1, V_MB2, V_MB3, V_N1G, V_N1S, V_CB, V_N2G, V_N2S, V_EB = range(9)
V_EDGE = 12
V_ROWS = 24


def dot_nn(left, right):
    return lax.dot_general(left, right, (((1,), (0,)), ((), ())), preferred_element_type=F32)


def dot_nt(left, right):
    return lax.dot_general(left, right, (((1,), (1,)), ((), ())), preferred_element_type=F32)


def dot_tn(left, right):
    return lax.dot_general(left, right, (((0,), (0,)), ((), ())), preferred_element_type=F32)


def split_low(values):
    high = values.astype(BF16)
    return high, (values - high.astype(F32)).astype(BF16)


def dot_split(dot, left, right):
    high, rest = split_low(left)
    return dot(high, right) + dot(rest, right)


def dot_split_right(dot, left, right):
    high, rest = split_low(right)
    return dot(left, high) + dot(left, rest)


def gelu_pair(v):
    size = jnp.abs(v)
    den = 1.0 + (0.3275911 / math.sqrt(2.0)) * size
    t = pl.reciprocal(den, approx=True)
    t = t * (2.0 - den * t)
    e = jnp.exp2((v * v) * (-0.5 * math.log2(math.e)))
    poly = 0.5 * 1.061405429
    poly = poly * t + 0.5 * -1.453152027
    poly = poly * t + 0.5 * 1.421413741
    poly = poly * t + 0.5 * -0.284496736
    poly = poly * t + 0.5 * 0.254829592
    tail = poly * t * e
    phi_sum = jnp.where(v < 0, tail, 1.0 - tail)
    return v * phi_sum, phi_sum + (v * (1.0 / math.sqrt(2.0 * math.pi))) * e


def norm_parts(values):
    average = jnp.mean(values, axis=-1, keepdims=True)
    centred = values - average
    variance = jnp.mean(centred * centred, axis=-1, keepdims=True)
    scale = lax.rsqrt(variance + EPSILON)
    return centred * scale, scale


def norm_back(xhat, scale, gain, upstream):
    w = upstream * gain
    mean_w = jnp.mean(w, axis=-1, keepdims=True)
    mean_wx = jnp.mean(w * xhat, axis=-1, keepdims=True)
    return (w - mean_w - xhat * mean_wx) * scale


def edge_onehot(pos_ref, table_rows):
    pairs = pos_ref.shape[2]
    lane = lax.broadcasted_iota(jnp.int32, (LANES, table_rows), 1)
    return jnp.concatenate(
        [(pos_ref[0, :, p : p + 1] == lane).astype(F32).astype(BF16) for p in range(pairs)], axis=0
    )


def prepare_kernel(me_ref, idx_ref, mask_ref, *refs, parts, cap, steps, wide, narrow):
    wide_refs = refs[:wide]
    narrow_refs = refs[wide : wide + narrow]
    pos_ref, select_ref, ids_ref, count_ref, vec_ref = refs[wide + narrow :]
    rows, width = count_ref.shape
    total = rows * parts
    table = rows + parts * cap
    me = me_ref[0]
    pair_rows = idx_ref.shape[0]
    residue = lax.broadcasted_iota(jnp.int32, (total, LANES), 0)
    owner = residue // rows
    within = residue - owner * rows
    hits = jnp.zeros((total, LANES), F32)
    for j in range(pair_rows):
        hits = jnp.where(idx_ref[j : j + 1, :] == residue, 1.0, hits)
    hit = jnp.max(hits, axis=1, keepdims=True)
    own = owner == me
    wanted = jnp.where(own, 0.0, jnp.broadcast_to(hit, (total, LANES)))
    low_row = lax.broadcasted_iota(jnp.int32, (rows, rows), 0)
    low_col = lax.broadcasted_iota(jnp.int32, (rows, rows), 1)
    lower = (low_col <= low_row).astype(F32).astype(BF16)
    wanted_low = wanted.astype(BF16)
    place = jnp.concatenate(
        [dot_nn(lower, wanted_low[o * rows : (o + 1) * rows]) for o in range(parts)], axis=0
    )
    place = jnp.clip(place - 1.0, 0.0, cap - 1.0)
    pos = jnp.where(own, within.astype(F32), (rows + owner * cap).astype(F32) + place)
    picked = [
        jnp.sum(jnp.where(idx_ref[j : j + 1, :] == residue, pos, 0.0), axis=0, keepdims=True)
        for j in range(pair_rows)
    ]
    picked.append(jnp.zeros((LANES - pair_rows, LANES), F32))
    turned = jnp.concatenate(picked, axis=0).T.astype(jnp.int32)
    per = pair_rows // steps
    for s in range(steps):
        pos_ref[s] = turned[:, s * per : (s + 1) * per]
    lane = lax.broadcasted_iota(jnp.int32, (total, table), 1).astype(F32)
    live = jnp.where(own, 1.0, wanted)
    chosen = jnp.where(lane == pos[:, :1], jnp.broadcast_to(live[:, :1], (total, table)), 0.0)
    select_ref[...] = chosen.astype(BF16)
    asked_row = jnp.broadcast_to(within[:, :1].astype(F32), (total, parts * cap))
    ids = jnp.sum(chosen[:, rows:] * asked_row, axis=0, keepdims=True)
    ids_ref[...] = ids.astype(jnp.int32)
    ones = jnp.ones((mask_ref.shape[0], width), F32).astype(BF16)
    count_ref[...] = dot_tn(mask_ref[...].astype(F32).astype(BF16), ones)
    vec_ref[...] = jnp.zeros_like(vec_ref)
    at = 0
    for ref in wide_refs:
        for c in range(ref.shape[0] // width):
            part = ref[c * width : (c + 1) * width]
            vec_ref[at : at + 1, :] = part.astype(F32).reshape(1, width)
            at += 1
    for ref in narrow_refs:
        vec_ref[at : at + 1, : ref.shape[0]] = ref[...].astype(F32).reshape(1, ref.shape[0])
        at += 1


def node_kernel(
    edge_ref,
    pos_ref,
    select_ref,
    all_ref,
    self_ref,
    count_ref,
    asked_ref,
    vec_ref,
    w1_ref,
    w2_ref,
    w3_ref,
    expand_hbm,
    contract_hbm,
    act1_ref,
    slope1_ref,
    slope2_ref,
    fresh_ref,
    outgoing_ref,
    table_ref,
    mixed1_ref,
    mixed2_ref,
    low_ref,
    slope_e_ref,
    act_sum_ref,
    proj_ref,
    self_pre_ref,
    expand_ref,
    contract_ref,
    sems,
):
    step = pl.program_id(0)
    last = pl.num_programs(0) - 1
    rows, width = self_ref.shape
    slots = edge_ref.shape[0]
    edge_width = edge_ref.shape[2]
    table_rows = table_ref.shape[0]
    expand_copy = pltpu.make_async_copy(expand_hbm, expand_ref, sems.at[0])
    contract_copy = pltpu.make_async_copy(contract_hbm, contract_ref, sems.at[1])

    @pl.when(step == 0)
    def _():
        expand_copy.start()
        contract_copy.start()
        table = dot_tn(select_ref[...], all_ref[...]).astype(BF16)
        table_ref[...] = table
        proj_ref[...] = dot_nn(table, w1_ref[width : 2 * width]).astype(BF16)
        self_pre_ref[...] = (
            dot_nn(self_ref[...], w1_ref[:width]) + vec_ref[V_MB1 : V_MB1 + 1, :]
        )
        act_sum_ref[...] = jnp.zeros_like(act_sum_ref)

    onehot = edge_onehot(pos_ref, table_rows)
    features = edge_ref[...].reshape(slots * rows, edge_width)
    pre1 = dot_nn(features, w1_ref[2 * width :]) + dot_nn(onehot, proj_ref[...])
    self_pre = self_pre_ref[...]
    act1 = []
    for k in range(slots):
        part = pl.ds(k * rows, rows)
        act, slope = gelu_pair(pre1[k * rows : (k + 1) * rows] + self_pre)
        act = act.astype(BF16)
        act1.append(act)
        act1_ref[part, :] = act
        slope1_ref[part, :] = slope.astype(BF16)
    pre2 = dot_nn(jnp.concatenate(act1, axis=0), w2_ref[...])
    bias2 = vec_ref[V_MB2 : V_MB2 + 1, :]
    act_sum = act_sum_ref[...]
    counts = count_ref[...]
    for k in range(slots):
        act, slope = gelu_pair(pre2[k * rows : (k + 1) * rows] + bias2)
        valid = counts > (step * slots + k).astype(F32)
        act_sum = act_sum + jnp.where(valid, act.astype(BF16).astype(F32), 0.0)
        slope2_ref[pl.ds(k * rows, rows), :] = jnp.where(valid, slope, 0.0).astype(BF16)
    act_sum_ref[...] = act_sum

    @pl.when(step == last)
    def _():
        summed = dot_split(dot_nn, act_sum_ref[...], w3_ref[...])
        summed = summed + counts * vec_ref[V_MB3 : V_MB3 + 1, :]
        mixed1 = self_ref[...].astype(F32) + summed / counts
        mixed1_ref[...] = mixed1
        xhat1, _ = norm_parts(mixed1)
        updated = xhat1 * vec_ref[V_N1G : V_N1G + 1, :] + vec_ref[V_N1S : V_N1S + 1, :]
        low = updated.astype(BF16)
        low_ref[...] = low
        expand_copy.wait()
        contract_copy.wait()
        mixed2 = updated + vec_ref[V_CB : V_CB + 1, :]
        for c in range(expand_ref.shape[1] // width):
            cols = slice(c * width, (c + 1) * width)
            pre = dot_nn(low, expand_ref[:, cols]) + vec_ref[V_EB + c : V_EB + c + 1, :]
            act, slope = gelu_pair(pre)
            act = act.astype(BF16)
            slope_e_ref[:, cols] = slope
            mixed2 = mixed2 + dot_nn(act, contract_ref[cols, :])
        mixed2_ref[...] = mixed2
        xhat2, _ = norm_parts(mixed2)
        fresh = (xhat2 * vec_ref[V_N2G : V_N2G + 1, :] + vec_ref[V_N2S : V_N2S + 1, :]).astype(BF16)
        fresh_ref[...] = fresh
        asked = asked_onehot(asked_ref, rows)
        outgoing_ref[...] = dot_tn(asked, fresh).astype(BF16)


def asked_onehot(asked_ref, rows):
    row = lax.broadcasted_iota(jnp.int32, (rows, asked_ref.shape[1]), 0)
    return (asked_ref[...] == row).astype(F32).astype(BF16)


def edge_kernel(
    edge_ref,
    cot_ref,
    pos_ref,
    fresh_ref,
    incoming_ref,
    count_ref,
    vec_ref,
    w1t_ref,
    w2_ref,
    w3_ref,
    out_ref,
    grad_ref,
    first_ref,
    own_ref,
    away_ref,
    pack_ref,
    vec_out_ref,
    table_ref,
    proj_ref,
    self_pre_ref,
    back_ref,
    dw3_ref,
    dw2_ref,
    dw1_ref,
    sums_ref,
):
    step = pl.program_id(0)
    last = pl.num_programs(0) - 1
    rows, width = fresh_ref.shape
    slots, _, edge_width = edge_ref.shape
    block = slots * rows
    table_rows = table_ref.shape[0]
    own_t = w1t_ref[:, :width]
    nbr_t = w1t_ref[:, width : 2 * width]
    feat_t = w1t_ref[:, 2 * width :]

    def vector(i):
        return vec_ref[V_EDGE + i : V_EDGE + i + 1, :edge_width]

    @pl.when(step == 0)
    def _():
        table_ref[:rows] = fresh_ref[...]
        table_ref[rows:] = incoming_ref[...]
        proj_ref[...] = dot_nt(table_ref[...], nbr_t).astype(BF16)
        self_pre_ref[...] = dot_nt(fresh_ref[...], own_t) + vector(0)
        for ref in (back_ref, dw3_ref, dw2_ref, dw1_ref, sums_ref, first_ref):
            ref[...] = jnp.zeros_like(ref)

    def flat(values):
        return values.reshape(block, edge_width)

    def deep(values):
        return values.reshape(slots, rows, edge_width)

    onehot = edge_onehot(pos_ref, table_rows)
    features = flat(edge_ref[...])
    pre1 = dot_nt(features, feat_t) + dot_nn(onehot, proj_ref[...])
    pre1 = deep(pre1) + self_pre_ref[...][None]
    act1, slope1 = gelu_pair(flat(pre1))
    act1 = act1.astype(BF16)
    pre2 = dot_nn(act1, w2_ref[...]) + vector(1)
    act2, slope2 = gelu_pair(pre2)
    act2 = act2.astype(BF16)
    mixed3 = features.astype(F32) + (dot_nn(act2, w3_ref[...]) + vector(2))
    xhat, scale = norm_parts(mixed3)
    gain = vector(3)
    slot = lax.broadcasted_iota(jnp.int32, (slots, rows, edge_width), 0) + step * slots
    valid = count_ref[...][None, :, :edge_width] > slot.astype(F32)
    out_ref[...] = jnp.where(valid, deep(xhat * gain + vector(4)), 0.0).astype(BF16)
    upstream = flat(jnp.where(valid, cot_ref[...].astype(F32), 0.0))
    sums_ref[3] += jnp.sum(deep(upstream * xhat), axis=0)
    sums_ref[4] += jnp.sum(deep(upstream), axis=0)
    grad_mixed = norm_back(xhat, scale, gain, upstream)
    grad_delta = grad_mixed.astype(BF16)
    dw3_ref[...] += dot_tn(act2, grad_delta)
    sums_ref[2] += jnp.sum(deep(grad_delta.astype(F32)), axis=0)
    grad2 = (dot_nt(grad_delta, w3_ref[...]) * slope2).astype(BF16)
    dw2_ref[...] += dot_tn(act1, grad2)
    sums_ref[1] += jnp.sum(deep(grad2.astype(F32)), axis=0)
    grad1 = (dot_nt(grad2, w2_ref[...]) * slope1).astype(BF16)
    dw1_ref[...] += dot_tn(grad1, features)
    first_ref[...] += jnp.sum(deep(grad1.astype(F32)), axis=0)
    back_ref[...] += dot_tn(onehot, grad1)
    grad_ref[...] = deep(grad_mixed + dot_nn(grad1, feat_t))

    @pl.when(step == last)
    def _():
        first = first_ref[...]
        back = back_ref[...]
        own_ref[...] = back[:rows]
        away_ref[...] = back[rows:].astype(BF16)
        first_high, first_rest = split_low(first)
        back_high, back_rest = split_low(back)
        own_grad = dot_tn(first_high, fresh_ref[...]) + dot_tn(first_rest, fresh_ref[...])
        nbr_grad = dot_tn(back_high, table_ref[...]) + dot_tn(back_rest, table_ref[...])
        pack_ref[:edge_width, :] = own_grad.astype(BF16)
        pack_ref[edge_width : 2 * edge_width, :] = nbr_grad.astype(BF16)
        pad = jnp.zeros((edge_width, width // 2 - edge_width), BF16)
        third = [dw1_ref[...].astype(BF16), pad, dw2_ref[...].astype(BF16), pad]
        pack_ref[2 * edge_width : 3 * edge_width, :] = jnp.concatenate(third, axis=1)
        fourth = [dw3_ref[...].astype(BF16), pad, jnp.zeros((edge_width, width // 2), BF16)]
        pack_ref[3 * edge_width :, :] = jnp.concatenate(fourth, axis=1)
        vec_out_ref[...] = jnp.zeros_like(vec_out_ref)
        vec_out_ref[0:1, :edge_width] = jnp.sum(first, axis=0, keepdims=True)
        for i in range(1, 5):
            vec_out_ref[i : i + 1, :edge_width] = jnp.sum(sums_ref[i], axis=0, keepdims=True)


def feed_kernel(
    cot_ref,
    first_ref,
    own_ref,
    arrived_ref,
    asked_ref,
    count_ref,
    vec_ref,
    w1t_ref,
    mixed1_ref,
    mixed2_ref,
    slope_ref,
    act_sum_ref,
    expand_ref,
    contract_ref,
    w3_ref,
    edge_vec_ref,
    pack_ref,
    contracted_ref,
    spread_ref,
    grad_mixed1_ref,
):
    rows, width = cot_ref.shape
    hidden = expand_ref.shape[1]
    own_t = w1t_ref[:, :width]
    nbr_t = w1t_ref[:, width : 2 * width]
    counts = count_ref[...]

    def vector(i):
        return vec_ref[i : i + 1, :]

    def total(values):
        return jnp.sum(values.astype(F32), axis=0, keepdims=True)

    back = own_ref[...] + dot_nn(asked_onehot(asked_ref, rows), arrived_ref[...])
    grad_fresh = (
        cot_ref[...].astype(F32)
        + dot_split(dot_nn, first_ref[...], own_t)
        + dot_split(dot_nn, back, nbr_t)
    )
    xhat2, scale2 = norm_parts(mixed2_ref[...])
    grad_mixed2 = norm_back(xhat2, scale2, vector(V_N2G), grad_fresh)
    grad_contracted = grad_mixed2.astype(BF16)
    contracted_ref[...] = grad_contracted
    grad_updated = grad_mixed2
    for c in range(hidden // width):
        cols = slice(c * width, (c + 1) * width)
        pre = dot_nt(grad_contracted, contract_ref[cols, :]) * slope_ref[:, cols]
        grad_updated = grad_updated + dot_nt(pre.astype(BF16), expand_ref[:, cols])
    xhat1, scale1 = norm_parts(mixed1_ref[...])
    grad_mixed1 = norm_back(xhat1, scale1, vector(V_N1G), grad_updated)
    grad_mixed1_ref[...] = grad_mixed1
    grad_message = (grad_mixed1 / counts).astype(BF16)
    spread_ref[...] = dot_nt(grad_message, w3_ref[...])
    pack_ref[:width, :] = dot_split(dot_tn, act_sum_ref[...], grad_message).astype(BF16)
    vectors = [
        total(counts * grad_message.astype(F32)),
        total(grad_updated * xhat1),
        total(grad_updated),
        total(grad_fresh * xhat2),
        total(grad_fresh),
        edge_vec_ref[...],
    ]
    vectors = jnp.concatenate(vectors, axis=0)
    vectors = jnp.concatenate(
        [vectors, jnp.zeros((pack_ref.shape[0] - width - vectors.shape[0], width), F32)], axis=0
    )
    pack_ref[width:, :] = vectors.astype(BF16)


def feed_weight_kernel(
    core_ref,
    low_a_ref,
    low_b_ref,
    grad_a_ref,
    grad_b_ref,
    expand_ref,
    bias_ref,
    contract_ref,
    expand_out_ref,
    contract_out_ref,
    bias_out_ref,
    last_bias_ref,
    turned_ref,
):
    del core_ref
    chunk = pl.program_id(0)
    step = pl.program_id(1)
    units = expand_ref.shape[1]
    weight_t = expand_ref[...].T
    bias = jnp.broadcast_to(bias_ref[0:1, :], (8, units)).T[:, :1]
    turned = jnp.zeros((units, low_a_ref.shape[1]), F32)
    contracted = jnp.zeros((units, low_a_ref.shape[1]), F32)
    sums = jnp.zeros((8, units), F32)
    ones = jnp.ones((8, low_a_ref.shape[0]), F32).astype(BF16)
    for low_ref, grad_ref in ((low_a_ref, grad_a_ref), (low_b_ref, grad_b_ref)):
        act, slope = gelu_pair(dot_nt(weight_t, low_ref[...]) + bias)
        contracted = contracted + dot_nn(act.astype(BF16), grad_ref[...])
        pre = (dot_nt(contract_ref[...], grad_ref[...]) * slope).astype(BF16)
        turned = turned + dot_nn(pre, low_ref[...])
        sums = sums + dot_nt(ones, pre)

    @pl.when(step == 0)
    def _():
        turned_ref[...] = turned
        contract_out_ref[...] = contracted
        bias_out_ref[...] = sums

    @pl.when(step > 0)
    def _():
        turned_ref[...] += turned
        contract_out_ref[...] += contracted
        bias_out_ref[...] += sums

    @pl.when(step == pl.num_programs(1) - 1)
    def _():
        expand_out_ref[...] = turned_ref[...].T

    @pl.when((chunk == 0) & (step == 0))
    def _():
        last_bias_ref[...] = jnp.zeros_like(last_bias_ref)

    @pl.when(chunk == 0)
    def _():
        last_bias_ref[...] += dot_nn(ones, grad_a_ref[...]) + dot_nn(ones, grad_b_ref[...])


def message_kernel(
    edge_ref,
    pos_ref,
    act1_ref,
    slope1_ref,
    slope2_ref,
    partial_ref,
    spread_ref,
    table_ref,
    w1_ref,
    w2_ref,
    edge_pack_ref,
    feed_pack_ref,
    grad_ref,
    first_ref,
    own_ref,
    away_ref,
    pack_ref,
    back_ref,
    dw2_ref,
    dw1_ref,
    bias2_ref,
):
    step = pl.program_id(0)
    last = pl.num_programs(0) - 1
    slots, rows, edge_width = edge_ref.shape
    width = act1_ref.shape[1]
    block = slots * rows
    table_rows = table_ref.shape[0]

    @pl.when(step == 0)
    def _():
        for ref in (back_ref, dw2_ref, dw1_ref, bias2_ref, first_ref):
            ref[...] = jnp.zeros_like(ref)

    spread = spread_ref[...]
    grad2 = []
    bias2 = bias2_ref[...]
    for k in range(slots):
        part = (spread * slope2_ref[pl.ds(k * rows, rows), :].astype(F32)).astype(BF16)
        bias2 = bias2 + part.astype(F32)
        grad2.append(part)
    bias2_ref[...] = bias2
    grad2 = jnp.concatenate(grad2, axis=0)
    dw2_ref[...] += dot_tn(act1_ref[...], grad2)
    grad1 = (dot_nt(grad2, w2_ref[...]) * slope1_ref[...].astype(F32)).astype(BF16)
    first_ref[...] += jnp.sum(grad1.astype(F32).reshape(slots, rows, width), axis=0)
    onehot = edge_onehot(pos_ref, table_rows)
    back_ref[...] += dot_tn(onehot, grad1)
    features = edge_ref[...].reshape(block, edge_width)
    dw1_ref[...] += dot_tn(features, grad1)
    grad_ref[...] = partial_ref[...] + dot_nt(grad1, w1_ref[2 * width :]).reshape(
        slots, rows, edge_width
    )

    @pl.when(step == last)
    def _():
        first = first_ref[...]
        back = back_ref[...]
        own_ref[...] = back[:rows]
        away_ref[...] = back[rows:].astype(BF16)
        pack_ref[0, :width] = dot_split_right(dot_tn, table_ref[:rows], first).astype(BF16)
        pack_ref[0, width : 2 * width] = dot_split_right(dot_tn, table_ref[...], back).astype(BF16)
        pack_ref[0, 2 * width :] = feed_pack_ref[:width]
        base = edge_width
        pack_ref[1, :base] = dw1_ref[...].astype(BF16)
        pack_ref[1, base : base + width] = dw2_ref[...].astype(BF16)
        base = base + width
        pack_ref[1, base : base + 4 * edge_width] = edge_pack_ref[...]
        base = base + 4 * edge_width
        vectors = [
            feed_pack_ref[width:].astype(F32),
            jnp.sum(first, axis=0, keepdims=True),
            jnp.sum(bias2_ref[...], axis=0, keepdims=True),
        ]
        vectors = jnp.concatenate(vectors, axis=0)
        fill = pack_ref.shape[1] - base - vectors.shape[0]
        vectors = jnp.concatenate([vectors, jnp.zeros((fill, width), F32)], axis=0)
        pack_ref[1, base:] = vectors.astype(BF16)


def node_grad_kernel(grad_ref, first_ref, own_ref, arrived_ref, asked_ref, w1_ref, out_ref):
    rows, width = grad_ref.shape
    back = own_ref[...] + dot_nn(asked_onehot(asked_ref, rows), arrived_ref[...])
    out_ref[...] = (
        grad_ref[...]
        + dot_split(dot_nt, first_ref[...], w1_ref[:width])
        + dot_split(dot_nt, back, w1_ref[width : 2 * width])
    )


def unpack_kernel(core_ref, mine_ref, other_ref, bias_ref, last_bias_ref, *refs):
    (
        message1_ref,
        message1_bias_ref,
        message2_ref,
        message2_bias_ref,
        message3_ref,
        message3_bias_ref,
        gain1_ref,
        shift1_ref,
        expand_bias_ref,
        contract_bias_ref,
        gain2_ref,
        shift2_ref,
        edge1_ref,
        edge1_bias_ref,
        edge2_ref,
        edge2_bias_ref,
        edge3_ref,
        edge3_bias_ref,
        gain3_ref,
        shift3_ref,
    ) = refs
    width = mine_ref.shape[1]
    edge_width = edge2_ref.shape[0]
    half = width // 2
    first_core = core_ref[0] == 0

    def lower(start, stop):
        return jnp.where(first_core, mine_ref[start:stop], other_ref[start:stop]).astype(F32)

    def upper(start, stop):
        return jnp.where(first_core, other_ref[start:stop], mine_ref[start:stop]).astype(F32)

    message1_ref[: 2 * width] = lower(0, 2 * width)
    message3_ref[...] = lower(2 * width, 3 * width)
    message1_ref[2 * width :] = upper(0, edge_width)
    base = edge_width
    message2_ref[...] = upper(base, base + width)
    base = base + width
    edge1_ref[:, :width] = upper(base, base + edge_width)
    edge1_ref[:, width : 2 * width] = upper(base + edge_width, base + 2 * edge_width)
    third = upper(base + 2 * edge_width, base + 3 * edge_width)
    edge1_ref[:, 2 * width :] = third[:, :edge_width]
    edge2_ref[...] = third[:, half : half + edge_width]
    edge3_ref[...] = upper(base + 3 * edge_width, base + 4 * edge_width)[:, :edge_width]
    base = base + 4 * edge_width
    vectors = upper(base, mine_ref.shape[0])
    targets = (message3_bias_ref, gain1_ref, shift1_ref, gain2_ref, shift2_ref)
    for i, ref in enumerate(targets):
        ref[...] = vectors[i]
    targets = (edge1_bias_ref, edge2_bias_ref, edge3_bias_ref, gain3_ref, shift3_ref)
    for i, ref in enumerate(targets):
        ref[...] = vectors[5 + i, :edge_width]
    message1_bias_ref[...] = vectors[16]
    message2_bias_ref[...] = vectors[17]
    expand_bias_ref[...] = bias_ref[0]
    contract_bias_ref[...] = last_bias_ref[0]


def gather_copies(values, axes):
    size = lax.axis_size(axes)
    copies = jnp.broadcast_to(values[None], (size, *values.shape))
    return lax.all_to_all(copies, axes, split_axis=0, concat_axis=0, tiled=True)


def exchange(values, parts):
    grouped = values.reshape(parts, values.shape[0] // parts, values.shape[1])
    arrived = lax.all_to_all(grouped, RES, split_axis=0, concat_axis=0, tiled=True)
    return arrived.reshape(values.shape)


def other_core(values):
    return lax.ppermute(values, "core", [(0, 1), (1, 0)])


def whole(shape):
    return pl.BlockSpec(shape, lambda *_: (0,) * len(shape))


def params():
    return pltpu.CompilerParams(vmem_limit_bytes=VMEM_BYTES)


def cost(microseconds):
    return pl.CostEstimate(
        flops=int(microseconds * 1.15e9),
        bytes_accessed=int(microseconds * 3.69e6),
        transcendentals=0,
    )


def body(
    node_states,
    edge_states,
    neighbour_index,
    edge_mask,
    node_cotangent,
    edge_cotangent,
    message_weight1,
    message_bias1,
    message_weight2,
    message_bias2,
    message_weight3,
    message_bias3,
    norm1_gain,
    norm1_shift,
    expand_weight,
    expand_bias,
    contract_weight,
    contract_bias,
    norm2_gain,
    norm2_shift,
    edge_weight1,
    edge_bias1,
    edge_weight2,
    edge_bias2,
    edge_weight3,
    edge_bias3,
    norm3_gain,
    norm3_shift,
):
    self_rows = node_states[0]
    rows, width = self_rows.shape
    slots = neighbour_index.shape[2]
    edge_width = edge_states.shape[3]
    hidden = expand_weight.shape[1]
    edges = rows * slots
    parts = lax.axis_size(RES)
    cap = ROW_CAP
    table_rows = rows + parts * cap
    steps = 5
    block_slots = slots // steps
    block = block_slots * rows
    pairs = block // LANES

    everyone = gather_copies(self_rows, RES).reshape(parts * rows, width)
    core = lax.axis_index("core").astype(jnp.int32).reshape(1)
    me = lax.axis_index(RES).astype(jnp.int32).reshape(1)
    edge_rows = edge_states[0].transpose(1, 0, 2)
    edge_cot = edge_cotangent[0].transpose(1, 0, 2)
    idx_rows = neighbour_index[0].T.reshape(edges // LANES, LANES)
    edge_w1t = edge_weight1.T
    wide = (
        message_bias1,
        message_bias2,
        message_bias3,
        norm1_gain,
        norm1_shift,
        contract_bias,
        norm2_gain,
        norm2_shift,
        expand_bias,
    )
    narrow = (edge_bias1, edge_bias2, edge_bias3, norm3_gain, norm3_shift)
    vmem = pl.BlockSpec(memory_space=pltpu.VMEM)

    def shape(dims, kind):
        return jax.ShapeDtypeStruct(dims, kind)

    pos, select, ids, counts, vectors = pl.pallas_call(
        functools.partial(
            prepare_kernel, parts=parts, cap=cap, steps=steps, wide=len(wide), narrow=len(narrow)
        ),
        out_shape=(
            shape((steps, LANES, pairs), jnp.int32),
            shape((parts * rows, table_rows), BF16),
            shape((1, parts * cap), jnp.int32),
            shape((rows, width), F32),
            shape((V_ROWS, width), F32),
        ),
        in_specs=[pl.BlockSpec(memory_space=pltpu.SMEM)] + [vmem] * (2 + len(wide) + len(narrow)),
        out_specs=(vmem,) * 5,
        compiler_params=params(),
        cost_estimate=cost(6),
        name="prepare",
    )(me, idx_rows, edge_mask[0].T, *wide, *narrow)
    asked = lax.all_to_all(ids.reshape(parts, cap), RES, split_axis=0, concat_axis=0, tiled=True)
    asked = asked.reshape(1, parts * cap)

    edge_spec = pl.BlockSpec((block_slots, rows, edge_width), lambda i: (i, 0, 0))
    flat_spec = pl.BlockSpec((block, width), lambda i: (i, 0))
    pos_spec = pl.BlockSpec((1, LANES, pairs), lambda i: (i, 0, 0))
    any_spec = pl.BlockSpec(memory_space=pl.ANY)
    node_spec = whole((rows, width))
    away_spec = whole((parts * cap, width))

    (
        act1,
        slope1,
        slope2,
        fresh,
        outgoing,
        table,
        mixed1,
        mixed2,
        low,
        slope_e,
        act_sum,
    ) = pl.pallas_call(
        node_kernel,
        grid=(steps,),
        in_specs=[
            edge_spec,
            pos_spec,
            whole((parts * rows, table_rows)),
            whole((parts * rows, width)),
            node_spec,
            node_spec,
            whole((1, parts * cap)),
            whole((V_ROWS, width)),
            whole(message_weight1.shape),
            whole((width, width)),
            whole((width, width)),
            any_spec,
            any_spec,
        ],
        out_specs=[
            flat_spec,
            flat_spec,
            flat_spec,
            node_spec,
            away_spec,
            whole((table_rows, width)),
            node_spec,
            node_spec,
            node_spec,
            whole((rows, hidden)),
            node_spec,
        ],
        out_shape=[
            shape((edges, width), BF16),
            shape((edges, width), BF16),
            shape((edges, width), BF16),
            shape((rows, width), BF16),
            shape((parts * cap, width), BF16),
            shape((table_rows, width), BF16),
            shape((rows, width), F32),
            shape((rows, width), F32),
            shape((rows, width), BF16),
            shape((rows, hidden), F32),
            shape((rows, width), F32),
        ],
        scratch_shapes=[
            pltpu.VMEM((table_rows, width), BF16),
            pltpu.VMEM((rows, width), F32),
            pltpu.VMEM((width, hidden), BF16),
            pltpu.VMEM((hidden, width), BF16),
            pltpu.SemaphoreType.DMA((2,)),
        ],
        compiler_params=params(),
        cost_estimate=cost(26),
        name="node_forward",
    )(
        edge_rows,
        pos,
        select,
        everyone,
        self_rows,
        counts,
        asked,
        vectors,
        message_weight1,
        message_weight2,
        message_weight3,
        expand_weight,
        contract_weight,
    )
    incoming = exchange(outgoing, parts)
    low_all = lax.all_gather(low, ALL, axis=0, tiled=True)

    edge_pack_rows = 4 * edge_width
    edge_out, grad_partial, edge_first, edge_own, edge_away, edge_pack, edge_vec = pl.pallas_call(
        edge_kernel,
        grid=(steps,),
        in_specs=[
            edge_spec,
            edge_spec,
            pos_spec,
            node_spec,
            away_spec,
            node_spec,
            whole((V_ROWS, width)),
            whole(edge_w1t.shape),
            whole((edge_width, edge_width)),
            whole((edge_width, edge_width)),
        ],
        out_specs=[
            edge_spec,
            edge_spec,
            whole((rows, edge_width)),
            whole((rows, edge_width)),
            whole((parts * cap, edge_width)),
            whole((edge_pack_rows, width)),
            whole((8, width)),
        ],
        out_shape=[
            shape((slots, rows, edge_width), BF16),
            shape((slots, rows, edge_width), F32),
            shape((rows, edge_width), F32),
            shape((rows, edge_width), F32),
            shape((parts * cap, edge_width), BF16),
            shape((edge_pack_rows, width), BF16),
            shape((8, width), F32),
        ],
        scratch_shapes=[
            pltpu.VMEM((table_rows, width), BF16),
            pltpu.VMEM((table_rows, edge_width), BF16),
            pltpu.VMEM((rows, edge_width), F32),
            pltpu.VMEM((table_rows, edge_width), F32),
            pltpu.VMEM((edge_width, edge_width), F32),
            pltpu.VMEM((edge_width, edge_width), F32),
            pltpu.VMEM((edge_width, edge_width), F32),
            pltpu.VMEM((5, rows, edge_width), F32),
        ],
        compiler_params=params(),
        cost_estimate=cost(21),
        name="edge_both",
    )(
        edge_rows,
        edge_cot,
        pos,
        fresh,
        incoming,
        counts,
        vectors,
        edge_w1t,
        edge_weight2,
        edge_weight3,
    )
    edge_arrived = exchange(edge_away, parts)

    feed_rows = width + 16
    feed_pack, grad_contracted, spread, grad_mixed1 = pl.pallas_call(
        feed_kernel,
        in_specs=[vmem] * 16,
        out_specs=[vmem] * 4,
        out_shape=[
            shape((feed_rows, width), BF16),
            shape((rows, width), BF16),
            shape((rows, width), F32),
            shape((rows, width), F32),
        ],
        compiler_params=params(),
        cost_estimate=cost(7),
        name="feed_backward",
    )(
        node_cotangent[0],
        edge_first,
        edge_own,
        edge_arrived,
        asked,
        counts,
        vectors,
        edge_w1t,
        mixed1,
        mixed2,
        slope_e,
        act_sum,
        expand_weight,
        contract_weight,
        message_weight3,
        edge_vec,
    )
    spread, low_all = lax.optimization_barrier((spread, low_all))
    grad_mine = gather_copies(grad_contracted, SIDE)
    side = grad_mine.shape[0]
    grad_mine = grad_mine.reshape(side * rows, width)

    half_rows = 3 * width
    edge_grad, first, own, away, pack = pl.pallas_call(
        message_kernel,
        grid=(steps,),
        in_specs=[
            edge_spec,
            pos_spec,
            flat_spec,
            flat_spec,
            flat_spec,
            edge_spec,
            node_spec,
            whole((table_rows, width)),
            whole(message_weight1.shape),
            whole((width, width)),
            whole((edge_pack_rows, width)),
            whole((feed_rows, width)),
        ],
        out_specs=[
            edge_spec,
            node_spec,
            node_spec,
            away_spec,
            whole((CORES, half_rows, width)),
        ],
        out_shape=[
            shape((slots, rows, edge_width), F32),
            shape((rows, width), F32),
            shape((rows, width), F32),
            shape((parts * cap, width), BF16),
            shape((CORES, half_rows, width), BF16),
        ],
        scratch_shapes=[
            pltpu.VMEM((table_rows, width), F32),
            pltpu.VMEM((width, width), F32),
            pltpu.VMEM((edge_width, width), F32),
            pltpu.VMEM((rows, width), F32),
        ],
        compiler_params=params(),
        cost_estimate=cost(14),
        name="message_backward",
    )(
        edge_rows,
        pos,
        act1,
        slope1,
        slope2,
        grad_partial,
        spread,
        table,
        message_weight1,
        message_weight2,
        edge_pack,
        feed_pack,
    )
    grad_other = other_core(grad_mine)
    keep = lax.dynamic_index_in_dim(pack, core[0], axis=0, keepdims=False)
    came = other_core(lax.dynamic_index_in_dim(pack, 1 - core[0], axis=0, keepdims=False))
    share = half_rows // side
    halves = (keep.astype(F32) + came.astype(F32)).astype(BF16).reshape(side, share, width)
    my_y = lax.axis_index("y")
    same_y = jnp.arange(side, dtype=jnp.int32) // parts == my_y
    riding = jnp.tile(away.reshape(parts, cap, width), (side // parts, 1, 1))
    riding = jnp.where(same_y[:, None, None], riding, jnp.zeros_like(riding))
    arrived = lax.all_to_all(
        jnp.concatenate([halves, riding], axis=1), SIDE, split_axis=0, concat_axis=0, tiled=True
    )
    summed = jnp.sum(arrived[:, :share].astype(F32), axis=0).astype(BF16)
    returned = lax.dynamic_slice_in_dim(arrived[:, share:], my_y * parts, parts, axis=0)
    returned = returned.reshape(parts * cap, width)
    mine = lax.all_gather(summed, SIDE, axis=0, tiled=True)
    other = other_core(mine)
    node_grad = pl.pallas_call(
        node_grad_kernel,
        in_specs=[vmem] * 6,
        out_specs=vmem,
        out_shape=shape((rows, width), F32),
        compiler_params=params(),
        cost_estimate=cost(3),
        name="node_gradient",
    )(grad_mixed1, first, own, returned, asked, message_weight1)

    units = 256
    row_block = parts * rows
    bias_row = vectors[V_EB : V_EB + hidden // width].reshape(1, hidden)
    grad_expand, grad_contract, expand_bias_sum, contract_bias_sum = pl.pallas_call(
        feed_weight_kernel,
        grid_spec=pltpu.PrefetchScalarGridSpec(
            num_scalar_prefetch=1,
            grid=(hidden // units, side // parts),
            in_specs=[
                pl.BlockSpec((row_block, width), lambda c, r, core: (CORES * r + core[0], 0)),
                pl.BlockSpec((row_block, width), lambda c, r, core: (CORES * r + 1 - core[0], 0)),
                pl.BlockSpec((row_block, width), lambda c, r, core: (r, 0)),
                pl.BlockSpec((row_block, width), lambda c, r, core: (r, 0)),
                pl.BlockSpec((width, units), lambda c, r, core: (0, c)),
                pl.BlockSpec((1, units), lambda c, r, core: (0, c)),
                pl.BlockSpec((units, width), lambda c, r, core: (c, 0)),
            ],
            out_specs=[
                pl.BlockSpec((width, units), lambda c, r, core: (0, c)),
                pl.BlockSpec((units, width), lambda c, r, core: (c, 0)),
                pl.BlockSpec((8, units), lambda c, r, core: (0, c)),
                whole((8, width)),
            ],
            scratch_shapes=[pltpu.VMEM((units, width), F32)],
        ),
        out_shape=[
            shape((width, hidden), F32),
            shape((hidden, width), F32),
            shape((8, hidden), F32),
            shape((8, width), F32),
        ],
        compiler_params=params(),
        cost_estimate=cost(35),
        name="feed_weights",
    )(core, low_all, low_all, grad_mine, grad_other, expand_weight, bias_row, contract_weight)

    vec = shape((width,), F32)
    thin = shape((edge_width,), F32)
    square = shape((width, width), F32)
    small = shape((edge_width, edge_width), F32)
    (
        grad_message1,
        grad_mb1,
        grad_message2,
        grad_mb2,
        grad_message3,
        grad_mb3,
        grad_n1g,
        grad_n1s,
        grad_eb,
        grad_cb,
        grad_n2g,
        grad_n2s,
        grad_edge1_t,
        grad_eb1,
        grad_edge2,
        grad_eb2,
        grad_edge3,
        grad_eb3,
        grad_n3g,
        grad_n3s,
    ) = pl.pallas_call(
        unpack_kernel,
        in_specs=[pl.BlockSpec(memory_space=pltpu.SMEM)] + [vmem] * 4,
        out_specs=[vmem] * 20,
        out_shape=[
            shape(message_weight1.shape, F32),
            vec,
            square,
            vec,
            square,
            vec,
            vec,
            vec,
            shape((hidden,), F32),
            vec,
            vec,
            vec,
            shape(edge_w1t.shape, F32),
            thin,
            small,
            thin,
            small,
            thin,
            thin,
            thin,
        ],
        compiler_params=params(),
        cost_estimate=cost(4),
        name="unpack",
    )(core, mine, other, expand_bias_sum, contract_bias_sum)
    return (
        fresh[None],
        edge_out.transpose(1, 0, 2)[None],
        node_grad[None],
        edge_grad.transpose(1, 0, 2)[None],
        grad_message1,
        grad_mb1,
        grad_message2,
        grad_mb2,
        grad_message3,
        grad_mb3,
        grad_n1g,
        grad_n1s,
        grad_expand,
        grad_eb,
        grad_contract,
        grad_cb,
        grad_n2g,
        grad_n2s,
        grad_edge1_t.T,
        grad_eb1,
        grad_edge2,
        grad_eb2,
        grad_edge3,
        grad_eb3,
        grad_n3g,
        grad_n3s,
    )


def solution(mesh):
    batch, res = mesh.shape["batch"], mesh.shape["res"]
    x_size = 1 << ((res.bit_length() - 1) // 2)
    sizes = (batch // CORES, CORES, res // x_size, x_size)
    fine = jax.sharding.Mesh(mesh.devices.reshape(sizes), ALL)
    row_spec = P(("y", "core"), RES, None)
    edge_spec = P(("y", "core"), RES, None, None)
    return jax.shard_map(
        body,
        mesh=fine,
        in_specs=(row_spec, edge_spec, row_spec, row_spec, row_spec, edge_spec) + (P(),) * 22,
        out_specs=(row_spec, edge_spec, row_spec, edge_spec) + (P(),) * 22,
        check_vma=False,
    )
```

```python
import functools
import math

import jax
import jax.numpy as jnp
from jax import lax
from jax.experimental import pallas as pl
from jax.experimental.pallas import tpu as pltpu
from jax.sharding import PartitionSpec as P

ROW_CAP = 8
CORES = 2
RES = ("z", "x")
PLANE = ("y", "x")
SIDE = ("y", "z", "x")
ALL = ("y", "core", "z", "x")
BY_CORE = ("core", "y", "z", "x")
EPSILON = 1e-05
LANES = 128
VMEM_BYTES = 56 * 1024 * 1024
F32 = jnp.float32
BF16 = jnp.bfloat16

V_MB1, V_MB2, V_MB3, V_N1G, V_N1S, V_CB, V_N2G, V_N2S, V_EB = range(9)
V_EDGE = 12
V_ROWS = 24


def dot_nn(left, right):
    return lax.dot_general(left, right, (((1,), (0,)), ((), ())), preferred_element_type=F32)


def dot_nt(left, right):
    return lax.dot_general(left, right, (((1,), (1,)), ((), ())), preferred_element_type=F32)


def dot_tn(left, right):
    return lax.dot_general(left, right, (((0,), (0,)), ((), ())), preferred_element_type=F32)


def split_low(values):
    high = values.astype(BF16)
    return high, (values - high.astype(F32)).astype(BF16)


def dot_split(dot, left, right):
    high, rest = split_low(left)
    return dot(high, right) + dot(rest, right)


def dot_split_right(dot, left, right):
    high, rest = split_low(right)
    return dot(left, high) + dot(left, rest)


def gelu_pair(v):
    size = jnp.abs(v)
    den = 1.0 + (0.3275911 / math.sqrt(2.0)) * size
    t = pl.reciprocal(den, approx=True)
    t = t * (2.0 - den * t)
    e = jnp.exp2((v * v) * (-0.5 * math.log2(math.e)))
    poly = 0.5 * 1.061405429
    poly = poly * t + 0.5 * -1.453152027
    poly = poly * t + 0.5 * 1.421413741
    poly = poly * t + 0.5 * -0.284496736
    poly = poly * t + 0.5 * 0.254829592
    tail = poly * t * e
    phi_sum = jnp.where(v < 0, tail, 1.0 - tail)
    return v * phi_sum, phi_sum + (v * (1.0 / math.sqrt(2.0 * math.pi))) * e


def norm_parts(values):
    average = jnp.mean(values, axis=-1, keepdims=True)
    centred = values - average
    variance = jnp.mean(centred * centred, axis=-1, keepdims=True)
    scale = lax.rsqrt(variance + EPSILON)
    return centred * scale, scale


def norm_back(xhat, scale, gain, upstream):
    w = upstream * gain
    mean_w = jnp.mean(w, axis=-1, keepdims=True)
    mean_wx = jnp.mean(w * xhat, axis=-1, keepdims=True)
    return (w - mean_w - xhat * mean_wx) * scale


def edge_onehot(pos_ref, table_rows):
    pairs = pos_ref.shape[2]
    lane = lax.broadcasted_iota(jnp.int32, (LANES, table_rows), 1)
    return jnp.concatenate(
        [(pos_ref[0, :, p : p + 1] == lane).astype(F32).astype(BF16) for p in range(pairs)], axis=0
    )


def prepare_kernel(me_ref, idx_ref, mask_ref, *refs, parts, cap, steps, wide, narrow):
    wide_refs = refs[:wide]
    narrow_refs = refs[wide : wide + narrow]
    pos_ref, select_ref, ids_ref, count_ref, vec_ref = refs[wide + narrow :]
    rows, width = count_ref.shape
    total = rows * parts
    table = rows + parts * cap
    me = me_ref[0]
    pair_rows = idx_ref.shape[0]
    residue = lax.broadcasted_iota(jnp.int32, (total, LANES), 0)
    owner = residue // rows
    within = residue - owner * rows
    hits = jnp.zeros((total, LANES), F32)
    for j in range(pair_rows):
        hits = jnp.where(idx_ref[j : j + 1, :] == residue, 1.0, hits)
    hit = jnp.max(hits, axis=1, keepdims=True)
    own = owner == me
    wanted = jnp.where(own, 0.0, jnp.broadcast_to(hit, (total, LANES)))
    low_row = lax.broadcasted_iota(jnp.int32, (rows, rows), 0)
    low_col = lax.broadcasted_iota(jnp.int32, (rows, rows), 1)
    lower = (low_col <= low_row).astype(F32).astype(BF16)
    wanted_low = wanted.astype(BF16)
    place = jnp.concatenate(
        [dot_nn(lower, wanted_low[o * rows : (o + 1) * rows]) for o in range(parts)], axis=0
    )
    place = jnp.clip(place - 1.0, 0.0, cap - 1.0)
    pos = jnp.where(own, within.astype(F32), (rows + owner * cap).astype(F32) + place)
    picked = [
        jnp.sum(jnp.where(idx_ref[j : j + 1, :] == residue, pos, 0.0), axis=0, keepdims=True)
        for j in range(pair_rows)
    ]
    picked.append(jnp.zeros((LANES - pair_rows, LANES), F32))
    turned = jnp.concatenate(picked, axis=0).T.astype(jnp.int32)
    per = pair_rows // steps
    for s in range(steps):
        pos_ref[s] = turned[:, s * per : (s + 1) * per]
    lane = lax.broadcasted_iota(jnp.int32, (total, table), 1).astype(F32)
    live = jnp.where(own, 1.0, wanted)
    chosen = jnp.where(lane == pos[:, :1], jnp.broadcast_to(live[:, :1], (total, table)), 0.0)
    select_ref[...] = chosen.astype(BF16)
    asked_row = jnp.broadcast_to(within[:, :1].astype(F32), (total, parts * cap))
    ids = jnp.sum(chosen[:, rows:] * asked_row, axis=0, keepdims=True)
    ids_ref[...] = ids.astype(jnp.int32)
    ones = jnp.ones((mask_ref.shape[0], width), F32).astype(BF16)
    count_ref[...] = dot_tn(mask_ref[...].astype(F32).astype(BF16), ones)
    vec_ref[...] = jnp.zeros_like(vec_ref)
    at = 0
    for ref in wide_refs:
        for c in range(ref.shape[0] // width):
            part = ref[c * width : (c + 1) * width]
            vec_ref[at : at + 1, :] = part.astype(F32).reshape(1, width)
            at += 1
    for ref in narrow_refs:
        vec_ref[at : at + 1, : ref.shape[0]] = ref[...].astype(F32).reshape(1, ref.shape[0])
        at += 1


def node_kernel(
    edge_ref,
    pos_ref,
    select_ref,
    all_ref,
    self_ref,
    count_ref,
    vec_ref,
    w1_ref,
    w2_ref,
    w3_ref,
    expand_hbm,
    contract_hbm,
    act1_ref,
    slope1_ref,
    slope2_ref,
    fresh_ref,
    table_ref,
    mixed1_ref,
    mixed2_ref,
    low_ref,
    slope_e_ref,
    act_sum_ref,
    proj_ref,
    self_pre_ref,
    expand_ref,
    contract_ref,
    sems,
):
    step = pl.program_id(0)
    last = pl.num_programs(0) - 1
    rows, width = self_ref.shape
    slots = edge_ref.shape[0]
    edge_width = edge_ref.shape[2]
    table_rows = table_ref.shape[0]
    expand_copy = pltpu.make_async_copy(expand_hbm, expand_ref, sems.at[0])
    contract_copy = pltpu.make_async_copy(contract_hbm, contract_ref, sems.at[1])

    @pl.when(step == 0)
    def _():
        expand_copy.start()
        contract_copy.start()
        table = dot_tn(select_ref[...], all_ref[...]).astype(BF16)
        table_ref[...] = table
        proj_ref[...] = dot_nn(table, w1_ref[width : 2 * width]).astype(BF16)
        self_pre_ref[...] = (
            dot_nn(self_ref[...], w1_ref[:width]) + vec_ref[V_MB1 : V_MB1 + 1, :]
        )
        act_sum_ref[...] = jnp.zeros_like(act_sum_ref)

    onehot = edge_onehot(pos_ref, table_rows)
    features = edge_ref[...].reshape(slots * rows, edge_width)
    pre1 = dot_nn(features, w1_ref[2 * width :]) + dot_nn(onehot, proj_ref[...])
    self_pre = self_pre_ref[...]
    act1 = []
    for k in range(slots):
        part = pl.ds(k * rows, rows)
        act, slope = gelu_pair(pre1[k * rows : (k + 1) * rows] + self_pre)
        act = act.astype(BF16)
        act1.append(act)
        act1_ref[part, :] = act
        slope1_ref[part, :] = slope.astype(BF16)
    pre2 = dot_nn(jnp.concatenate(act1, axis=0), w2_ref[...])
    bias2 = vec_ref[V_MB2 : V_MB2 + 1, :]
    act_sum = act_sum_ref[...]
    counts = count_ref[...]
    for k in range(slots):
        act, slope = gelu_pair(pre2[k * rows : (k + 1) * rows] + bias2)
        valid = counts > (step * slots + k).astype(F32)
        act_sum = act_sum + jnp.where(valid, act.astype(BF16).astype(F32), 0.0)
        slope2_ref[pl.ds(k * rows, rows), :] = jnp.where(valid, slope, 0.0).astype(BF16)
    act_sum_ref[...] = act_sum

    @pl.when(step == last)
    def _():
        summed = dot_split(dot_nn, act_sum_ref[...], w3_ref[...])
        summed = summed + counts * vec_ref[V_MB3 : V_MB3 + 1, :]
        mixed1 = self_ref[...].astype(F32) + summed / counts
        mixed1_ref[...] = mixed1
        xhat1, _ = norm_parts(mixed1)
        updated = xhat1 * vec_ref[V_N1G : V_N1G + 1, :] + vec_ref[V_N1S : V_N1S + 1, :]
        low = updated.astype(BF16)
        low_ref[...] = low
        expand_copy.wait()
        contract_copy.wait()
        mixed2 = updated + vec_ref[V_CB : V_CB + 1, :]
        for c in range(expand_ref.shape[1] // width):
            cols = slice(c * width, (c + 1) * width)
            pre = dot_nn(low, expand_ref[:, cols]) + vec_ref[V_EB + c : V_EB + c + 1, :]
            act, slope = gelu_pair(pre)
            act = act.astype(BF16)
            slope_e_ref[:, cols] = slope
            mixed2 = mixed2 + dot_nn(act, contract_ref[cols, :])
        mixed2_ref[...] = mixed2
        xhat2, _ = norm_parts(mixed2)
        fresh = (xhat2 * vec_ref[V_N2G : V_N2G + 1, :] + vec_ref[V_N2S : V_N2S + 1, :]).astype(BF16)
        fresh_ref[...] = fresh


def asked_onehot(asked_ref, rows):
    row = lax.broadcasted_iota(jnp.int32, (rows, asked_ref.shape[1]), 0)
    return (asked_ref[...] == row).astype(F32).astype(BF16)


def pick_kernel(asked_ref, fresh_ref, out_ref):
    out_ref[...] = dot_tn(asked_onehot(asked_ref, fresh_ref.shape[0]), fresh_ref[...]).astype(BF16)


def edge_kernel(
    edge_ref,
    cot_ref,
    pos_ref,
    fresh_ref,
    incoming_ref,
    count_ref,
    vec_ref,
    w1t_ref,
    w2_ref,
    w3_ref,
    out_ref,
    grad_ref,
    first_ref,
    own_ref,
    away_ref,
    pack_ref,
    vec_out_ref,
    table_ref,
    proj_ref,
    self_pre_ref,
    back_ref,
    dw3_ref,
    dw2_ref,
    dw1_ref,
    sums_ref,
):
    step = pl.program_id(0)
    last = pl.num_programs(0) - 1
    rows, width = fresh_ref.shape
    slots, _, edge_width = edge_ref.shape
    block = slots * rows
    table_rows = table_ref.shape[0]
    own_t = w1t_ref[:, :width]
    nbr_t = w1t_ref[:, width : 2 * width]
    feat_t = w1t_ref[:, 2 * width :]

    def vector(i):
        return vec_ref[V_EDGE + i : V_EDGE + i + 1, :edge_width]

    @pl.when(step == 0)
    def _():
        table_ref[:rows] = fresh_ref[...]
        table_ref[rows:] = incoming_ref[...]
        proj_ref[...] = dot_nt(table_ref[...], nbr_t).astype(BF16)
        self_pre_ref[...] = dot_nt(fresh_ref[...], own_t) + vector(0)
        for ref in (back_ref, dw3_ref, dw2_ref, dw1_ref, sums_ref, first_ref):
            ref[...] = jnp.zeros_like(ref)

    def flat(values):
        return values.reshape(block, edge_width)

    def deep(values):
        return values.reshape(slots, rows, edge_width)

    onehot = edge_onehot(pos_ref, table_rows)
    features = flat(edge_ref[...])
    pre1 = dot_nt(features, feat_t) + dot_nn(onehot, proj_ref[...])
    pre1 = deep(pre1) + self_pre_ref[...][None]
    act1, slope1 = gelu_pair(flat(pre1))
    act1 = act1.astype(BF16)
    pre2 = dot_nn(act1, w2_ref[...]) + vector(1)
    act2, slope2 = gelu_pair(pre2)
    act2 = act2.astype(BF16)
    mixed3 = features.astype(F32) + (dot_nn(act2, w3_ref[...]) + vector(2))
    xhat, scale = norm_parts(mixed3)
    gain = vector(3)
    slot = lax.broadcasted_iota(jnp.int32, (slots, rows, edge_width), 0) + step * slots
    valid = count_ref[...][None, :, :edge_width] > slot.astype(F32)
    out_ref[...] = jnp.where(valid, deep(xhat * gain + vector(4)), 0.0).astype(BF16)
    upstream = flat(jnp.where(valid, cot_ref[...].astype(F32), 0.0))
    sums_ref[3] += jnp.sum(deep(upstream * xhat), axis=0)
    sums_ref[4] += jnp.sum(deep(upstream), axis=0)
    grad_mixed = norm_back(xhat, scale, gain, upstream)
    grad_delta = grad_mixed.astype(BF16)
    dw3_ref[...] += dot_tn(act2, grad_delta)
    sums_ref[2] += jnp.sum(deep(grad_delta.astype(F32)), axis=0)
    grad2 = (dot_nt(grad_delta, w3_ref[...]) * slope2).astype(BF16)
    dw2_ref[...] += dot_tn(act1, grad2)
    sums_ref[1] += jnp.sum(deep(grad2.astype(F32)), axis=0)
    grad1 = (dot_nt(grad2, w2_ref[...]) * slope1).astype(BF16)
    dw1_ref[...] += dot_tn(grad1, features)
    first_ref[...] += jnp.sum(deep(grad1.astype(F32)), axis=0)
    back_ref[...] += dot_tn(onehot, grad1)
    grad_ref[...] = deep(grad_mixed + dot_nn(grad1, feat_t))

    @pl.when(step == last)
    def _():
        first = first_ref[...]
        back = back_ref[...]
        own_ref[...] = back[:rows]
        away_ref[...] = back[rows:].astype(BF16)
        first_high, first_rest = split_low(first)
        back_high, back_rest = split_low(back)
        own_grad = dot_tn(first_high, fresh_ref[...]) + dot_tn(first_rest, fresh_ref[...])
        nbr_grad = dot_tn(back_high, table_ref[...]) + dot_tn(back_rest, table_ref[...])
        pack_ref[:edge_width, :] = own_grad.astype(BF16)
        pack_ref[edge_width : 2 * edge_width, :] = nbr_grad.astype(BF16)
        pad = jnp.zeros((edge_width, width // 2 - edge_width), BF16)
        third = [dw1_ref[...].astype(BF16), pad, dw2_ref[...].astype(BF16), pad]
        pack_ref[2 * edge_width : 3 * edge_width, :] = jnp.concatenate(third, axis=1)
        fourth = [dw3_ref[...].astype(BF16), pad, jnp.zeros((edge_width, width // 2), BF16)]
        pack_ref[3 * edge_width :, :] = jnp.concatenate(fourth, axis=1)
        vec_out_ref[...] = jnp.zeros_like(vec_out_ref)
        vec_out_ref[0:1, :edge_width] = jnp.sum(first, axis=0, keepdims=True)
        for i in range(1, 5):
            vec_out_ref[i : i + 1, :edge_width] = jnp.sum(sums_ref[i], axis=0, keepdims=True)


def feed_kernel(
    cot_ref,
    first_ref,
    own_ref,
    arrived_ref,
    asked_ref,
    count_ref,
    vec_ref,
    w1t_ref,
    mixed1_ref,
    mixed2_ref,
    slope_ref,
    act_sum_ref,
    expand_ref,
    contract_ref,
    w3_ref,
    edge_vec_ref,
    pack_ref,
    contracted_ref,
    spread_ref,
    grad_mixed1_ref,
):
    rows, width = cot_ref.shape
    hidden = expand_ref.shape[1]
    own_t = w1t_ref[:, :width]
    nbr_t = w1t_ref[:, width : 2 * width]
    counts = count_ref[...]

    def vector(i):
        return vec_ref[i : i + 1, :]

    def total(values):
        return jnp.sum(values.astype(F32), axis=0, keepdims=True)

    back = own_ref[...] + dot_nn(asked_onehot(asked_ref, rows), arrived_ref[...])
    grad_fresh = (
        cot_ref[...].astype(F32)
        + dot_split(dot_nn, first_ref[...], own_t)
        + dot_split(dot_nn, back, nbr_t)
    )
    xhat2, scale2 = norm_parts(mixed2_ref[...])
    grad_mixed2 = norm_back(xhat2, scale2, vector(V_N2G), grad_fresh)
    grad_contracted = grad_mixed2.astype(BF16)
    contracted_ref[...] = grad_contracted
    grad_updated = grad_mixed2
    for c in range(hidden // width):
        cols = slice(c * width, (c + 1) * width)
        pre = dot_nt(grad_contracted, contract_ref[cols, :]) * slope_ref[:, cols]
        grad_updated = grad_updated + dot_nt(pre.astype(BF16), expand_ref[:, cols])
    xhat1, scale1 = norm_parts(mixed1_ref[...])
    grad_mixed1 = norm_back(xhat1, scale1, vector(V_N1G), grad_updated)
    grad_mixed1_ref[...] = grad_mixed1
    grad_message = (grad_mixed1 / counts).astype(BF16)
    spread_ref[...] = dot_nt(grad_message, w3_ref[...])
    pack_ref[:width, :] = dot_split(dot_tn, act_sum_ref[...], grad_message).astype(BF16)
    vectors = [
        total(counts * grad_message.astype(F32)),
        total(grad_updated * xhat1),
        total(grad_updated),
        total(grad_fresh * xhat2),
        total(grad_fresh),
        edge_vec_ref[...],
    ]
    vectors = jnp.concatenate(vectors, axis=0)
    vectors = jnp.concatenate(
        [vectors, jnp.zeros((pack_ref.shape[0] - width - vectors.shape[0], width), F32)], axis=0
    )
    pack_ref[width:, :] = vectors.astype(BF16)


def feed_weight_kernel(core_ref, low_ref, grad_ref, expand_ref, bias_ref, contract_ref, *refs, more):
    del core_ref
    sums_in = refs[:4] if more else None
    expand_out_ref, contract_out_ref, bias_out_ref, last_bias_ref, turned_ref = refs[-5:]
    chunk = pl.program_id(0)
    step = pl.program_id(1)
    units = expand_ref.shape[1]
    weight_t = expand_ref[...].T
    bias = jnp.broadcast_to(bias_ref[0:1, :], (8, units)).T[:, :1]
    ones = jnp.ones((8, low_ref.shape[0]), F32).astype(BF16)
    act, slope = gelu_pair(dot_nt(weight_t, low_ref[...]) + bias)
    contracted = dot_nn(act.astype(BF16), grad_ref[...])
    pre = (dot_nt(contract_ref[...], grad_ref[...]) * slope).astype(BF16)
    turned = dot_nn(pre, low_ref[...])
    sums = dot_nt(ones, pre)

    @pl.when(step == 0)
    def _():
        turned_ref[...] = turned
        contract_out_ref[...] = contracted + sums_in[1][...] if more else contracted
        bias_out_ref[...] = sums + sums_in[2][...] if more else sums

    @pl.when(step > 0)
    def _():
        turned_ref[...] += turned
        contract_out_ref[...] += contracted
        bias_out_ref[...] += sums

    @pl.when(step == pl.num_programs(1) - 1)
    def _():
        whole_turned = turned_ref[...].T
        expand_out_ref[...] = whole_turned + sums_in[0][...] if more else whole_turned

    @pl.when((chunk == 0) & (step == 0))
    def _():
        last_bias_ref[...] = sums_in[3][...] if more else jnp.zeros_like(last_bias_ref)

    @pl.when(chunk == 0)
    def _():
        last_bias_ref[...] += dot_nn(ones, grad_ref[...])


def message_kernel(
    core_ref,
    edge_ref,
    pos_ref,
    act1_ref,
    slope1_ref,
    slope2_ref,
    partial_ref,
    spread_ref,
    table_ref,
    w1_ref,
    w2_ref,
    edge_pack_ref,
    feed_pack_ref,
    grad_ref,
    first_ref,
    own_ref,
    away_ref,
    send_ref,
    keep_ref,
    back_ref,
    dw2_ref,
    dw1_ref,
    bias2_ref,
):
    step = pl.program_id(0)
    last = pl.num_programs(0) - 1
    slots, rows, edge_width = edge_ref.shape
    width = act1_ref.shape[1]
    block = slots * rows
    table_rows = table_ref.shape[0]

    @pl.when(step == 0)
    def _():
        for ref in (back_ref, dw2_ref, dw1_ref, bias2_ref, first_ref):
            ref[...] = jnp.zeros_like(ref)

    spread = spread_ref[...]
    grad2 = []
    bias2 = bias2_ref[...]
    for k in range(slots):
        part = (spread * slope2_ref[pl.ds(k * rows, rows), :].astype(F32)).astype(BF16)
        bias2 = bias2 + part.astype(F32)
        grad2.append(part)
    bias2_ref[...] = bias2
    grad2 = jnp.concatenate(grad2, axis=0)
    dw2_ref[...] += dot_tn(act1_ref[...], grad2)
    grad1 = (dot_nt(grad2, w2_ref[...]) * slope1_ref[...].astype(F32)).astype(BF16)
    first_ref[...] += jnp.sum(grad1.astype(F32).reshape(slots, rows, width), axis=0)
    onehot = edge_onehot(pos_ref, table_rows)
    back_ref[...] += dot_tn(onehot, grad1)
    features = edge_ref[...].reshape(block, edge_width)
    dw1_ref[...] += dot_tn(features, grad1)
    grad_ref[...] = partial_ref[...] + dot_nt(grad1, w1_ref[2 * width :]).reshape(
        slots, rows, edge_width
    )

    @pl.when(step == last)
    def _():
        first = first_ref[...]
        back = back_ref[...]
        own_ref[...] = back[:rows]
        away_ref[...] = back[rows:].astype(BF16)
        own_grad = dot_split_right(dot_tn, table_ref[:rows], first).astype(BF16)
        nbr_grad = dot_split_right(dot_tn, table_ref[...], back).astype(BF16)
        vectors = [
            feed_pack_ref[width:].astype(F32),
            jnp.sum(first, axis=0, keepdims=True),
            jnp.sum(bias2_ref[...], axis=0, keepdims=True),
        ]
        lower = [own_grad, nbr_grad, feed_pack_ref[:width]]
        upper = [dw1_ref[...].astype(BF16), dw2_ref[...].astype(BF16), edge_pack_ref[...]]

        def fill(ref, pieces, tail):
            base = 0
            for piece in pieces:
                ref[base : base + piece.shape[0]] = piece
                base += piece.shape[0]
            if base < ref.shape[0]:
                gap = ref.shape[0] - base - sum(v.shape[0] for v in tail)
                rest = jnp.concatenate(tail + [jnp.zeros((gap, width), F32)], axis=0)
                ref[base:] = rest.astype(BF16)

        @pl.when(core_ref[0] == 0)
        def _():
            fill(keep_ref, lower, [])
            fill(send_ref, upper, vectors)

        @pl.when(core_ref[0] != 0)
        def _():
            fill(send_ref, lower, [])
            fill(keep_ref, upper, vectors)


def pair_kernel(y_ref, keep_ref, came_ref, away_ref, out_ref, *, parts, cap):
    peers, total, _ = out_ref.shape
    x_size = lax.axis_size("x")
    z_size = parts // x_size
    riders = z_size * cap
    share = total - riders
    for p in range(peers):
        y, x = divmod(p, x_size)
        part = pl.ds(p * share, share)
        out_ref[p, riders:] = (
            keep_ref[part, :].astype(F32) + came_ref[part, :].astype(F32)
        ).astype(BF16)
        rows = [
            away_ref[pl.ds((z * x_size + x) * cap, cap), :].astype(F32) for z in range(z_size)
        ]
        rows = jnp.where(y_ref[0] == y, jnp.concatenate(rows, axis=0), 0.0)
        out_ref[p, :riders] = rows.astype(BF16)


def plane_kernel(y_ref, came_ref, out_ref, *, cap):
    peers = came_ref.shape[0]
    z_size, total, _ = out_ref.shape
    x_size = lax.axis_size("x")
    riders = x_size * cap
    share = total - riders
    first = z_size * cap
    for z in range(z_size):
        part = pl.ds(first + z * share, share)
        value = came_ref[0, part, :].astype(F32)
        for p in range(1, peers):
            value = value + came_ref[p, part, :].astype(F32)
        out_ref[z, riders:] = value.astype(BF16)
    rows = []
    for x in range(x_size):
        value = came_ref[x, :first].astype(F32)
        for y in range(1, peers // x_size):
            value = jnp.where(y_ref[0] == y, came_ref[y * x_size + x, :first].astype(F32), value)
        rows.append(value)
    for z in range(z_size):
        part = [value[z * cap : (z + 1) * cap] for value in rows]
        out_ref[z, :riders] = jnp.concatenate(part, axis=0).astype(BF16)


def column_kernel(came_ref, copies_ref, returned_ref):
    z_size, total, _ = came_ref.shape
    riders = returned_ref.shape[0] // z_size
    value = came_ref[0, riders:].astype(F32)
    for z in range(1, z_size):
        value = value + came_ref[z, riders:].astype(F32)
    for z in range(z_size):
        copies_ref[z] = value.astype(BF16)
        returned_ref[z * riders : (z + 1) * riders, :] = came_ref[z, :riders]


def node_grad_kernel(grad_ref, first_ref, own_ref, arrived_ref, asked_ref, w1_ref, out_ref):
    rows, width = grad_ref.shape
    back = own_ref[...] + dot_nn(asked_onehot(asked_ref, rows), arrived_ref[...])
    out_ref[...] = (
        grad_ref[...]
        + dot_split(dot_nt, first_ref[...], w1_ref[:width])
        + dot_split(dot_nt, back, w1_ref[width : 2 * width])
    )


def unpack_kernel(core_ref, mine_ref, other_ref, bias_ref, last_bias_ref, *refs):
    (
        message1_ref,
        message1_bias_ref,
        message2_ref,
        message2_bias_ref,
        message3_ref,
        message3_bias_ref,
        gain1_ref,
        shift1_ref,
        expand_bias_ref,
        contract_bias_ref,
        gain2_ref,
        shift2_ref,
        edge1_ref,
        edge1_bias_ref,
        edge2_ref,
        edge2_bias_ref,
        edge3_ref,
        edge3_bias_ref,
        gain3_ref,
        shift3_ref,
    ) = refs
    width = mine_ref.shape[1]
    edge_width = edge2_ref.shape[0]
    half = width // 2
    first_core = core_ref[0] == 0

    def lower(start, stop):
        return jnp.where(first_core, mine_ref[start:stop], other_ref[start:stop]).astype(F32)

    def upper(start, stop):
        return jnp.where(first_core, other_ref[start:stop], mine_ref[start:stop]).astype(F32)

    message1_ref[: 2 * width] = lower(0, 2 * width)
    message3_ref[...] = lower(2 * width, 3 * width)
    message1_ref[2 * width :] = upper(0, edge_width)
    base = edge_width
    message2_ref[...] = upper(base, base + width)
    base = base + width
    edge1_ref[:, :width] = upper(base, base + edge_width)
    edge1_ref[:, width : 2 * width] = upper(base + edge_width, base + 2 * edge_width)
    third = upper(base + 2 * edge_width, base + 3 * edge_width)
    edge1_ref[:, 2 * width :] = third[:, :edge_width]
    edge2_ref[...] = third[:, half : half + edge_width]
    edge3_ref[...] = upper(base + 3 * edge_width, base + 4 * edge_width)[:, :edge_width]
    base = base + 4 * edge_width
    vectors = upper(base, mine_ref.shape[0])
    targets = (message3_bias_ref, gain1_ref, shift1_ref, gain2_ref, shift2_ref)
    for i, ref in enumerate(targets):
        ref[...] = vectors[i]
    targets = (edge1_bias_ref, edge2_bias_ref, edge3_bias_ref, gain3_ref, shift3_ref)
    for i, ref in enumerate(targets):
        ref[...] = vectors[5 + i, :edge_width]
    message1_bias_ref[...] = vectors[16]
    message2_bias_ref[...] = vectors[17]
    expand_bias_ref[...] = bias_ref[0]
    contract_bias_ref[...] = last_bias_ref[0]


def gather_copies(values, axes):
    size = lax.axis_size(axes)
    copies = jnp.broadcast_to(values[None], (size, *values.shape))
    return lax.all_to_all(copies, axes, split_axis=0, concat_axis=0, tiled=True)


def exchange(values, parts):
    grouped = values.reshape(parts, values.shape[0] // parts, values.shape[1])
    arrived = lax.all_to_all(grouped, RES, split_axis=0, concat_axis=0, tiled=True)
    return arrived.reshape(values.shape)


def other_core(values):
    return lax.ppermute(values, "core", [(0, 1), (1, 0)])


def whole(shape):
    return pl.BlockSpec(shape, lambda *_: (0,) * len(shape))


def params():
    return pltpu.CompilerParams(vmem_limit_bytes=VMEM_BYTES)


def cost(microseconds):
    return pl.CostEstimate(
        flops=int(microseconds * 1.15e9),
        bytes_accessed=int(microseconds * 3.69e6),
        transcendentals=0,
    )


def body(
    node_states,
    edge_states,
    neighbour_index,
    edge_mask,
    node_cotangent,
    edge_cotangent,
    message_weight1,
    message_bias1,
    message_weight2,
    message_bias2,
    message_weight3,
    message_bias3,
    norm1_gain,
    norm1_shift,
    expand_weight,
    expand_bias,
    contract_weight,
    contract_bias,
    norm2_gain,
    norm2_shift,
    edge_weight1,
    edge_bias1,
    edge_weight2,
    edge_bias2,
    edge_weight3,
    edge_bias3,
    norm3_gain,
    norm3_shift,
):
    self_rows = node_states[0]
    rows, width = self_rows.shape
    slots = neighbour_index.shape[2]
    edge_width = edge_states.shape[3]
    hidden = expand_weight.shape[1]
    edges = rows * slots
    parts = lax.axis_size(RES)
    cap = ROW_CAP
    table_rows = rows + parts * cap
    steps = 5
    block_slots = slots // steps
    block = block_slots * rows
    pairs = block // LANES

    everyone = gather_copies(self_rows, RES).reshape(parts * rows, width)
    core = lax.axis_index("core").astype(jnp.int32).reshape(1)
    me = lax.axis_index(RES).astype(jnp.int32).reshape(1)
    edge_rows = edge_states[0].transpose(1, 0, 2)
    edge_cot = edge_cotangent[0].transpose(1, 0, 2)
    idx_rows = neighbour_index[0].T.reshape(edges // LANES, LANES)
    edge_w1t = edge_weight1.T
    wide = (
        message_bias1,
        message_bias2,
        message_bias3,
        norm1_gain,
        norm1_shift,
        contract_bias,
        norm2_gain,
        norm2_shift,
        expand_bias,
    )
    narrow = (edge_bias1, edge_bias2, edge_bias3, norm3_gain, norm3_shift)
    vmem = pl.BlockSpec(memory_space=pltpu.VMEM)

    def shape(dims, kind):
        return jax.ShapeDtypeStruct(dims, kind)

    pos, select, ids, counts, vectors = pl.pallas_call(
        functools.partial(
            prepare_kernel, parts=parts, cap=cap, steps=steps, wide=len(wide), narrow=len(narrow)
        ),
        out_shape=(
            shape((steps, LANES, pairs), jnp.int32),
            shape((parts * rows, table_rows), BF16),
            shape((1, parts * cap), jnp.int32),
            shape((rows, width), F32),
            shape((V_ROWS, width), F32),
        ),
        in_specs=[pl.BlockSpec(memory_space=pltpu.SMEM)] + [vmem] * (2 + len(wide) + len(narrow)),
        out_specs=(vmem,) * 5,
        compiler_params=params(),
        cost_estimate=cost(6),
        name="prepare",
    )(me, idx_rows, edge_mask[0].T, *wide, *narrow)
    ids, everyone = lax.optimization_barrier((ids, everyone))
    asked = lax.all_to_all(ids.reshape(parts, cap), RES, split_axis=0, concat_axis=0, tiled=True)
    asked = asked.reshape(1, parts * cap)

    edge_spec = pl.BlockSpec((block_slots, rows, edge_width), lambda i: (i, 0, 0))
    flat_spec = pl.BlockSpec((block, width), lambda i: (i, 0))
    pos_spec = pl.BlockSpec((1, LANES, pairs), lambda i: (i, 0, 0))
    any_spec = pl.BlockSpec(memory_space=pl.ANY)
    node_spec = whole((rows, width))
    away_spec = whole((parts * cap, width))

    (
        act1,
        slope1,
        slope2,
        fresh,
        table,
        mixed1,
        mixed2,
        low,
        slope_e,
        act_sum,
    ) = pl.pallas_call(
        node_kernel,
        grid=(steps,),
        in_specs=[
            edge_spec,
            pos_spec,
            whole((parts * rows, table_rows)),
            whole((parts * rows, width)),
            node_spec,
            node_spec,
            whole((V_ROWS, width)),
            whole(message_weight1.shape),
            whole((width, width)),
            whole((width, width)),
            any_spec,
            any_spec,
        ],
        out_specs=[
            flat_spec,
            flat_spec,
            flat_spec,
            node_spec,
            whole((table_rows, width)),
            node_spec,
            node_spec,
            node_spec,
            whole((rows, hidden)),
            node_spec,
        ],
        out_shape=[
            shape((edges, width), BF16),
            shape((edges, width), BF16),
            shape((edges, width), BF16),
            shape((rows, width), BF16),
            shape((table_rows, width), BF16),
            shape((rows, width), F32),
            shape((rows, width), F32),
            shape((rows, width), BF16),
            shape((rows, hidden), F32),
            shape((rows, width), F32),
        ],
        scratch_shapes=[
            pltpu.VMEM((table_rows, width), BF16),
            pltpu.VMEM((rows, width), F32),
            pltpu.VMEM((width, hidden), BF16),
            pltpu.VMEM((hidden, width), BF16),
            pltpu.SemaphoreType.DMA((2,)),
        ],
        compiler_params=params(),
        cost_estimate=cost(26),
        name="node_forward",
    )(
        edge_rows,
        pos,
        select,
        everyone,
        self_rows,
        counts,
        vectors,
        message_weight1,
        message_weight2,
        message_weight3,
        expand_weight,
        contract_weight,
    )
    outgoing = pl.pallas_call(
        pick_kernel,
        in_specs=[vmem] * 2,
        out_specs=vmem,
        out_shape=shape((parts * cap, width), BF16),
        compiler_params=params(),
        cost_estimate=cost(1),
        name="pick",
    )(asked, fresh)
    incoming = exchange(outgoing, parts)
    low_all = lax.all_gather(low, BY_CORE, axis=0, tiled=True)

    edge_pack_rows = 4 * edge_width
    edge_out, grad_partial, edge_first, edge_own, edge_away, edge_pack, edge_vec = pl.pallas_call(
        edge_kernel,
        grid=(steps,),
        in_specs=[
            edge_spec,
            edge_spec,
            pos_spec,
            node_spec,
            away_spec,
            node_spec,
            whole((V_ROWS, width)),
            whole(edge_w1t.shape),
            whole((edge_width, edge_width)),
            whole((edge_width, edge_width)),
        ],
        out_specs=[
            edge_spec,
            edge_spec,
            whole((rows, edge_width)),
            whole((rows, edge_width)),
            whole((parts * cap, edge_width)),
            whole((edge_pack_rows, width)),
            whole((8, width)),
        ],
        out_shape=[
            shape((slots, rows, edge_width), BF16),
            shape((slots, rows, edge_width), F32),
            shape((rows, edge_width), F32),
            shape((rows, edge_width), F32),
            shape((parts * cap, edge_width), BF16),
            shape((edge_pack_rows, width), BF16),
            shape((8, width), F32),
        ],
        scratch_shapes=[
            pltpu.VMEM((table_rows, width), BF16),
            pltpu.VMEM((table_rows, edge_width), BF16),
            pltpu.VMEM((rows, edge_width), F32),
            pltpu.VMEM((table_rows, edge_width), F32),
            pltpu.VMEM((edge_width, edge_width), F32),
            pltpu.VMEM((edge_width, edge_width), F32),
            pltpu.VMEM((edge_width, edge_width), F32),
            pltpu.VMEM((5, rows, edge_width), F32),
        ],
        compiler_params=params(),
        cost_estimate=cost(21),
        name="edge_both",
    )(
        edge_rows,
        edge_cot,
        pos,
        fresh,
        incoming,
        counts,
        vectors,
        edge_w1t,
        edge_weight2,
        edge_weight3,
    )
    edge_arrived = exchange(edge_away, parts)

    feed_rows = width + 16
    feed_pack, grad_contracted, spread, grad_mixed1 = pl.pallas_call(
        feed_kernel,
        in_specs=[vmem] * 16,
        out_specs=[vmem] * 4,
        out_shape=[
            shape((feed_rows, width), BF16),
            shape((rows, width), BF16),
            shape((rows, width), F32),
            shape((rows, width), F32),
        ],
        compiler_params=params(),
        cost_estimate=cost(7),
        name="feed_backward",
    )(
        node_cotangent[0],
        edge_first,
        edge_own,
        edge_arrived,
        asked,
        counts,
        vectors,
        edge_w1t,
        mixed1,
        mixed2,
        slope_e,
        act_sum,
        expand_weight,
        contract_weight,
        message_weight3,
        edge_vec,
    )
    grad_mine = gather_copies(grad_contracted, SIDE)
    side = grad_mine.shape[0]
    grad_mine = grad_mine.reshape(side * rows, width)

    unit = 16 * side
    half_rows = (3 * width + unit - 1) // unit * unit
    edge_grad, first, own, away, send, keep = pl.pallas_call(
        message_kernel,
        grid=(steps,),
        in_specs=[
            pl.BlockSpec(memory_space=pltpu.SMEM),
            edge_spec,
            pos_spec,
            flat_spec,
            flat_spec,
            flat_spec,
            edge_spec,
            node_spec,
            whole((table_rows, width)),
            whole(message_weight1.shape),
            whole((width, width)),
            whole((edge_pack_rows, width)),
            whole((feed_rows, width)),
        ],
        out_specs=[
            edge_spec,
            node_spec,
            node_spec,
            away_spec,
            whole((half_rows, width)),
            whole((half_rows, width)),
        ],
        out_shape=[
            shape((slots, rows, edge_width), F32),
            shape((rows, width), F32),
            shape((rows, width), F32),
            shape((parts * cap, width), BF16),
            shape((half_rows, width), BF16),
            shape((half_rows, width), BF16),
        ],
        scratch_shapes=[
            pltpu.VMEM((table_rows, width), F32),
            pltpu.VMEM((width, width), F32),
            pltpu.VMEM((edge_width, width), F32),
            pltpu.VMEM((rows, width), F32),
        ],
        compiler_params=params(),
        cost_estimate=cost(14),
        name="message_backward",
    )(
        core,
        edge_rows,
        pos,
        act1,
        slope1,
        slope2,
        grad_partial,
        spread,
        table,
        message_weight1,
        message_weight2,
        edge_pack,
        feed_pack,
    )
    send, grad_mine, low_all = lax.optimization_barrier((send, grad_mine, low_all))
    came = other_core(send)
    y_size = lax.axis_size("y")
    x_size = lax.axis_size("x")
    z_size = lax.axis_size("z")
    my_y = lax.axis_index("y").astype(jnp.int32).reshape(1)
    peers = y_size * x_size
    smem = pl.BlockSpec(memory_space=pltpu.SMEM)
    payload = pl.pallas_call(
        functools.partial(pair_kernel, parts=parts, cap=cap),
        in_specs=[smem] + [vmem] * 3,
        out_specs=vmem,
        out_shape=shape((peers, half_rows // peers + z_size * cap, width), BF16),
        compiler_params=params(),
        cost_estimate=cost(3),
        name="pair_sum",
    )(my_y, keep, came, away)
    grad_other = other_core(grad_mine)
    payload, grad_mine, grad_other, low_all = lax.optimization_barrier(
        (payload, grad_mine, grad_other, low_all)
    )
    arrived = lax.all_to_all(payload, PLANE, split_axis=0, concat_axis=0, tiled=True)
    bias_row = vectors[V_EB : V_EB + hidden // width].reshape(1, hidden)

    def feed_weights(low_values, grad_values, near, sums):
        units = 256
        row_block = min(side * rows, 1024)
        blocks = side * rows // row_block

        def low_block(c, r, core):
            return ((core[0] if near else 1 - core[0]) * blocks + r, 0)

        sum_specs = [
            pl.BlockSpec((width, units), lambda c, r, core: (0, c)),
            pl.BlockSpec((units, width), lambda c, r, core: (c, 0)),
            pl.BlockSpec((8, units), lambda c, r, core: (0, c)),
            whole((8, width)),
        ]
        return pl.pallas_call(
            functools.partial(feed_weight_kernel, more=bool(sums)),
            grid_spec=pltpu.PrefetchScalarGridSpec(
                num_scalar_prefetch=1,
                grid=(hidden // units, blocks),
                in_specs=[
                    pl.BlockSpec((row_block, width), low_block),
                    pl.BlockSpec((row_block, width), lambda c, r, core: (r, 0)),
                    pl.BlockSpec((width, units), lambda c, r, core: (0, c)),
                    pl.BlockSpec((1, units), lambda c, r, core: (0, c)),
                    pl.BlockSpec((units, width), lambda c, r, core: (c, 0)),
                ]
                + (sum_specs if sums else []),
                out_specs=sum_specs,
                scratch_shapes=[pltpu.VMEM((units, width), F32)],
            ),
            out_shape=[
                shape((width, hidden), F32),
                shape((hidden, width), F32),
                shape((8, hidden), F32),
                shape((8, width), F32),
            ],
            compiler_params=params(),
            cost_estimate=cost(21),
            name="feed_weights_near" if near else "feed_weights_far",
        )(core, low_values, grad_values, expand_weight, bias_row, contract_weight, *sums)

    sums = feed_weights(low_all, grad_mine, True, ())
    arrived, *sums = lax.optimization_barrier((arrived, *sums))
    payload = pl.pallas_call(
        functools.partial(plane_kernel, cap=cap),
        in_specs=[smem, vmem],
        out_specs=vmem,
        out_shape=shape((z_size, half_rows // side + x_size * cap, width), BF16),
        compiler_params=params(),
        cost_estimate=cost(3),
        name="plane_sum",
    )(my_y, arrived)
    arrived = lax.all_to_all(payload, "z", split_axis=0, concat_axis=0, tiled=True)
    copies, returned = pl.pallas_call(
        column_kernel,
        in_specs=[vmem],
        out_specs=[vmem] * 2,
        out_shape=[
            shape((z_size, half_rows // side, width), BF16),
            shape((parts * cap, width), BF16),
        ],
        compiler_params=params(),
        cost_estimate=cost(1),
        name="column_sum",
    )(arrived)
    column = lax.all_to_all(copies, "z", split_axis=0, concat_axis=0, tiled=True)
    column, grad_other, low_all, *sums = lax.optimization_barrier(
        (column, grad_other, low_all, *sums)
    )
    mine = gather_copies(column.reshape(half_rows // peers, width), PLANE).reshape(half_rows, width)
    sums = feed_weights(low_all, grad_other, False, tuple(sums))
    mine, *sums = lax.optimization_barrier((mine, *sums))
    grad_expand, grad_contract, expand_bias_sum, contract_bias_sum = sums
    other = other_core(mine)
    node_grad = pl.pallas_call(
        node_grad_kernel,
        in_specs=[vmem] * 6,
        out_specs=vmem,
        out_shape=shape((rows, width), F32),
        compiler_params=params(),
        cost_estimate=cost(3),
        name="node_gradient",
    )(grad_mixed1, first, own, returned, asked, message_weight1)

    vec = shape((width,), F32)
    thin = shape((edge_width,), F32)
    square = shape((width, width), F32)
    small = shape((edge_width, edge_width), F32)
    (
        grad_message1,
        grad_mb1,
        grad_message2,
        grad_mb2,
        grad_message3,
        grad_mb3,
        grad_n1g,
        grad_n1s,
        grad_eb,
        grad_cb,
        grad_n2g,
        grad_n2s,
        grad_edge1_t,
        grad_eb1,
        grad_edge2,
        grad_eb2,
        grad_edge3,
        grad_eb3,
        grad_n3g,
        grad_n3s,
    ) = pl.pallas_call(
        unpack_kernel,
        in_specs=[smem] + [vmem] * 4,
        out_specs=[vmem] * 20,
        out_shape=[
            shape(message_weight1.shape, F32),
            vec,
            square,
            vec,
            square,
            vec,
            vec,
            vec,
            shape((hidden,), F32),
            vec,
            vec,
            vec,
            shape(edge_w1t.shape, F32),
            thin,
            small,
            thin,
            small,
            thin,
            thin,
            thin,
        ],
        compiler_params=params(),
        cost_estimate=cost(4),
        name="unpack",
    )(core, mine, other, expand_bias_sum, contract_bias_sum)
    return (
        fresh[None],
        edge_out.transpose(1, 0, 2)[None],
        node_grad[None],
        edge_grad.transpose(1, 0, 2)[None],
        grad_message1,
        grad_mb1,
        grad_message2,
        grad_mb2,
        grad_message3,
        grad_mb3,
        grad_n1g,
        grad_n1s,
        grad_expand,
        grad_eb,
        grad_contract,
        grad_cb,
        grad_n2g,
        grad_n2s,
        grad_edge1_t.T,
        grad_eb1,
        grad_edge2,
        grad_eb2,
        grad_edge3,
        grad_eb3,
        grad_n3g,
        grad_n3s,
    )


def solution(mesh):
    batch, res = mesh.shape["batch"], mesh.shape["res"]
    x_size = 1 << ((res.bit_length() - 1) // 2)
    sizes = (batch // CORES, CORES, res // x_size, x_size)
    fine = jax.sharding.Mesh(mesh.devices.reshape(sizes), ALL)
    row_spec = P(("y", "core"), RES, None)
    edge_spec = P(("y", "core"), RES, None, None)
    return jax.shard_map(
        body,
        mesh=fine,
        in_specs=(row_spec, edge_spec, row_spec, row_spec, row_spec, edge_spec) + (P(),) * 22,
        out_specs=(row_spec, edge_spec, row_spec, edge_spec) + (P(),) * 22,
        check_vma=False,
    )
```

```python
import functools
import math

import jax
import jax.numpy as jnp
from jax import lax
from jax.experimental import pallas as pl
from jax.experimental.pallas import tpu as pltpu
from jax.sharding import PartitionSpec as P

ROW_CAP = 8
CORES = 2
RES = ("z", "x")
PLANE = ("y", "x")
SIDE = ("y", "z", "x")
ALL = ("y", "core", "z", "x")
BY_CORE = ("core", "y", "z", "x")
EPSILON = 1e-05
LANES = 128
MIB = 1024 * 1024
F32 = jnp.float32
BF16 = jnp.bfloat16

V_MB1, V_MB2, V_MB3, V_N1G, V_N1S, V_CB, V_N2G, V_N2S, V_EB = range(9)
V_EDGE = 12
V_ROWS = 24


def dot_nn(left, right):
    return lax.dot_general(left, right, (((1,), (0,)), ((), ())), preferred_element_type=F32)


def dot_nt(left, right):
    return lax.dot_general(left, right, (((1,), (1,)), ((), ())), preferred_element_type=F32)


def dot_tn(left, right):
    return lax.dot_general(left, right, (((0,), (0,)), ((), ())), preferred_element_type=F32)


def split_low(values):
    high = values.astype(BF16)
    return high, (values - high.astype(F32)).astype(BF16)


def dot_split(dot, left, right):
    high, rest = split_low(left)
    return dot(high, right) + dot(rest, right)


def dot_split_right(dot, left, right):
    high, rest = split_low(right)
    return dot(left, high) + dot(left, rest)


def gelu_pair(v):
    t = pltpu.reciprocal(1.0 + (0.3275911 / math.sqrt(2.0)) * jnp.abs(v), approx=True)
    e = jnp.exp2((v * v) * (-0.5 * math.log2(math.e)))
    poly = 0.5 * 1.061405429
    poly = poly * t + 0.5 * -1.453152027
    poly = poly * t + 0.5 * 1.421413741
    poly = poly * t + 0.5 * -0.284496736
    poly = poly * t + 0.5 * 0.254829592
    tail = poly * t * e
    phi_sum = jnp.where(v < 0, tail, 1.0 - tail)
    return v * phi_sum, phi_sum + (v * (1.0 / math.sqrt(2.0 * math.pi))) * e


def gelu_pair_erf(v):
    e = jnp.exp2((v * v) * (-0.5 * math.log2(math.e)))
    phi_sum = 0.5 + 0.5 * lax.erf(v * math.sqrt(0.5))
    return v * phi_sum, phi_sum + (v * (1.0 / math.sqrt(2.0 * math.pi))) * e


def norm_parts(values):
    average = jnp.mean(values, axis=-1, keepdims=True)
    centred = values - average
    variance = jnp.mean(centred * centred, axis=-1, keepdims=True)
    scale = lax.rsqrt(variance + EPSILON)
    return centred * scale, scale


def norm_back(xhat, scale, gain, upstream):
    w = upstream * gain
    mean_w = jnp.mean(w, axis=-1, keepdims=True)
    mean_wx = jnp.mean(w * xhat, axis=-1, keepdims=True)
    return (w - mean_w - xhat * mean_wx) * scale


def edge_onehot(pos_ref, table_rows):
    pairs = pos_ref.shape[2]
    lane = lax.broadcasted_iota(jnp.int32, (LANES, table_rows), 1)
    return jnp.concatenate(
        [(pos_ref[0, :, p : p + 1] == lane).astype(F32).astype(BF16) for p in range(pairs)], axis=0
    )


def prepare_kernel(me_ref, idx_ref, mask_ref, *refs, parts, cap, steps, wide, narrow):
    wide_refs = refs[:wide]
    narrow_refs = refs[wide : wide + narrow]
    pos_ref, select_ref, ids_ref, count_ref, vec_ref, expand_bias_ref = refs[wide + narrow :]
    rows, width = count_ref.shape
    total = rows * parts
    table = rows + parts * cap
    me = me_ref[0]
    pair_rows = idx_ref.shape[0] // 2
    named = [
        jnp.concatenate([idx_ref[2 * j], idx_ref[2 * j + 1]], axis=1) for j in range(pair_rows)
    ]
    residue = lax.broadcasted_iota(jnp.int32, (total, LANES), 0)
    owner = residue // rows
    within = residue - owner * rows
    hits = jnp.zeros((total, LANES), F32)
    for j in range(pair_rows):
        hits = jnp.where(named[j] == residue, 1.0, hits)
    hit = jnp.max(hits, axis=1, keepdims=True)
    own = owner == me
    wanted = jnp.where(own, 0.0, jnp.broadcast_to(hit, (total, LANES)))
    low_row = lax.broadcasted_iota(jnp.int32, (rows, rows), 0)
    low_col = lax.broadcasted_iota(jnp.int32, (rows, rows), 1)
    lower = (low_col <= low_row).astype(F32).astype(BF16)
    wanted_low = wanted.astype(BF16)
    place = jnp.concatenate(
        [dot_nn(lower, wanted_low[o * rows : (o + 1) * rows]) for o in range(parts)], axis=0
    )
    place = jnp.clip(place - 1.0, 0.0, cap - 1.0)
    pos = jnp.where(own, within.astype(F32), (rows + owner * cap).astype(F32) + place)
    picked = [
        jnp.sum(jnp.where(named[j] == residue, pos, 0.0), axis=0, keepdims=True)
        for j in range(pair_rows)
    ]
    picked.append(jnp.zeros((LANES - pair_rows, LANES), F32))
    turned = jnp.concatenate(picked, axis=0).T.astype(jnp.int32)
    per = pair_rows // steps
    for s in range(steps):
        pos_ref[s] = turned[:, s * per : (s + 1) * per]
    lane = lax.broadcasted_iota(jnp.int32, (total, table), 1).astype(F32)
    live = jnp.where(own, 1.0, wanted)
    chosen = jnp.where(lane == pos[:, :1], jnp.broadcast_to(live[:, :1], (total, table)), 0.0)
    select_ref[...] = chosen.astype(BF16)
    asked_row = jnp.broadcast_to(within[:, :1].astype(F32), (total, parts * cap))
    ids = jnp.sum(chosen[:, rows:] * asked_row, axis=0, keepdims=True)
    ids = ids.astype(jnp.int32)
    for o in range(parts):
        ids_ref[o : o + 1, :] = ids[:, o * cap : (o + 1) * cap]
    count = mask_ref[0]
    for k in range(1, mask_ref.shape[0]):
        count = count + mask_ref[k]
    count = jnp.concatenate([count.astype(F32), jnp.zeros((7, rows), F32)], axis=0)
    count_ref[...] = dot_tn(count.astype(BF16), jnp.ones((8, width), F32).astype(BF16))
    expand_bias_ref[...] = wide_refs[-1][...].astype(F32).reshape(expand_bias_ref.shape)
    vec_ref[...] = jnp.zeros_like(vec_ref)
    at = 0
    for ref in wide_refs:
        for c in range(ref.shape[0] // width):
            part = ref[c * width : (c + 1) * width]
            vec_ref[at : at + 1, :] = part.astype(F32).reshape(1, width)
            at += 1
    for ref in narrow_refs:
        vec_ref[at : at + 1, : ref.shape[0]] = ref[...].astype(F32).reshape(1, ref.shape[0])
        at += 1


def node_kernel(
    edge_ref,
    pos_ref,
    select_ref,
    all_ref,
    self_ref,
    count_ref,
    vec_ref,
    w1_ref,
    w2_ref,
    w3_ref,
    expand_hbm,
    contract_hbm,
    act1_ref,
    slope1_ref,
    slope2_ref,
    fresh_ref,
    table_ref,
    mixed1_ref,
    mixed2_ref,
    low_ref,
    slope_e_ref,
    act_sum_ref,
    proj_ref,
    self_pre_ref,
    expand_ref,
    contract_ref,
    sems,
):
    step = pl.program_id(0)
    last = pl.num_programs(0) - 1
    rows, width = self_ref.shape
    slots = edge_ref.shape[0]
    edge_width = edge_ref.shape[2]
    table_rows = table_ref.shape[0]
    expand_copy = pltpu.make_async_copy(expand_hbm, expand_ref, sems.at[0])
    contract_copy = pltpu.make_async_copy(contract_hbm, contract_ref, sems.at[1])

    @pl.when(step == 0)
    def _():
        expand_copy.start()
        contract_copy.start()
        table = dot_tn(select_ref[...], all_ref[...]).astype(BF16)
        table_ref[...] = table
        proj_ref[...] = dot_nn(table, w1_ref[width : 2 * width]).astype(BF16)
        self_pre_ref[...] = (
            dot_nn(self_ref[...], w1_ref[:width]) + vec_ref[V_MB1 : V_MB1 + 1, :]
        )
        act_sum_ref[...] = jnp.zeros_like(act_sum_ref)

    onehot = edge_onehot(pos_ref, table_rows)
    features = edge_ref[...].reshape(slots * rows, edge_width)
    pre1 = dot_nn(features, w1_ref[2 * width :]) + dot_nn(onehot, proj_ref[...])
    self_pre = self_pre_ref[...]
    act1 = []
    for k in range(slots):
        part = pl.ds(k * rows, rows)
        act, slope = gelu_pair_erf(pre1[k * rows : (k + 1) * rows] + self_pre)
        act = act.astype(BF16)
        act1.append(act)
        act1_ref[part, :] = act
        slope1_ref[part, :] = slope.astype(BF16)
    pre2 = dot_nn(jnp.concatenate(act1, axis=0), w2_ref[...])
    bias2 = vec_ref[V_MB2 : V_MB2 + 1, :]
    act_sum = act_sum_ref[...]
    counts = count_ref[...]
    for k in range(slots):
        act, slope = gelu_pair_erf(pre2[k * rows : (k + 1) * rows] + bias2)
        valid = counts > (step * slots + k).astype(F32)
        act_sum = act_sum + jnp.where(valid, act.astype(BF16).astype(F32), 0.0)
        slope2_ref[pl.ds(k * rows, rows), :] = jnp.where(valid, slope, 0.0).astype(BF16)
    act_sum_ref[...] = act_sum

    @pl.when(step == last)
    def _():
        summed = dot_split(dot_nn, act_sum_ref[...], w3_ref[...])
        summed = summed + counts * vec_ref[V_MB3 : V_MB3 + 1, :]
        mixed1 = self_ref[...].astype(F32) + summed / counts
        mixed1_ref[...] = mixed1
        xhat1, _ = norm_parts(mixed1)
        updated = xhat1 * vec_ref[V_N1G : V_N1G + 1, :] + vec_ref[V_N1S : V_N1S + 1, :]
        low = updated.astype(BF16)
        low_ref[...] = low
        expand_copy.wait()
        contract_copy.wait()
        mixed2 = updated + vec_ref[V_CB : V_CB + 1, :]
        for c in range(expand_ref.shape[1] // width):
            cols = slice(c * width, (c + 1) * width)
            pre = dot_nn(low, expand_ref[:, cols]) + vec_ref[V_EB + c : V_EB + c + 1, :]
            act, slope = gelu_pair_erf(pre)
            act = act.astype(BF16)
            slope_e_ref[:, cols] = slope
            mixed2 = mixed2 + dot_nn(act, contract_ref[cols, :])
        mixed2_ref[...] = mixed2
        xhat2, _ = norm_parts(mixed2)
        fresh = (xhat2 * vec_ref[V_N2G : V_N2G + 1, :] + vec_ref[V_N2S : V_N2S + 1, :]).astype(BF16)
        fresh_ref[...] = fresh


def asked_onehot(asked_ref, rows):
    parts = asked_ref.shape[0]
    asked = jnp.concatenate([asked_ref[o : o + 1, :] for o in range(parts)], axis=1)
    row = lax.broadcasted_iota(jnp.int32, (rows, asked.shape[1]), 0)
    return (asked == row).astype(F32).astype(BF16)


def pick_kernel(asked_ref, fresh_ref, out_ref):
    out_ref[...] = dot_tn(asked_onehot(asked_ref, fresh_ref.shape[0]), fresh_ref[...]).astype(BF16)


def edge_kernel(
    edge_ref,
    cot_ref,
    pos_ref,
    fresh_ref,
    incoming_ref,
    count_ref,
    vec_ref,
    w1t_ref,
    w2_ref,
    w3_ref,
    out_ref,
    grad_ref,
    first_ref,
    own_ref,
    away_ref,
    pack_ref,
    vec_out_ref,
    table_ref,
    proj_ref,
    self_pre_ref,
    back_ref,
    dw3_ref,
    dw2_ref,
    dw1_ref,
    sums_ref,
):
    step = pl.program_id(0)
    last = pl.num_programs(0) - 1
    rows, width = fresh_ref.shape
    slots, _, edge_width = edge_ref.shape
    block = slots * rows
    table_rows = table_ref.shape[0]
    own_t = w1t_ref[:, :width]
    nbr_t = w1t_ref[:, width : 2 * width]
    feat_t = w1t_ref[:, 2 * width :]

    def vector(i):
        return vec_ref[V_EDGE + i : V_EDGE + i + 1, :edge_width]

    @pl.when(step == 0)
    def _():
        table_ref[:rows] = fresh_ref[...]
        table_ref[rows:] = incoming_ref[...]
        proj_ref[...] = dot_nt(table_ref[...], nbr_t).astype(BF16)
        self_pre_ref[...] = dot_nt(fresh_ref[...], own_t) + vector(0)
        for ref in (back_ref, dw3_ref, dw2_ref, dw1_ref, sums_ref, first_ref):
            ref[...] = jnp.zeros_like(ref)

    def flat(values):
        return values.reshape(block, edge_width)

    def deep(values):
        return values.reshape(slots, rows, edge_width)

    onehot = edge_onehot(pos_ref, table_rows)
    features = flat(edge_ref[...])
    pre1 = dot_nt(features, feat_t) + dot_nn(onehot, proj_ref[...])
    pre1 = deep(pre1) + self_pre_ref[...][None]
    act1, slope1 = gelu_pair_erf(flat(pre1))
    act1 = act1.astype(BF16)
    pre2 = dot_nn(act1, w2_ref[...]) + vector(1)
    act2, slope2 = gelu_pair_erf(pre2)
    act2 = act2.astype(BF16)
    mixed3 = features.astype(F32) + (dot_nn(act2, w3_ref[...]) + vector(2))
    xhat, scale = norm_parts(mixed3)
    gain = vector(3)
    slot = lax.broadcasted_iota(jnp.int32, (slots, rows, edge_width), 0) + step * slots
    valid = count_ref[...][None, :, :edge_width] > slot.astype(F32)
    out_ref[...] = jnp.where(valid, deep(xhat * gain + vector(4)), 0.0).astype(BF16)
    upstream = flat(jnp.where(valid, cot_ref[...].astype(F32), 0.0))
    sums_ref[3] += jnp.sum(deep(upstream * xhat), axis=0)
    sums_ref[4] += jnp.sum(deep(upstream), axis=0)
    grad_mixed = norm_back(xhat, scale, gain, upstream)
    grad_delta = grad_mixed.astype(BF16)
    dw3_ref[...] += dot_tn(act2, grad_delta)
    sums_ref[2] += jnp.sum(deep(grad_delta.astype(F32)), axis=0)
    grad2 = (dot_nt(grad_delta, w3_ref[...]) * slope2).astype(BF16)
    dw2_ref[...] += dot_tn(act1, grad2)
    sums_ref[1] += jnp.sum(deep(grad2.astype(F32)), axis=0)
    grad1 = (dot_nt(grad2, w2_ref[...]) * slope1).astype(BF16)
    dw1_ref[...] += dot_tn(grad1, features)
    first_ref[...] += jnp.sum(deep(grad1.astype(F32)), axis=0)
    back_ref[...] += dot_tn(onehot, grad1)
    grad_ref[...] = deep(grad_mixed + dot_nn(grad1, feat_t))

    @pl.when(step == last)
    def _():
        first = first_ref[...]
        back = back_ref[...]
        own_ref[...] = back[:rows]
        away_ref[...] = back[rows:].astype(BF16)
        first_high, first_rest = split_low(first)
        back_high, back_rest = split_low(back)
        own_grad = dot_tn(first_high, fresh_ref[...]) + dot_tn(first_rest, fresh_ref[...])
        nbr_grad = dot_tn(back_high, table_ref[...]) + dot_tn(back_rest, table_ref[...])
        pack_ref[:edge_width, :] = own_grad.astype(BF16)
        pack_ref[edge_width : 2 * edge_width, :] = nbr_grad.astype(BF16)
        pad = jnp.zeros((edge_width, width // 2 - edge_width), BF16)
        third = [dw1_ref[...].astype(BF16), pad, dw2_ref[...].astype(BF16), pad]
        pack_ref[2 * edge_width : 3 * edge_width, :] = jnp.concatenate(third, axis=1)
        fourth = [dw3_ref[...].astype(BF16), pad, jnp.zeros((edge_width, width // 2), BF16)]
        pack_ref[3 * edge_width :, :] = jnp.concatenate(fourth, axis=1)
        vec_out_ref[...] = jnp.zeros_like(vec_out_ref)
        vec_out_ref[0:1, :edge_width] = jnp.sum(first, axis=0, keepdims=True)
        for i in range(1, 5):
            vec_out_ref[i : i + 1, :edge_width] = jnp.sum(sums_ref[i], axis=0, keepdims=True)


def feed_kernel(
    cot_ref,
    first_ref,
    own_ref,
    arrived_ref,
    asked_ref,
    count_ref,
    vec_ref,
    w1t_ref,
    mixed1_ref,
    mixed2_ref,
    slope_ref,
    act_sum_ref,
    expand_ref,
    contract_ref,
    w3_ref,
    edge_vec_ref,
    pack_ref,
    copies_ref,
    spread_ref,
    grad_mixed1_ref,
):
    rows, width = cot_ref.shape
    hidden = expand_ref.shape[1]
    own_t = w1t_ref[:, :width]
    nbr_t = w1t_ref[:, width : 2 * width]
    counts = count_ref[...]

    def vector(i):
        return vec_ref[i : i + 1, :]

    def total(values):
        return jnp.sum(values.astype(F32), axis=0, keepdims=True)

    back = own_ref[...] + dot_nn(asked_onehot(asked_ref, rows), arrived_ref[...])
    grad_fresh = (
        cot_ref[...].astype(F32)
        + dot_split(dot_nn, first_ref[...], own_t)
        + dot_split(dot_nn, back, nbr_t)
    )
    xhat2, scale2 = norm_parts(mixed2_ref[...])
    grad_mixed2 = norm_back(xhat2, scale2, vector(V_N2G), grad_fresh)
    grad_contracted = grad_mixed2.astype(BF16)
    for p in range(copies_ref.shape[0]):
        copies_ref[p] = grad_contracted
    grad_updated = grad_mixed2
    for c in range(hidden // width):
        cols = slice(c * width, (c + 1) * width)
        pre = dot_nt(grad_contracted, contract_ref[cols, :]) * slope_ref[:, cols]
        grad_updated = grad_updated + dot_nt(pre.astype(BF16), expand_ref[:, cols])
    xhat1, scale1 = norm_parts(mixed1_ref[...])
    grad_mixed1 = norm_back(xhat1, scale1, vector(V_N1G), grad_updated)
    grad_mixed1_ref[...] = grad_mixed1
    grad_message = (grad_mixed1 / counts).astype(BF16)
    spread_ref[...] = dot_nt(grad_message, w3_ref[...])
    pack_ref[:width, :] = dot_split(dot_tn, act_sum_ref[...], grad_message).astype(BF16)
    vectors = [
        total(counts * grad_message.astype(F32)),
        total(grad_updated * xhat1),
        total(grad_updated),
        total(grad_fresh * xhat2),
        total(grad_fresh),
        edge_vec_ref[...],
    ]
    vectors = jnp.concatenate(vectors, axis=0)
    vectors = jnp.concatenate(
        [vectors, jnp.zeros((pack_ref.shape[0] - width - vectors.shape[0], width), F32)], axis=0
    )
    pack_ref[width:, :] = vectors.astype(BF16)


def feed_weight_kernel(core_ref, low_ref, grad_ref, expand_ref, bias_ref, contract_ref, *refs, more):
    del core_ref
    sums_in = refs[:4] if more else None
    expand_out_ref, contract_out_ref, bias_out_ref, last_bias_ref, turned_ref = refs[-5:]
    chunk = pl.program_id(0)
    step = pl.program_id(1)
    units = expand_ref.shape[1]
    weight_t = expand_ref[...].T
    bias = jnp.broadcast_to(bias_ref[0:1, :], (8, units)).T[:, :1]
    ones = jnp.ones((8, low_ref.shape[0]), F32).astype(BF16)
    act, slope = gelu_pair(dot_nt(weight_t, low_ref[...]) + bias)
    contracted = dot_nn(act.astype(BF16), grad_ref[...])
    pre = (dot_nt(contract_ref[...], grad_ref[...]) * slope).astype(BF16)
    turned = dot_nn(pre, low_ref[...])
    sums = dot_nt(ones, pre)

    @pl.when(step == 0)
    def _():
        turned_ref[...] = turned
        contract_out_ref[...] = contracted + sums_in[1][...] if more else contracted
        bias_out_ref[...] = sums + sums_in[2][...] if more else sums

    @pl.when(step > 0)
    def _():
        turned_ref[...] += turned
        contract_out_ref[...] += contracted
        bias_out_ref[...] += sums

    @pl.when(step == pl.num_programs(1) - 1)
    def _():
        whole_turned = turned_ref[...].T
        expand_out_ref[...] = whole_turned + sums_in[0][...] if more else whole_turned

    @pl.when((chunk == 0) & (step == 0))
    def _():
        last_bias_ref[...] = sums_in[3][...] if more else jnp.zeros_like(last_bias_ref)

    @pl.when(chunk == 0)
    def _():
        last_bias_ref[...] += dot_nn(ones, grad_ref[...])


def message_kernel(
    core_ref,
    edge_ref,
    pos_ref,
    act1_ref,
    slope1_ref,
    slope2_ref,
    partial_ref,
    spread_ref,
    table_ref,
    w1_ref,
    w2_ref,
    edge_pack_ref,
    feed_pack_ref,
    grad_ref,
    first_ref,
    own_ref,
    away_ref,
    send_ref,
    keep_ref,
    back_ref,
    dw2_ref,
    dw1_ref,
    bias2_ref,
):
    step = pl.program_id(0)
    last = pl.num_programs(0) - 1
    slots, rows, edge_width = edge_ref.shape
    width = act1_ref.shape[1]
    block = slots * rows
    table_rows = table_ref.shape[0]

    @pl.when(step == 0)
    def _():
        for ref in (back_ref, dw2_ref, dw1_ref, bias2_ref, first_ref):
            ref[...] = jnp.zeros_like(ref)

    spread = spread_ref[...]
    grad2 = []
    bias2 = bias2_ref[...]
    for k in range(slots):
        part = (spread * slope2_ref[pl.ds(k * rows, rows), :].astype(F32)).astype(BF16)
        bias2 = bias2 + part.astype(F32)
        grad2.append(part)
    bias2_ref[...] = bias2
    grad2 = jnp.concatenate(grad2, axis=0)
    dw2_ref[...] += dot_tn(act1_ref[...], grad2)
    grad1 = (dot_nt(grad2, w2_ref[...]) * slope1_ref[...].astype(F32)).astype(BF16)
    first_ref[...] += jnp.sum(grad1.astype(F32).reshape(slots, rows, width), axis=0)
    onehot = edge_onehot(pos_ref, table_rows)
    back_ref[...] += dot_tn(onehot, grad1)
    features = edge_ref[...].reshape(block, edge_width)
    dw1_ref[...] += dot_tn(features, grad1)
    grad_ref[...] = partial_ref[...] + dot_nt(grad1, w1_ref[2 * width :]).reshape(
        slots, rows, edge_width
    )

    @pl.when(step == last)
    def _():
        first = first_ref[...]
        back = back_ref[...]
        own_ref[...] = back[:rows]
        away_ref[...] = back[rows:].astype(BF16)
        own_grad = dot_split_right(dot_tn, table_ref[:rows], first).astype(BF16)
        nbr_grad = dot_split_right(dot_tn, table_ref[...], back).astype(BF16)
        vectors = [
            feed_pack_ref[width:].astype(F32),
            jnp.sum(first, axis=0, keepdims=True),
            jnp.sum(bias2_ref[...], axis=0, keepdims=True),
        ]
        lower = [own_grad, nbr_grad, feed_pack_ref[:width]]
        upper = [dw1_ref[...].astype(BF16), dw2_ref[...].astype(BF16), edge_pack_ref[...]]

        def fill(ref, pieces, tail):
            base = 0
            for piece in pieces:
                ref[base : base + piece.shape[0]] = piece
                base += piece.shape[0]
            if base < ref.shape[0]:
                gap = ref.shape[0] - base - sum(v.shape[0] for v in tail)
                rest = jnp.concatenate(tail + [jnp.zeros((gap, width), F32)], axis=0)
                ref[base:] = rest.astype(BF16)

        @pl.when(core_ref[0] == 0)
        def _():
            fill(keep_ref, lower, [])
            fill(send_ref, upper, vectors)

        @pl.when(core_ref[0] != 0)
        def _():
            fill(send_ref, lower, [])
            fill(keep_ref, upper, vectors)


def pair_kernel(y_ref, keep_ref, came_ref, away_ref, out_ref, *, parts, cap):
    peers, total, _ = out_ref.shape
    x_size = lax.axis_size("x")
    z_size = parts // x_size
    riders = z_size * cap
    share = total - riders
    for p in range(peers):
        y, x = divmod(p, x_size)
        part = pl.ds(p * share, share)
        out_ref[p, riders:] = (
            keep_ref[part, :].astype(F32) + came_ref[part, :].astype(F32)
        ).astype(BF16)
        rows = [
            away_ref[pl.ds((z * x_size + x) * cap, cap), :].astype(F32) for z in range(z_size)
        ]
        rows = jnp.where(y_ref[0] == y, jnp.concatenate(rows, axis=0), 0.0)
        out_ref[p, :riders] = rows.astype(BF16)


def plane_kernel(y_ref, came_ref, out_ref, *, cap):
    peers = came_ref.shape[0]
    z_size, total, _ = out_ref.shape
    x_size = lax.axis_size("x")
    riders = x_size * cap
    share = total - riders
    first = z_size * cap
    for z in range(z_size):
        part = pl.ds(first + z * share, share)
        value = came_ref[0, part, :].astype(F32)
        for p in range(1, peers):
            value = value + came_ref[p, part, :].astype(F32)
        out_ref[z, riders:] = value.astype(BF16)
    rows = []
    for x in range(x_size):
        value = came_ref[x, :first].astype(F32)
        for y in range(1, peers // x_size):
            value = jnp.where(y_ref[0] == y, came_ref[y * x_size + x, :first].astype(F32), value)
        rows.append(value)
    for z in range(z_size):
        part = [value[z * cap : (z + 1) * cap] for value in rows]
        out_ref[z, :riders] = jnp.concatenate(part, axis=0).astype(BF16)


def column_kernel(came_ref, copies_ref, returned_ref):
    z_size, total, _ = came_ref.shape
    riders = returned_ref.shape[0] // z_size
    value = came_ref[0, riders:].astype(F32)
    for z in range(1, z_size):
        value = value + came_ref[z, riders:].astype(F32)
    for z in range(z_size):
        copies_ref[z] = value.astype(BF16)
        returned_ref[z * riders : (z + 1) * riders, :] = came_ref[z, :riders]


def node_grad_kernel(grad_ref, first_ref, own_ref, arrived_ref, asked_ref, w1_ref, out_ref):
    rows, width = grad_ref.shape
    back = own_ref[...] + dot_nn(asked_onehot(asked_ref, rows), arrived_ref[...])
    out_ref[...] = (
        grad_ref[...]
        + dot_split(dot_nt, first_ref[...], w1_ref[:width])
        + dot_split(dot_nt, back, w1_ref[width : 2 * width])
    )


def unpack_kernel(core_ref, mine_ref, other_ref, bias_ref, last_bias_ref, *refs):
    (
        message1_ref,
        message1_bias_ref,
        message2_ref,
        message2_bias_ref,
        message3_ref,
        message3_bias_ref,
        gain1_ref,
        shift1_ref,
        expand_bias_ref,
        contract_bias_ref,
        gain2_ref,
        shift2_ref,
        edge1_ref,
        edge1_bias_ref,
        edge2_ref,
        edge2_bias_ref,
        edge3_ref,
        edge3_bias_ref,
        gain3_ref,
        shift3_ref,
    ) = refs
    width = mine_ref.shape[1]
    edge_width = edge2_ref.shape[0]
    half = width // 2
    first_core = core_ref[0] == 0

    def lower(start, stop):
        return jnp.where(first_core, mine_ref[start:stop], other_ref[start:stop]).astype(F32)

    def upper(start, stop):
        return jnp.where(first_core, other_ref[start:stop], mine_ref[start:stop]).astype(F32)

    message1_ref[: 2 * width] = lower(0, 2 * width)
    message3_ref[...] = lower(2 * width, 3 * width)
    message1_ref[2 * width :] = upper(0, edge_width)
    base = edge_width
    message2_ref[...] = upper(base, base + width)
    base = base + width
    edge1_ref[:, :width] = upper(base, base + edge_width)
    edge1_ref[:, width : 2 * width] = upper(base + edge_width, base + 2 * edge_width)
    third = upper(base + 2 * edge_width, base + 3 * edge_width)
    edge1_ref[:, 2 * width :] = third[:, :edge_width]
    edge2_ref[...] = third[:, half : half + edge_width]
    edge3_ref[...] = upper(base + 3 * edge_width, base + 4 * edge_width)[:, :edge_width]
    base = base + 4 * edge_width
    vectors = upper(base, mine_ref.shape[0])
    targets = (message3_bias_ref, gain1_ref, shift1_ref, gain2_ref, shift2_ref)
    for i, ref in enumerate(targets):
        ref[...] = vectors[i]
    targets = (edge1_bias_ref, edge2_bias_ref, edge3_bias_ref, gain3_ref, shift3_ref)
    for i, ref in enumerate(targets):
        ref[...] = vectors[5 + i, :edge_width]
    message1_bias_ref[...] = vectors[16]
    message2_bias_ref[...] = vectors[17]
    expand_bias_ref[...] = bias_ref[0]
    contract_bias_ref[...] = last_bias_ref[0]


def gather_copies(copies, axes):
    return lax.all_to_all(copies, axes, split_axis=0, concat_axis=0, tiled=True)


def copies_of(values, axes):
    return jnp.broadcast_to(values[None], (lax.axis_size(axes), *values.shape))


def exchange(values, parts):
    grouped = values.reshape(parts, values.shape[0] // parts, values.shape[1])
    arrived = lax.all_to_all(grouped, RES, split_axis=0, concat_axis=0, tiled=True)
    return arrived.reshape(values.shape)


def other_core(values):
    return lax.ppermute(values, "core", [(0, 1), (1, 0)])


def whole(shape):
    return pl.BlockSpec(shape, lambda *_: (0,) * len(shape))


def params(mebibytes):
    return pltpu.CompilerParams(vmem_limit_bytes=mebibytes * MIB)


def cost(microseconds):
    return pl.CostEstimate(
        flops=int(microseconds * 1.15e9),
        bytes_accessed=int(microseconds * 3.69e6),
        transcendentals=0,
    )


def body(
    node_states,
    edge_states,
    neighbour_index,
    edge_mask,
    node_cotangent,
    edge_cotangent,
    message_weight1,
    message_bias1,
    message_weight2,
    message_bias2,
    message_weight3,
    message_bias3,
    norm1_gain,
    norm1_shift,
    expand_weight,
    expand_bias,
    contract_weight,
    contract_bias,
    norm2_gain,
    norm2_shift,
    edge_weight1,
    edge_bias1,
    edge_weight2,
    edge_bias2,
    edge_weight3,
    edge_bias3,
    norm3_gain,
    norm3_shift,
):
    self_rows = node_states[0]
    rows, width = self_rows.shape
    slots = neighbour_index.shape[2]
    edge_width = edge_states.shape[3]
    hidden = expand_weight.shape[1]
    edges = rows * slots
    parts = lax.axis_size(RES)
    cap = ROW_CAP
    table_rows = rows + parts * cap
    steps = 5
    block_slots = slots // steps
    block = block_slots * rows
    pairs = block // LANES

    everyone = gather_copies(copies_of(self_rows, RES), RES).reshape(parts * rows, width)
    core = lax.axis_index("core").astype(jnp.int32).reshape(1)
    me = lax.axis_index(RES).astype(jnp.int32).reshape(1)
    edge_rows = edge_states[0].transpose(1, 0, 2)
    edge_cot = edge_cotangent[0].transpose(1, 0, 2)
    slot_index = neighbour_index.transpose(2, 0, 1)
    slot_mask = edge_mask.transpose(2, 0, 1)
    edge_w1t = edge_weight1.T
    wide = (
        message_bias1,
        message_bias2,
        message_bias3,
        norm1_gain,
        norm1_shift,
        contract_bias,
        norm2_gain,
        norm2_shift,
        expand_bias,
    )
    narrow = (edge_bias1, edge_bias2, edge_bias3, norm3_gain, norm3_shift)
    vmem = pl.BlockSpec(memory_space=pltpu.VMEM)

    def shape(dims, kind):
        return jax.ShapeDtypeStruct(dims, kind)

    pos, select, ids, counts, vectors, bias_row = pl.pallas_call(
        functools.partial(
            prepare_kernel, parts=parts, cap=cap, steps=steps, wide=len(wide), narrow=len(narrow)
        ),
        out_shape=(
            shape((steps, LANES, pairs), jnp.int32),
            shape((parts * rows, table_rows), BF16),
            shape((parts, cap), jnp.int32),
            shape((rows, width), F32),
            shape((V_ROWS, width), F32),
            shape((1, hidden), F32),
        ),
        in_specs=[pl.BlockSpec(memory_space=pltpu.SMEM)] + [vmem] * (2 + len(wide) + len(narrow)),
        out_specs=(vmem,) * 6,
        compiler_params=params(56),
        cost_estimate=cost(6),
        name="prepare",
    )(me, slot_index, slot_mask, *wide, *narrow)
    ids, everyone = lax.optimization_barrier((ids, everyone))
    asked = lax.all_to_all(ids, RES, split_axis=0, concat_axis=0, tiled=True)

    edge_spec = pl.BlockSpec((block_slots, rows, edge_width), lambda i: (i, 0, 0))
    flat_spec = pl.BlockSpec((block, width), lambda i: (i, 0))
    pos_spec = pl.BlockSpec((1, LANES, pairs), lambda i: (i, 0, 0))
    any_spec = pl.BlockSpec(memory_space=pl.ANY)
    node_spec = whole((rows, width))
    away_spec = whole((parts * cap, width))

    (
        act1,
        slope1,
        slope2,
        fresh,
        table,
        mixed1,
        mixed2,
        low,
        slope_e,
        act_sum,
    ) = pl.pallas_call(
        node_kernel,
        grid=(steps,),
        in_specs=[
            edge_spec,
            pos_spec,
            whole((parts * rows, table_rows)),
            whole((parts * rows, width)),
            node_spec,
            node_spec,
            whole((V_ROWS, width)),
            whole(message_weight1.shape),
            whole((width, width)),
            whole((width, width)),
            any_spec,
            any_spec,
        ],
        out_specs=[
            flat_spec,
            flat_spec,
            flat_spec,
            node_spec,
            whole((table_rows, width)),
            node_spec,
            node_spec,
            node_spec,
            whole((rows, hidden)),
            node_spec,
        ],
        out_shape=[
            shape((edges, width), BF16),
            shape((edges, width), BF16),
            shape((edges, width), BF16),
            shape((rows, width), BF16),
            shape((table_rows, width), BF16),
            shape((rows, width), F32),
            shape((rows, width), F32),
            shape((rows, width), BF16),
            shape((rows, hidden), F32),
            shape((rows, width), F32),
        ],
        scratch_shapes=[
            pltpu.VMEM((table_rows, width), BF16),
            pltpu.VMEM((rows, width), F32),
            pltpu.VMEM((width, hidden), BF16),
            pltpu.VMEM((hidden, width), BF16),
            pltpu.SemaphoreType.DMA((2,)),
        ],
        compiler_params=params(56),
        cost_estimate=cost(26),
        name="node_forward",
    )(
        edge_rows,
        pos,
        select,
        everyone,
        self_rows,
        counts,
        vectors,
        message_weight1,
        message_weight2,
        message_weight3,
        expand_weight,
        contract_weight,
    )
    outgoing = pl.pallas_call(
        pick_kernel,
        in_specs=[vmem] * 2,
        out_specs=vmem,
        out_shape=shape((parts * cap, width), BF16),
        compiler_params=params(8),
        cost_estimate=cost(1),
        name="pick",
    )(asked, fresh)
    incoming = exchange(outgoing, parts)
    low_all = lax.all_gather(low, BY_CORE, axis=0, tiled=True)

    edge_pack_rows = 4 * edge_width
    edge_out, grad_partial, edge_first, edge_own, edge_away, edge_pack, edge_vec = pl.pallas_call(
        edge_kernel,
        grid=(steps,),
        in_specs=[
            edge_spec,
            edge_spec,
            pos_spec,
            node_spec,
            away_spec,
            node_spec,
            whole((V_ROWS, width)),
            whole(edge_w1t.shape),
            whole((edge_width, edge_width)),
            whole((edge_width, edge_width)),
        ],
        out_specs=[
            edge_spec,
            edge_spec,
            whole((rows, edge_width)),
            whole((rows, edge_width)),
            whole((parts * cap, edge_width)),
            whole((edge_pack_rows, width)),
            whole((8, width)),
        ],
        out_shape=[
            shape((slots, rows, edge_width), BF16),
            shape((slots, rows, edge_width), F32),
            shape((rows, edge_width), F32),
            shape((rows, edge_width), F32),
            shape((parts * cap, edge_width), BF16),
            shape((edge_pack_rows, width), BF16),
            shape((8, width), F32),
        ],
        scratch_shapes=[
            pltpu.VMEM((table_rows, width), BF16),
            pltpu.VMEM((table_rows, edge_width), BF16),
            pltpu.VMEM((rows, edge_width), F32),
            pltpu.VMEM((table_rows, edge_width), F32),
            pltpu.VMEM((edge_width, edge_width), F32),
            pltpu.VMEM((edge_width, edge_width), F32),
            pltpu.VMEM((edge_width, edge_width), F32),
            pltpu.VMEM((5, rows, edge_width), F32),
        ],
        compiler_params=params(56),
        cost_estimate=cost(21),
        name="edge_both",
    )(
        edge_rows,
        edge_cot,
        pos,
        fresh,
        incoming,
        counts,
        vectors,
        edge_w1t,
        edge_weight2,
        edge_weight3,
    )
    edge_arrived = exchange(edge_away, parts)

    feed_rows = width + 16
    side = lax.axis_size(SIDE)
    feed_pack, grad_copies, spread, grad_mixed1 = pl.pallas_call(
        feed_kernel,
        in_specs=[vmem] * 16,
        out_specs=[vmem] * 4,
        out_shape=[
            shape((feed_rows, width), BF16),
            shape((side, rows, width), BF16),
            shape((rows, width), F32),
            shape((rows, width), F32),
        ],
        compiler_params=params(24),
        cost_estimate=cost(7),
        name="feed_backward",
    )(
        node_cotangent[0],
        edge_first,
        edge_own,
        edge_arrived,
        asked,
        counts,
        vectors,
        edge_w1t,
        mixed1,
        mixed2,
        slope_e,
        act_sum,
        expand_weight,
        contract_weight,
        message_weight3,
        edge_vec,
    )
    grad_mine = gather_copies(grad_copies, SIDE).reshape(side * rows, width)

    unit = 16 * side
    half_rows = (3 * width + unit - 1) // unit * unit
    edge_grad, first, own, away, send, keep = pl.pallas_call(
        message_kernel,
        grid=(steps,),
        in_specs=[
            pl.BlockSpec(memory_space=pltpu.SMEM),
            edge_spec,
            pos_spec,
            flat_spec,
            flat_spec,
            flat_spec,
            edge_spec,
            node_spec,
            whole((table_rows, width)),
            whole(message_weight1.shape),
            whole((width, width)),
            whole((edge_pack_rows, width)),
            whole((feed_rows, width)),
        ],
        out_specs=[
            edge_spec,
            node_spec,
            node_spec,
            away_spec,
            whole((half_rows, width)),
            whole((half_rows, width)),
        ],
        out_shape=[
            shape((slots, rows, edge_width), F32),
            shape((rows, width), F32),
            shape((rows, width), F32),
            shape((parts * cap, width), BF16),
            shape((half_rows, width), BF16),
            shape((half_rows, width), BF16),
        ],
        scratch_shapes=[
            pltpu.VMEM((table_rows, width), F32),
            pltpu.VMEM((width, width), F32),
            pltpu.VMEM((edge_width, width), F32),
            pltpu.VMEM((rows, width), F32),
        ],
        compiler_params=params(56),
        cost_estimate=cost(14),
        name="message_backward",
    )(
        core,
        edge_rows,
        pos,
        act1,
        slope1,
        slope2,
        grad_partial,
        spread,
        table,
        message_weight1,
        message_weight2,
        edge_pack,
        feed_pack,
    )
    send, low_all = lax.optimization_barrier((send, low_all))
    came = other_core(send)
    y_size = lax.axis_size("y")
    x_size = lax.axis_size("x")
    z_size = lax.axis_size("z")
    my_y = lax.axis_index("y").astype(jnp.int32).reshape(1)
    peers = y_size * x_size
    smem = pl.BlockSpec(memory_space=pltpu.SMEM)
    payload = pl.pallas_call(
        functools.partial(pair_kernel, parts=parts, cap=cap),
        in_specs=[smem] + [vmem] * 3,
        out_specs=vmem,
        out_shape=shape((peers, half_rows // peers + z_size * cap, width), BF16),
        compiler_params=params(20),
        cost_estimate=cost(3),
        name="pair_sum",
    )(my_y, keep, came, away)
    payload, grad_mine = lax.optimization_barrier((payload, grad_mine))
    grad_other = other_core(grad_mine)
    arrived = lax.all_to_all(payload, PLANE, split_axis=0, concat_axis=0, tiled=True)
    def feed_weights(low_values, grad_values, near, sums):
        units = 256
        row_block = min(side * rows, 1024)
        blocks = side * rows // row_block

        def low_block(c, r, core):
            return ((core[0] if near else 1 - core[0]) * blocks + r, 0)

        sum_specs = [
            pl.BlockSpec((width, units), lambda c, r, core: (0, c)),
            pl.BlockSpec((units, width), lambda c, r, core: (c, 0)),
            pl.BlockSpec((8, units), lambda c, r, core: (0, c)),
            whole((8, width)),
        ]
        return pl.pallas_call(
            functools.partial(feed_weight_kernel, more=bool(sums)),
            grid_spec=pltpu.PrefetchScalarGridSpec(
                num_scalar_prefetch=1,
                grid=(hidden // units, blocks),
                in_specs=[
                    pl.BlockSpec((row_block, width), low_block),
                    pl.BlockSpec((row_block, width), lambda c, r, core: (r, 0)),
                    pl.BlockSpec((width, units), lambda c, r, core: (0, c)),
                    pl.BlockSpec((1, units), lambda c, r, core: (0, c)),
                    pl.BlockSpec((units, width), lambda c, r, core: (c, 0)),
                ]
                + (sum_specs if sums else []),
                out_specs=sum_specs,
                scratch_shapes=[pltpu.VMEM((units, width), F32)],
            ),
            out_shape=[
                shape((width, hidden), F32),
                shape((hidden, width), F32),
                shape((8, hidden), F32),
                shape((8, width), F32),
            ],
            compiler_params=params(40),
            cost_estimate=cost(21),
            name="feed_weights_near" if near else "feed_weights_far",
        )(core, low_values, grad_values, expand_weight, bias_row, contract_weight, *sums)

    sums = feed_weights(low_all, grad_mine, True, ())
    arrived, *sums = lax.optimization_barrier((arrived, *sums))
    payload = pl.pallas_call(
        functools.partial(plane_kernel, cap=cap),
        in_specs=[smem, vmem],
        out_specs=vmem,
        out_shape=shape((z_size, half_rows // side + x_size * cap, width), BF16),
        compiler_params=params(16),
        cost_estimate=cost(3),
        name="plane_sum",
    )(my_y, arrived)
    arrived = lax.all_to_all(payload, "z", split_axis=0, concat_axis=0, tiled=True)
    copies, returned = pl.pallas_call(
        column_kernel,
        in_specs=[vmem],
        out_specs=[vmem] * 2,
        out_shape=[
            shape((z_size, half_rows // side, width), BF16),
            shape((parts * cap, width), BF16),
        ],
        compiler_params=params(8),
        cost_estimate=cost(1),
        name="column_sum",
    )(arrived)
    column = lax.all_to_all(copies, "z", split_axis=0, concat_axis=0, tiled=True)
    column, grad_other, low_all, *sums = lax.optimization_barrier(
        (column, grad_other, low_all, *sums)
    )
    column = copies_of(column.reshape(half_rows // peers, width), PLANE)
    mine = gather_copies(column, PLANE).reshape(half_rows, width)
    sums = feed_weights(low_all, grad_other, False, tuple(sums))
    mine, *sums = lax.optimization_barrier((mine, *sums))
    grad_expand, grad_contract, expand_bias_sum, contract_bias_sum = sums
    other = other_core(mine)
    node_grad = pl.pallas_call(
        node_grad_kernel,
        in_specs=[vmem] * 6,
        out_specs=vmem,
        out_shape=shape((rows, width), F32),
        compiler_params=params(12),
        cost_estimate=cost(3),
        name="node_gradient",
    )(grad_mixed1, first, own, returned, asked, message_weight1)

    vec = shape((width,), F32)
    thin = shape((edge_width,), F32)
    square = shape((width, width), F32)
    small = shape((edge_width, edge_width), F32)
    (
        grad_message1,
        grad_mb1,
        grad_message2,
        grad_mb2,
        grad_message3,
        grad_mb3,
        grad_n1g,
        grad_n1s,
        grad_eb,
        grad_cb,
        grad_n2g,
        grad_n2s,
        grad_edge1_t,
        grad_eb1,
        grad_edge2,
        grad_eb2,
        grad_edge3,
        grad_eb3,
        grad_n3g,
        grad_n3s,
    ) = pl.pallas_call(
        unpack_kernel,
        in_specs=[smem] + [vmem] * 4,
        out_specs=[vmem] * 20,
        out_shape=[
            shape(message_weight1.shape, F32),
            vec,
            square,
            vec,
            square,
            vec,
            vec,
            vec,
            shape((hidden,), F32),
            vec,
            vec,
            vec,
            shape(edge_w1t.shape, F32),
            thin,
            small,
            thin,
            small,
            thin,
            thin,
            thin,
        ],
        compiler_params=params(24),
        cost_estimate=cost(4),
        name="unpack",
    )(core, mine, other, expand_bias_sum, contract_bias_sum)
    return (
        fresh[None],
        edge_out.transpose(1, 0, 2)[None],
        node_grad[None],
        edge_grad.transpose(1, 0, 2)[None],
        grad_message1,
        grad_mb1,
        grad_message2,
        grad_mb2,
        grad_message3,
        grad_mb3,
        grad_n1g,
        grad_n1s,
        grad_expand,
        grad_eb,
        grad_contract,
        grad_cb,
        grad_n2g,
        grad_n2s,
        grad_edge1_t.T,
        grad_eb1,
        grad_edge2,
        grad_eb2,
        grad_edge3,
        grad_eb3,
        grad_n3g,
        grad_n3s,
    )


def solution(mesh):
    batch, res = mesh.shape["batch"], mesh.shape["res"]
    x_size = 1 << ((res.bit_length() - 1) // 2)
    sizes = (batch // CORES, CORES, res // x_size, x_size)
    fine = jax.sharding.Mesh(mesh.devices.reshape(sizes), ALL)
    row_spec = P(("y", "core"), RES, None)
    edge_spec = P(("y", "core"), RES, None, None)
    return jax.shard_map(
        body,
        mesh=fine,
        in_specs=(row_spec, edge_spec, row_spec, row_spec, row_spec, edge_spec) + (P(),) * 22,
        out_specs=(row_spec, edge_spec, row_spec, edge_spec) + (P(),) * 22,
        check_vma=False,
    )
```

```python
import functools
import math

import jax
import jax.numpy as jnp
from jax import lax
from jax.experimental import pallas as pl
from jax.experimental.pallas import tpu as pltpu
from jax.sharding import PartitionSpec as P

ROW_CAP = 8
CORES = 2
RES = ("z", "x")
PLANE = ("y", "x")
SIDE = ("y", "z", "x")
ALL = ("y", "core", "z", "x")
BY_CORE = ("core", "y", "z", "x")
EPSILON = 1e-05
LANES = 128
MIB = 1024 * 1024
F32 = jnp.float32
BF16 = jnp.bfloat16

V_MB1, V_MB2, V_MB3, V_N1G, V_N1S, V_CB, V_N2G, V_N2S, V_EB = range(9)
V_EDGE = 12
V_ROWS = 24
VEC_ROWS = 64
FEED_PARTS = 4


def dot_nn(left, right):
    return lax.dot_general(left, right, (((1,), (0,)), ((), ())), preferred_element_type=F32)


def dot_nt(left, right):
    return lax.dot_general(left, right, (((1,), (1,)), ((), ())), preferred_element_type=F32)


def dot_tn(left, right):
    return lax.dot_general(left, right, (((0,), (0,)), ((), ())), preferred_element_type=F32)


def split_low(values):
    high = values.astype(BF16)
    return high, (values - high.astype(F32)).astype(BF16)


def dot_split(dot, left, right):
    high, rest = split_low(left)
    return dot(high, right) + dot(rest, right)


def dot_split_right(dot, left, right):
    high, rest = split_low(right)
    return dot(left, high) + dot(left, rest)


def gelu_pair(v):
    e = jnp.exp2((v * v) * (-0.5 * math.log2(math.e)))
    phi_sum = 0.5 + 0.5 * lax.erf(v * math.sqrt(0.5))
    return v * phi_sum, phi_sum + (v * (1.0 / math.sqrt(2.0 * math.pi))) * e


def norm_parts(values):
    average = jnp.mean(values, axis=-1, keepdims=True)
    centred = values - average
    variance = jnp.mean(centred * centred, axis=-1, keepdims=True)
    scale = lax.rsqrt(variance + EPSILON)
    return centred * scale, scale


def norm_back(xhat, scale, gain, upstream):
    w = upstream * gain
    mean_w = jnp.mean(w, axis=-1, keepdims=True)
    mean_wx = jnp.mean(w * xhat, axis=-1, keepdims=True)
    return (w - mean_w - xhat * mean_wx) * scale


def edge_onehot_turned(row_ref, table_rows):
    row = lax.broadcasted_iota(jnp.int32, (table_rows, row_ref.shape[2]), 0)
    return (row_ref[0] == row).astype(F32).astype(BF16)


def edge_onehot(pos_ref, table_rows):
    pairs = pos_ref.shape[2]
    lane = lax.broadcasted_iota(jnp.int32, (LANES, table_rows), 1)
    return jnp.concatenate(
        [(pos_ref[0, :, p : p + 1] == lane).astype(F32).astype(BF16) for p in range(pairs)], axis=0
    )


def prepare_kernel(me_ref, idx_ref, mask_ref, *refs, parts, cap, steps, wide, narrow):
    wide_refs = refs[:wide]
    narrow_refs = refs[wide : wide + narrow]
    outputs = refs[wide + narrow :]
    pos_ref, row_ref, select_ref, ids_ref, count_ref, vec_ref, expand_bias_ref = outputs
    rows, width = count_ref.shape
    total = rows * parts
    table = rows + parts * cap
    me = me_ref[0]
    pair_rows = idx_ref.shape[0] // 2
    named = [
        jnp.concatenate([idx_ref[2 * j], idx_ref[2 * j + 1]], axis=1) for j in range(pair_rows)
    ]
    residue = lax.broadcasted_iota(jnp.int32, (total, LANES), 0)
    owner = residue // rows
    within = residue - owner * rows
    hits = jnp.zeros((total, LANES), F32)
    for j in range(pair_rows):
        hits = jnp.where(named[j] == residue, 1.0, hits)
    hit = jnp.max(hits, axis=1, keepdims=True)
    own = owner == me
    wanted = jnp.where(own, 0.0, jnp.broadcast_to(hit, (total, LANES)))
    low_row = lax.broadcasted_iota(jnp.int32, (rows, rows), 0)
    low_col = lax.broadcasted_iota(jnp.int32, (rows, rows), 1)
    lower = (low_col <= low_row).astype(F32).astype(BF16)
    wanted_low = wanted.astype(BF16)
    place = jnp.concatenate(
        [dot_nn(lower, wanted_low[o * rows : (o + 1) * rows]) for o in range(parts)], axis=0
    )
    place = jnp.clip(place - 1.0, 0.0, cap - 1.0)
    pos = jnp.where(own, within.astype(F32), (rows + owner * cap).astype(F32) + place)
    picked = [
        jnp.sum(jnp.where(named[j] == residue, pos, 0.0), axis=0, keepdims=True)
        for j in range(pair_rows)
    ]
    picked.append(jnp.zeros((LANES - pair_rows, LANES), F32))
    turned = jnp.concatenate(picked, axis=0).T.astype(jnp.int32)
    per = pair_rows // steps
    for s in range(steps):
        pos_ref[s] = turned[:, s * per : (s + 1) * per]
        part = jnp.concatenate(picked[s * per : (s + 1) * per], axis=1)
        row_ref[s] = part.astype(jnp.int32)
    lane = lax.broadcasted_iota(jnp.int32, (total, table), 1).astype(F32)
    live = jnp.where(own, 1.0, wanted)
    chosen = jnp.where(lane == pos[:, :1], jnp.broadcast_to(live[:, :1], (total, table)), 0.0)
    select_ref[...] = chosen.astype(BF16)
    asked_row = jnp.broadcast_to(within[:, :1].astype(F32), (total, parts * cap))
    ids = jnp.sum(chosen[:, rows:] * asked_row, axis=0, keepdims=True)
    ids = ids.astype(jnp.int32)
    for o in range(parts):
        ids_ref[o : o + 1, :] = ids[:, o * cap : (o + 1) * cap]
    count = mask_ref[0]
    for k in range(1, mask_ref.shape[0]):
        count = count + mask_ref[k]
    count = jnp.concatenate([count.astype(F32), jnp.zeros((7, rows), F32)], axis=0)
    count_ref[...] = dot_tn(count.astype(BF16), jnp.ones((8, width), F32).astype(BF16))
    expand_bias_ref[...] = wide_refs[-1][...].astype(F32).reshape(expand_bias_ref.shape)
    vec_ref[...] = jnp.zeros_like(vec_ref)
    at = 0
    for ref in wide_refs:
        for c in range(ref.shape[0] // width):
            part = ref[c * width : (c + 1) * width]
            vec_ref[at : at + 1, :] = part.astype(F32).reshape(1, width)
            at += 1
    for ref in narrow_refs:
        vec_ref[at : at + 1, : ref.shape[0]] = ref[...].astype(F32).reshape(1, ref.shape[0])
        at += 1


def node_kernel(
    edge_ref,
    pos_ref,
    select_ref,
    all_ref,
    self_ref,
    count_ref,
    vec_ref,
    w1_ref,
    w2_ref,
    w3_ref,
    expand_hbm,
    contract_hbm,
    act1_ref,
    slope1_ref,
    slope2_ref,
    fresh_ref,
    table_ref,
    mixed1_ref,
    mixed2_ref,
    low_ref,
    slope_e_ref,
    act_sum_ref,
    proj_ref,
    self_pre_ref,
    expand_ref,
    contract_ref,
    sems,
):
    step = pl.program_id(0)
    last = pl.num_programs(0) - 1
    rows, width = self_ref.shape
    slots = edge_ref.shape[0]
    edge_width = edge_ref.shape[2]
    table_rows = table_ref.shape[0]
    expand_copy = pltpu.make_async_copy(expand_hbm, expand_ref, sems.at[0])
    contract_copy = pltpu.make_async_copy(contract_hbm, contract_ref, sems.at[1])

    @pl.when(step == 0)
    def _():
        expand_copy.start()
        contract_copy.start()
        table = dot_tn(select_ref[...], all_ref[...]).astype(BF16)
        table_ref[...] = table
        proj_ref[...] = dot_nn(table, w1_ref[width : 2 * width]).astype(BF16)
        self_pre_ref[...] = (
            dot_nn(self_ref[...], w1_ref[:width]) + vec_ref[V_MB1 : V_MB1 + 1, :]
        )
        act_sum_ref[...] = jnp.zeros_like(act_sum_ref)

    onehot = edge_onehot(pos_ref, table_rows)
    features = edge_ref[...].reshape(slots * rows, edge_width)
    pre1 = dot_nn(features, w1_ref[2 * width :]) + dot_nn(onehot, proj_ref[...])
    self_pre = self_pre_ref[...]
    act1 = []
    for k in range(slots):
        part = pl.ds(k * rows, rows)
        act, slope = gelu_pair(pre1[k * rows : (k + 1) * rows] + self_pre)
        act = act.astype(BF16)
        act1.append(act)
        slope1_ref[part, :] = slope.astype(BF16)
    act1 = jnp.concatenate(act1, axis=0)
    act1_ref[...] = act1.T
    pre2 = dot_nn(act1, w2_ref[...])
    bias2 = vec_ref[V_MB2 : V_MB2 + 1, :]
    act_sum = act_sum_ref[...]
    counts = count_ref[...]
    for k in range(slots):
        act, slope = gelu_pair(pre2[k * rows : (k + 1) * rows] + bias2)
        valid = counts > (step * slots + k).astype(F32)
        act_sum = act_sum + jnp.where(valid, act.astype(BF16).astype(F32), 0.0)
        slope2_ref[pl.ds(k * rows, rows), :] = jnp.where(valid, slope, 0.0).astype(BF16)
    act_sum_ref[...] = act_sum

    @pl.when(step == last)
    def _():
        summed = dot_split(dot_nn, act_sum_ref[...], w3_ref[...])
        summed = summed + counts * vec_ref[V_MB3 : V_MB3 + 1, :]
        mixed1 = self_ref[...].astype(F32) + summed / counts
        mixed1_ref[...] = mixed1
        xhat1, _ = norm_parts(mixed1)
        updated = xhat1 * vec_ref[V_N1G : V_N1G + 1, :] + vec_ref[V_N1S : V_N1S + 1, :]
        low = updated.astype(BF16)
        low_ref[...] = low
        expand_copy.wait()
        contract_copy.wait()
        mixed2 = updated + vec_ref[V_CB : V_CB + 1, :]
        for c in range(expand_ref.shape[1] // width):
            cols = slice(c * width, (c + 1) * width)
            pre = dot_nn(low, expand_ref[:, cols]) + vec_ref[V_EB + c : V_EB + c + 1, :]
            act, slope = gelu_pair(pre)
            act = act.astype(BF16)
            slope_e_ref[:, cols] = slope
            mixed2 = mixed2 + dot_nn(act, contract_ref[cols, :])
        mixed2_ref[...] = mixed2
        xhat2, _ = norm_parts(mixed2)
        fresh = (xhat2 * vec_ref[V_N2G : V_N2G + 1, :] + vec_ref[V_N2S : V_N2S + 1, :]).astype(BF16)
        fresh_ref[...] = fresh


def asked_onehot(asked_ref, rows):
    parts = asked_ref.shape[0]
    asked = jnp.concatenate([asked_ref[o : o + 1, :] for o in range(parts)], axis=1)
    row = lax.broadcasted_iota(jnp.int32, (rows, asked.shape[1]), 0)
    return (asked == row).astype(F32).astype(BF16)


def pick_kernel(asked_ref, fresh_ref, out_ref):
    out_ref[...] = dot_tn(asked_onehot(asked_ref, fresh_ref.shape[0]), fresh_ref[...]).astype(BF16)


def edge_kernel(
    edge_ref,
    cot_ref,
    pos_ref,
    row_ref,
    fresh_ref,
    incoming_ref,
    count_ref,
    vec_ref,
    w1t_ref,
    w2_ref,
    w3_ref,
    out_ref,
    grad_ref,
    first_ref,
    own_ref,
    away_ref,
    pack_ref,
    vec_out_ref,
    table_ref,
    proj_ref,
    self_pre_ref,
    back_ref,
    dw3_ref,
    dw2_ref,
    dw1_ref,
    sums_ref,
):
    step = pl.program_id(0)
    last = pl.num_programs(0) - 1
    rows, width = fresh_ref.shape
    slots, _, edge_width = edge_ref.shape
    block = slots * rows
    table_rows = table_ref.shape[0]
    own_t = w1t_ref[:, :width]
    nbr_t = w1t_ref[:, width : 2 * width]
    feat_t = w1t_ref[:, 2 * width :]

    def vector(i):
        return vec_ref[V_EDGE + i : V_EDGE + i + 1, :edge_width]

    @pl.when(step == 0)
    def _():
        table_ref[:rows] = fresh_ref[...]
        table_ref[rows:] = incoming_ref[...]
        proj_ref[...] = dot_nt(table_ref[...], nbr_t).astype(BF16)
        self_pre_ref[...] = dot_nt(fresh_ref[...], own_t) + vector(0)
        for ref in (back_ref, dw3_ref, dw2_ref, dw1_ref, sums_ref, first_ref):
            ref[...] = jnp.zeros_like(ref)

    def flat(values):
        return values.reshape(block, edge_width)

    def deep(values):
        return values.reshape(slots, rows, edge_width)

    onehot = edge_onehot(pos_ref, table_rows)
    features = flat(edge_ref[...])
    pre1 = dot_nt(features, feat_t) + dot_nn(onehot, proj_ref[...])
    pre1 = deep(pre1) + self_pre_ref[...][None]
    act1, slope1 = gelu_pair(flat(pre1))
    act1 = act1.astype(BF16)
    pre2 = dot_nn(act1, w2_ref[...]) + vector(1)
    act2, slope2 = gelu_pair(pre2)
    act2 = act2.astype(BF16)
    mixed3 = features.astype(F32) + (dot_nn(act2, w3_ref[...]) + vector(2))
    xhat, scale = norm_parts(mixed3)
    gain = vector(3)
    slot = lax.broadcasted_iota(jnp.int32, (slots, rows, edge_width), 0) + step * slots
    valid = count_ref[...][None, :, :edge_width] > slot.astype(F32)
    out_ref[...] = jnp.where(valid, deep(xhat * gain + vector(4)), 0.0).astype(BF16)
    upstream = flat(jnp.where(valid, cot_ref[...].astype(F32), 0.0))
    sums_ref[3] += jnp.sum(deep(upstream * xhat), axis=0)
    sums_ref[4] += jnp.sum(deep(upstream), axis=0)
    grad_mixed = norm_back(xhat, scale, gain, upstream)
    grad_delta = grad_mixed.astype(BF16)
    dw3_ref[...] += dot_tn(act2, grad_delta)
    sums_ref[2] += jnp.sum(deep(grad_delta.astype(F32)), axis=0)
    grad2 = (dot_nt(grad_delta, w3_ref[...]) * slope2).astype(BF16)
    dw2_ref[...] += dot_tn(act1, grad2)
    sums_ref[1] += jnp.sum(deep(grad2.astype(F32)), axis=0)
    grad1 = (dot_nt(grad2, w2_ref[...]) * slope1).astype(BF16)
    dw1_ref[...] += dot_tn(grad1, features)
    first_ref[...] += jnp.sum(deep(grad1.astype(F32)), axis=0)
    back_ref[...] += dot_nn(edge_onehot_turned(row_ref, table_rows), grad1)
    grad_ref[...] = deep(grad_mixed + dot_nn(grad1, feat_t))

    @pl.when(step == last)
    def _():
        first = first_ref[...]
        back = back_ref[...]
        own_ref[...] = back[:rows]
        away_ref[...] = back[rows:].astype(BF16)
        first_high, first_rest = split_low(first)
        back_high, back_rest = split_low(back)
        own_grad = dot_tn(first_high, fresh_ref[...]) + dot_tn(first_rest, fresh_ref[...])
        nbr_grad = dot_tn(back_high, table_ref[...]) + dot_tn(back_rest, table_ref[...])
        pack_ref[:edge_width, :] = own_grad.astype(BF16)
        pack_ref[edge_width : 2 * edge_width, :] = nbr_grad.astype(BF16)
        pad = jnp.zeros((edge_width, width // 2 - edge_width), BF16)
        third = [dw1_ref[...].astype(BF16), pad, dw2_ref[...].astype(BF16), pad]
        pack_ref[2 * edge_width : 3 * edge_width, :] = jnp.concatenate(third, axis=1)
        fourth = [dw3_ref[...].astype(BF16), pad, jnp.zeros((edge_width, width // 2), BF16)]
        pack_ref[3 * edge_width :, :] = jnp.concatenate(fourth, axis=1)
        vec_out_ref[...] = jnp.zeros_like(vec_out_ref)
        vec_out_ref[0:1, :edge_width] = jnp.sum(first, axis=0, keepdims=True)
        for i in range(1, 5):
            vec_out_ref[i : i + 1, :edge_width] = jnp.sum(sums_ref[i], axis=0, keepdims=True)


def feed_kernel(
    cot_ref,
    first_ref,
    own_ref,
    arrived_ref,
    asked_ref,
    count_ref,
    vec_ref,
    w1t_ref,
    mixed1_ref,
    mixed2_ref,
    slope_ref,
    act_sum_ref,
    expand_ref,
    contract_ref,
    w3_ref,
    edge_vec_ref,
    pack_ref,
    copies_ref,
    spread_ref,
    grad_mixed1_ref,
):
    rows, width = cot_ref.shape
    hidden = expand_ref.shape[1]
    own_t = w1t_ref[:, :width]
    nbr_t = w1t_ref[:, width : 2 * width]
    counts = count_ref[...]

    def vector(i):
        return vec_ref[i : i + 1, :]

    def total(values):
        return jnp.sum(values.astype(F32), axis=0, keepdims=True)

    back = own_ref[...] + dot_nn(asked_onehot(asked_ref, rows), arrived_ref[...])
    grad_fresh = (
        cot_ref[...].astype(F32)
        + dot_split(dot_nn, first_ref[...], own_t)
        + dot_split(dot_nn, back, nbr_t)
    )
    xhat2, scale2 = norm_parts(mixed2_ref[...])
    grad_mixed2 = norm_back(xhat2, scale2, vector(V_N2G), grad_fresh)
    grad_contracted = grad_mixed2.astype(BF16)
    for p in range(copies_ref.shape[0]):
        copies_ref[p] = grad_contracted
    grad_updated = grad_mixed2
    for c in range(hidden // width):
        cols = slice(c * width, (c + 1) * width)
        pre = dot_nt(grad_contracted, contract_ref[cols, :]) * slope_ref[:, cols]
        grad_updated = grad_updated + dot_nt(pre.astype(BF16), expand_ref[:, cols])
    xhat1, scale1 = norm_parts(mixed1_ref[...])
    grad_mixed1 = norm_back(xhat1, scale1, vector(V_N1G), grad_updated)
    grad_mixed1_ref[...] = grad_mixed1
    grad_message = (grad_mixed1 / counts).astype(BF16)
    spread_ref[...] = dot_nt(grad_message, w3_ref[...])
    pack_ref[:width, :] = dot_split(dot_tn, act_sum_ref[...], grad_message).astype(BF16)
    vectors = [
        total(counts * grad_message.astype(F32)),
        total(grad_updated * xhat1),
        total(grad_updated),
        total(grad_fresh * xhat2),
        total(grad_fresh),
        edge_vec_ref[...],
    ]
    vectors = jnp.concatenate(vectors, axis=0)
    vectors = jnp.concatenate(
        [vectors, jnp.zeros((pack_ref.shape[0] - width - vectors.shape[0], width), F32)], axis=0
    )
    pack_ref[width:, :] = vectors.astype(BF16)


def feed_weight_kernel(
    core_ref, low_a_ref, low_b_ref, grad_a_ref, grad_b_ref, expand_ref, bias_ref, contract_ref, *refs
):
    del core_ref
    expand_out_ref, contract_out_ref, bias_out_ref, last_bias_ref, turned_ref = refs[-5:]
    chunk = pl.program_id(0)
    step = pl.program_id(1)
    units = expand_ref.shape[1]
    weight_t = expand_ref[...].T
    bias = jnp.broadcast_to(bias_ref[0:1, :], (8, units)).T[:, :1]
    ones = jnp.ones((8, low_a_ref.shape[0]), F32).astype(BF16)
    turned = jnp.zeros((units, low_a_ref.shape[1]), F32)
    contracted = jnp.zeros((units, low_a_ref.shape[1]), F32)
    sums = jnp.zeros((8, units), F32)
    for low_ref, grad_ref in ((low_a_ref, grad_a_ref), (low_b_ref, grad_b_ref)):
        act, slope = gelu_pair(dot_nt(weight_t, low_ref[...]) + bias)
        contracted = contracted + dot_nn(act.astype(BF16), grad_ref[...])
        pre = (dot_nt(contract_ref[...], grad_ref[...]) * slope).astype(BF16)
        turned = turned + dot_nn(pre, low_ref[...])
        sums = sums + dot_nt(ones, pre)

    @pl.when(step == 0)
    def _():
        turned_ref[...] = turned
        contract_out_ref[...] = contracted
        bias_out_ref[...] = sums

    @pl.when(step > 0)
    def _():
        turned_ref[...] += turned
        contract_out_ref[...] += contracted
        bias_out_ref[...] += sums

    @pl.when(step == pl.num_programs(1) - 1)
    def _():
        expand_out_ref[...] = turned_ref[...].T

    @pl.when((chunk == 0) & (step == 0))
    def _():
        last_bias_ref[...] = jnp.zeros_like(last_bias_ref)

    @pl.when(chunk == 0)
    def _():
        last_bias_ref[...] += dot_nn(ones, grad_a_ref[...]) + dot_nn(ones, grad_b_ref[...])


def message_kernel(
    core_ref,
    edge_ref,
    row_ref,
    act1_ref,
    slope1_ref,
    slope2_ref,
    partial_ref,
    spread_ref,
    table_ref,
    w1_ref,
    w2_ref,
    edge_pack_ref,
    feed_pack_ref,
    grad_ref,
    first_ref,
    own_ref,
    away_ref,
    send_a_ref,
    send_b_ref,
    keep_a_ref,
    keep_b_ref,
    back_ref,
    dw2_ref,
    dw1_ref,
    bias2_ref,
):
    step = pl.program_id(0)
    last = pl.num_programs(0) - 1
    slots, rows, edge_width = edge_ref.shape
    width = act1_ref.shape[0]
    block = slots * rows
    table_rows = table_ref.shape[0]

    @pl.when(step == 0)
    def _():
        for ref in (back_ref, dw2_ref, dw1_ref, bias2_ref, first_ref):
            ref[...] = jnp.zeros_like(ref)

    spread = spread_ref[...]
    grad2 = []
    bias2 = bias2_ref[...]
    for k in range(slots):
        part = (spread * slope2_ref[pl.ds(k * rows, rows), :].astype(F32)).astype(BF16)
        bias2 = bias2 + part.astype(F32)
        grad2.append(part)
    bias2_ref[...] = bias2
    grad2 = jnp.concatenate(grad2, axis=0)
    dw2_ref[...] += dot_nn(act1_ref[...], grad2)
    grad1 = (dot_nt(grad2, w2_ref[...]) * slope1_ref[...].astype(F32)).astype(BF16)
    first_ref[...] += jnp.sum(grad1.astype(F32).reshape(slots, rows, width), axis=0)
    back_ref[...] += dot_nn(edge_onehot_turned(row_ref, table_rows), grad1)
    features = edge_ref[...].reshape(block, edge_width)
    dw1_ref[...] += dot_tn(features, grad1)
    grad_ref[...] = partial_ref[...] + dot_nt(grad1, w1_ref[2 * width :]).reshape(
        slots, rows, edge_width
    )

    @pl.when(step == last)
    def _():
        first = first_ref[...]
        back = back_ref[...]
        own_ref[...] = back[:rows]
        away_ref[...] = back[rows:].astype(BF16)
        own_grad = dot_split_right(dot_tn, table_ref[:rows], first).astype(BF16)
        nbr_grad = dot_split_right(dot_tn, table_ref[...], back).astype(BF16)
        vectors = [
            feed_pack_ref[width:].astype(F32),
            jnp.sum(first, axis=0, keepdims=True),
            jnp.sum(bias2_ref[...], axis=0, keepdims=True),
        ]
        lower = [own_grad, nbr_grad, feed_pack_ref[:width]]
        upper = [dw1_ref[...].astype(BF16), dw2_ref[...].astype(BF16), edge_pack_ref[...]]

        gap = VEC_ROWS - sum(v.shape[0] for v in vectors)
        vectors = jnp.concatenate(vectors + [jnp.zeros((gap, width), F32)], axis=0)
        upper = upper + [vectors.astype(BF16)]

        def fill(refs, pieces):
            rows_each = refs[0].shape[0]
            missing = len(refs) * rows_each - sum(piece.shape[0] for piece in pieces)
            if missing:
                pieces = pieces + [jnp.zeros((missing, width), BF16)]
            at = 0
            for piece in pieces:
                done = 0
                while done < piece.shape[0]:
                    which, offset = divmod(at, rows_each)
                    count = min(piece.shape[0] - done, rows_each - offset)
                    refs[which][offset : offset + count] = piece[done : done + count]
                    done += count
                    at += count

        @pl.when(core_ref[0] == 0)
        def _():
            fill([keep_a_ref, keep_b_ref], lower)
            fill([send_a_ref, send_b_ref], upper)

        @pl.when(core_ref[0] != 0)
        def _():
            fill([send_a_ref, send_b_ref], lower)
            fill([keep_a_ref, keep_b_ref], upper)


def pair_kernel(keep_ref, came_ref, out_ref):
    out_ref[...] = (keep_ref[...].astype(F32) + came_ref[...].astype(F32)).astype(BF16)


def plane_kernel(came_ref, out_ref):
    value = came_ref[0].astype(F32)
    for p in range(1, came_ref.shape[0]):
        value = value + came_ref[p].astype(F32)
    out_ref[...] = value.astype(BF16)


def node_grad_kernel(grad_ref, first_ref, own_ref, arrived_ref, asked_ref, w1_ref, out_ref):
    rows, width = grad_ref.shape
    back = own_ref[...] + dot_nn(asked_onehot(asked_ref, rows), arrived_ref[...])
    out_ref[...] = (
        grad_ref[...]
        + dot_split(dot_nt, first_ref[...], w1_ref[:width])
        + dot_split(dot_nt, back, w1_ref[width : 2 * width])
    )


def unpack_kernel(core_ref, *refs):
    mine_refs, other_refs, refs = refs[:2], refs[2:4], refs[4:]
    (
        bias_ref,
        last_bias_ref,
        message1_ref,
        message1_bias_ref,
        message2_ref,
        message2_bias_ref,
        message3_ref,
        message3_bias_ref,
        gain1_ref,
        shift1_ref,
        expand_bias_ref,
        contract_bias_ref,
        gain2_ref,
        shift2_ref,
        edge1_ref,
        edge1_bias_ref,
        edge2_ref,
        edge2_bias_ref,
        edge3_ref,
        edge3_bias_ref,
        gain3_ref,
        shift3_ref,
    ) = refs
    chunk, width = mine_refs[0].shape
    edge_width = edge2_ref.shape[0]
    half = width // 2
    first_core = core_ref[0] == 0

    def rows_of(mine_first, start, stop):
        parts = []
        while start < stop:
            which, offset = divmod(start, chunk)
            count = min(stop - start, chunk - offset)
            part = slice(offset, offset + count)
            pick = first_core if mine_first else jnp.logical_not(first_core)
            parts.append(jnp.where(pick, mine_refs[which][part], other_refs[which][part]))
            start += count
        values = parts[0] if len(parts) == 1 else jnp.concatenate(parts, axis=0)
        return values.astype(F32)

    def lower(start, stop):
        return rows_of(True, start, stop)

    def upper(start, stop):
        return rows_of(False, start, stop)

    message1_ref[: 2 * width] = lower(0, 2 * width)
    message3_ref[...] = lower(2 * width, 3 * width)
    message1_ref[2 * width :] = upper(0, edge_width)
    base = edge_width
    message2_ref[...] = upper(base, base + width)
    base = base + width
    edge1_ref[:, :width] = upper(base, base + edge_width)
    edge1_ref[:, width : 2 * width] = upper(base + edge_width, base + 2 * edge_width)
    third = upper(base + 2 * edge_width, base + 3 * edge_width)
    edge1_ref[:, 2 * width :] = third[:, :edge_width]
    edge2_ref[...] = third[:, half : half + edge_width]
    edge3_ref[...] = upper(base + 3 * edge_width, base + 4 * edge_width)[:, :edge_width]
    base = base + 4 * edge_width
    vectors = upper(base, base + VEC_ROWS)
    targets = (message3_bias_ref, gain1_ref, shift1_ref, gain2_ref, shift2_ref)
    for i, ref in enumerate(targets):
        ref[...] = vectors[i]
    targets = (edge1_bias_ref, edge2_bias_ref, edge3_bias_ref, gain3_ref, shift3_ref)
    for i, ref in enumerate(targets):
        ref[...] = vectors[5 + i, :edge_width]
    message1_bias_ref[...] = vectors[16]
    message2_bias_ref[...] = vectors[17]
    expand_bias_ref[...] = bias_ref[0]
    contract_bias_ref[...] = last_bias_ref[0]


def gather_copies(copies, axes):
    return lax.all_to_all(copies, axes, split_axis=0, concat_axis=0, tiled=True)


def copies_of(values, axes):
    return jnp.broadcast_to(values[None], (lax.axis_size(axes), *values.shape))


def exchange(values, parts):
    grouped = values.reshape(parts, values.shape[0] // parts, values.shape[1])
    arrived = lax.all_to_all(grouped, RES, split_axis=0, concat_axis=0, tiled=True)
    return arrived.reshape(values.shape)


def other_core(values):
    return lax.ppermute(values, "core", [(0, 1), (1, 0)])


def whole(shape):
    return pl.BlockSpec(shape, lambda *_: (0,) * len(shape))


def params(mebibytes):
    return pltpu.CompilerParams(vmem_limit_bytes=mebibytes * MIB)


def cost(microseconds):
    return pl.CostEstimate(
        flops=int(microseconds * 1.15e9),
        bytes_accessed=int(microseconds * 3.69e6),
        transcendentals=0,
    )


def body(
    node_states,
    edge_states,
    neighbour_index,
    edge_mask,
    node_cotangent,
    edge_cotangent,
    message_weight1,
    message_bias1,
    message_weight2,
    message_bias2,
    message_weight3,
    message_bias3,
    norm1_gain,
    norm1_shift,
    expand_weight,
    expand_bias,
    contract_weight,
    contract_bias,
    norm2_gain,
    norm2_shift,
    edge_weight1,
    edge_bias1,
    edge_weight2,
    edge_bias2,
    edge_weight3,
    edge_bias3,
    norm3_gain,
    norm3_shift,
):
    self_rows = node_states[0]
    rows, width = self_rows.shape
    slots = neighbour_index.shape[2]
    edge_width = edge_states.shape[3]
    hidden = expand_weight.shape[1]
    edges = rows * slots
    parts = lax.axis_size(RES)
    cap = ROW_CAP
    table_rows = rows + parts * cap
    steps = 5
    block_slots = slots // steps
    block = block_slots * rows
    pairs = block // LANES

    everyone = gather_copies(copies_of(self_rows, RES), RES).reshape(parts * rows, width)
    core = lax.axis_index("core").astype(jnp.int32).reshape(1)
    me = lax.axis_index(RES).astype(jnp.int32).reshape(1)
    edge_rows = edge_states[0].transpose(1, 0, 2)
    edge_cot = edge_cotangent[0].transpose(1, 0, 2)
    slot_index = neighbour_index.transpose(2, 0, 1)
    slot_mask = edge_mask.transpose(2, 0, 1)
    edge_w1t = edge_weight1.T
    wide = (
        message_bias1,
        message_bias2,
        message_bias3,
        norm1_gain,
        norm1_shift,
        contract_bias,
        norm2_gain,
        norm2_shift,
        expand_bias,
    )
    narrow = (edge_bias1, edge_bias2, edge_bias3, norm3_gain, norm3_shift)
    vmem = pl.BlockSpec(memory_space=pltpu.VMEM)

    def shape(dims, kind):
        return jax.ShapeDtypeStruct(dims, kind)

    pos, pos_row, select, ids, counts, vectors, bias_row = pl.pallas_call(
        functools.partial(
            prepare_kernel, parts=parts, cap=cap, steps=steps, wide=len(wide), narrow=len(narrow)
        ),
        out_shape=(
            shape((steps, LANES, pairs), jnp.int32),
            shape((steps, 1, block), jnp.int32),
            shape((parts * rows, table_rows), BF16),
            shape((parts, cap), jnp.int32),
            shape((rows, width), F32),
            shape((V_ROWS, width), F32),
            shape((1, hidden), F32),
        ),
        in_specs=[pl.BlockSpec(memory_space=pltpu.SMEM)] + [vmem] * (2 + len(wide) + len(narrow)),
        out_specs=(vmem,) * 7,
        compiler_params=params(56),
        cost_estimate=cost(6),
        name="prepare",
    )(me, slot_index, slot_mask, *wide, *narrow)
    ids, everyone = lax.optimization_barrier((ids, everyone))
    asked = lax.all_to_all(ids, RES, split_axis=0, concat_axis=0, tiled=True)

    edge_spec = pl.BlockSpec((block_slots, rows, edge_width), lambda i: (i, 0, 0))
    flat_spec = pl.BlockSpec((block, width), lambda i: (i, 0))
    turned_spec = pl.BlockSpec((width, block), lambda i: (0, i))
    row_spec = pl.BlockSpec((1, 1, block), lambda i: (i, 0, 0))
    pos_spec = pl.BlockSpec((1, LANES, pairs), lambda i: (i, 0, 0))
    any_spec = pl.BlockSpec(memory_space=pl.ANY)
    node_spec = whole((rows, width))
    away_spec = whole((parts * cap, width))

    (
        act1,
        slope1,
        slope2,
        fresh,
        table,
        mixed1,
        mixed2,
        low,
        slope_e,
        act_sum,
    ) = pl.pallas_call(
        node_kernel,
        grid=(steps,),
        in_specs=[
            edge_spec,
            pos_spec,
            whole((parts * rows, table_rows)),
            whole((parts * rows, width)),
            node_spec,
            node_spec,
            whole((V_ROWS, width)),
            whole(message_weight1.shape),
            whole((width, width)),
            whole((width, width)),
            any_spec,
            any_spec,
        ],
        out_specs=[
            turned_spec,
            flat_spec,
            flat_spec,
            node_spec,
            whole((table_rows, width)),
            node_spec,
            node_spec,
            node_spec,
            whole((rows, hidden)),
            node_spec,
        ],
        out_shape=[
            shape((width, edges), BF16),
            shape((edges, width), BF16),
            shape((edges, width), BF16),
            shape((rows, width), BF16),
            shape((table_rows, width), BF16),
            shape((rows, width), F32),
            shape((rows, width), F32),
            shape((rows, width), BF16),
            shape((rows, hidden), F32),
            shape((rows, width), F32),
        ],
        scratch_shapes=[
            pltpu.VMEM((table_rows, width), BF16),
            pltpu.VMEM((rows, width), F32),
            pltpu.VMEM((width, hidden), BF16),
            pltpu.VMEM((hidden, width), BF16),
            pltpu.SemaphoreType.DMA((2,)),
        ],
        compiler_params=params(56),
        cost_estimate=cost(26),
        name="node_forward",
    )(
        edge_rows,
        pos,
        select,
        everyone,
        self_rows,
        counts,
        vectors,
        message_weight1,
        message_weight2,
        message_weight3,
        expand_weight,
        contract_weight,
    )
    outgoing = pl.pallas_call(
        pick_kernel,
        in_specs=[vmem] * 2,
        out_specs=vmem,
        out_shape=shape((parts * cap, width), BF16),
        compiler_params=params(8),
        cost_estimate=cost(1),
        name="pick",
    )(asked, fresh)
    incoming = exchange(outgoing, parts)
    low_all = lax.all_gather(low, BY_CORE, axis=0, tiled=True)

    edge_pack_rows = 4 * edge_width
    edge_out, grad_partial, edge_first, edge_own, edge_away, edge_pack, edge_vec = pl.pallas_call(
        edge_kernel,
        grid=(steps,),
        in_specs=[
            edge_spec,
            edge_spec,
            pos_spec,
            row_spec,
            node_spec,
            away_spec,
            node_spec,
            whole((V_ROWS, width)),
            whole(edge_w1t.shape),
            whole((edge_width, edge_width)),
            whole((edge_width, edge_width)),
        ],
        out_specs=[
            edge_spec,
            edge_spec,
            whole((rows, edge_width)),
            whole((rows, edge_width)),
            whole((parts * cap, edge_width)),
            whole((edge_pack_rows, width)),
            whole((8, width)),
        ],
        out_shape=[
            shape((slots, rows, edge_width), BF16),
            shape((slots, rows, edge_width), F32),
            shape((rows, edge_width), F32),
            shape((rows, edge_width), F32),
            shape((parts * cap, edge_width), BF16),
            shape((edge_pack_rows, width), BF16),
            shape((8, width), F32),
        ],
        scratch_shapes=[
            pltpu.VMEM((table_rows, width), BF16),
            pltpu.VMEM((table_rows, edge_width), BF16),
            pltpu.VMEM((rows, edge_width), F32),
            pltpu.VMEM((table_rows, edge_width), F32),
            pltpu.VMEM((edge_width, edge_width), F32),
            pltpu.VMEM((edge_width, edge_width), F32),
            pltpu.VMEM((edge_width, edge_width), F32),
            pltpu.VMEM((5, rows, edge_width), F32),
        ],
        compiler_params=params(56),
        cost_estimate=cost(21),
        name="edge_both",
    )(
        edge_rows,
        edge_cot,
        pos,
        pos_row,
        fresh,
        incoming,
        counts,
        vectors,
        edge_w1t,
        edge_weight2,
        edge_weight3,
    )
    edge_arrived = exchange(edge_away, parts)

    feed_rows = width + 16
    side = lax.axis_size(SIDE)
    feed_pack, grad_copies, spread, grad_mixed1 = pl.pallas_call(
        feed_kernel,
        in_specs=[vmem] * 16,
        out_specs=[vmem] * 4,
        out_shape=[
            shape((feed_rows, width), BF16),
            shape((side, rows, width), BF16),
            shape((rows, width), F32),
            shape((rows, width), F32),
        ],
        compiler_params=params(56),
        cost_estimate=cost(7),
        name="feed_backward",
    )(
        node_cotangent[0],
        edge_first,
        edge_own,
        edge_arrived,
        asked,
        counts,
        vectors,
        edge_w1t,
        mixed1,
        mixed2,
        slope_e,
        act_sum,
        expand_weight,
        contract_weight,
        message_weight3,
        edge_vec,
    )
    grad_mine = gather_copies(grad_copies, SIDE).reshape(side * rows, width)

    y_size = lax.axis_size("y")
    x_size = lax.axis_size("x")
    peers = y_size * x_size
    unit = 2 * 16 * peers
    chunk_rows = (3 * width + unit - 1) // unit * unit // 2
    edge_grad, first, own, away, *chunks = pl.pallas_call(
        message_kernel,
        grid=(steps,),
        in_specs=[
            pl.BlockSpec(memory_space=pltpu.SMEM),
            edge_spec,
            row_spec,
            turned_spec,
            flat_spec,
            flat_spec,
            edge_spec,
            node_spec,
            whole((table_rows, width)),
            whole(message_weight1.shape),
            whole((width, width)),
            whole((edge_pack_rows, width)),
            whole((feed_rows, width)),
        ],
        out_specs=[
            edge_spec,
            node_spec,
            node_spec,
            away_spec,
            *[whole((chunk_rows, width))] * 4,
        ],
        out_shape=[
            shape((slots, rows, edge_width), F32),
            shape((rows, width), F32),
            shape((rows, width), F32),
            shape((parts * cap, width), BF16),
            *[shape((chunk_rows, width), BF16)] * 4,
        ],
        scratch_shapes=[
            pltpu.VMEM((table_rows, width), F32),
            pltpu.VMEM((width, width), F32),
            pltpu.VMEM((edge_width, width), F32),
            pltpu.VMEM((rows, width), F32),
        ],
        compiler_params=params(56),
        cost_estimate=cost(14),
        name="message_backward",
    )(
        core,
        edge_rows,
        pos_row,
        act1,
        slope1,
        slope2,
        grad_partial,
        spread,
        table,
        message_weight1,
        message_weight2,
        edge_pack,
        feed_pack,
    )
    send_a, send_b, keep_a, keep_b = chunks
    smem = pl.BlockSpec(memory_space=pltpu.SMEM)
    send_a, low_all = lax.optimization_barrier((send_a, low_all))
    share = chunk_rows // peers

    def pair_sum(keep, send):
        return pl.pallas_call(
            pair_kernel,
            in_specs=[vmem] * 2,
            out_specs=vmem,
            out_shape=shape((chunk_rows, width), BF16),
            compiler_params=params(12),
            cost_estimate=cost(1),
            name="pair_sum",
        )(keep, other_core(send))

    def plane_exchange(values):
        grouped = values.reshape(peers, share, width)
        return lax.all_to_all(grouped, PLANE, split_axis=0, concat_axis=0, tiled=True)

    def plane_sum(values):
        return pl.pallas_call(
            plane_kernel,
            in_specs=[vmem],
            out_specs=vmem,
            out_shape=shape((share, width), BF16),
            compiler_params=params(12),
            cost_estimate=cost(1),
            name="plane_sum",
        )(values)

    feed_shapes = [
        shape((width, hidden), F32),
        shape((hidden, width), F32),
        shape((8, hidden), F32),
    ]

    def feed_weights(part, filled):
        units = 256
        block_rows = min(side * rows, 1024)
        blocks = side * rows // block_rows
        first_chunk = part * (hidden // FEED_PARTS // units)
        row_spec = pl.BlockSpec((block_rows, width), lambda c, r, core: (r, 0))
        sum_specs = [
            pl.BlockSpec((width, units), lambda c, r, core: (0, first_chunk + c)),
            pl.BlockSpec((units, width), lambda c, r, core: (first_chunk + c, 0)),
            pl.BlockSpec((8, units), lambda c, r, core: (0, first_chunk + c)),
        ]
        results = pl.pallas_call(
            feed_weight_kernel,
            grid_spec=pltpu.PrefetchScalarGridSpec(
                num_scalar_prefetch=1,
                grid=(hidden // FEED_PARTS // units, blocks),
                in_specs=[
                    pl.BlockSpec(
                        (block_rows, width), lambda c, r, core: (core[0] * blocks + r, 0)
                    ),
                    pl.BlockSpec(
                        (block_rows, width), lambda c, r, core: ((1 - core[0]) * blocks + r, 0)
                    ),
                    row_spec,
                    row_spec,
                    sum_specs[0],
                    pl.BlockSpec((1, units), lambda c, r, core: (0, first_chunk + c)),
                    sum_specs[1],
                    *[any_spec] * len(filled),
                ],
                out_specs=[*sum_specs, whole((8, width))],
                scratch_shapes=[pltpu.VMEM((units, width), F32)],
            ),
            out_shape=[*feed_shapes, shape((8, width), F32)],
            input_output_aliases={8 + i: i for i in range(len(filled))},
            compiler_params=params(56),
            cost_estimate=cost(7),
            name=f"feed_weights_{part}",
        )(
            core,
            low_all,
            low_all,
            grad_mine,
            grad_other,
            expand_weight,
            bias_row,
            contract_weight,
            *filled,
        )
        return tuple(results[:3]), results[3]

    pair_a = pair_sum(keep_a, send_a)
    pair_b = pair_sum(keep_b, send_b)
    pair_a, grad_mine, away = lax.optimization_barrier((pair_a, grad_mine, away))
    plane_a = plane_exchange(pair_a)
    grad_other = other_core(grad_mine)
    returned = exchange(away, parts)
    filled, contract_bias_sum = feed_weights(0, ())
    plane_a, filled, returned = lax.optimization_barrier((plane_a, filled, returned))
    total_a = plane_sum(plane_a)
    pair_b, total_a = lax.optimization_barrier((pair_b, total_a))
    total_a = lax.psum(total_a, "z")
    plane_b = plane_exchange(pair_b)
    filled, pair_b = lax.optimization_barrier((filled, pair_b))
    filled, _ = feed_weights(1, filled)
    plane_b, filled = lax.optimization_barrier((plane_b, filled))
    total_b = plane_sum(plane_b)
    node_grad = pl.pallas_call(
        node_grad_kernel,
        in_specs=[vmem] * 6,
        out_specs=vmem,
        out_shape=shape((rows, width), F32),
        compiler_params=params(56),
        cost_estimate=cost(3),
        name="node_gradient",
    )(grad_mixed1, first, own, returned, asked, message_weight1)
    total_a, total_b, node_grad = lax.optimization_barrier((total_a, total_b, node_grad))
    total_b = lax.psum(total_b, "z")
    mine_a = gather_copies(copies_of(total_a, PLANE), PLANE)
    filled, total_a = lax.optimization_barrier((filled, total_a))
    filled, _ = feed_weights(2, filled)
    total_b, mine_a, filled = lax.optimization_barrier((total_b, mine_a, filled))
    mine_a = mine_a.reshape(chunk_rows, width)
    mine_b = gather_copies(copies_of(total_b, PLANE), PLANE)
    other_a = other_core(mine_a)
    filled, _ = feed_weights(3, filled)
    mine_b, filled = lax.optimization_barrier((mine_b, filled))
    mine_b = mine_b.reshape(chunk_rows, width)
    other_b = other_core(mine_b)
    grad_expand, grad_contract, expand_bias_sum = filled
    vec = shape((width,), F32)
    thin = shape((edge_width,), F32)
    square = shape((width, width), F32)
    small = shape((edge_width, edge_width), F32)
    (
        grad_message1,
        grad_mb1,
        grad_message2,
        grad_mb2,
        grad_message3,
        grad_mb3,
        grad_n1g,
        grad_n1s,
        grad_eb,
        grad_cb,
        grad_n2g,
        grad_n2s,
        grad_edge1_t,
        grad_eb1,
        grad_edge2,
        grad_eb2,
        grad_edge3,
        grad_eb3,
        grad_n3g,
        grad_n3s,
    ) = pl.pallas_call(
        unpack_kernel,
        in_specs=[smem] + [vmem] * 6,
        out_specs=[vmem] * 20,
        out_shape=[
            shape(message_weight1.shape, F32),
            vec,
            square,
            vec,
            square,
            vec,
            vec,
            vec,
            shape((hidden,), F32),
            vec,
            vec,
            vec,
            shape(edge_w1t.shape, F32),
            thin,
            small,
            thin,
            small,
            thin,
            thin,
            thin,
        ],
        compiler_params=params(24),
        cost_estimate=cost(4),
        name="unpack",
    )(core, mine_a, mine_b, other_a, other_b, expand_bias_sum, contract_bias_sum)
    return (
        fresh[None],
        edge_out.transpose(1, 0, 2)[None],
        node_grad[None],
        edge_grad.transpose(1, 0, 2)[None],
        grad_message1,
        grad_mb1,
        grad_message2,
        grad_mb2,
        grad_message3,
        grad_mb3,
        grad_n1g,
        grad_n1s,
        grad_expand,
        grad_eb,
        grad_contract,
        grad_cb,
        grad_n2g,
        grad_n2s,
        grad_edge1_t.T,
        grad_eb1,
        grad_edge2,
        grad_eb2,
        grad_edge3,
        grad_eb3,
        grad_n3g,
        grad_n3s,
    )


def solution(mesh):
    batch, res = mesh.shape["batch"], mesh.shape["res"]
    x_size = 1 << ((res.bit_length() - 1) // 2)
    sizes = (batch // CORES, CORES, res // x_size, x_size)
    fine = jax.sharding.Mesh(mesh.devices.reshape(sizes), ALL)
    row_spec = P(("y", "core"), RES, None)
    edge_spec = P(("y", "core"), RES, None, None)
    return jax.shard_map(
        body,
        mesh=fine,
        in_specs=(row_spec, edge_spec, row_spec, row_spec, row_spec, edge_spec) + (P(),) * 22,
        out_specs=(row_spec, edge_spec, row_spec, edge_spec) + (P(),) * 22,
        check_vma=False,
    )
```

```python
import functools
import math

import jax
import jax.numpy as jnp
from jax import lax
from jax.experimental import pallas as pl
from jax.experimental.pallas import tpu as pltpu
from jax.sharding import PartitionSpec as P

ROW_CAP = 8
CORES = 2
RES = ("z", "x")
PLANE = ("y", "x")
SIDE = ("y", "z", "x")
ALL = ("y", "core", "z", "x")
EPSILON = 1e-05
LANES = 128
MIB = 1024 * 1024
F32 = jnp.float32
BF16 = jnp.bfloat16

V_MB1, V_MB2, V_MB3, V_N1G, V_N1S, V_CB, V_N2G, V_N2S, V_EB = range(9)
V_EDGE = 12
V_ROWS = 24


def dot_nn(left, right):
    return lax.dot_general(left, right, (((1,), (0,)), ((), ())), preferred_element_type=F32)


def dot_nt(left, right):
    return lax.dot_general(left, right, (((1,), (1,)), ((), ())), preferred_element_type=F32)


def dot_tn(left, right):
    return lax.dot_general(left, right, (((0,), (0,)), ((), ())), preferred_element_type=F32)


def split_low(values):
    high = values.astype(BF16)
    return high, (values - high.astype(F32)).astype(BF16)


def dot_split(dot, left, right):
    high, rest = split_low(left)
    return dot(high, right) + dot(rest, right)


def dot_split_right(dot, left, right):
    high, rest = split_low(right)
    return dot(left, high) + dot(left, rest)


def gelu_pair(v):
    e = jnp.exp2((v * v) * (-0.5 * math.log2(math.e)))
    phi_sum = 0.5 + 0.5 * lax.erf(v * math.sqrt(0.5))
    return v * phi_sum, phi_sum + (v * (1.0 / math.sqrt(2.0 * math.pi))) * e


def norm_parts(values):
    average = jnp.mean(values, axis=-1, keepdims=True)
    centred = values - average
    variance = jnp.mean(centred * centred, axis=-1, keepdims=True)
    scale = lax.rsqrt(variance + EPSILON)
    return centred * scale, scale


def norm_back(xhat, scale, gain, upstream):
    w = upstream * gain
    mean_w = jnp.mean(w, axis=-1, keepdims=True)
    mean_wx = jnp.mean(w * xhat, axis=-1, keepdims=True)
    return (w - mean_w - xhat * mean_wx) * scale


def edge_onehot(pos_ref, table_rows):
    pairs = pos_ref.shape[2]
    lane = lax.broadcasted_iota(jnp.int32, (LANES, table_rows), 1)
    return jnp.concatenate(
        [(pos_ref[0, :, p : p + 1] == lane).astype(F32).astype(BF16) for p in range(pairs)], axis=0
    )


def prepare_kernel(me_ref, idx_ref, mask_ref, *refs, parts, cap, steps, wide, narrow):
    wide_refs = refs[:wide]
    narrow_refs = refs[wide : wide + narrow]
    pos_ref, select_ref, ids_ref, count_ref, vec_ref, expand_bias_ref = refs[wide + narrow :]
    rows, width = count_ref.shape
    total = rows * parts
    table = rows + parts * cap
    me = me_ref[0]
    pair_rows = idx_ref.shape[0] // 2
    named = [
        jnp.concatenate([idx_ref[2 * j], idx_ref[2 * j + 1]], axis=1) for j in range(pair_rows)
    ]
    residue = lax.broadcasted_iota(jnp.int32, (total, LANES), 0)
    owner = residue // rows
    within = residue - owner * rows
    hits = jnp.zeros((total, LANES), F32)
    for j in range(pair_rows):
        hits = jnp.where(named[j] == residue, 1.0, hits)
    hit = jnp.max(hits, axis=1, keepdims=True)
    own = owner == me
    wanted = jnp.where(own, 0.0, jnp.broadcast_to(hit, (total, LANES)))
    low_row = lax.broadcasted_iota(jnp.int32, (rows, rows), 0)
    low_col = lax.broadcasted_iota(jnp.int32, (rows, rows), 1)
    lower = (low_col <= low_row).astype(F32).astype(BF16)
    wanted_low = wanted.astype(BF16)
    place = jnp.concatenate(
        [dot_nn(lower, wanted_low[o * rows : (o + 1) * rows]) for o in range(parts)], axis=0
    )
    place = jnp.clip(place - 1.0, 0.0, cap - 1.0)
    pos = jnp.where(own, within.astype(F32), (rows + owner * cap).astype(F32) + place)
    picked = [
        jnp.sum(jnp.where(named[j] == residue, pos, 0.0), axis=0, keepdims=True)
        for j in range(pair_rows)
    ]
    picked.append(jnp.zeros((LANES - pair_rows, LANES), F32))
    turned = jnp.concatenate(picked, axis=0).T.astype(jnp.int32)
    per = pair_rows // steps
    for s in range(steps):
        pos_ref[s] = turned[:, s * per : (s + 1) * per]
    lane = lax.broadcasted_iota(jnp.int32, (total, table), 1).astype(F32)
    live = jnp.where(own, 1.0, wanted)
    chosen = jnp.where(lane == pos[:, :1], jnp.broadcast_to(live[:, :1], (total, table)), 0.0)
    select_ref[...] = chosen.astype(BF16)
    asked_row = jnp.broadcast_to(within[:, :1].astype(F32), (total, parts * cap))
    ids = jnp.sum(chosen[:, rows:] * asked_row, axis=0, keepdims=True)
    ids = ids.astype(jnp.int32)
    for o in range(parts):
        ids_ref[o : o + 1, :] = ids[:, o * cap : (o + 1) * cap]
    count = mask_ref[0]
    for k in range(1, mask_ref.shape[0]):
        count = count + mask_ref[k]
    count = jnp.concatenate([count.astype(F32), jnp.zeros((7, rows), F32)], axis=0)
    count_ref[...] = dot_tn(count.astype(BF16), jnp.ones((8, width), F32).astype(BF16))
    expand_bias_ref[...] = wide_refs[-1][...].astype(F32).reshape(expand_bias_ref.shape)
    vec_ref[...] = jnp.zeros_like(vec_ref)
    at = 0
    for ref in wide_refs:
        for c in range(ref.shape[0] // width):
            part = ref[c * width : (c + 1) * width]
            vec_ref[at : at + 1, :] = part.astype(F32).reshape(1, width)
            at += 1
    for ref in narrow_refs:
        vec_ref[at : at + 1, : ref.shape[0]] = ref[...].astype(F32).reshape(1, ref.shape[0])
        at += 1


def node_kernel(
    edge_ref,
    pos_ref,
    select_ref,
    all_ref,
    self_ref,
    count_ref,
    vec_ref,
    w1_ref,
    w2_ref,
    w3_ref,
    expand_hbm,
    contract_hbm,
    act1_ref,
    slope1_ref,
    slope2_ref,
    fresh_ref,
    table_ref,
    mixed1_ref,
    mixed2_ref,
    low_ref,
    slope_e_ref,
    act_sum_ref,
    proj_ref,
    self_pre_ref,
    expand_ref,
    contract_ref,
    sems,
):
    step = pl.program_id(0)
    last = pl.num_programs(0) - 1
    rows, width = self_ref.shape
    slots = edge_ref.shape[0]
    edge_width = edge_ref.shape[2]
    table_rows = table_ref.shape[0]
    expand_copy = pltpu.make_async_copy(expand_hbm, expand_ref, sems.at[0])
    contract_copy = pltpu.make_async_copy(contract_hbm, contract_ref, sems.at[1])

    @pl.when(step == 0)
    def _():
        expand_copy.start()
        contract_copy.start()
        table = dot_tn(select_ref[...], all_ref[...]).astype(BF16)
        table_ref[...] = table
        proj_ref[...] = dot_nn(table, w1_ref[width : 2 * width]).astype(BF16)
        self_pre_ref[...] = (
            dot_nn(self_ref[...], w1_ref[:width]) + vec_ref[V_MB1 : V_MB1 + 1, :]
        )
        act_sum_ref[...] = jnp.zeros_like(act_sum_ref)

    onehot = edge_onehot(pos_ref, table_rows)
    features = edge_ref[...].reshape(slots * rows, edge_width)
    pre1 = dot_nn(features, w1_ref[2 * width :]) + dot_nn(onehot, proj_ref[...])
    self_pre = self_pre_ref[...]
    act1 = []
    for k in range(slots):
        part = pl.ds(k * rows, rows)
        act, slope = gelu_pair(pre1[k * rows : (k + 1) * rows] + self_pre)
        act = act.astype(BF16)
        act1.append(act)
        act1_ref[part, :] = act
        slope1_ref[part, :] = slope.astype(BF16)
    pre2 = dot_nn(jnp.concatenate(act1, axis=0), w2_ref[...])
    bias2 = vec_ref[V_MB2 : V_MB2 + 1, :]
    act_sum = act_sum_ref[...]
    counts = count_ref[...]
    for k in range(slots):
        act, slope = gelu_pair(pre2[k * rows : (k + 1) * rows] + bias2)
        valid = counts > (step * slots + k).astype(F32)
        act_sum = act_sum + jnp.where(valid, act.astype(BF16).astype(F32), 0.0)
        slope2_ref[pl.ds(k * rows, rows), :] = jnp.where(valid, slope, 0.0).astype(BF16)
    act_sum_ref[...] = act_sum

    @pl.when(step == last)
    def _():
        summed = dot_split(dot_nn, act_sum_ref[...], w3_ref[...])
        summed = summed + counts * vec_ref[V_MB3 : V_MB3 + 1, :]
        mixed1 = self_ref[...].astype(F32) + summed / counts
        mixed1_ref[...] = mixed1
        xhat1, _ = norm_parts(mixed1)
        updated = xhat1 * vec_ref[V_N1G : V_N1G + 1, :] + vec_ref[V_N1S : V_N1S + 1, :]
        low = updated.astype(BF16)
        for p in range(low_ref.shape[0]):
            low_ref[p] = low
        expand_copy.wait()
        contract_copy.wait()
        mixed2 = updated + vec_ref[V_CB : V_CB + 1, :]
        for c in range(expand_ref.shape[1] // width):
            cols = slice(c * width, (c + 1) * width)
            pre = dot_nn(low, expand_ref[:, cols]) + vec_ref[V_EB + c : V_EB + c + 1, :]
            act, slope = gelu_pair(pre)
            act = act.astype(BF16)
            slope_e_ref[cols, :] = slope.T
            mixed2 = mixed2 + dot_nn(act, contract_ref[cols, :])
        mixed2_ref[...] = mixed2
        xhat2, _ = norm_parts(mixed2)
        fresh = (xhat2 * vec_ref[V_N2G : V_N2G + 1, :] + vec_ref[V_N2S : V_N2S + 1, :]).astype(BF16)
        fresh_ref[...] = fresh


def asked_onehot(asked_ref, rows):
    parts = asked_ref.shape[0]
    asked = jnp.concatenate([asked_ref[o : o + 1, :] for o in range(parts)], axis=1)
    row = lax.broadcasted_iota(jnp.int32, (rows, asked.shape[1]), 0)
    return (asked == row).astype(F32).astype(BF16)


def pick_kernel(asked_ref, fresh_ref, out_ref):
    out_ref[...] = dot_tn(asked_onehot(asked_ref, fresh_ref.shape[0]), fresh_ref[...]).astype(BF16)


def edge_kernel(
    edge_ref,
    cot_ref,
    pos_ref,
    fresh_ref,
    incoming_ref,
    count_ref,
    vec_ref,
    w1t_ref,
    w2_ref,
    w3_ref,
    out_ref,
    grad_ref,
    first_ref,
    own_ref,
    away_ref,
    pack_ref,
    vec_out_ref,
    table_ref,
    proj_ref,
    self_pre_ref,
    back_ref,
    dw3_ref,
    dw2_ref,
    dw1_ref,
    sums_ref,
    turned_ref,
):
    step = pl.program_id(0)
    last = pl.num_programs(0) - 1
    rows, width = fresh_ref.shape
    slots, _, edge_width = edge_ref.shape
    block = slots * rows
    table_rows = table_ref.shape[0]
    own_t = w1t_ref[:, :width]
    nbr_t = w1t_ref[:, width : 2 * width]
    feat_t = w1t_ref[:, 2 * width :]

    def vector(i):
        return vec_ref[V_EDGE + i : V_EDGE + i + 1, :edge_width]

    @pl.when(step == 0)
    def _():
        table_ref[:rows] = fresh_ref[...]
        table_ref[rows:] = incoming_ref[...]
        proj_ref[...] = dot_nt(table_ref[...], nbr_t).astype(BF16)
        self_pre_ref[...] = dot_nt(fresh_ref[...], own_t) + vector(0)
        for ref in (back_ref, dw3_ref, dw2_ref, dw1_ref, sums_ref, first_ref):
            ref[...] = jnp.zeros_like(ref)
        turned_ref[0] = feat_t.T
        turned_ref[1] = w2_ref[...].T
        turned_ref[2] = w3_ref[...].T

    def flat(values):
        return values.reshape(block, edge_width)

    def deep(values):
        return values.reshape(slots, rows, edge_width)

    onehot = edge_onehot(pos_ref, table_rows)
    features = flat(edge_ref[...])
    pre1 = dot_nn(features, turned_ref[0]) + dot_nn(onehot, proj_ref[...])
    pre1 = deep(pre1) + self_pre_ref[...][None]
    act1, slope1 = gelu_pair(flat(pre1))
    act1 = act1.astype(BF16)
    pre2 = dot_nn(act1, w2_ref[...]) + vector(1)
    act2, slope2 = gelu_pair(pre2)
    act2 = act2.astype(BF16)
    mixed3 = features.astype(F32) + (dot_nn(act2, w3_ref[...]) + vector(2))
    xhat, scale = norm_parts(mixed3)
    gain = vector(3)
    slot = lax.broadcasted_iota(jnp.int32, (slots, rows, edge_width), 0) + step * slots
    valid = count_ref[...][None, :, :edge_width] > slot.astype(F32)
    out_ref[...] = jnp.where(valid, deep(xhat * gain + vector(4)), 0.0).astype(BF16)
    upstream = flat(jnp.where(valid, cot_ref[...].astype(F32), 0.0))
    sums_ref[3] += jnp.sum(deep(upstream * xhat), axis=0)
    sums_ref[4] += jnp.sum(deep(upstream), axis=0)
    grad_mixed = norm_back(xhat, scale, gain, upstream)
    grad_delta = grad_mixed.astype(BF16)
    dw3_ref[...] += dot_tn(act2, grad_delta)
    sums_ref[2] += jnp.sum(deep(grad_delta.astype(F32)), axis=0)
    grad2 = (dot_nn(grad_delta, turned_ref[2]) * slope2).astype(BF16)
    dw2_ref[...] += dot_tn(act1, grad2)
    sums_ref[1] += jnp.sum(deep(grad2.astype(F32)), axis=0)
    grad1 = (dot_nn(grad2, turned_ref[1]) * slope1).astype(BF16)
    dw1_ref[...] += dot_tn(grad1, features)
    first_ref[...] += jnp.sum(deep(grad1.astype(F32)), axis=0)
    back_ref[...] += dot_tn(onehot, grad1)
    grad_ref[...] = deep(grad_mixed + dot_nn(grad1, feat_t))

    @pl.when(step == last)
    def _():
        first = first_ref[...]
        back = back_ref[...]
        own_ref[...] = back[:rows]
        away_ref[...] = back[rows:].astype(BF16)
        first_high, first_rest = split_low(first)
        back_high, back_rest = split_low(back)
        own_grad = dot_tn(first_high, fresh_ref[...]) + dot_tn(first_rest, fresh_ref[...])
        nbr_grad = dot_tn(back_high, table_ref[...]) + dot_tn(back_rest, table_ref[...])
        pack_ref[:edge_width, :] = own_grad.astype(BF16)
        pack_ref[edge_width : 2 * edge_width, :] = nbr_grad.astype(BF16)
        pad = jnp.zeros((edge_width, width // 2 - edge_width), BF16)
        third = [dw1_ref[...].astype(BF16), pad, dw2_ref[...].astype(BF16), pad]
        pack_ref[2 * edge_width : 3 * edge_width, :] = jnp.concatenate(third, axis=1)
        fourth = [dw3_ref[...].astype(BF16), pad, jnp.zeros((edge_width, width // 2), BF16)]
        pack_ref[3 * edge_width :, :] = jnp.concatenate(fourth, axis=1)
        vec_out_ref[...] = jnp.zeros_like(vec_out_ref)
        vec_out_ref[0:1, :edge_width] = jnp.sum(first, axis=0, keepdims=True)
        for i in range(1, 5):
            vec_out_ref[i : i + 1, :edge_width] = jnp.sum(sums_ref[i], axis=0, keepdims=True)


def feed_kernel(
    cot_ref,
    first_ref,
    own_ref,
    arrived_ref,
    asked_ref,
    count_ref,
    vec_ref,
    w1t_ref,
    mixed1_ref,
    mixed2_ref,
    slope_ref,
    act_sum_ref,
    expand_ref,
    contract_ref,
    w3_ref,
    edge_vec_ref,
    pack_ref,
    copies_ref,
    spread_ref,
    grad_mixed1_ref,
):
    rows, width = cot_ref.shape
    hidden = expand_ref.shape[1]
    own_t = w1t_ref[:, :width]
    nbr_t = w1t_ref[:, width : 2 * width]
    counts = count_ref[...]

    def vector(i):
        return vec_ref[i : i + 1, :]

    def total(values):
        return jnp.sum(values.astype(F32), axis=0, keepdims=True)

    back = own_ref[...] + dot_nn(asked_onehot(asked_ref, rows), arrived_ref[...])
    grad_fresh = (
        cot_ref[...].astype(F32)
        + dot_split(dot_nn, first_ref[...], own_t)
        + dot_split(dot_nn, back, nbr_t)
    )
    xhat2, scale2 = norm_parts(mixed2_ref[...])
    grad_mixed2 = norm_back(xhat2, scale2, vector(V_N2G), grad_fresh)
    grad_contracted = grad_mixed2.astype(BF16)
    for p in range(copies_ref.shape[0]):
        copies_ref[p] = grad_contracted
    turned = grad_contracted.T
    updated = jnp.zeros((width, rows), F32)
    for c in range(hidden // width):
        cols = slice(c * width, (c + 1) * width)
        pre = dot_nn(contract_ref[cols, :], turned) * slope_ref[cols, :]
        updated = updated + dot_nn(expand_ref[:, cols], pre.astype(BF16))
    grad_updated = grad_mixed2 + updated.T
    xhat1, scale1 = norm_parts(mixed1_ref[...])
    grad_mixed1 = norm_back(xhat1, scale1, vector(V_N1G), grad_updated)
    grad_mixed1_ref[...] = grad_mixed1
    grad_message = (grad_mixed1 / counts).astype(BF16)
    spread_ref[...] = dot_nt(grad_message, w3_ref[...])
    pack_ref[:width, :] = dot_split(dot_tn, act_sum_ref[...], grad_message).astype(BF16)
    vectors = [
        total(counts * grad_message.astype(F32)),
        total(grad_updated * xhat1),
        total(grad_updated),
        total(grad_fresh * xhat2),
        total(grad_fresh),
        edge_vec_ref[...],
    ]
    vectors = jnp.concatenate(vectors, axis=0)
    vectors = jnp.concatenate(
        [vectors, jnp.zeros((pack_ref.shape[0] - width - vectors.shape[0], width), F32)], axis=0
    )
    pack_ref[width:, :] = vectors.astype(BF16)


def feed_weight_kernel(low_ref, grad_ref, expand_ref, bias_ref, contract_ref, *refs, more):
    sums_in = refs[:4] if more else None
    expand_out_ref, contract_out_ref, bias_out_ref, last_bias_ref = refs[-6:-2]
    low_turned_ref, grad_turned_ref = refs[-2:]
    chunk = pl.program_id(1)
    ones = jnp.ones((8, low_ref.shape[0]), F32).astype(BF16)

    @pl.when(chunk == 0)
    def _():
        low_turned_ref[...] = low_ref[...].T
        grad_turned_ref[...] = grad_ref[...].T

    act, slope = gelu_pair(dot_nn(low_ref[...], expand_ref[...]) + bias_ref[0:1, :])
    act = act.astype(BF16)
    pre = (dot_nt(grad_ref[...], contract_ref[...]) * slope).astype(BF16)
    expanded = dot_nn(low_turned_ref[...], pre)
    contracted = dot_nn(grad_turned_ref[...], act).T
    sums = dot_nn(ones, pre)
    if more:
        expanded = expanded + sums_in[0][...]
        contracted = contracted + sums_in[1][...]
        sums = sums + sums_in[2][...]
    expand_out_ref[...] = expanded
    contract_out_ref[...] = contracted
    bias_out_ref[...] = sums

    @pl.when(chunk == 0)
    def _():
        last = dot_nn(ones, grad_ref[...])
        last_bias_ref[...] = last + sums_in[3][...] if more else last


def message_kernel(
    core_ref,
    edge_ref,
    pos_ref,
    act1_ref,
    slope1_ref,
    slope2_ref,
    partial_ref,
    spread_ref,
    table_ref,
    w1_ref,
    w2_ref,
    edge_pack_ref,
    feed_pack_ref,
    grad_ref,
    first_ref,
    own_ref,
    away_ref,
    send_ref,
    keep_ref,
    joint_ref,
    dw2_ref,
    bias2_ref,
    w2_turned_ref,
    w1_turned_ref,
):
    step = pl.program_id(0)
    last = pl.num_programs(0) - 1
    slots, rows, edge_width = edge_ref.shape
    width = act1_ref.shape[1]
    block = slots * rows
    table_rows = table_ref.shape[0]

    @pl.when(step == 0)
    def _():
        for ref in (joint_ref, dw2_ref, bias2_ref, first_ref):
            ref[...] = jnp.zeros_like(ref)
        w2_turned_ref[...] = w2_ref[...].T
        w1_turned_ref[...] = w1_ref[2 * width :].T

    spread = spread_ref[...]
    grad2 = []
    bias2 = bias2_ref[...]
    for k in range(slots):
        part = (spread * slope2_ref[pl.ds(k * rows, rows), :].astype(F32)).astype(BF16)
        bias2 = bias2 + part.astype(F32)
        grad2.append(part)
    bias2_ref[...] = bias2
    grad2 = jnp.concatenate(grad2, axis=0)
    dw2_ref[...] += dot_tn(act1_ref[...], grad2)
    grad1 = (dot_nn(grad2, w2_turned_ref[...]) * slope1_ref[...].astype(F32)).astype(BF16)
    first_ref[...] += jnp.sum(grad1.astype(F32).reshape(slots, rows, width), axis=0)
    onehot = edge_onehot(pos_ref, table_rows)
    features = edge_ref[...].reshape(block, edge_width)
    joint_ref[...] += dot_tn(jnp.concatenate([onehot, features], axis=1), grad1)
    grad_ref[...] = partial_ref[...] + dot_nn(grad1, w1_turned_ref[...]).reshape(
        slots, rows, edge_width
    )

    @pl.when(step == last)
    def _():
        first = first_ref[...]
        back = joint_ref[:table_rows]
        own_ref[...] = back[:rows]
        away_ref[...] = back[rows:].astype(BF16)
        own_grad = dot_split_right(dot_tn, table_ref[:rows], first).astype(BF16)
        nbr_grad = dot_split_right(dot_tn, table_ref[...], back).astype(BF16)
        vectors = [
            feed_pack_ref[width:].astype(F32),
            jnp.sum(first, axis=0, keepdims=True),
            jnp.sum(bias2_ref[...], axis=0, keepdims=True),
        ]
        lower = [own_grad, nbr_grad, feed_pack_ref[:width]]
        upper = [joint_ref[table_rows:].astype(BF16), dw2_ref[...].astype(BF16), edge_pack_ref[...]]

        def fill(ref, pieces, tail):
            base = 0
            for piece in pieces:
                ref[base : base + piece.shape[0]] = piece
                base += piece.shape[0]
            if base < ref.shape[0]:
                gap = ref.shape[0] - base - sum(v.shape[0] for v in tail)
                rest = jnp.concatenate(tail + [jnp.zeros((gap, width), F32)], axis=0)
                ref[base:] = rest.astype(BF16)

        @pl.when(core_ref[0] == 0)
        def _():
            fill(keep_ref, lower, [])
            fill(send_ref, upper, vectors)

        @pl.when(core_ref[0] != 0)
        def _():
            fill(send_ref, lower, [])
            fill(keep_ref, upper, vectors)


def pair_kernel(y_ref, keep_ref, came_ref, away_ref, out_ref, *, parts, cap):
    peers, total, _ = out_ref.shape
    x_size = lax.axis_size("x")
    z_size = parts // x_size
    riders = z_size * cap
    share = total - riders
    for p in range(peers):
        y, x = divmod(p, x_size)
        part = pl.ds(p * share, share)
        out_ref[p, riders:] = (
            keep_ref[part, :].astype(F32) + came_ref[part, :].astype(F32)
        ).astype(BF16)
        rows = [
            away_ref[pl.ds((z * x_size + x) * cap, cap), :].astype(F32) for z in range(z_size)
        ]
        rows = jnp.where(y_ref[0] == y, jnp.concatenate(rows, axis=0), 0.0)
        out_ref[p, :riders] = rows.astype(BF16)


def plane_kernel(y_ref, came_ref, out_ref, *, cap):
    peers = came_ref.shape[0]
    z_size, total, _ = out_ref.shape
    x_size = lax.axis_size("x")
    riders = x_size * cap
    share = total - riders
    first = z_size * cap
    for z in range(z_size):
        part = pl.ds(first + z * share, share)
        value = came_ref[0, part, :].astype(F32)
        for p in range(1, peers):
            value = value + came_ref[p, part, :].astype(F32)
        out_ref[z, riders:] = value.astype(BF16)
    rows = []
    for x in range(x_size):
        value = came_ref[x, :first].astype(F32)
        for y in range(1, peers // x_size):
            value = jnp.where(y_ref[0] == y, came_ref[y * x_size + x, :first].astype(F32), value)
        rows.append(value)
    for z in range(z_size):
        part = [value[z * cap : (z + 1) * cap] for value in rows]
        out_ref[z, :riders] = jnp.concatenate(part, axis=0).astype(BF16)


def column_kernel(came_ref, copies_ref, returned_ref):
    z_size, total, _ = came_ref.shape
    riders = returned_ref.shape[0] // z_size
    value = came_ref[0, riders:].astype(F32)
    for z in range(1, z_size):
        value = value + came_ref[z, riders:].astype(F32)
    for z in range(z_size):
        copies_ref[z] = value.astype(BF16)
        returned_ref[z * riders : (z + 1) * riders, :] = came_ref[z, :riders]


def node_grad_kernel(grad_ref, first_ref, own_ref, arrived_ref, asked_ref, w1_ref, out_ref):
    rows, width = grad_ref.shape
    back = own_ref[...] + dot_nn(asked_onehot(asked_ref, rows), arrived_ref[...])
    out_ref[...] = (
        grad_ref[...]
        + dot_split(dot_nt, first_ref[...], w1_ref[:width])
        + dot_split(dot_nt, back, w1_ref[width : 2 * width])
    )


def unpack_kernel(core_ref, mine_ref, other_ref, bias_ref, last_bias_ref, *refs):
    (
        message1_ref,
        message1_bias_ref,
        message2_ref,
        message2_bias_ref,
        message3_ref,
        message3_bias_ref,
        gain1_ref,
        shift1_ref,
        expand_bias_ref,
        contract_bias_ref,
        gain2_ref,
        shift2_ref,
        edge1_ref,
        edge1_bias_ref,
        edge2_ref,
        edge2_bias_ref,
        edge3_ref,
        edge3_bias_ref,
        gain3_ref,
        shift3_ref,
    ) = refs
    width = mine_ref.shape[1]
    edge_width = edge2_ref.shape[0]
    half = width // 2
    first_core = core_ref[0] == 0

    def lower(start, stop):
        return jnp.where(first_core, mine_ref[start:stop], other_ref[start:stop]).astype(F32)

    def upper(start, stop):
        return jnp.where(first_core, other_ref[start:stop], mine_ref[start:stop]).astype(F32)

    message1_ref[: 2 * width] = lower(0, 2 * width)
    message3_ref[...] = lower(2 * width, 3 * width)
    message1_ref[2 * width :] = upper(0, edge_width)
    base = edge_width
    message2_ref[...] = upper(base, base + width)
    base = base + width
    edge1_ref[:, :width] = upper(base, base + edge_width)
    edge1_ref[:, width : 2 * width] = upper(base + edge_width, base + 2 * edge_width)
    third = upper(base + 2 * edge_width, base + 3 * edge_width)
    edge1_ref[:, 2 * width :] = third[:, :edge_width]
    edge2_ref[...] = third[:, half : half + edge_width]
    edge3_ref[...] = upper(base + 3 * edge_width, base + 4 * edge_width)[:, :edge_width]
    base = base + 4 * edge_width
    vectors = upper(base, mine_ref.shape[0])
    targets = (message3_bias_ref, gain1_ref, shift1_ref, gain2_ref, shift2_ref)
    for i, ref in enumerate(targets):
        ref[...] = vectors[i]
    targets = (edge1_bias_ref, edge2_bias_ref, edge3_bias_ref, gain3_ref, shift3_ref)
    for i, ref in enumerate(targets):
        ref[...] = vectors[5 + i, :edge_width]
    message1_bias_ref[...] = vectors[16]
    message2_bias_ref[...] = vectors[17]
    expand_bias_ref[...] = bias_ref[0]
    contract_bias_ref[...] = last_bias_ref[0]


def gather_copies(copies, axes):
    return lax.all_to_all(copies, axes, split_axis=0, concat_axis=0, tiled=True)


def copies_of(values, axes):
    return jnp.broadcast_to(values[None], (lax.axis_size(axes), *values.shape))


def exchange(values, parts):
    grouped = values.reshape(parts, values.shape[0] // parts, values.shape[1])
    arrived = lax.all_to_all(grouped, RES, split_axis=0, concat_axis=0, tiled=True)
    return arrived.reshape(values.shape)


def other_core(values):
    return lax.ppermute(values, "core", [(0, 1), (1, 0)])


def whole(shape):
    return pl.BlockSpec(shape, lambda *_: (0,) * len(shape))


def params(mebibytes):
    return pltpu.CompilerParams(vmem_limit_bytes=mebibytes * MIB)


def cost(microseconds):
    return pl.CostEstimate(
        flops=int(microseconds * 1.15e9),
        bytes_accessed=int(microseconds * 3.69e6),
        transcendentals=0,
    )


def body(
    node_states,
    edge_states,
    neighbour_index,
    edge_mask,
    node_cotangent,
    edge_cotangent,
    message_weight1,
    message_bias1,
    message_weight2,
    message_bias2,
    message_weight3,
    message_bias3,
    norm1_gain,
    norm1_shift,
    expand_weight,
    expand_bias,
    contract_weight,
    contract_bias,
    norm2_gain,
    norm2_shift,
    edge_weight1,
    edge_bias1,
    edge_weight2,
    edge_bias2,
    edge_weight3,
    edge_bias3,
    norm3_gain,
    norm3_shift,
):
    self_rows = node_states[0]
    rows, width = self_rows.shape
    slots = neighbour_index.shape[2]
    edge_width = edge_states.shape[3]
    hidden = expand_weight.shape[1]
    edges = rows * slots
    parts = lax.axis_size(RES)
    cap = ROW_CAP
    table_rows = rows + parts * cap
    side = lax.axis_size(SIDE)
    steps = 5
    block_slots = slots // steps
    block = block_slots * rows
    pairs = block // LANES

    everyone = gather_copies(copies_of(self_rows, RES), RES).reshape(parts * rows, width)
    core = lax.axis_index("core").astype(jnp.int32).reshape(1)
    me = lax.axis_index(RES).astype(jnp.int32).reshape(1)
    edge_rows = edge_states[0].transpose(1, 0, 2)
    edge_cot = edge_cotangent[0].transpose(1, 0, 2)
    slot_index = neighbour_index.transpose(2, 0, 1)
    slot_mask = edge_mask.transpose(2, 0, 1)
    edge_w1t = edge_weight1.T
    wide = (
        message_bias1,
        message_bias2,
        message_bias3,
        norm1_gain,
        norm1_shift,
        contract_bias,
        norm2_gain,
        norm2_shift,
        expand_bias,
    )
    narrow = (edge_bias1, edge_bias2, edge_bias3, norm3_gain, norm3_shift)
    vmem = pl.BlockSpec(memory_space=pltpu.VMEM)

    def shape(dims, kind):
        return jax.ShapeDtypeStruct(dims, kind)

    pos, select, ids, counts, vectors, bias_row = pl.pallas_call(
        functools.partial(
            prepare_kernel, parts=parts, cap=cap, steps=steps, wide=len(wide), narrow=len(narrow)
        ),
        out_shape=(
            shape((steps, LANES, pairs), jnp.int32),
            shape((parts * rows, table_rows), BF16),
            shape((parts, cap), jnp.int32),
            shape((rows, width), F32),
            shape((V_ROWS, width), F32),
            shape((1, hidden), F32),
        ),
        in_specs=[pl.BlockSpec(memory_space=pltpu.SMEM)] + [vmem] * (2 + len(wide) + len(narrow)),
        out_specs=(vmem,) * 6,
        compiler_params=params(56),
        cost_estimate=cost(6),
        name="prepare",
    )(me, slot_index, slot_mask, *wide, *narrow)
    ids, everyone = lax.optimization_barrier((ids, everyone))
    asked = lax.all_to_all(ids, RES, split_axis=0, concat_axis=0, tiled=True)

    edge_spec = pl.BlockSpec((block_slots, rows, edge_width), lambda i: (i, 0, 0))
    flat_spec = pl.BlockSpec((block, width), lambda i: (i, 0))
    pos_spec = pl.BlockSpec((1, LANES, pairs), lambda i: (i, 0, 0))
    any_spec = pl.BlockSpec(memory_space=pl.ANY)
    node_spec = whole((rows, width))
    away_spec = whole((parts * cap, width))

    (
        act1,
        slope1,
        slope2,
        fresh,
        table,
        mixed1,
        mixed2,
        low,
        slope_e,
        act_sum,
    ) = pl.pallas_call(
        node_kernel,
        grid=(steps,),
        in_specs=[
            edge_spec,
            pos_spec,
            whole((parts * rows, table_rows)),
            whole((parts * rows, width)),
            node_spec,
            node_spec,
            whole((V_ROWS, width)),
            whole(message_weight1.shape),
            whole((width, width)),
            whole((width, width)),
            any_spec,
            any_spec,
        ],
        out_specs=[
            flat_spec,
            flat_spec,
            flat_spec,
            node_spec,
            whole((table_rows, width)),
            node_spec,
            node_spec,
            whole((side, rows, width)),
            whole((hidden, rows)),
            node_spec,
        ],
        out_shape=[
            shape((edges, width), BF16),
            shape((edges, width), BF16),
            shape((edges, width), BF16),
            shape((rows, width), BF16),
            shape((table_rows, width), BF16),
            shape((rows, width), F32),
            shape((rows, width), F32),
            shape((side, rows, width), BF16),
            shape((hidden, rows), F32),
            shape((rows, width), F32),
        ],
        scratch_shapes=[
            pltpu.VMEM((table_rows, width), BF16),
            pltpu.VMEM((rows, width), F32),
            pltpu.VMEM((width, hidden), BF16),
            pltpu.VMEM((hidden, width), BF16),
            pltpu.SemaphoreType.DMA((2,)),
        ],
        compiler_params=params(56),
        cost_estimate=cost(26),
        name="node_forward",
    )(
        edge_rows,
        pos,
        select,
        everyone,
        self_rows,
        counts,
        vectors,
        message_weight1,
        message_weight2,
        message_weight3,
        expand_weight,
        contract_weight,
    )
    outgoing = pl.pallas_call(
        pick_kernel,
        in_specs=[vmem] * 2,
        out_specs=vmem,
        out_shape=shape((parts * cap, width), BF16),
        compiler_params=params(8),
        cost_estimate=cost(1),
        name="pick",
    )(asked, fresh)
    incoming = exchange(outgoing, parts)
    low_mine = gather_copies(low, SIDE).reshape(side * rows, width)

    edge_pack_rows = 4 * edge_width
    edge_out, grad_partial, edge_first, edge_own, edge_away, edge_pack, edge_vec = pl.pallas_call(
        edge_kernel,
        grid=(steps,),
        in_specs=[
            edge_spec,
            edge_spec,
            pos_spec,
            node_spec,
            away_spec,
            node_spec,
            whole((V_ROWS, width)),
            whole(edge_w1t.shape),
            whole((edge_width, edge_width)),
            whole((edge_width, edge_width)),
        ],
        out_specs=[
            edge_spec,
            edge_spec,
            whole((rows, edge_width)),
            whole((rows, edge_width)),
            whole((parts * cap, edge_width)),
            whole((edge_pack_rows, width)),
            whole((8, width)),
        ],
        out_shape=[
            shape((slots, rows, edge_width), BF16),
            shape((slots, rows, edge_width), F32),
            shape((rows, edge_width), F32),
            shape((rows, edge_width), F32),
            shape((parts * cap, edge_width), BF16),
            shape((edge_pack_rows, width), BF16),
            shape((8, width), F32),
        ],
        scratch_shapes=[
            pltpu.VMEM((table_rows, width), BF16),
            pltpu.VMEM((table_rows, edge_width), BF16),
            pltpu.VMEM((rows, edge_width), F32),
            pltpu.VMEM((table_rows, edge_width), F32),
            pltpu.VMEM((edge_width, edge_width), F32),
            pltpu.VMEM((edge_width, edge_width), F32),
            pltpu.VMEM((edge_width, edge_width), F32),
            pltpu.VMEM((5, rows, edge_width), F32),
            pltpu.VMEM((3, edge_width, edge_width), BF16),
        ],
        compiler_params=params(56),
        cost_estimate=cost(21),
        name="edge_both",
    )(
        edge_rows,
        edge_cot,
        pos,
        fresh,
        incoming,
        counts,
        vectors,
        edge_w1t,
        edge_weight2,
        edge_weight3,
    )
    edge_away, low_mine = lax.optimization_barrier((edge_away, low_mine))
    edge_arrived = exchange(edge_away, parts)

    feed_rows = width + 16
    feed_pack, grad_copies, spread, grad_mixed1 = pl.pallas_call(
        feed_kernel,
        in_specs=[vmem] * 16,
        out_specs=[vmem] * 4,
        out_shape=[
            shape((feed_rows, width), BF16),
            shape((side, rows, width), BF16),
            shape((rows, width), F32),
            shape((rows, width), F32),
        ],
        compiler_params=params(56),
        cost_estimate=cost(7),
        name="feed_backward",
    )(
        node_cotangent[0],
        edge_first,
        edge_own,
        edge_arrived,
        asked,
        counts,
        vectors,
        edge_w1t,
        mixed1,
        mixed2,
        slope_e,
        act_sum,
        expand_weight,
        contract_weight,
        message_weight3,
        edge_vec,
    )
    grad_mine = gather_copies(grad_copies, SIDE).reshape(side * rows, width)

    unit = 16 * side
    half_rows = (3 * width + unit - 1) // unit * unit
    edge_grad, first, own, away, send, keep = pl.pallas_call(
        message_kernel,
        grid=(steps,),
        in_specs=[
            pl.BlockSpec(memory_space=pltpu.SMEM),
            edge_spec,
            pos_spec,
            flat_spec,
            flat_spec,
            flat_spec,
            edge_spec,
            node_spec,
            whole((table_rows, width)),
            whole(message_weight1.shape),
            whole((width, width)),
            whole((edge_pack_rows, width)),
            whole((feed_rows, width)),
        ],
        out_specs=[
            edge_spec,
            node_spec,
            node_spec,
            away_spec,
            whole((half_rows, width)),
            whole((half_rows, width)),
        ],
        out_shape=[
            shape((slots, rows, edge_width), F32),
            shape((rows, width), F32),
            shape((rows, width), F32),
            shape((parts * cap, width), BF16),
            shape((half_rows, width), BF16),
            shape((half_rows, width), BF16),
        ],
        scratch_shapes=[
            pltpu.VMEM((table_rows + edge_width, width), F32),
            pltpu.VMEM((width, width), F32),
            pltpu.VMEM((rows, width), F32),
            pltpu.VMEM((width, width), BF16),
            pltpu.VMEM((width, edge_width), BF16),
        ],
        compiler_params=params(56),
        cost_estimate=cost(14),
        name="message_backward",
    )(
        core,
        edge_rows,
        pos,
        act1,
        slope1,
        slope2,
        grad_partial,
        spread,
        table,
        message_weight1,
        message_weight2,
        edge_pack,
        feed_pack,
    )
    came = other_core(send)
    y_size = lax.axis_size("y")
    x_size = lax.axis_size("x")
    z_size = lax.axis_size("z")
    my_y = lax.axis_index("y").astype(jnp.int32).reshape(1)
    peers = y_size * x_size
    smem = pl.BlockSpec(memory_space=pltpu.SMEM)
    payload = pl.pallas_call(
        functools.partial(pair_kernel, parts=parts, cap=cap),
        in_specs=[smem] + [vmem] * 3,
        out_specs=vmem,
        out_shape=shape((peers, half_rows // peers + z_size * cap, width), BF16),
        compiler_params=params(20),
        cost_estimate=cost(3),
        name="pair_sum",
    )(my_y, keep, came, away)
    payload, grad_mine, low_mine = lax.optimization_barrier((payload, grad_mine, low_mine))
    grad_other = other_core(grad_mine)
    low_other = other_core(low_mine)
    arrived = lax.all_to_all(payload, PLANE, split_axis=0, concat_axis=0, tiled=True)
    def feed_weights(low_values, grad_values, sums):
        units = 256
        block_rows = low_values.shape[0]
        row_spec = whole((block_rows, width))
        sum_specs = [
            pl.BlockSpec((width, units), lambda _, c: (0, c)),
            pl.BlockSpec((units, width), lambda _, c: (c, 0)),
            pl.BlockSpec((8, units), lambda _, c: (0, c)),
            whole((8, width)),
        ]
        return pl.pallas_call(
            functools.partial(feed_weight_kernel, more=bool(sums)),
            grid=(1, hidden // units),
            in_specs=[
                row_spec,
                row_spec,
                sum_specs[0],
                pl.BlockSpec((1, units), lambda _, c: (0, c)),
                sum_specs[1],
                *(sum_specs if sums else []),
            ],
            out_specs=sum_specs,
            out_shape=[
                shape((width, hidden), F32),
                shape((hidden, width), F32),
                shape((8, hidden), F32),
                shape((8, width), F32),
            ],
            scratch_shapes=[
                pltpu.VMEM((width, block_rows), BF16),
                pltpu.VMEM((width, block_rows), BF16),
            ],
            compiler_params=params(56),
            cost_estimate=cost(12),
            name="feed_weights_more" if sums else "feed_weights",
        )(low_values, grad_values, expand_weight, bias_row, contract_weight, *sums)

    def feed_side(low_values, grad_values, sums):
        block_rows = min(side * rows, 1024)
        for at in range(0, side * rows, block_rows):
            part = slice(at, at + block_rows)
            sums = tuple(feed_weights(low_values[part], grad_values[part], sums))
        return sums

    sums = feed_side(low_mine, grad_mine, ())
    arrived, *sums = lax.optimization_barrier((arrived, *sums))
    payload = pl.pallas_call(
        functools.partial(plane_kernel, cap=cap),
        in_specs=[smem, vmem],
        out_specs=vmem,
        out_shape=shape((z_size, half_rows // side + x_size * cap, width), BF16),
        compiler_params=params(16),
        cost_estimate=cost(3),
        name="plane_sum",
    )(my_y, arrived)
    arrived = lax.all_to_all(payload, "z", split_axis=0, concat_axis=0, tiled=True)
    copies, returned = pl.pallas_call(
        column_kernel,
        in_specs=[vmem],
        out_specs=[vmem] * 2,
        out_shape=[
            shape((z_size, half_rows // side, width), BF16),
            shape((parts * cap, width), BF16),
        ],
        compiler_params=params(8),
        cost_estimate=cost(1),
        name="column_sum",
    )(arrived)
    column = lax.all_to_all(copies, "z", split_axis=0, concat_axis=0, tiled=True)
    column, grad_other, low_other, *sums = lax.optimization_barrier(
        (column, grad_other, low_other, *sums)
    )
    column = copies_of(column.reshape(half_rows // peers, width), PLANE)
    mine = gather_copies(column, PLANE).reshape(half_rows, width)
    sums = feed_side(low_other, grad_other, tuple(sums))
    mine, *sums = lax.optimization_barrier((mine, *sums))
    grad_expand, grad_contract, expand_bias_sum, contract_bias_sum = sums
    other = other_core(mine)
    node_grad = pl.pallas_call(
        node_grad_kernel,
        in_specs=[vmem] * 6,
        out_specs=vmem,
        out_shape=shape((rows, width), F32),
        compiler_params=params(12),
        cost_estimate=cost(3),
        name="node_gradient",
    )(grad_mixed1, first, own, returned, asked, message_weight1)

    vec = shape((width,), F32)
    thin = shape((edge_width,), F32)
    square = shape((width, width), F32)
    small = shape((edge_width, edge_width), F32)
    (
        grad_message1,
        grad_mb1,
        grad_message2,
        grad_mb2,
        grad_message3,
        grad_mb3,
        grad_n1g,
        grad_n1s,
        grad_eb,
        grad_cb,
        grad_n2g,
        grad_n2s,
        grad_edge1_t,
        grad_eb1,
        grad_edge2,
        grad_eb2,
        grad_edge3,
        grad_eb3,
        grad_n3g,
        grad_n3s,
    ) = pl.pallas_call(
        unpack_kernel,
        in_specs=[smem] + [vmem] * 4,
        out_specs=[vmem] * 20,
        out_shape=[
            shape(message_weight1.shape, F32),
            vec,
            square,
            vec,
            square,
            vec,
            vec,
            vec,
            shape((hidden,), F32),
            vec,
            vec,
            vec,
            shape(edge_w1t.shape, F32),
            thin,
            small,
            thin,
            small,
            thin,
            thin,
            thin,
        ],
        compiler_params=params(24),
        cost_estimate=cost(4),
        name="unpack",
    )(core, mine, other, expand_bias_sum, contract_bias_sum)
    return (
        fresh[None],
        edge_out.transpose(1, 0, 2)[None],
        node_grad[None],
        edge_grad.transpose(1, 0, 2)[None],
        grad_message1,
        grad_mb1,
        grad_message2,
        grad_mb2,
        grad_message3,
        grad_mb3,
        grad_n1g,
        grad_n1s,
        grad_expand,
        grad_eb,
        grad_contract,
        grad_cb,
        grad_n2g,
        grad_n2s,
        grad_edge1_t.T,
        grad_eb1,
        grad_edge2,
        grad_eb2,
        grad_edge3,
        grad_eb3,
        grad_n3g,
        grad_n3s,
    )


def solution(mesh):
    batch, res = mesh.shape["batch"], mesh.shape["res"]
    x_size = 1 << ((res.bit_length() - 1) // 2)
    sizes = (batch // CORES, CORES, res // x_size, x_size)
    fine = jax.sharding.Mesh(mesh.devices.reshape(sizes), ALL)
    row_spec = P(("y", "core"), RES, None)
    edge_spec = P(("y", "core"), RES, None, None)
    return jax.shard_map(
        body,
        mesh=fine,
        in_specs=(row_spec, edge_spec, row_spec, row_spec, row_spec, edge_spec) + (P(),) * 22,
        out_specs=(row_spec, edge_spec, row_spec, edge_spec) + (P(),) * 22,
        check_vma=False,
    )
```

```python
import functools
import math

import jax
import jax.numpy as jnp
from jax import lax
from jax.experimental import pallas as pl
from jax.experimental.pallas import tpu as pltpu
from jax.sharding import PartitionSpec as P

ROW_CAP = 8
CORES = 2
RES = ("z", "x")
PLANE = ("y", "x")
SIDE = ("y", "z", "x")
ALL = ("y", "core", "z", "x")
EPSILON = 1e-05
LANES = 128
MIB = 1024 * 1024
SUB_SLOTS = 4
F32 = jnp.float32
BF16 = jnp.bfloat16

V_MB1, V_MB2, V_MB3, V_N1G, V_N1S, V_CB, V_N2G, V_N2S, V_EB = range(9)
V_EDGE = 12
V_ROWS = 24


def dot_nn(left, right):
    return lax.dot_general(left, right, (((1,), (0,)), ((), ())), preferred_element_type=F32)


def dot_nt(left, right):
    return lax.dot_general(left, right, (((1,), (1,)), ((), ())), preferred_element_type=F32)


def dot_tn(left, right):
    return lax.dot_general(left, right, (((0,), (0,)), ((), ())), preferred_element_type=F32)


def split_low(values):
    high = values.astype(BF16)
    return high, (values - high.astype(F32)).astype(BF16)


def dot_split(dot, left, right):
    high, rest = split_low(left)
    return dot(high, right) + dot(rest, right)


def dot_split_right(dot, left, right):
    high, rest = split_low(right)
    return dot(left, high) + dot(left, rest)


def gelu_pair(v):
    e = jnp.exp2((v * v) * (-0.5 * math.log2(math.e)))
    phi_sum = 0.5 + 0.5 * lax.erf(v * math.sqrt(0.5))
    return v * phi_sum, phi_sum + (v * (1.0 / math.sqrt(2.0 * math.pi))) * e


def norm_parts(values):
    average = jnp.mean(values, axis=-1, keepdims=True)
    centred = values - average
    variance = jnp.mean(centred * centred, axis=-1, keepdims=True)
    scale = lax.rsqrt(variance + EPSILON)
    return centred * scale, scale


def norm_back(xhat, scale, gain, upstream):
    w = upstream * gain
    mean_w = jnp.mean(w, axis=-1, keepdims=True)
    mean_wx = jnp.mean(w * xhat, axis=-1, keepdims=True)
    return (w - mean_w - xhat * mean_wx) * scale


def edge_onehot(pos_ref, table_rows, start, count):
    lane = lax.broadcasted_iota(jnp.int32, (LANES, table_rows), 1)
    pairs = range(start // LANES, (start + count) // LANES)
    return jnp.concatenate(
        [(pos_ref[0, :, p : p + 1] == lane).astype(F32).astype(BF16) for p in pairs], axis=0
    )


def prepare_kernel(me_ref, idx_ref, mask_ref, *refs, parts, cap, steps, wide, narrow):
    wide_refs = refs[:wide]
    narrow_refs = refs[wide : wide + narrow]
    pos_ref, select_ref, ids_ref, count_ref, vec_ref, expand_bias_ref = refs[wide + narrow :]
    rows, width = count_ref.shape
    total = rows * parts
    table = rows + parts * cap
    me = me_ref[0]
    pair_rows = idx_ref.shape[0] // 2
    named = [
        jnp.concatenate([idx_ref[2 * j], idx_ref[2 * j + 1]], axis=1) for j in range(pair_rows)
    ]
    residue = lax.broadcasted_iota(jnp.int32, (total, LANES), 0)
    owner = residue // rows
    within = residue - owner * rows
    hits = jnp.zeros((total, LANES), F32)
    for j in range(pair_rows):
        hits = jnp.where(named[j] == residue, 1.0, hits)
    hit = jnp.max(hits, axis=1, keepdims=True)
    own = owner == me
    wanted = jnp.where(own, 0.0, jnp.broadcast_to(hit, (total, LANES)))
    low_row = lax.broadcasted_iota(jnp.int32, (rows, rows), 0)
    low_col = lax.broadcasted_iota(jnp.int32, (rows, rows), 1)
    lower = (low_col <= low_row).astype(F32).astype(BF16)
    wanted_low = wanted.astype(BF16)
    place = jnp.concatenate(
        [dot_nn(lower, wanted_low[o * rows : (o + 1) * rows]) for o in range(parts)], axis=0
    )
    place = jnp.clip(place - 1.0, 0.0, cap - 1.0)
    pos = jnp.where(own, within.astype(F32), (rows + owner * cap).astype(F32) + place)
    picked = [
        jnp.sum(jnp.where(named[j] == residue, pos, 0.0), axis=0, keepdims=True)
        for j in range(pair_rows)
    ]
    picked.append(jnp.zeros((LANES - pair_rows, LANES), F32))
    turned = jnp.concatenate(picked, axis=0).T.astype(jnp.int32)
    per = pair_rows // steps
    for s in range(steps):
        pos_ref[s] = turned[:, s * per : (s + 1) * per]
    lane = lax.broadcasted_iota(jnp.int32, (total, table), 1).astype(F32)
    live = jnp.where(own, 1.0, wanted)
    chosen = jnp.where(lane == pos[:, :1], jnp.broadcast_to(live[:, :1], (total, table)), 0.0)
    select_ref[...] = chosen.astype(BF16)
    asked_row = jnp.broadcast_to(within[:, :1].astype(F32), (total, parts * cap))
    ids = jnp.sum(chosen[:, rows:] * asked_row, axis=0, keepdims=True)
    ids = ids.astype(jnp.int32)
    for o in range(parts):
        ids_ref[o : o + 1, :] = ids[:, o * cap : (o + 1) * cap]
    count = mask_ref[0]
    for k in range(1, mask_ref.shape[0]):
        count = count + mask_ref[k]
    count = jnp.concatenate([count.astype(F32), jnp.zeros((7, rows), F32)], axis=0)
    count_ref[...] = dot_tn(count.astype(BF16), jnp.ones((8, width), F32).astype(BF16))
    expand_bias_ref[...] = wide_refs[-1][...].astype(F32).reshape(expand_bias_ref.shape)
    vec_ref[...] = jnp.zeros_like(vec_ref)
    at = 0
    for ref in wide_refs:
        for c in range(ref.shape[0] // width):
            part = ref[c * width : (c + 1) * width]
            vec_ref[at : at + 1, :] = part.astype(F32).reshape(1, width)
            at += 1
    for ref in narrow_refs:
        vec_ref[at : at + 1, : ref.shape[0]] = ref[...].astype(F32).reshape(1, ref.shape[0])
        at += 1


def node_kernel(
    edge_ref,
    pos_ref,
    select_ref,
    all_ref,
    self_ref,
    count_ref,
    vec_ref,
    w1_ref,
    w2_ref,
    w3_ref,
    expand_hbm,
    contract_hbm,
    act1_ref,
    slope1_ref,
    slope2_ref,
    fresh_ref,
    table_ref,
    mixed1_ref,
    mixed2_ref,
    low_ref,
    slope_e_ref,
    act_sum_ref,
    proj_ref,
    self_pre_ref,
    expand_ref,
    contract_ref,
    sems,
):
    step = pl.program_id(0)
    last = pl.num_programs(0) - 1
    rows, width = self_ref.shape
    slots = edge_ref.shape[0]
    edge_width = edge_ref.shape[2]
    table_rows = table_ref.shape[0]
    expand_copy = pltpu.make_async_copy(expand_hbm, expand_ref, sems.at[0])
    contract_copy = pltpu.make_async_copy(contract_hbm, contract_ref, sems.at[1])

    @pl.when(step == 0)
    def _():
        expand_copy.start()
        contract_copy.start()
        table = dot_tn(select_ref[...], all_ref[...]).astype(BF16)
        table_ref[...] = table
        proj_ref[...] = dot_nn(table, w1_ref[width : 2 * width]).astype(BF16)
        self_pre_ref[...] = (
            dot_nn(self_ref[...], w1_ref[:width]) + vec_ref[V_MB1 : V_MB1 + 1, :]
        )
        act_sum_ref[...] = jnp.zeros_like(act_sum_ref)

    self_pre = self_pre_ref[...]
    bias2 = vec_ref[V_MB2 : V_MB2 + 1, :]
    act_sum = act_sum_ref[...]
    counts = count_ref[...]
    for first in range(0, slots, SUB_SLOTS):
        features = edge_ref[first : first + SUB_SLOTS].reshape(SUB_SLOTS * rows, edge_width)
        onehot = edge_onehot(pos_ref, table_rows, first * rows, SUB_SLOTS * rows)
        pre1 = dot_nn(features, w1_ref[2 * width :]) + dot_nn(onehot, proj_ref[...])
        act1 = []
        for k in range(SUB_SLOTS):
            part = pl.ds((first + k) * rows, rows)
            act, slope = gelu_pair(pre1[k * rows : (k + 1) * rows] + self_pre)
            act = act.astype(BF16)
            act1.append(act)
            act1_ref[part, :] = act
            slope1_ref[part, :] = slope.astype(BF16)
        pre2 = dot_nn(jnp.concatenate(act1, axis=0), w2_ref[...])
        for k in range(SUB_SLOTS):
            part = pl.ds((first + k) * rows, rows)
            act, slope = gelu_pair(pre2[k * rows : (k + 1) * rows] + bias2)
            valid = counts > (step * slots + first + k).astype(F32)
            act_sum = act_sum + jnp.where(valid, act.astype(BF16).astype(F32), 0.0)
            slope2_ref[part, :] = jnp.where(valid, slope, 0.0).astype(BF16)
    act_sum_ref[...] = act_sum

    @pl.when(step == last)
    def _():
        summed = dot_split(dot_nn, act_sum_ref[...], w3_ref[...])
        summed = summed + counts * vec_ref[V_MB3 : V_MB3 + 1, :]
        mixed1 = self_ref[...].astype(F32) + summed / counts
        mixed1_ref[...] = mixed1
        xhat1, _ = norm_parts(mixed1)
        updated = xhat1 * vec_ref[V_N1G : V_N1G + 1, :] + vec_ref[V_N1S : V_N1S + 1, :]
        low = updated.astype(BF16)
        for p in range(low_ref.shape[0]):
            low_ref[p] = low
        expand_copy.wait()
        contract_copy.wait()
        mixed2 = updated + vec_ref[V_CB : V_CB + 1, :]
        for c in range(expand_ref.shape[1] // width):
            cols = slice(c * width, (c + 1) * width)
            pre = dot_nn(low, expand_ref[:, cols]) + vec_ref[V_EB + c : V_EB + c + 1, :]
            act, slope = gelu_pair(pre)
            act = act.astype(BF16)
            slope_e_ref[:, cols] = slope
            mixed2 = mixed2 + dot_nn(act, contract_ref[cols, :])
        mixed2_ref[...] = mixed2
        xhat2, _ = norm_parts(mixed2)
        fresh = (xhat2 * vec_ref[V_N2G : V_N2G + 1, :] + vec_ref[V_N2S : V_N2S + 1, :]).astype(BF16)
        fresh_ref[...] = fresh


def asked_onehot(asked_ref, rows):
    parts = asked_ref.shape[0]
    asked = jnp.concatenate([asked_ref[o : o + 1, :] for o in range(parts)], axis=1)
    row = lax.broadcasted_iota(jnp.int32, (rows, asked.shape[1]), 0)
    return (asked == row).astype(F32).astype(BF16)


def pick_kernel(asked_ref, fresh_ref, out_ref):
    out_ref[...] = dot_tn(asked_onehot(asked_ref, fresh_ref.shape[0]), fresh_ref[...]).astype(BF16)


def edge_kernel(
    edge_ref,
    cot_ref,
    pos_ref,
    fresh_ref,
    incoming_ref,
    count_ref,
    vec_ref,
    w1t_ref,
    w2_ref,
    w3_ref,
    out_ref,
    grad_ref,
    first_ref,
    own_ref,
    away_ref,
    pack_ref,
    vec_out_ref,
    table_ref,
    proj_ref,
    self_pre_ref,
    back_ref,
    dw3_ref,
    dw2_ref,
    dw1_ref,
    sums_ref,
    turned_ref,
):
    step = pl.program_id(0)
    last = pl.num_programs(0) - 1
    rows, width = fresh_ref.shape
    slots, _, edge_width = edge_ref.shape
    table_rows = table_ref.shape[0]
    own_t = w1t_ref[:, :width]
    nbr_t = w1t_ref[:, width : 2 * width]
    feat_t = w1t_ref[:, 2 * width :]

    def vector(i):
        return vec_ref[V_EDGE + i : V_EDGE + i + 1, :edge_width]

    @pl.when(step == 0)
    def _():
        table_ref[:rows] = fresh_ref[...]
        table_ref[rows:] = incoming_ref[...]
        proj_ref[...] = dot_nt(table_ref[...], nbr_t).astype(BF16)
        self_pre_ref[...] = dot_nt(fresh_ref[...], own_t) + vector(0)
        for ref in (back_ref, dw3_ref, dw2_ref, dw1_ref, sums_ref, first_ref):
            ref[...] = jnp.zeros_like(ref)
        turned_ref[0] = feat_t.T
        turned_ref[1] = w2_ref[...].T
        turned_ref[2] = w3_ref[...].T

    gain = vector(3)
    counts = count_ref[:, :edge_width]
    for first in range(0, slots, SUB_SLOTS):
        sub = slice(first, first + SUB_SLOTS)

        def flat(values):
            return values.reshape(SUB_SLOTS * rows, edge_width)

        def deep(values):
            return values.reshape(SUB_SLOTS, rows, edge_width)

        onehot = edge_onehot(pos_ref, table_rows, first * rows, SUB_SLOTS * rows)
        features = flat(edge_ref[sub])
        pre1 = dot_nn(features, turned_ref[0]) + dot_nn(onehot, proj_ref[...])
        pre1 = deep(pre1) + self_pre_ref[...][None]
        act1, slope1 = gelu_pair(flat(pre1))
        act1 = act1.astype(BF16)
        pre2 = dot_nn(act1, w2_ref[...]) + vector(1)
        act2, slope2 = gelu_pair(pre2)
        act2 = act2.astype(BF16)
        mixed3 = features.astype(F32) + (dot_nn(act2, w3_ref[...]) + vector(2))
        xhat, scale = norm_parts(mixed3)
        slot = lax.broadcasted_iota(jnp.int32, (SUB_SLOTS, rows, edge_width), 0)
        valid = counts[None] > (slot + step * slots + first).astype(F32)
        out_ref[sub] = jnp.where(valid, deep(xhat * gain + vector(4)), 0.0).astype(BF16)
        upstream = flat(jnp.where(valid, cot_ref[sub].astype(F32), 0.0))
        sums_ref[3] += jnp.sum(deep(upstream * xhat), axis=0)
        sums_ref[4] += jnp.sum(deep(upstream), axis=0)
        grad_mixed = norm_back(xhat, scale, gain, upstream)
        grad_delta = grad_mixed.astype(BF16)
        dw3_ref[...] += dot_tn(act2, grad_delta)
        sums_ref[2] += jnp.sum(deep(grad_delta.astype(F32)), axis=0)
        grad2 = (dot_nn(grad_delta, turned_ref[2]) * slope2).astype(BF16)
        dw2_ref[...] += dot_tn(act1, grad2)
        sums_ref[1] += jnp.sum(deep(grad2.astype(F32)), axis=0)
        grad1 = (dot_nn(grad2, turned_ref[1]) * slope1).astype(BF16)
        dw1_ref[...] += dot_tn(grad1, features)
        first_ref[...] += jnp.sum(deep(grad1.astype(F32)), axis=0)
        back_ref[...] += dot_tn(onehot, grad1)
        grad_ref[sub] = deep(grad_mixed + dot_nn(grad1, feat_t))

    @pl.when(step == last)
    def _():
        first = first_ref[...]
        back = back_ref[...]
        own_ref[...] = back[:rows]
        away_ref[...] = back[rows:].astype(BF16)
        first_high, first_rest = split_low(first)
        back_high, back_rest = split_low(back)
        own_grad = dot_tn(first_high, fresh_ref[...]) + dot_tn(first_rest, fresh_ref[...])
        nbr_grad = dot_tn(back_high, table_ref[...]) + dot_tn(back_rest, table_ref[...])
        pack_ref[:edge_width, :] = own_grad.astype(BF16)
        pack_ref[edge_width : 2 * edge_width, :] = nbr_grad.astype(BF16)
        pad = jnp.zeros((edge_width, width // 2 - edge_width), BF16)
        third = [dw1_ref[...].astype(BF16), pad, dw2_ref[...].astype(BF16), pad]
        pack_ref[2 * edge_width : 3 * edge_width, :] = jnp.concatenate(third, axis=1)
        fourth = [dw3_ref[...].astype(BF16), pad, jnp.zeros((edge_width, width // 2), BF16)]
        pack_ref[3 * edge_width :, :] = jnp.concatenate(fourth, axis=1)
        vec_out_ref[...] = jnp.zeros_like(vec_out_ref)
        vec_out_ref[0:1, :edge_width] = jnp.sum(first, axis=0, keepdims=True)
        for i in range(1, 5):
            vec_out_ref[i : i + 1, :edge_width] = jnp.sum(sums_ref[i], axis=0, keepdims=True)


def feed_kernel(
    cot_ref,
    first_ref,
    own_ref,
    arrived_ref,
    asked_ref,
    count_ref,
    vec_ref,
    w1t_ref,
    mixed1_ref,
    mixed2_ref,
    slope_ref,
    act_sum_ref,
    expand_ref,
    contract_ref,
    w3_ref,
    edge_vec_ref,
    pack_ref,
    copies_ref,
    spread_ref,
    grad_mixed1_ref,
):
    rows, width = cot_ref.shape
    hidden = expand_ref.shape[1]
    own_t = w1t_ref[:, :width]
    nbr_t = w1t_ref[:, width : 2 * width]
    counts = count_ref[...]

    def vector(i):
        return vec_ref[i : i + 1, :]

    def total(values):
        return jnp.sum(values.astype(F32), axis=0, keepdims=True)

    back = own_ref[...] + dot_nn(asked_onehot(asked_ref, rows), arrived_ref[...])
    grad_fresh = (
        cot_ref[...].astype(F32)
        + dot_split(dot_nn, first_ref[...], own_t)
        + dot_split(dot_nn, back, nbr_t)
    )
    xhat2, scale2 = norm_parts(mixed2_ref[...])
    grad_mixed2 = norm_back(xhat2, scale2, vector(V_N2G), grad_fresh)
    grad_contracted = grad_mixed2.astype(BF16)
    for p in range(copies_ref.shape[0]):
        copies_ref[p] = grad_contracted
    grad_updated = grad_mixed2
    for c in range(hidden // width):
        cols = slice(c * width, (c + 1) * width)
        pre = dot_nt(grad_contracted, contract_ref[cols, :]) * slope_ref[:, cols]
        grad_updated = grad_updated + dot_nt(pre.astype(BF16), expand_ref[:, cols])
    xhat1, scale1 = norm_parts(mixed1_ref[...])
    grad_mixed1 = norm_back(xhat1, scale1, vector(V_N1G), grad_updated)
    grad_mixed1_ref[...] = grad_mixed1
    grad_message = (grad_mixed1 / counts).astype(BF16)
    spread_ref[...] = dot_nt(grad_message, w3_ref[...])
    pack_ref[:width, :] = dot_split(dot_tn, act_sum_ref[...], grad_message).astype(BF16)
    vectors = [
        total(counts * grad_message.astype(F32)),
        total(grad_updated * xhat1),
        total(grad_updated),
        total(grad_fresh * xhat2),
        total(grad_fresh),
        edge_vec_ref[...],
    ]
    vectors = jnp.concatenate(vectors, axis=0)
    vectors = jnp.concatenate(
        [vectors, jnp.zeros((pack_ref.shape[0] - width - vectors.shape[0], width), F32)], axis=0
    )
    pack_ref[width:, :] = vectors.astype(BF16)


def feed_weight_kernel(low_ref, grad_ref, expand_ref, bias_ref, contract_ref, *refs, more):
    sums_in = refs[:4] if more else None
    expand_out_ref, contract_out_ref, bias_out_ref, last_bias_ref = refs[-6:-2]
    low_turned_ref, grad_turned_ref = refs[-2:]
    chunk = pl.program_id(1)
    ones = jnp.ones((8, low_ref.shape[0]), F32).astype(BF16)

    @pl.when(chunk == 0)
    def _():
        low_turned_ref[...] = low_ref[...].T
        grad_turned_ref[...] = grad_ref[...].T

    act, slope = gelu_pair(dot_nn(low_ref[...], expand_ref[...]) + bias_ref[0:1, :])
    act = act.astype(BF16)
    pre = (dot_nt(grad_ref[...], contract_ref[...]) * slope).astype(BF16)
    expanded = dot_nn(low_turned_ref[...], pre)
    contracted = dot_nn(grad_turned_ref[...], act).T
    sums = dot_nn(ones, pre)
    if more:
        expanded = expanded + sums_in[0][...]
        contracted = contracted + sums_in[1][...]
        sums = sums + sums_in[2][...]
    expand_out_ref[...] = expanded
    contract_out_ref[...] = contracted
    bias_out_ref[...] = sums

    @pl.when(chunk == 0)
    def _():
        last = dot_nn(ones, grad_ref[...])
        last_bias_ref[...] = last + sums_in[3][...] if more else last


def message_kernel(
    core_ref,
    edge_ref,
    pos_ref,
    act1_ref,
    slope1_ref,
    slope2_ref,
    partial_ref,
    spread_ref,
    table_ref,
    w1_ref,
    w2_ref,
    edge_pack_ref,
    feed_pack_ref,
    grad_ref,
    first_ref,
    own_ref,
    away_ref,
    send_ref,
    keep_ref,
    joint_ref,
    dw2_ref,
    bias2_ref,
    w2_turned_ref,
    w1_turned_ref,
):
    step = pl.program_id(0)
    last = pl.num_programs(0) - 1
    slots, rows, edge_width = edge_ref.shape
    width = act1_ref.shape[1]
    block = slots * rows
    table_rows = table_ref.shape[0]

    @pl.when(step == 0)
    def _():
        for ref in (joint_ref, dw2_ref, bias2_ref, first_ref):
            ref[...] = jnp.zeros_like(ref)
        w2_turned_ref[...] = w2_ref[...].T
        w1_turned_ref[...] = w1_ref[2 * width :].T

    spread = spread_ref[...]
    grad2 = []
    bias2 = bias2_ref[...]
    for k in range(slots):
        part = (spread * slope2_ref[pl.ds(k * rows, rows), :].astype(F32)).astype(BF16)
        bias2 = bias2 + part.astype(F32)
        grad2.append(part)
    bias2_ref[...] = bias2
    grad2 = jnp.concatenate(grad2, axis=0)
    dw2_ref[...] += dot_tn(act1_ref[...], grad2)
    grad1 = (dot_nn(grad2, w2_turned_ref[...]) * slope1_ref[...].astype(F32)).astype(BF16)
    first_ref[...] += jnp.sum(grad1.astype(F32).reshape(slots, rows, width), axis=0)
    onehot = edge_onehot(pos_ref, table_rows, 0, block)
    features = edge_ref[...].reshape(block, edge_width)
    joint_ref[...] += dot_tn(jnp.concatenate([onehot, features], axis=1), grad1)
    grad_ref[...] = partial_ref[...] + dot_nn(grad1, w1_turned_ref[...]).reshape(
        slots, rows, edge_width
    )

    @pl.when(step == last)
    def _():
        first = first_ref[...]
        back = joint_ref[:table_rows]
        own_ref[...] = back[:rows]
        away_ref[...] = back[rows:].astype(BF16)
        own_grad = dot_split_right(dot_tn, table_ref[:rows], first).astype(BF16)
        nbr_grad = dot_split_right(dot_tn, table_ref[...], back).astype(BF16)
        vectors = [
            feed_pack_ref[width:].astype(F32),
            jnp.sum(first, axis=0, keepdims=True),
            jnp.sum(bias2_ref[...], axis=0, keepdims=True),
        ]
        lower = [own_grad, nbr_grad, feed_pack_ref[:width]]
        upper = [joint_ref[table_rows:].astype(BF16), dw2_ref[...].astype(BF16), edge_pack_ref[...]]

        def fill(ref, pieces, tail):
            base = 0
            for piece in pieces:
                ref[base : base + piece.shape[0]] = piece
                base += piece.shape[0]
            if base < ref.shape[0]:
                gap = ref.shape[0] - base - sum(v.shape[0] for v in tail)
                rest = jnp.concatenate(tail + [jnp.zeros((gap, width), F32)], axis=0)
                ref[base:] = rest.astype(BF16)

        @pl.when(core_ref[0] == 0)
        def _():
            fill(keep_ref, lower, [])
            fill(send_ref, upper, vectors)

        @pl.when(core_ref[0] != 0)
        def _():
            fill(send_ref, lower, [])
            fill(keep_ref, upper, vectors)


def pair_kernel(y_ref, keep_ref, came_ref, away_ref, out_ref, *, parts, cap):
    peers, total, _ = out_ref.shape
    x_size = lax.axis_size("x")
    z_size = parts // x_size
    riders = z_size * cap
    share = total - riders
    for p in range(peers):
        y, x = divmod(p, x_size)
        part = pl.ds(p * share, share)
        out_ref[p, riders:] = (
            keep_ref[part, :].astype(F32) + came_ref[part, :].astype(F32)
        ).astype(BF16)
        rows = [
            away_ref[pl.ds((z * x_size + x) * cap, cap), :].astype(F32) for z in range(z_size)
        ]
        rows = jnp.where(y_ref[0] == y, jnp.concatenate(rows, axis=0), 0.0)
        out_ref[p, :riders] = rows.astype(BF16)


def plane_kernel(y_ref, came_ref, out_ref, *, cap):
    peers = came_ref.shape[0]
    z_size, total, _ = out_ref.shape
    x_size = lax.axis_size("x")
    riders = x_size * cap
    share = total - riders
    first = z_size * cap
    for z in range(z_size):
        part = pl.ds(first + z * share, share)
        value = came_ref[0, part, :].astype(F32)
        for p in range(1, peers):
            value = value + came_ref[p, part, :].astype(F32)
        out_ref[z, riders:] = value.astype(BF16)
    rows = []
    for x in range(x_size):
        value = came_ref[x, :first].astype(F32)
        for y in range(1, peers // x_size):
            value = jnp.where(y_ref[0] == y, came_ref[y * x_size + x, :first].astype(F32), value)
        rows.append(value)
    for z in range(z_size):
        part = [value[z * cap : (z + 1) * cap] for value in rows]
        out_ref[z, :riders] = jnp.concatenate(part, axis=0).astype(BF16)


def column_kernel(came_ref, copies_ref, returned_ref):
    z_size, total, _ = came_ref.shape
    riders = returned_ref.shape[0] // z_size
    value = came_ref[0, riders:].astype(F32)
    for z in range(1, z_size):
        value = value + came_ref[z, riders:].astype(F32)
    for z in range(z_size):
        copies_ref[z] = value.astype(BF16)
        returned_ref[z * riders : (z + 1) * riders, :] = came_ref[z, :riders]


def node_grad_kernel(grad_ref, first_ref, own_ref, arrived_ref, asked_ref, w1_ref, out_ref):
    rows, width = grad_ref.shape
    back = own_ref[...] + dot_nn(asked_onehot(asked_ref, rows), arrived_ref[...])
    out_ref[...] = (
        grad_ref[...]
        + dot_split(dot_nt, first_ref[...], w1_ref[:width])
        + dot_split(dot_nt, back, w1_ref[width : 2 * width])
    )


def unpack_kernel(core_ref, mine_ref, other_ref, bias_ref, last_bias_ref, *refs):
    (
        message1_ref,
        message1_bias_ref,
        message2_ref,
        message2_bias_ref,
        message3_ref,
        message3_bias_ref,
        gain1_ref,
        shift1_ref,
        expand_bias_ref,
        contract_bias_ref,
        gain2_ref,
        shift2_ref,
        edge1_ref,
        edge1_bias_ref,
        edge2_ref,
        edge2_bias_ref,
        edge3_ref,
        edge3_bias_ref,
        gain3_ref,
        shift3_ref,
    ) = refs
    width = mine_ref.shape[1]
    edge_width = edge2_ref.shape[0]
    half = width // 2
    first_core = core_ref[0] == 0

    def lower(start, stop):
        return jnp.where(first_core, mine_ref[start:stop], other_ref[start:stop]).astype(F32)

    def upper(start, stop):
        return jnp.where(first_core, other_ref[start:stop], mine_ref[start:stop]).astype(F32)

    message1_ref[: 2 * width] = lower(0, 2 * width)
    message3_ref[...] = lower(2 * width, 3 * width)
    message1_ref[2 * width :] = upper(0, edge_width)
    base = edge_width
    message2_ref[...] = upper(base, base + width)
    base = base + width
    edge1_ref[:, :width] = upper(base, base + edge_width)
    edge1_ref[:, width : 2 * width] = upper(base + edge_width, base + 2 * edge_width)
    third = upper(base + 2 * edge_width, base + 3 * edge_width)
    edge1_ref[:, 2 * width :] = third[:, :edge_width]
    edge2_ref[...] = third[:, half : half + edge_width]
    edge3_ref[...] = upper(base + 3 * edge_width, base + 4 * edge_width)[:, :edge_width]
    base = base + 4 * edge_width
    vectors = upper(base, mine_ref.shape[0])
    targets = (message3_bias_ref, gain1_ref, shift1_ref, gain2_ref, shift2_ref)
    for i, ref in enumerate(targets):
        ref[...] = vectors[i]
    targets = (edge1_bias_ref, edge2_bias_ref, edge3_bias_ref, gain3_ref, shift3_ref)
    for i, ref in enumerate(targets):
        ref[...] = vectors[5 + i, :edge_width]
    message1_bias_ref[...] = vectors[16]
    message2_bias_ref[...] = vectors[17]
    expand_bias_ref[...] = bias_ref[0]
    contract_bias_ref[...] = last_bias_ref[0]


def gather_copies(copies, axes):
    return lax.all_to_all(copies, axes, split_axis=0, concat_axis=0, tiled=True)


def copies_of(values, axes):
    return jnp.broadcast_to(values[None], (lax.axis_size(axes), *values.shape))


def exchange(values, parts):
    grouped = values.reshape(parts, values.shape[0] // parts, values.shape[1])
    arrived = lax.all_to_all(grouped, RES, split_axis=0, concat_axis=0, tiled=True)
    return arrived.reshape(values.shape)


def other_core(values):
    return lax.ppermute(values, "core", [(0, 1), (1, 0)])


def whole(shape):
    return pl.BlockSpec(shape, lambda *_: (0,) * len(shape))


def params(mebibytes):
    return pltpu.CompilerParams(vmem_limit_bytes=mebibytes * MIB)


def cost(microseconds):
    return pl.CostEstimate(
        flops=int(microseconds * 1.15e9),
        bytes_accessed=int(microseconds * 3.69e6),
        transcendentals=0,
    )


def body(
    node_states,
    edge_states,
    neighbour_index,
    edge_mask,
    node_cotangent,
    edge_cotangent,
    message_weight1,
    message_bias1,
    message_weight2,
    message_bias2,
    message_weight3,
    message_bias3,
    norm1_gain,
    norm1_shift,
    expand_weight,
    expand_bias,
    contract_weight,
    contract_bias,
    norm2_gain,
    norm2_shift,
    edge_weight1,
    edge_bias1,
    edge_weight2,
    edge_bias2,
    edge_weight3,
    edge_bias3,
    norm3_gain,
    norm3_shift,
):
    self_rows = node_states[0]
    rows, width = self_rows.shape
    slots = neighbour_index.shape[2]
    edge_width = edge_states.shape[3]
    hidden = expand_weight.shape[1]
    edges = rows * slots
    parts = lax.axis_size(RES)
    cap = ROW_CAP
    table_rows = rows + parts * cap
    side = lax.axis_size(SIDE)
    steps = 5
    block_slots = slots // steps
    block = block_slots * rows
    pairs = block // LANES

    everyone = gather_copies(copies_of(self_rows, RES), RES).reshape(parts * rows, width)
    core = lax.axis_index("core").astype(jnp.int32).reshape(1)
    me = lax.axis_index(RES).astype(jnp.int32).reshape(1)
    edge_rows = edge_states[0].transpose(1, 0, 2)
    edge_cot = edge_cotangent[0].transpose(1, 0, 2)
    slot_index = neighbour_index.transpose(2, 0, 1)
    slot_mask = edge_mask.transpose(2, 0, 1)
    edge_w1t = edge_weight1.T
    wide = (
        message_bias1,
        message_bias2,
        message_bias3,
        norm1_gain,
        norm1_shift,
        contract_bias,
        norm2_gain,
        norm2_shift,
        expand_bias,
    )
    narrow = (edge_bias1, edge_bias2, edge_bias3, norm3_gain, norm3_shift)
    vmem = pl.BlockSpec(memory_space=pltpu.VMEM)

    def shape(dims, kind):
        return jax.ShapeDtypeStruct(dims, kind)

    pos, select, ids, counts, vectors, bias_row = pl.pallas_call(
        functools.partial(
            prepare_kernel, parts=parts, cap=cap, steps=steps, wide=len(wide), narrow=len(narrow)
        ),
        out_shape=(
            shape((steps, LANES, pairs), jnp.int32),
            shape((parts * rows, table_rows), BF16),
            shape((parts, cap), jnp.int32),
            shape((rows, width), F32),
            shape((V_ROWS, width), F32),
            shape((1, hidden), F32),
        ),
        in_specs=[pl.BlockSpec(memory_space=pltpu.SMEM)] + [vmem] * (2 + len(wide) + len(narrow)),
        out_specs=(vmem,) * 6,
        compiler_params=params(56),
        cost_estimate=cost(6),
        name="prepare",
    )(me, slot_index, slot_mask, *wide, *narrow)
    ids, everyone = lax.optimization_barrier((ids, everyone))
    asked = lax.all_to_all(ids, RES, split_axis=0, concat_axis=0, tiled=True)

    edge_spec = pl.BlockSpec((block_slots, rows, edge_width), lambda i: (i, 0, 0))
    flat_spec = pl.BlockSpec((block, width), lambda i: (i, 0))
    pos_spec = pl.BlockSpec((1, LANES, pairs), lambda i: (i, 0, 0))
    any_spec = pl.BlockSpec(memory_space=pl.ANY)
    node_spec = whole((rows, width))
    away_spec = whole((parts * cap, width))

    (
        act1,
        slope1,
        slope2,
        fresh,
        table,
        mixed1,
        mixed2,
        low,
        slope_e,
        act_sum,
    ) = pl.pallas_call(
        node_kernel,
        grid=(steps,),
        in_specs=[
            edge_spec,
            pos_spec,
            whole((parts * rows, table_rows)),
            whole((parts * rows, width)),
            node_spec,
            node_spec,
            whole((V_ROWS, width)),
            whole(message_weight1.shape),
            whole((width, width)),
            whole((width, width)),
            any_spec,
            any_spec,
        ],
        out_specs=[
            flat_spec,
            flat_spec,
            flat_spec,
            node_spec,
            whole((table_rows, width)),
            node_spec,
            node_spec,
            whole((side, rows, width)),
            whole((rows, hidden)),
            node_spec,
        ],
        out_shape=[
            shape((edges, width), BF16),
            shape((edges, width), BF16),
            shape((edges, width), BF16),
            shape((rows, width), BF16),
            shape((table_rows, width), BF16),
            shape((rows, width), F32),
            shape((rows, width), F32),
            shape((side, rows, width), BF16),
            shape((rows, hidden), F32),
            shape((rows, width), F32),
        ],
        scratch_shapes=[
            pltpu.VMEM((table_rows, width), BF16),
            pltpu.VMEM((rows, width), F32),
            pltpu.VMEM((width, hidden), BF16),
            pltpu.VMEM((hidden, width), BF16),
            pltpu.SemaphoreType.DMA((2,)),
        ],
        compiler_params=params(56),
        cost_estimate=cost(26),
        name="node_forward",
    )(
        edge_rows,
        pos,
        select,
        everyone,
        self_rows,
        counts,
        vectors,
        message_weight1,
        message_weight2,
        message_weight3,
        expand_weight,
        contract_weight,
    )
    outgoing = pl.pallas_call(
        pick_kernel,
        in_specs=[vmem] * 2,
        out_specs=vmem,
        out_shape=shape((parts * cap, width), BF16),
        compiler_params=params(8),
        cost_estimate=cost(1),
        name="pick",
    )(asked, fresh)
    incoming = exchange(outgoing, parts)
    low_mine = gather_copies(low, SIDE).reshape(side * rows, width)

    edge_pack_rows = 4 * edge_width
    edge_out, grad_partial, edge_first, edge_own, edge_away, edge_pack, edge_vec = pl.pallas_call(
        edge_kernel,
        grid=(steps,),
        in_specs=[
            edge_spec,
            edge_spec,
            pos_spec,
            node_spec,
            away_spec,
            node_spec,
            whole((V_ROWS, width)),
            whole(edge_w1t.shape),
            whole((edge_width, edge_width)),
            whole((edge_width, edge_width)),
        ],
        out_specs=[
            edge_spec,
            edge_spec,
            whole((rows, edge_width)),
            whole((rows, edge_width)),
            whole((parts * cap, edge_width)),
            whole((edge_pack_rows, width)),
            whole((8, width)),
        ],
        out_shape=[
            shape((slots, rows, edge_width), BF16),
            shape((slots, rows, edge_width), F32),
            shape((rows, edge_width), F32),
            shape((rows, edge_width), F32),
            shape((parts * cap, edge_width), BF16),
            shape((edge_pack_rows, width), BF16),
            shape((8, width), F32),
        ],
        scratch_shapes=[
            pltpu.VMEM((table_rows, width), BF16),
            pltpu.VMEM((table_rows, edge_width), BF16),
            pltpu.VMEM((rows, edge_width), F32),
            pltpu.VMEM((table_rows, edge_width), F32),
            pltpu.VMEM((edge_width, edge_width), F32),
            pltpu.VMEM((edge_width, edge_width), F32),
            pltpu.VMEM((edge_width, edge_width), F32),
            pltpu.VMEM((5, rows, edge_width), F32),
            pltpu.VMEM((3, edge_width, edge_width), BF16),
        ],
        compiler_params=params(56),
        cost_estimate=cost(5),
        name="edge_both",
    )(
        edge_rows,
        edge_cot,
        pos,
        fresh,
        incoming,
        counts,
        vectors,
        edge_w1t,
        edge_weight2,
        edge_weight3,
    )
    edge_arrived = exchange(edge_away, parts)
    edge_arrived, low_mine = lax.optimization_barrier((edge_arrived, low_mine))

    feed_rows = width + 16
    feed_pack, grad_copies, spread, grad_mixed1 = pl.pallas_call(
        feed_kernel,
        in_specs=[vmem] * 16,
        out_specs=[vmem] * 4,
        out_shape=[
            shape((feed_rows, width), BF16),
            shape((side, rows, width), BF16),
            shape((rows, width), F32),
            shape((rows, width), F32),
        ],
        compiler_params=params(56),
        cost_estimate=cost(7),
        name="feed_backward",
    )(
        node_cotangent[0],
        edge_first,
        edge_own,
        edge_arrived,
        asked,
        counts,
        vectors,
        edge_w1t,
        mixed1,
        mixed2,
        slope_e,
        act_sum,
        expand_weight,
        contract_weight,
        message_weight3,
        edge_vec,
    )
    grad_mine = gather_copies(grad_copies, SIDE).reshape(side * rows, width)

    unit = 16 * side
    half_rows = (3 * width + unit - 1) // unit * unit
    edge_grad, first, own, away, send, keep = pl.pallas_call(
        message_kernel,
        grid=(steps,),
        in_specs=[
            pl.BlockSpec(memory_space=pltpu.SMEM),
            edge_spec,
            pos_spec,
            flat_spec,
            flat_spec,
            flat_spec,
            edge_spec,
            node_spec,
            whole((table_rows, width)),
            whole(message_weight1.shape),
            whole((width, width)),
            whole((edge_pack_rows, width)),
            whole((feed_rows, width)),
        ],
        out_specs=[
            edge_spec,
            node_spec,
            node_spec,
            away_spec,
            whole((half_rows, width)),
            whole((half_rows, width)),
        ],
        out_shape=[
            shape((slots, rows, edge_width), F32),
            shape((rows, width), F32),
            shape((rows, width), F32),
            shape((parts * cap, width), BF16),
            shape((half_rows, width), BF16),
            shape((half_rows, width), BF16),
        ],
        scratch_shapes=[
            pltpu.VMEM((table_rows + edge_width, width), F32),
            pltpu.VMEM((width, width), F32),
            pltpu.VMEM((rows, width), F32),
            pltpu.VMEM((width, width), BF16),
            pltpu.VMEM((width, edge_width), BF16),
        ],
        compiler_params=params(56),
        cost_estimate=cost(14),
        name="message_backward",
    )(
        core,
        edge_rows,
        pos,
        act1,
        slope1,
        slope2,
        grad_partial,
        spread,
        table,
        message_weight1,
        message_weight2,
        edge_pack,
        feed_pack,
    )
    came = other_core(send)
    y_size = lax.axis_size("y")
    x_size = lax.axis_size("x")
    z_size = lax.axis_size("z")
    my_y = lax.axis_index("y").astype(jnp.int32).reshape(1)
    peers = y_size * x_size
    smem = pl.BlockSpec(memory_space=pltpu.SMEM)
    payload = pl.pallas_call(
        functools.partial(pair_kernel, parts=parts, cap=cap),
        in_specs=[smem] + [vmem] * 3,
        out_specs=vmem,
        out_shape=shape((peers, half_rows // peers + z_size * cap, width), BF16),
        compiler_params=params(20),
        cost_estimate=cost(3),
        name="pair_sum",
    )(my_y, keep, came, away)
    payload, grad_mine, low_mine = lax.optimization_barrier((payload, grad_mine, low_mine))
    grad_other = other_core(grad_mine)
    low_other = other_core(low_mine)
    arrived = lax.all_to_all(payload, PLANE, split_axis=0, concat_axis=0, tiled=True)
    def feed_weights(low_values, grad_values, sums):
        units = 256
        block_rows = low_values.shape[0]
        row_spec = whole((block_rows, width))
        sum_specs = [
            pl.BlockSpec((width, units), lambda _, c: (0, c)),
            pl.BlockSpec((units, width), lambda _, c: (c, 0)),
            pl.BlockSpec((8, units), lambda _, c: (0, c)),
            whole((8, width)),
        ]
        return pl.pallas_call(
            functools.partial(feed_weight_kernel, more=bool(sums)),
            grid=(1, hidden // units),
            in_specs=[
                row_spec,
                row_spec,
                sum_specs[0],
                pl.BlockSpec((1, units), lambda _, c: (0, c)),
                sum_specs[1],
                *(sum_specs if sums else []),
            ],
            out_specs=sum_specs,
            out_shape=[
                shape((width, hidden), F32),
                shape((hidden, width), F32),
                shape((8, hidden), F32),
                shape((8, width), F32),
            ],
            scratch_shapes=[
                pltpu.VMEM((width, block_rows), BF16),
                pltpu.VMEM((width, block_rows), BF16),
            ],
            compiler_params=params(56),
            cost_estimate=cost(12),
            name="feed_weights_more" if sums else "feed_weights",
        )(low_values, grad_values, expand_weight, bias_row, contract_weight, *sums)

    def feed_side(low_values, grad_values, sums):
        block_rows = min(side * rows, 1024)
        for at in range(0, side * rows, block_rows):
            part = slice(at, at + block_rows)
            sums = tuple(feed_weights(low_values[part], grad_values[part], sums))
        return sums

    sums = feed_side(low_mine, grad_mine, ())
    arrived, *sums = lax.optimization_barrier((arrived, *sums))
    payload = pl.pallas_call(
        functools.partial(plane_kernel, cap=cap),
        in_specs=[smem, vmem],
        out_specs=vmem,
        out_shape=shape((z_size, half_rows // side + x_size * cap, width), BF16),
        compiler_params=params(16),
        cost_estimate=cost(3),
        name="plane_sum",
    )(my_y, arrived)
    arrived = lax.all_to_all(payload, "z", split_axis=0, concat_axis=0, tiled=True)
    copies, returned = pl.pallas_call(
        column_kernel,
        in_specs=[vmem],
        out_specs=[vmem] * 2,
        out_shape=[
            shape((z_size, half_rows // side, width), BF16),
            shape((parts * cap, width), BF16),
        ],
        compiler_params=params(8),
        cost_estimate=cost(1),
        name="column_sum",
    )(arrived)
    column = lax.all_to_all(copies, "z", split_axis=0, concat_axis=0, tiled=True)
    column, grad_other, low_other, *sums = lax.optimization_barrier(
        (column, grad_other, low_other, *sums)
    )
    column = copies_of(column.reshape(half_rows // peers, width), PLANE)
    mine = gather_copies(column, PLANE).reshape(half_rows, width)
    sums = feed_side(low_other, grad_other, tuple(sums))
    mine, *sums = lax.optimization_barrier((mine, *sums))
    grad_expand, grad_contract, expand_bias_sum, contract_bias_sum = sums
    other = other_core(mine)
    node_grad = pl.pallas_call(
        node_grad_kernel,
        in_specs=[vmem] * 6,
        out_specs=vmem,
        out_shape=shape((rows, width), F32),
        compiler_params=params(12),
        cost_estimate=cost(3),
        name="node_gradient",
    )(grad_mixed1, first, own, returned, asked, message_weight1)

    vec = shape((width,), F32)
    thin = shape((edge_width,), F32)
    square = shape((width, width), F32)
    small = shape((edge_width, edge_width), F32)
    (
        grad_message1,
        grad_mb1,
        grad_message2,
        grad_mb2,
        grad_message3,
        grad_mb3,
        grad_n1g,
        grad_n1s,
        grad_eb,
        grad_cb,
        grad_n2g,
        grad_n2s,
        grad_edge1_t,
        grad_eb1,
        grad_edge2,
        grad_eb2,
        grad_edge3,
        grad_eb3,
        grad_n3g,
        grad_n3s,
    ) = pl.pallas_call(
        unpack_kernel,
        in_specs=[smem] + [vmem] * 4,
        out_specs=[vmem] * 20,
        out_shape=[
            shape(message_weight1.shape, F32),
            vec,
            square,
            vec,
            square,
            vec,
            vec,
            vec,
            shape((hidden,), F32),
            vec,
            vec,
            vec,
            shape(edge_w1t.shape, F32),
            thin,
            small,
            thin,
            small,
            thin,
            thin,
            thin,
        ],
        compiler_params=params(24),
        cost_estimate=cost(4),
        name="unpack",
    )(core, mine, other, expand_bias_sum, contract_bias_sum)
    return (
        fresh[None],
        edge_out.transpose(1, 0, 2)[None],
        node_grad[None],
        edge_grad.transpose(1, 0, 2)[None],
        grad_message1,
        grad_mb1,
        grad_message2,
        grad_mb2,
        grad_message3,
        grad_mb3,
        grad_n1g,
        grad_n1s,
        grad_expand,
        grad_eb,
        grad_contract,
        grad_cb,
        grad_n2g,
        grad_n2s,
        grad_edge1_t.T,
        grad_eb1,
        grad_edge2,
        grad_eb2,
        grad_edge3,
        grad_eb3,
        grad_n3g,
        grad_n3s,
    )


def solution(mesh):
    batch, res = mesh.shape["batch"], mesh.shape["res"]
    x_size = 1 << ((res.bit_length() - 1) // 2)
    sizes = (batch // CORES, CORES, res // x_size, x_size)
    fine = jax.sharding.Mesh(mesh.devices.reshape(sizes), ALL)
    row_spec = P(("y", "core"), RES, None)
    edge_spec = P(("y", "core"), RES, None, None)
    return jax.shard_map(
        body,
        mesh=fine,
        in_specs=(row_spec, edge_spec, row_spec, row_spec, row_spec, edge_spec) + (P(),) * 22,
        out_specs=(row_spec, edge_spec, row_spec, edge_spec) + (P(),) * 22,
        check_vma=False,
    )
```

```python
import functools
import math

import jax
import jax.numpy as jnp
from jax import lax
from jax.experimental import pallas as pl
from jax.experimental.pallas import tpu as pltpu
from jax.sharding import PartitionSpec as P

ROW_CAP = 8
CORES = 2
RES = ("z", "x")
PLANE = ("y", "x")
SIDE = ("y", "z", "x")
ALL = ("y", "core", "z", "x")
EPSILON = 1e-05
LANES = 128
MIB = 1024 * 1024
STEPS = 3
EARLY_ROWS = 48
F32 = jnp.float32
BF16 = jnp.bfloat16

V_MB1, V_MB2, V_MB3, V_N1G, V_N1S, V_CB, V_N2G, V_N2S, V_EB = range(9)
V_EDGE = 12
V_ROWS = 24


def dot_nn(left, right):
    return lax.dot_general(left, right, (((1,), (0,)), ((), ())), preferred_element_type=F32)


def dot_nt(left, right):
    return lax.dot_general(left, right, (((1,), (1,)), ((), ())), preferred_element_type=F32)


def dot_tn(left, right):
    return lax.dot_general(left, right, (((0,), (0,)), ((), ())), preferred_element_type=F32)


def split_low(values):
    high = values.astype(BF16)
    return high, (values - high.astype(F32)).astype(BF16)


def dot_split(dot, left, right):
    high, rest = split_low(left)
    return dot(high, right) + dot(rest, right)


def dot_split_right(dot, left, right):
    high, rest = split_low(right)
    return dot(left, high) + dot(left, rest)


def gelu_pair(v):
    e = jnp.exp2((v * v) * (-0.5 * math.log2(math.e)))
    phi_sum = 0.5 + 0.5 * lax.erf(v * math.sqrt(0.5))
    return v * phi_sum, phi_sum + (v * (1.0 / math.sqrt(2.0 * math.pi))) * e


def norm_parts(values):
    average = jnp.mean(values, axis=-1, keepdims=True)
    centred = values - average
    variance = jnp.mean(centred * centred, axis=-1, keepdims=True)
    scale = lax.rsqrt(variance + EPSILON)
    return centred * scale, scale


def norm_back(xhat, scale, gain, upstream):
    w = upstream * gain
    mean_w = jnp.mean(w, axis=-1, keepdims=True)
    mean_wx = jnp.mean(w * xhat, axis=-1, keepdims=True)
    return (w - mean_w - xhat * mean_wx) * scale


def edge_onehot(pos_ref, table_rows):
    pairs = pos_ref.shape[2]
    lane = lax.broadcasted_iota(jnp.int32, (LANES, table_rows), 1)
    return jnp.concatenate(
        [(pos_ref[0, :, p : p + 1] == lane).astype(F32).astype(BF16) for p in range(pairs)], axis=0
    )


def prepare_kernel(me_ref, idx_ref, mask_ref, *refs, parts, cap, steps, wide, narrow):
    wide_refs = refs[:wide]
    narrow_refs = refs[wide : wide + narrow]
    pos_ref, select_ref, ids_ref, count_ref, vec_ref, expand_bias_ref = refs[wide + narrow :]
    rows, width = count_ref.shape
    total = rows * parts
    table = rows + parts * cap
    me = me_ref[0]
    pair_rows = idx_ref.shape[0] // 2
    named = [
        jnp.concatenate([idx_ref[2 * j], idx_ref[2 * j + 1]], axis=1) for j in range(pair_rows)
    ]
    residue = lax.broadcasted_iota(jnp.int32, (total, LANES), 0)
    owner = residue // rows
    within = residue - owner * rows
    hits = jnp.zeros((total, LANES), F32)
    for j in range(pair_rows):
        hits = jnp.where(named[j] == residue, 1.0, hits)
    hit = jnp.max(hits, axis=1, keepdims=True)
    own = owner == me
    wanted = jnp.where(own, 0.0, jnp.broadcast_to(hit, (total, LANES)))
    low_row = lax.broadcasted_iota(jnp.int32, (rows, rows), 0)
    low_col = lax.broadcasted_iota(jnp.int32, (rows, rows), 1)
    lower = (low_col <= low_row).astype(F32).astype(BF16)
    wanted_low = wanted.astype(BF16)
    place = jnp.concatenate(
        [dot_nn(lower, wanted_low[o * rows : (o + 1) * rows]) for o in range(parts)], axis=0
    )
    place = jnp.clip(place - 1.0, 0.0, cap - 1.0)
    pos = jnp.where(own, within.astype(F32), (rows + owner * cap).astype(F32) + place)
    picked = [
        jnp.sum(jnp.where(named[j] == residue, pos, 0.0), axis=0, keepdims=True)
        for j in range(pair_rows)
    ]
    picked.append(jnp.zeros((LANES - pair_rows, LANES), F32))
    turned = jnp.concatenate(picked, axis=0).T.astype(jnp.int32)
    per = pair_rows // steps
    for s in range(steps):
        pos_ref[s] = turned[:, s * per : (s + 1) * per]
    lane = lax.broadcasted_iota(jnp.int32, (total, table), 1).astype(F32)
    live = jnp.where(own, 1.0, wanted)
    chosen = jnp.where(lane == pos[:, :1], jnp.broadcast_to(live[:, :1], (total, table)), 0.0)
    select_ref[...] = chosen.astype(BF16)
    asked_row = jnp.broadcast_to(within[:, :1].astype(F32), (total, parts * cap))
    ids = jnp.sum(chosen[:, rows:] * asked_row, axis=0, keepdims=True)
    ids = ids.astype(jnp.int32)
    for o in range(parts):
        ids_ref[o : o + 1, :] = ids[:, o * cap : (o + 1) * cap]
    count = mask_ref[0]
    for k in range(1, mask_ref.shape[0]):
        count = count + mask_ref[k]
    count = jnp.concatenate([count.astype(F32), jnp.zeros((7, rows), F32)], axis=0)
    count_ref[...] = dot_tn(count.astype(BF16), jnp.ones((8, width), F32).astype(BF16))
    expand_bias_ref[...] = wide_refs[-1][...].astype(F32).reshape(expand_bias_ref.shape)
    vec_ref[...] = jnp.zeros_like(vec_ref)
    at = 0
    for ref in wide_refs:
        for c in range(ref.shape[0] // width):
            part = ref[c * width : (c + 1) * width]
            vec_ref[at : at + 1, :] = part.astype(F32).reshape(1, width)
            at += 1
    for ref in narrow_refs:
        vec_ref[at : at + 1, : ref.shape[0]] = ref[...].astype(F32).reshape(1, ref.shape[0])
        at += 1


def node_kernel(
    edge_ref,
    pos_ref,
    select_ref,
    all_ref,
    self_ref,
    count_ref,
    vec_ref,
    w1_ref,
    w2_ref,
    w3_ref,
    expand_hbm,
    contract_hbm,
    act1_ref,
    slope1_ref,
    slope2_ref,
    fresh_ref,
    table_ref,
    mixed1_ref,
    mixed2_ref,
    low_ref,
    low_late_ref,
    slope_e_ref,
    act_sum_ref,
    proj_ref,
    self_pre_ref,
    expand_ref,
    contract_ref,
    sems,
):
    step = pl.program_id(0)
    last = pl.num_programs(0) - 1
    rows, width = self_ref.shape
    slots = edge_ref.shape[0]
    edge_width = edge_ref.shape[2]
    table_rows = table_ref.shape[0]
    expand_copy = pltpu.make_async_copy(expand_hbm, expand_ref, sems.at[0])
    contract_copy = pltpu.make_async_copy(contract_hbm, contract_ref, sems.at[1])

    @pl.when(step == 0)
    def _():
        expand_copy.start()
        contract_copy.start()
        table = dot_tn(select_ref[...], all_ref[...]).astype(BF16)
        table_ref[...] = table
        proj_ref[...] = dot_nn(table, w1_ref[width : 2 * width]).astype(BF16)
        self_pre_ref[...] = (
            dot_nn(self_ref[...], w1_ref[:width]) + vec_ref[V_MB1 : V_MB1 + 1, :]
        )
        act_sum_ref[...] = jnp.zeros_like(act_sum_ref)

    onehot = edge_onehot(pos_ref, table_rows)
    features = edge_ref[...].reshape(slots * rows, edge_width)
    pre1 = dot_nn(features, w1_ref[2 * width :]) + dot_nn(onehot, proj_ref[...])
    self_pre = self_pre_ref[...]
    act1 = []
    for k in range(slots):
        part = pl.ds(k * rows, rows)
        act, slope = gelu_pair(pre1[k * rows : (k + 1) * rows] + self_pre)
        act = act.astype(BF16)
        act1.append(act)
        act1_ref[part, :] = act
        slope1_ref[part, :] = slope.astype(BF16)
    pre2 = dot_nn(jnp.concatenate(act1, axis=0), w2_ref[...])
    bias2 = vec_ref[V_MB2 : V_MB2 + 1, :]
    act_sum = act_sum_ref[...]
    counts = count_ref[...]
    for k in range(slots):
        act, slope = gelu_pair(pre2[k * rows : (k + 1) * rows] + bias2)
        valid = counts > (step * slots + k).astype(F32)
        act_sum = act_sum + jnp.where(valid, act.astype(BF16).astype(F32), 0.0)
        slope2_ref[pl.ds(k * rows, rows), :] = jnp.where(valid, slope, 0.0).astype(BF16)
    act_sum_ref[...] = act_sum

    @pl.when(step == last)
    def _():
        summed = dot_split(dot_nn, act_sum_ref[...], w3_ref[...])
        summed = summed + counts * vec_ref[V_MB3 : V_MB3 + 1, :]
        mixed1 = self_ref[...].astype(F32) + summed / counts
        mixed1_ref[...] = mixed1
        xhat1, _ = norm_parts(mixed1)
        updated = xhat1 * vec_ref[V_N1G : V_N1G + 1, :] + vec_ref[V_N1S : V_N1S + 1, :]
        low = updated.astype(BF16)
        for p in range(low_ref.shape[0]):
            low_ref[p] = low[: low_ref.shape[1]]
        low_late_ref[...] = low[low_ref.shape[1] :]
        expand_copy.wait()
        contract_copy.wait()
        mixed2 = updated + vec_ref[V_CB : V_CB + 1, :]
        for c in range(expand_ref.shape[1] // width):
            cols = slice(c * width, (c + 1) * width)
            pre = dot_nn(low, expand_ref[:, cols]) + vec_ref[V_EB + c : V_EB + c + 1, :]
            act, slope = gelu_pair(pre)
            act = act.astype(BF16)
            slope_e_ref[:, cols] = slope
            mixed2 = mixed2 + dot_nn(act, contract_ref[cols, :])
        mixed2_ref[...] = mixed2
        xhat2, _ = norm_parts(mixed2)
        fresh = (xhat2 * vec_ref[V_N2G : V_N2G + 1, :] + vec_ref[V_N2S : V_N2S + 1, :]).astype(BF16)
        fresh_ref[...] = fresh


def asked_onehot(asked_ref, rows):
    parts = asked_ref.shape[0]
    asked = jnp.concatenate([asked_ref[o : o + 1, :] for o in range(parts)], axis=1)
    row = lax.broadcasted_iota(jnp.int32, (rows, asked.shape[1]), 0)
    return (asked == row).astype(F32).astype(BF16)


def pick_kernel(asked_ref, fresh_ref, out_ref):
    out_ref[...] = dot_tn(asked_onehot(asked_ref, fresh_ref.shape[0]), fresh_ref[...]).astype(BF16)


def edge_kernel(
    edge_ref,
    cot_ref,
    pos_ref,
    fresh_ref,
    incoming_ref,
    count_ref,
    vec_ref,
    w1t_ref,
    w2_ref,
    w3_ref,
    out_ref,
    grad_ref,
    first_ref,
    own_ref,
    away_ref,
    pack_ref,
    vec_out_ref,
    table_ref,
    proj_ref,
    self_pre_ref,
    back_ref,
    dw3_ref,
    dw2_ref,
    dw1_ref,
    sums_ref,
    turned_ref,
):
    step = pl.program_id(0)
    last = pl.num_programs(0) - 1
    rows, width = fresh_ref.shape
    slots, _, edge_width = edge_ref.shape
    block = slots * rows
    table_rows = table_ref.shape[0]
    own_t = w1t_ref[:, :width]
    nbr_t = w1t_ref[:, width : 2 * width]
    feat_t = w1t_ref[:, 2 * width :]

    def vector(i):
        return vec_ref[V_EDGE + i : V_EDGE + i + 1, :edge_width]

    @pl.when(step == 0)
    def _():
        table_ref[:rows] = fresh_ref[...]
        table_ref[rows:] = incoming_ref[...]
        proj_ref[...] = dot_nt(table_ref[...], nbr_t).astype(BF16)
        self_pre_ref[...] = dot_nt(fresh_ref[...], own_t) + vector(0)
        for ref in (back_ref, dw3_ref, dw2_ref, dw1_ref, sums_ref, first_ref):
            ref[...] = jnp.zeros_like(ref)
        turned_ref[0] = feat_t.T
        turned_ref[1] = w2_ref[...].T
        turned_ref[2] = w3_ref[...].T

    def flat(values):
        return values.reshape(block, edge_width)

    def deep(values):
        return values.reshape(slots, rows, edge_width)

    onehot = edge_onehot(pos_ref, table_rows)
    features = flat(edge_ref[...])
    pre1 = dot_nn(features, turned_ref[0]) + dot_nn(onehot, proj_ref[...])
    pre1 = deep(pre1) + self_pre_ref[...][None]
    act1, slope1 = gelu_pair(flat(pre1))
    act1 = act1.astype(BF16)
    pre2 = dot_nn(act1, w2_ref[...]) + vector(1)
    act2, slope2 = gelu_pair(pre2)
    act2 = act2.astype(BF16)
    mixed3 = features.astype(F32) + (dot_nn(act2, w3_ref[...]) + vector(2))
    xhat, scale = norm_parts(mixed3)
    gain = vector(3)
    slot = lax.broadcasted_iota(jnp.int32, (slots, rows, edge_width), 0) + step * slots
    valid = count_ref[...][None, :, :edge_width] > slot.astype(F32)
    out_ref[...] = jnp.where(valid, deep(xhat * gain + vector(4)), 0.0).astype(BF16)
    upstream = flat(jnp.where(valid, cot_ref[...].astype(F32), 0.0))
    sums_ref[3] += jnp.sum(deep(upstream * xhat), axis=0)
    sums_ref[4] += jnp.sum(deep(upstream), axis=0)
    grad_mixed = norm_back(xhat, scale, gain, upstream)
    grad_delta = grad_mixed.astype(BF16)
    dw3_ref[...] += dot_tn(act2, grad_delta)
    sums_ref[2] += jnp.sum(deep(grad_delta.astype(F32)), axis=0)
    grad2 = (dot_nn(grad_delta, turned_ref[2]) * slope2).astype(BF16)
    dw2_ref[...] += dot_tn(act1, grad2)
    sums_ref[1] += jnp.sum(deep(grad2.astype(F32)), axis=0)
    grad1 = (dot_nn(grad2, turned_ref[1]) * slope1).astype(BF16)
    dw1_ref[...] += dot_tn(grad1, features)
    first_ref[...] += jnp.sum(deep(grad1.astype(F32)), axis=0)
    back_ref[...] += dot_tn(onehot, grad1)
    grad_ref[...] = deep(grad_mixed + dot_nn(grad1, feat_t))

    @pl.when(step == last)
    def _():
        first = first_ref[...]
        back = back_ref[...]
        own_ref[...] = back[:rows]
        away_ref[...] = back[rows:].astype(BF16)
        first_high, first_rest = split_low(first)
        back_high, back_rest = split_low(back)
        own_grad = dot_tn(first_high, fresh_ref[...]) + dot_tn(first_rest, fresh_ref[...])
        nbr_grad = dot_tn(back_high, table_ref[...]) + dot_tn(back_rest, table_ref[...])
        pack_ref[:edge_width, :] = own_grad.astype(BF16)
        pack_ref[edge_width : 2 * edge_width, :] = nbr_grad.astype(BF16)
        pad = jnp.zeros((edge_width, width // 2 - edge_width), BF16)
        third = [dw1_ref[...].astype(BF16), pad, dw2_ref[...].astype(BF16), pad]
        pack_ref[2 * edge_width : 3 * edge_width, :] = jnp.concatenate(third, axis=1)
        fourth = [dw3_ref[...].astype(BF16), pad, jnp.zeros((edge_width, width // 2), BF16)]
        pack_ref[3 * edge_width :, :] = jnp.concatenate(fourth, axis=1)
        vec_out_ref[...] = jnp.zeros_like(vec_out_ref)
        vec_out_ref[0:1, :edge_width] = jnp.sum(first, axis=0, keepdims=True)
        for i in range(1, 5):
            vec_out_ref[i : i + 1, :edge_width] = jnp.sum(sums_ref[i], axis=0, keepdims=True)


def feed_kernel(
    cot_ref,
    first_ref,
    own_ref,
    arrived_ref,
    asked_ref,
    count_ref,
    vec_ref,
    w1t_ref,
    mixed1_ref,
    mixed2_ref,
    slope_ref,
    act_sum_ref,
    expand_ref,
    contract_ref,
    w3_ref,
    edge_vec_ref,
    low_late_ref,
    pack_ref,
    copies_ref,
    spread_ref,
    grad_mixed1_ref,
):
    rows, width = cot_ref.shape
    hidden = expand_ref.shape[1]
    own_t = w1t_ref[:, :width]
    nbr_t = w1t_ref[:, width : 2 * width]
    counts = count_ref[...]

    def vector(i):
        return vec_ref[i : i + 1, :]

    def total(values):
        return jnp.sum(values.astype(F32), axis=0, keepdims=True)

    back = own_ref[...] + dot_nn(asked_onehot(asked_ref, rows), arrived_ref[...])
    grad_fresh = (
        cot_ref[...].astype(F32)
        + dot_split(dot_nn, first_ref[...], own_t)
        + dot_split(dot_nn, back, nbr_t)
    )
    xhat2, scale2 = norm_parts(mixed2_ref[...])
    grad_mixed2 = norm_back(xhat2, scale2, vector(V_N2G), grad_fresh)
    grad_contracted = grad_mixed2.astype(BF16)
    for p in range(copies_ref.shape[0]):
        copies_ref[p, :rows] = grad_contracted
        copies_ref[p, rows:] = low_late_ref[...]
    grad_updated = grad_mixed2
    for c in range(hidden // width):
        cols = slice(c * width, (c + 1) * width)
        pre = dot_nt(grad_contracted, contract_ref[cols, :]) * slope_ref[:, cols]
        grad_updated = grad_updated + dot_nt(pre.astype(BF16), expand_ref[:, cols])
    xhat1, scale1 = norm_parts(mixed1_ref[...])
    grad_mixed1 = norm_back(xhat1, scale1, vector(V_N1G), grad_updated)
    grad_mixed1_ref[...] = grad_mixed1
    grad_message = (grad_mixed1 / counts).astype(BF16)
    spread_ref[...] = dot_nt(grad_message, w3_ref[...])
    pack_ref[:width, :] = dot_split(dot_tn, act_sum_ref[...], grad_message).astype(BF16)
    vectors = [
        total(counts * grad_message.astype(F32)),
        total(grad_updated * xhat1),
        total(grad_updated),
        total(grad_fresh * xhat2),
        total(grad_fresh),
        edge_vec_ref[...],
    ]
    vectors = jnp.concatenate(vectors, axis=0)
    vectors = jnp.concatenate(
        [vectors, jnp.zeros((pack_ref.shape[0] - width - vectors.shape[0], width), F32)], axis=0
    )
    pack_ref[width:, :] = vectors.astype(BF16)


def feed_weight_kernel(early_ref, late_ref, expand_ref, bias_ref, contract_ref, *refs, more):
    sums_in = refs[:4] if more else None
    expand_out_ref, contract_out_ref, bias_out_ref, last_bias_ref = refs[-8:-4]
    low_ref, grad_ref, low_turned_ref, grad_turned_ref = refs[-4:]
    early = early_ref.shape[1]
    each = (early + late_ref.shape[1]) // 2
    chunk = pl.program_id(1)
    ones = jnp.ones((8, low_ref.shape[0]), F32).astype(BF16)

    @pl.when(chunk == 0)
    def _():
        for p in range(early_ref.shape[0]):
            low_ref[p * each : p * each + early] = early_ref[p]
            low_ref[p * each + early : (p + 1) * each] = late_ref[p, each:]
            grad_ref[p * each : (p + 1) * each] = late_ref[p, :each]
        low_turned_ref[...] = low_ref[...].T
        grad_turned_ref[...] = grad_ref[...].T

    act, slope = gelu_pair(dot_nn(low_ref[...], expand_ref[...]) + bias_ref[0:1, :])
    act = act.astype(BF16)
    pre = (dot_nt(grad_ref[...], contract_ref[...]) * slope).astype(BF16)
    expanded = dot_nn(low_turned_ref[...], pre)
    contracted = dot_nn(grad_turned_ref[...], act).T
    sums = dot_nn(ones, pre)
    if more:
        expanded = expanded + sums_in[0][...]
        contracted = contracted + sums_in[1][...]
        sums = sums + sums_in[2][...]
    expand_out_ref[...] = expanded
    contract_out_ref[...] = contracted
    bias_out_ref[...] = sums

    @pl.when(chunk == 0)
    def _():
        last = dot_nn(ones, grad_ref[...])
        last_bias_ref[...] = last + sums_in[3][...] if more else last


def message_kernel(
    core_ref,
    edge_ref,
    pos_ref,
    act1_ref,
    slope1_ref,
    slope2_ref,
    partial_ref,
    spread_ref,
    table_ref,
    w1_ref,
    w2_ref,
    edge_pack_ref,
    feed_pack_ref,
    grad_ref,
    first_ref,
    own_ref,
    away_ref,
    send_ref,
    keep_ref,
    joint_ref,
    dw2_ref,
    bias2_ref,
    w2_turned_ref,
    w1_turned_ref,
):
    step = pl.program_id(0)
    last = pl.num_programs(0) - 1
    slots, rows, edge_width = edge_ref.shape
    width = act1_ref.shape[1]
    block = slots * rows
    table_rows = table_ref.shape[0]

    @pl.when(step == 0)
    def _():
        for ref in (joint_ref, dw2_ref, bias2_ref, first_ref):
            ref[...] = jnp.zeros_like(ref)
        w2_turned_ref[...] = w2_ref[...].T
        w1_turned_ref[...] = w1_ref[2 * width :].T

    spread = spread_ref[...]
    grad2 = []
    bias2 = bias2_ref[...]
    for k in range(slots):
        part = (spread * slope2_ref[pl.ds(k * rows, rows), :].astype(F32)).astype(BF16)
        bias2 = bias2 + part.astype(F32)
        grad2.append(part)
    bias2_ref[...] = bias2
    grad2 = jnp.concatenate(grad2, axis=0)
    dw2_ref[...] += dot_tn(act1_ref[...], grad2)
    grad1 = (dot_nn(grad2, w2_turned_ref[...]) * slope1_ref[...].astype(F32)).astype(BF16)
    first_ref[...] += jnp.sum(grad1.astype(F32).reshape(slots, rows, width), axis=0)
    onehot = edge_onehot(pos_ref, table_rows)
    features = edge_ref[...].reshape(block, edge_width)
    joint_ref[...] += dot_tn(jnp.concatenate([onehot, features], axis=1), grad1)
    grad_ref[...] = partial_ref[...] + dot_nn(grad1, w1_turned_ref[...]).reshape(
        slots, rows, edge_width
    )

    @pl.when(step == last)
    def _():
        first = first_ref[...]
        back = joint_ref[:table_rows]
        own_ref[...] = back[:rows]
        away_ref[...] = back[rows:].astype(BF16)
        own_grad = dot_split_right(dot_tn, table_ref[:rows], first).astype(BF16)
        nbr_grad = dot_split_right(dot_tn, table_ref[...], back).astype(BF16)
        vectors = [
            feed_pack_ref[width:].astype(F32),
            jnp.sum(first, axis=0, keepdims=True),
            jnp.sum(bias2_ref[...], axis=0, keepdims=True),
        ]
        lower = [own_grad, nbr_grad, feed_pack_ref[:width]]
        upper = [joint_ref[table_rows:].astype(BF16), dw2_ref[...].astype(BF16), edge_pack_ref[...]]

        def fill(ref, pieces, tail):
            base = 0
            for piece in pieces:
                ref[base : base + piece.shape[0]] = piece
                base += piece.shape[0]
            if base < ref.shape[0]:
                gap = ref.shape[0] - base - sum(v.shape[0] for v in tail)
                rest = jnp.concatenate(tail + [jnp.zeros((gap, width), F32)], axis=0)
                ref[base:] = rest.astype(BF16)

        @pl.when(core_ref[0] == 0)
        def _():
            fill(keep_ref, lower, [])
            fill(send_ref, upper, vectors)

        @pl.when(core_ref[0] != 0)
        def _():
            fill(send_ref, lower, [])
            fill(keep_ref, upper, vectors)


def pair_kernel(y_ref, keep_ref, came_ref, away_ref, out_ref, *, parts, cap):
    peers, total, _ = out_ref.shape
    x_size = lax.axis_size("x")
    z_size = parts // x_size
    riders = z_size * cap
    share = total - riders
    for p in range(peers):
        y, x = divmod(p, x_size)
        part = pl.ds(p * share, share)
        out_ref[p, riders:] = (
            keep_ref[part, :].astype(F32) + came_ref[part, :].astype(F32)
        ).astype(BF16)
        rows = [
            away_ref[pl.ds((z * x_size + x) * cap, cap), :].astype(F32) for z in range(z_size)
        ]
        rows = jnp.where(y_ref[0] == y, jnp.concatenate(rows, axis=0), 0.0)
        out_ref[p, :riders] = rows.astype(BF16)


def plane_kernel(y_ref, came_ref, out_ref, *, cap):
    peers = came_ref.shape[0]
    z_size, total, _ = out_ref.shape
    x_size = lax.axis_size("x")
    riders = x_size * cap
    share = total - riders
    first = z_size * cap
    for z in range(z_size):
        part = pl.ds(first + z * share, share)
        value = came_ref[0, part, :].astype(F32)
        for p in range(1, peers):
            value = value + came_ref[p, part, :].astype(F32)
        out_ref[z, riders:] = value.astype(BF16)
    rows = []
    for x in range(x_size):
        value = came_ref[x, :first].astype(F32)
        for y in range(1, peers // x_size):
            value = jnp.where(y_ref[0] == y, came_ref[y * x_size + x, :first].astype(F32), value)
        rows.append(value)
    for z in range(z_size):
        part = [value[z * cap : (z + 1) * cap] for value in rows]
        out_ref[z, :riders] = jnp.concatenate(part, axis=0).astype(BF16)


def column_kernel(came_ref, copies_ref, returned_ref):
    z_size, total, _ = came_ref.shape
    riders = returned_ref.shape[0] // z_size
    value = came_ref[0, riders:].astype(F32)
    for z in range(1, z_size):
        value = value + came_ref[z, riders:].astype(F32)
    for z in range(z_size):
        copies_ref[z] = value.astype(BF16)
        returned_ref[z * riders : (z + 1) * riders, :] = came_ref[z, :riders]


def node_grad_kernel(grad_ref, first_ref, own_ref, arrived_ref, asked_ref, w1_ref, out_ref):
    rows, width = grad_ref.shape
    back = own_ref[...] + dot_nn(asked_onehot(asked_ref, rows), arrived_ref[...])
    out_ref[...] = (
        grad_ref[...]
        + dot_split(dot_nt, first_ref[...], w1_ref[:width])
        + dot_split(dot_nt, back, w1_ref[width : 2 * width])
    )


def unpack_kernel(core_ref, mine_ref, other_ref, bias_ref, last_bias_ref, *refs):
    (
        message1_ref,
        message1_bias_ref,
        message2_ref,
        message2_bias_ref,
        message3_ref,
        message3_bias_ref,
        gain1_ref,
        shift1_ref,
        expand_bias_ref,
        contract_bias_ref,
        gain2_ref,
        shift2_ref,
        edge1_ref,
        edge1_bias_ref,
        edge2_ref,
        edge2_bias_ref,
        edge3_ref,
        edge3_bias_ref,
        gain3_ref,
        shift3_ref,
    ) = refs
    width = mine_ref.shape[1]
    edge_width = edge2_ref.shape[0]
    half = width // 2
    first_core = core_ref[0] == 0

    def lower(start, stop):
        return jnp.where(first_core, mine_ref[start:stop], other_ref[start:stop]).astype(F32)

    def upper(start, stop):
        return jnp.where(first_core, other_ref[start:stop], mine_ref[start:stop]).astype(F32)

    message1_ref[: 2 * width] = lower(0, 2 * width)
    message3_ref[...] = lower(2 * width, 3 * width)
    message1_ref[2 * width :] = upper(0, edge_width)
    base = edge_width
    message2_ref[...] = upper(base, base + width)
    base = base + width
    edge1_ref[:, :width] = upper(base, base + edge_width)
    edge1_ref[:, width : 2 * width] = upper(base + edge_width, base + 2 * edge_width)
    third = upper(base + 2 * edge_width, base + 3 * edge_width)
    edge1_ref[:, 2 * width :] = third[:, :edge_width]
    edge2_ref[...] = third[:, half : half + edge_width]
    edge3_ref[...] = upper(base + 3 * edge_width, base + 4 * edge_width)[:, :edge_width]
    base = base + 4 * edge_width
    vectors = upper(base, mine_ref.shape[0])
    targets = (message3_bias_ref, gain1_ref, shift1_ref, gain2_ref, shift2_ref)
    for i, ref in enumerate(targets):
        ref[...] = vectors[i]
    targets = (edge1_bias_ref, edge2_bias_ref, edge3_bias_ref, gain3_ref, shift3_ref)
    for i, ref in enumerate(targets):
        ref[...] = vectors[5 + i, :edge_width]
    message1_bias_ref[...] = vectors[16]
    message2_bias_ref[...] = vectors[17]
    expand_bias_ref[...] = bias_ref[0]
    contract_bias_ref[...] = last_bias_ref[0]


def gather_copies(copies, axes):
    return lax.all_to_all(copies, axes, split_axis=0, concat_axis=0, tiled=True)


def copies_of(values, axes):
    return jnp.broadcast_to(values[None], (lax.axis_size(axes), *values.shape))


def exchange(values, parts):
    grouped = values.reshape(parts, values.shape[0] // parts, values.shape[1])
    arrived = lax.all_to_all(grouped, RES, split_axis=0, concat_axis=0, tiled=True)
    return arrived.reshape(values.shape)


def other_core(values):
    return lax.ppermute(values, "core", [(0, 1), (1, 0)])


def whole(shape):
    return pl.BlockSpec(shape, lambda *_: (0,) * len(shape))


def params(mebibytes):
    return pltpu.CompilerParams(vmem_limit_bytes=mebibytes * MIB)


def cost(microseconds):
    return pl.CostEstimate(
        flops=int(microseconds * 1.15e9),
        bytes_accessed=int(microseconds * 3.69e6),
        transcendentals=0,
    )


def body(
    node_states,
    edge_states,
    neighbour_index,
    edge_mask,
    node_cotangent,
    edge_cotangent,
    message_weight1,
    message_bias1,
    message_weight2,
    message_bias2,
    message_weight3,
    message_bias3,
    norm1_gain,
    norm1_shift,
    expand_weight,
    expand_bias,
    contract_weight,
    contract_bias,
    norm2_gain,
    norm2_shift,
    edge_weight1,
    edge_bias1,
    edge_weight2,
    edge_bias2,
    edge_weight3,
    edge_bias3,
    norm3_gain,
    norm3_shift,
):
    self_rows = node_states[0]
    rows, width = self_rows.shape
    slots = neighbour_index.shape[2]
    edge_width = edge_states.shape[3]
    hidden = expand_weight.shape[1]
    edges = rows * slots
    parts = lax.axis_size(RES)
    cap = ROW_CAP
    table_rows = rows + parts * cap
    side = lax.axis_size(SIDE)
    steps = STEPS
    block_slots = slots // steps
    block = block_slots * rows
    pairs = block // LANES

    everyone = gather_copies(copies_of(self_rows, RES), RES).reshape(parts * rows, width)
    core = lax.axis_index("core").astype(jnp.int32).reshape(1)
    me = lax.axis_index(RES).astype(jnp.int32).reshape(1)
    edge_rows = edge_states[0].transpose(1, 0, 2)
    edge_cot = edge_cotangent[0].transpose(1, 0, 2)
    slot_index = neighbour_index.transpose(2, 0, 1)
    slot_mask = edge_mask.transpose(2, 0, 1)
    edge_w1t = edge_weight1.T
    wide = (
        message_bias1,
        message_bias2,
        message_bias3,
        norm1_gain,
        norm1_shift,
        contract_bias,
        norm2_gain,
        norm2_shift,
        expand_bias,
    )
    narrow = (edge_bias1, edge_bias2, edge_bias3, norm3_gain, norm3_shift)
    vmem = pl.BlockSpec(memory_space=pltpu.VMEM)

    def shape(dims, kind):
        return jax.ShapeDtypeStruct(dims, kind)

    pos, select, ids, counts, vectors, bias_row = pl.pallas_call(
        functools.partial(
            prepare_kernel, parts=parts, cap=cap, steps=steps, wide=len(wide), narrow=len(narrow)
        ),
        out_shape=(
            shape((steps, LANES, pairs), jnp.int32),
            shape((parts * rows, table_rows), BF16),
            shape((parts, cap), jnp.int32),
            shape((rows, width), F32),
            shape((V_ROWS, width), F32),
            shape((1, hidden), F32),
        ),
        in_specs=[pl.BlockSpec(memory_space=pltpu.SMEM)] + [vmem] * (2 + len(wide) + len(narrow)),
        out_specs=(vmem,) * 6,
        compiler_params=params(56),
        cost_estimate=cost(6),
        name="prepare",
    )(me, slot_index, slot_mask, *wide, *narrow)
    ids, everyone = lax.optimization_barrier((ids, everyone))
    asked = lax.all_to_all(ids, RES, split_axis=0, concat_axis=0, tiled=True)

    edge_spec = pl.BlockSpec((block_slots, rows, edge_width), lambda i: (i, 0, 0))
    flat_spec = pl.BlockSpec((block, width), lambda i: (i, 0))
    pos_spec = pl.BlockSpec((1, LANES, pairs), lambda i: (i, 0, 0))
    any_spec = pl.BlockSpec(memory_space=pl.ANY)
    node_spec = whole((rows, width))
    away_spec = whole((parts * cap, width))

    (
        act1,
        slope1,
        slope2,
        fresh,
        table,
        mixed1,
        mixed2,
        low,
        low_late,
        slope_e,
        act_sum,
    ) = pl.pallas_call(
        node_kernel,
        grid=(steps,),
        in_specs=[
            edge_spec,
            pos_spec,
            whole((parts * rows, table_rows)),
            whole((parts * rows, width)),
            node_spec,
            node_spec,
            whole((V_ROWS, width)),
            whole(message_weight1.shape),
            whole((width, width)),
            whole((width, width)),
            any_spec,
            any_spec,
        ],
        out_specs=[
            flat_spec,
            flat_spec,
            flat_spec,
            node_spec,
            whole((table_rows, width)),
            node_spec,
            node_spec,
            whole((side, EARLY_ROWS, width)),
            whole((rows - EARLY_ROWS, width)),
            whole((rows, hidden)),
            node_spec,
        ],
        out_shape=[
            shape((edges, width), BF16),
            shape((edges, width), BF16),
            shape((edges, width), BF16),
            shape((rows, width), BF16),
            shape((table_rows, width), BF16),
            shape((rows, width), F32),
            shape((rows, width), F32),
            shape((side, EARLY_ROWS, width), BF16),
            shape((rows - EARLY_ROWS, width), BF16),
            shape((rows, hidden), F32),
            shape((rows, width), F32),
        ],
        scratch_shapes=[
            pltpu.VMEM((table_rows, width), BF16),
            pltpu.VMEM((rows, width), F32),
            pltpu.VMEM((width, hidden), BF16),
            pltpu.VMEM((hidden, width), BF16),
            pltpu.SemaphoreType.DMA((2,)),
        ],
        compiler_params=params(56),
        cost_estimate=cost(26),
        name="node_forward",
    )(
        edge_rows,
        pos,
        select,
        everyone,
        self_rows,
        counts,
        vectors,
        message_weight1,
        message_weight2,
        message_weight3,
        expand_weight,
        contract_weight,
    )
    outgoing = pl.pallas_call(
        pick_kernel,
        in_specs=[vmem] * 2,
        out_specs=vmem,
        out_shape=shape((parts * cap, width), BF16),
        compiler_params=params(8),
        cost_estimate=cost(1),
        name="pick",
    )(asked, fresh)
    incoming = exchange(outgoing, parts)
    low_mine = gather_copies(low, SIDE)

    edge_pack_rows = 4 * edge_width
    edge_out, grad_partial, edge_first, edge_own, edge_away, edge_pack, edge_vec = pl.pallas_call(
        edge_kernel,
        grid=(steps,),
        in_specs=[
            edge_spec,
            edge_spec,
            pos_spec,
            node_spec,
            away_spec,
            node_spec,
            whole((V_ROWS, width)),
            whole(edge_w1t.shape),
            whole((edge_width, edge_width)),
            whole((edge_width, edge_width)),
        ],
        out_specs=[
            edge_spec,
            edge_spec,
            whole((rows, edge_width)),
            whole((rows, edge_width)),
            whole((parts * cap, edge_width)),
            whole((edge_pack_rows, width)),
            whole((8, width)),
        ],
        out_shape=[
            shape((slots, rows, edge_width), BF16),
            shape((slots, rows, edge_width), F32),
            shape((rows, edge_width), F32),
            shape((rows, edge_width), F32),
            shape((parts * cap, edge_width), BF16),
            shape((edge_pack_rows, width), BF16),
            shape((8, width), F32),
        ],
        scratch_shapes=[
            pltpu.VMEM((table_rows, width), BF16),
            pltpu.VMEM((table_rows, edge_width), BF16),
            pltpu.VMEM((rows, edge_width), F32),
            pltpu.VMEM((table_rows, edge_width), F32),
            pltpu.VMEM((edge_width, edge_width), F32),
            pltpu.VMEM((edge_width, edge_width), F32),
            pltpu.VMEM((edge_width, edge_width), F32),
            pltpu.VMEM((5, rows, edge_width), F32),
            pltpu.VMEM((3, edge_width, edge_width), BF16),
        ],
        compiler_params=params(56),
        cost_estimate=cost(1),
        name="edge_both",
    )(
        edge_rows,
        edge_cot,
        pos,
        fresh,
        incoming,
        counts,
        vectors,
        edge_w1t,
        edge_weight2,
        edge_weight3,
    )
    edge_away, low_mine = lax.optimization_barrier((edge_away, low_mine))
    edge_arrived = exchange(edge_away, parts)

    feed_rows = width + 16
    feed_pack, grad_copies, spread, grad_mixed1 = pl.pallas_call(
        feed_kernel,
        in_specs=[vmem] * 17,
        out_specs=[vmem] * 4,
        out_shape=[
            shape((feed_rows, width), BF16),
            shape((side, 2 * rows - EARLY_ROWS, width), BF16),
            shape((rows, width), F32),
            shape((rows, width), F32),
        ],
        compiler_params=params(56),
        cost_estimate=cost(7),
        name="feed_backward",
    )(
        node_cotangent[0],
        edge_first,
        edge_own,
        edge_arrived,
        asked,
        counts,
        vectors,
        edge_w1t,
        mixed1,
        mixed2,
        slope_e,
        act_sum,
        expand_weight,
        contract_weight,
        message_weight3,
        edge_vec,
        low_late,
    )
    grad_mine = gather_copies(grad_copies, SIDE)

    unit = 16 * side
    half_rows = (3 * width + unit - 1) // unit * unit
    edge_grad, first, own, away, send, keep = pl.pallas_call(
        message_kernel,
        grid=(steps,),
        in_specs=[
            pl.BlockSpec(memory_space=pltpu.SMEM),
            edge_spec,
            pos_spec,
            flat_spec,
            flat_spec,
            flat_spec,
            edge_spec,
            node_spec,
            whole((table_rows, width)),
            whole(message_weight1.shape),
            whole((width, width)),
            whole((edge_pack_rows, width)),
            whole((feed_rows, width)),
        ],
        out_specs=[
            edge_spec,
            node_spec,
            node_spec,
            away_spec,
            whole((half_rows, width)),
            whole((half_rows, width)),
        ],
        out_shape=[
            shape((slots, rows, edge_width), F32),
            shape((rows, width), F32),
            shape((rows, width), F32),
            shape((parts * cap, width), BF16),
            shape((half_rows, width), BF16),
            shape((half_rows, width), BF16),
        ],
        scratch_shapes=[
            pltpu.VMEM((table_rows + edge_width, width), F32),
            pltpu.VMEM((width, width), F32),
            pltpu.VMEM((rows, width), F32),
            pltpu.VMEM((width, width), BF16),
            pltpu.VMEM((width, edge_width), BF16),
        ],
        compiler_params=params(56),
        cost_estimate=cost(14),
        name="message_backward",
    )(
        core,
        edge_rows,
        pos,
        act1,
        slope1,
        slope2,
        grad_partial,
        spread,
        table,
        message_weight1,
        message_weight2,
        edge_pack,
        feed_pack,
    )
    came = other_core(send)
    y_size = lax.axis_size("y")
    x_size = lax.axis_size("x")
    z_size = lax.axis_size("z")
    my_y = lax.axis_index("y").astype(jnp.int32).reshape(1)
    peers = y_size * x_size
    smem = pl.BlockSpec(memory_space=pltpu.SMEM)
    payload = pl.pallas_call(
        functools.partial(pair_kernel, parts=parts, cap=cap),
        in_specs=[smem] + [vmem] * 3,
        out_specs=vmem,
        out_shape=shape((peers, half_rows // peers + z_size * cap, width), BF16),
        compiler_params=params(20),
        cost_estimate=cost(3),
        name="pair_sum",
    )(my_y, keep, came, away)
    _, grad_mine, low_mine = lax.optimization_barrier((payload, grad_mine, low_mine))
    grad_other = other_core(grad_mine)
    low_other = other_core(low_mine)
    arrived = lax.all_to_all(payload, PLANE, split_axis=0, concat_axis=0, tiled=True)
    def feed_weights(early, late, sums):
        units = 256
        block_rows = early.shape[0] * rows
        sum_specs = [
            pl.BlockSpec((width, units), lambda _, c: (0, c)),
            pl.BlockSpec((units, width), lambda _, c: (c, 0)),
            pl.BlockSpec((8, units), lambda _, c: (0, c)),
            whole((8, width)),
        ]
        return pl.pallas_call(
            functools.partial(feed_weight_kernel, more=bool(sums)),
            grid=(1, hidden // units),
            in_specs=[
                whole(early.shape),
                whole(late.shape),
                sum_specs[0],
                pl.BlockSpec((1, units), lambda _, c: (0, c)),
                sum_specs[1],
                *(sum_specs if sums else []),
            ],
            out_specs=sum_specs,
            out_shape=[
                shape((width, hidden), F32),
                shape((hidden, width), F32),
                shape((8, hidden), F32),
                shape((8, width), F32),
            ],
            scratch_shapes=[
                pltpu.VMEM((block_rows, width), BF16),
                pltpu.VMEM((block_rows, width), BF16),
                pltpu.VMEM((width, block_rows), BF16),
                pltpu.VMEM((width, block_rows), BF16),
            ],
            compiler_params=params(56),
            cost_estimate=cost(12),
            name="feed_weights_more" if sums else "feed_weights",
        )(early, late, expand_weight, bias_row, contract_weight, *sums)

    def feed_side(early, late, sums):
        group = min(side, 16)
        for at in range(0, side, group):
            sums = tuple(feed_weights(early[at : at + group], late[at : at + group], sums))
        return sums

    sums = feed_side(low_mine, grad_mine, ())
    arrived, *sums = lax.optimization_barrier((arrived, *sums))
    payload = pl.pallas_call(
        functools.partial(plane_kernel, cap=cap),
        in_specs=[smem, vmem],
        out_specs=vmem,
        out_shape=shape((z_size, half_rows // side + x_size * cap, width), BF16),
        compiler_params=params(16),
        cost_estimate=cost(3),
        name="plane_sum",
    )(my_y, arrived)
    arrived = lax.all_to_all(payload, "z", split_axis=0, concat_axis=0, tiled=True)
    copies, returned = pl.pallas_call(
        column_kernel,
        in_specs=[vmem],
        out_specs=[vmem] * 2,
        out_shape=[
            shape((z_size, half_rows // side, width), BF16),
            shape((parts * cap, width), BF16),
        ],
        compiler_params=params(8),
        cost_estimate=cost(1),
        name="column_sum",
    )(arrived)
    column = lax.all_to_all(copies, "z", split_axis=0, concat_axis=0, tiled=True)
    column, grad_other, low_other, *sums = lax.optimization_barrier(
        (column, grad_other, low_other, *sums)
    )
    column = copies_of(column.reshape(half_rows // peers, width), PLANE)
    mine = gather_copies(column, PLANE).reshape(half_rows, width)
    sums = feed_side(low_other, grad_other, tuple(sums))
    mine, *sums = lax.optimization_barrier((mine, *sums))
    grad_expand, grad_contract, expand_bias_sum, contract_bias_sum = sums
    other = other_core(mine)
    node_grad = pl.pallas_call(
        node_grad_kernel,
        in_specs=[vmem] * 6,
        out_specs=vmem,
        out_shape=shape((rows, width), F32),
        compiler_params=params(12),
        cost_estimate=cost(3),
        name="node_gradient",
    )(grad_mixed1, first, own, returned, asked, message_weight1)

    vec = shape((width,), F32)
    thin = shape((edge_width,), F32)
    square = shape((width, width), F32)
    small = shape((edge_width, edge_width), F32)
    (
        grad_message1,
        grad_mb1,
        grad_message2,
        grad_mb2,
        grad_message3,
        grad_mb3,
        grad_n1g,
        grad_n1s,
        grad_eb,
        grad_cb,
        grad_n2g,
        grad_n2s,
        grad_edge1_t,
        grad_eb1,
        grad_edge2,
        grad_eb2,
        grad_edge3,
        grad_eb3,
        grad_n3g,
        grad_n3s,
    ) = pl.pallas_call(
        unpack_kernel,
        in_specs=[smem] + [vmem] * 4,
        out_specs=[vmem] * 20,
        out_shape=[
            shape(message_weight1.shape, F32),
            vec,
            square,
            vec,
            square,
            vec,
            vec,
            vec,
            shape((hidden,), F32),
            vec,
            vec,
            vec,
            shape(edge_w1t.shape, F32),
            thin,
            small,
            thin,
            small,
            thin,
            thin,
            thin,
        ],
        compiler_params=params(24),
        cost_estimate=cost(4),
        name="unpack",
    )(core, mine, other, expand_bias_sum, contract_bias_sum)
    return (
        fresh[None],
        edge_out.transpose(1, 0, 2)[None],
        node_grad[None],
        edge_grad.transpose(1, 0, 2)[None],
        grad_message1,
        grad_mb1,
        grad_message2,
        grad_mb2,
        grad_message3,
        grad_mb3,
        grad_n1g,
        grad_n1s,
        grad_expand,
        grad_eb,
        grad_contract,
        grad_cb,
        grad_n2g,
        grad_n2s,
        grad_edge1_t.T,
        grad_eb1,
        grad_edge2,
        grad_eb2,
        grad_edge3,
        grad_eb3,
        grad_n3g,
        grad_n3s,
    )


def solution(mesh):
    batch, res = mesh.shape["batch"], mesh.shape["res"]
    x_size = 1 << ((res.bit_length() - 1) // 2)
    sizes = (batch // CORES, CORES, res // x_size, x_size)
    fine = jax.sharding.Mesh(mesh.devices.reshape(sizes), ALL)
    row_spec = P(("y", "core"), RES, None)
    edge_spec = P(("y", "core"), RES, None, None)
    return jax.shard_map(
        body,
        mesh=fine,
        in_specs=(row_spec, edge_spec, row_spec, row_spec, row_spec, edge_spec) + (P(),) * 22,
        out_specs=(row_spec, edge_spec, row_spec, edge_spec) + (P(),) * 22,
        check_vma=False,
    )
```

```python
import functools
import math

import jax
import jax.numpy as jnp
from jax import lax
from jax.experimental import pallas as pl
from jax.experimental.pallas import tpu as pltpu
from jax.sharding import PartitionSpec as P

ROW_CAP = 8
CORES = 2
RES = ("z", "x")
PLANE = ("y", "x")
SIDE = ("y", "z", "x")
ALL = ("y", "core", "z", "x")
BY_CORE = ("core", "y", "z", "x")
EPSILON = 1e-05
LANES = 128
MIB = 1024 * 1024
STEPS = 3
F32 = jnp.float32
BF16 = jnp.bfloat16

V_MB1, V_MB2, V_MB3, V_N1G, V_N1S, V_CB, V_N2G, V_N2S, V_EB = range(9)
V_EDGE = 12
V_ROWS = 24


def dot_nn(left, right):
    return lax.dot_general(left, right, (((1,), (0,)), ((), ())), preferred_element_type=F32)


def dot_nt(left, right):
    return lax.dot_general(left, right, (((1,), (1,)), ((), ())), preferred_element_type=F32)


def dot_tn(left, right):
    return lax.dot_general(left, right, (((0,), (0,)), ((), ())), preferred_element_type=F32)


def split_low(values):
    high = values.astype(BF16)
    return high, (values - high.astype(F32)).astype(BF16)


def dot_split(dot, left, right):
    high, rest = split_low(left)
    return dot(high, right) + dot(rest, right)


def dot_split_right(dot, left, right):
    high, rest = split_low(right)
    return dot(left, high) + dot(left, rest)


def gelu_pair(v):
    e = jnp.exp2((v * v) * (-0.5 * math.log2(math.e)))
    phi_sum = 0.5 + 0.5 * lax.erf(v * math.sqrt(0.5))
    return v * phi_sum, phi_sum + (v * (1.0 / math.sqrt(2.0 * math.pi))) * e


def norm_parts(values):
    average = jnp.mean(values, axis=-1, keepdims=True)
    centred = values - average
    variance = jnp.mean(centred * centred, axis=-1, keepdims=True)
    scale = lax.rsqrt(variance + EPSILON)
    return centred * scale, scale


def norm_back(xhat, scale, gain, upstream):
    w = upstream * gain
    mean_w = jnp.mean(w, axis=-1, keepdims=True)
    mean_wx = jnp.mean(w * xhat, axis=-1, keepdims=True)
    return (w - mean_w - xhat * mean_wx) * scale


def edge_onehot(pos_ref, table_rows):
    pairs = pos_ref.shape[2]
    lane = lax.broadcasted_iota(jnp.int32, (LANES, table_rows), 1)
    return jnp.concatenate(
        [(pos_ref[0, :, p : p + 1] == lane).astype(F32).astype(BF16) for p in range(pairs)], axis=0
    )


def prepare_kernel(me_ref, idx_ref, mask_ref, *refs, parts, cap, steps, wide, narrow):
    wide_refs = refs[:wide]
    narrow_refs = refs[wide : wide + narrow]
    pos_ref, select_ref, ids_ref, count_ref, vec_ref, expand_bias_ref = refs[wide + narrow :]
    rows, width = count_ref.shape
    total = rows * parts
    table = rows + parts * cap
    me = me_ref[0]
    pair_rows = idx_ref.shape[0] // 2
    named = [
        jnp.concatenate([idx_ref[2 * j], idx_ref[2 * j + 1]], axis=1) for j in range(pair_rows)
    ]
    residue = lax.broadcasted_iota(jnp.int32, (total, LANES), 0)
    owner = residue // rows
    within = residue - owner * rows
    hits = jnp.zeros((total, LANES), F32)
    for j in range(pair_rows):
        hits = jnp.where(named[j] == residue, 1.0, hits)
    hit = jnp.max(hits, axis=1, keepdims=True)
    own = owner == me
    wanted = jnp.where(own, 0.0, jnp.broadcast_to(hit, (total, LANES)))
    low_row = lax.broadcasted_iota(jnp.int32, (rows, rows), 0)
    low_col = lax.broadcasted_iota(jnp.int32, (rows, rows), 1)
    lower = (low_col <= low_row).astype(F32).astype(BF16)
    wanted_low = wanted.astype(BF16)
    place = jnp.concatenate(
        [dot_nn(lower, wanted_low[o * rows : (o + 1) * rows]) for o in range(parts)], axis=0
    )
    place = jnp.clip(place - 1.0, 0.0, cap - 1.0)
    pos = jnp.where(own, within.astype(F32), (rows + owner * cap).astype(F32) + place)
    picked = [
        jnp.sum(jnp.where(named[j] == residue, pos, 0.0), axis=0, keepdims=True)
        for j in range(pair_rows)
    ]
    picked.append(jnp.zeros((LANES - pair_rows, LANES), F32))
    turned = jnp.concatenate(picked, axis=0).T.astype(jnp.int32)
    per = pair_rows // steps
    for s in range(steps):
        pos_ref[s] = turned[:, s * per : (s + 1) * per]
    lane = lax.broadcasted_iota(jnp.int32, (total, table), 1).astype(F32)
    live = jnp.where(own, 1.0, wanted)
    chosen = jnp.where(lane == pos[:, :1], jnp.broadcast_to(live[:, :1], (total, table)), 0.0)
    select_ref[...] = chosen.astype(BF16)
    asked_row = jnp.broadcast_to(within[:, :1].astype(F32), (total, parts * cap))
    ids = jnp.sum(chosen[:, rows:] * asked_row, axis=0, keepdims=True)
    ids = ids.astype(jnp.int32)
    for o in range(parts):
        ids_ref[o : o + 1, :] = ids[:, o * cap : (o + 1) * cap]
    count = mask_ref[0]
    for k in range(1, mask_ref.shape[0]):
        count = count + mask_ref[k]
    count = jnp.concatenate([count.astype(F32), jnp.zeros((7, rows), F32)], axis=0)
    count_ref[...] = dot_tn(count.astype(BF16), jnp.ones((8, width), F32).astype(BF16))
    expand_bias_ref[...] = wide_refs[-1][...].astype(F32).reshape(expand_bias_ref.shape)
    vec_ref[...] = jnp.zeros_like(vec_ref)
    at = 0
    for ref in wide_refs:
        for c in range(ref.shape[0] // width):
            part = ref[c * width : (c + 1) * width]
            vec_ref[at : at + 1, :] = part.astype(F32).reshape(1, width)
            at += 1
    for ref in narrow_refs:
        vec_ref[at : at + 1, : ref.shape[0]] = ref[...].astype(F32).reshape(1, ref.shape[0])
        at += 1


def node_kernel(
    edge_ref,
    pos_ref,
    select_ref,
    all_ref,
    self_ref,
    count_ref,
    vec_ref,
    w1_ref,
    w2_ref,
    w3_ref,
    expand_hbm,
    contract_hbm,
    act1_ref,
    slope1_ref,
    slope2_ref,
    fresh_ref,
    table_ref,
    mixed1_ref,
    mixed2_ref,
    low_ref,
    slope_e_ref,
    act_sum_ref,
    proj_ref,
    self_pre_ref,
    expand_ref,
    contract_ref,
    sems,
):
    step = pl.program_id(0)
    last = pl.num_programs(0) - 1
    rows, width = self_ref.shape
    slots = edge_ref.shape[0]
    edge_width = edge_ref.shape[2]
    table_rows = table_ref.shape[0]
    expand_copy = pltpu.make_async_copy(expand_hbm, expand_ref, sems.at[0])
    contract_copy = pltpu.make_async_copy(contract_hbm, contract_ref, sems.at[1])

    @pl.when(step == 0)
    def _():
        expand_copy.start()
        contract_copy.start()
        table = dot_tn(select_ref[...], all_ref[...]).astype(BF16)
        table_ref[...] = table
        proj_ref[...] = dot_nn(table, w1_ref[width : 2 * width]).astype(BF16)
        self_pre_ref[...] = (
            dot_nn(self_ref[...], w1_ref[:width]) + vec_ref[V_MB1 : V_MB1 + 1, :]
        )
        act_sum_ref[...] = jnp.zeros_like(act_sum_ref)

    onehot = edge_onehot(pos_ref, table_rows)
    features = edge_ref[...].reshape(slots * rows, edge_width)
    pre1 = dot_nn(features, w1_ref[2 * width :]) + dot_nn(onehot, proj_ref[...])
    self_pre = self_pre_ref[...]
    act1 = []
    for k in range(slots):
        part = pl.ds(k * rows, rows)
        act, slope = gelu_pair(pre1[k * rows : (k + 1) * rows] + self_pre)
        act = act.astype(BF16)
        act1.append(act)
        act1_ref[part, :] = act
        slope1_ref[part, :] = slope.astype(BF16)
    pre2 = dot_nn(jnp.concatenate(act1, axis=0), w2_ref[...])
    bias2 = vec_ref[V_MB2 : V_MB2 + 1, :]
    act_sum = act_sum_ref[...]
    counts = count_ref[...]
    for k in range(slots):
        act, slope = gelu_pair(pre2[k * rows : (k + 1) * rows] + bias2)
        valid = counts > (step * slots + k).astype(F32)
        act_sum = act_sum + jnp.where(valid, act.astype(BF16).astype(F32), 0.0)
        slope2_ref[pl.ds(k * rows, rows), :] = jnp.where(valid, slope, 0.0).astype(BF16)
    act_sum_ref[...] = act_sum

    @pl.when(step == last)
    def _():
        summed = dot_split(dot_nn, act_sum_ref[...], w3_ref[...])
        summed = summed + counts * vec_ref[V_MB3 : V_MB3 + 1, :]
        mixed1 = self_ref[...].astype(F32) + summed / counts
        mixed1_ref[...] = mixed1
        xhat1, _ = norm_parts(mixed1)
        updated = xhat1 * vec_ref[V_N1G : V_N1G + 1, :] + vec_ref[V_N1S : V_N1S + 1, :]
        low = updated.astype(BF16)
        low_ref[...] = low
        expand_copy.wait()
        contract_copy.wait()
        mixed2 = updated + vec_ref[V_CB : V_CB + 1, :]
        for c in range(expand_ref.shape[1] // width):
            cols = slice(c * width, (c + 1) * width)
            pre = dot_nn(low, expand_ref[:, cols]) + vec_ref[V_EB + c : V_EB + c + 1, :]
            act, slope = gelu_pair(pre)
            act = act.astype(BF16)
            slope_e_ref[:, cols] = slope
            mixed2 = mixed2 + dot_nn(act, contract_ref[cols, :])
        mixed2_ref[...] = mixed2
        xhat2, _ = norm_parts(mixed2)
        fresh = (xhat2 * vec_ref[V_N2G : V_N2G + 1, :] + vec_ref[V_N2S : V_N2S + 1, :]).astype(BF16)
        fresh_ref[...] = fresh


def asked_onehot(asked_ref, rows):
    parts = asked_ref.shape[0]
    asked = jnp.concatenate([asked_ref[o : o + 1, :] for o in range(parts)], axis=1)
    row = lax.broadcasted_iota(jnp.int32, (rows, asked.shape[1]), 0)
    return (asked == row).astype(F32).astype(BF16)


def pick_kernel(asked_ref, fresh_ref, out_ref):
    out_ref[...] = dot_tn(asked_onehot(asked_ref, fresh_ref.shape[0]), fresh_ref[...]).astype(BF16)


def edge_kernel(
    edge_ref,
    cot_ref,
    pos_ref,
    fresh_ref,
    incoming_ref,
    count_ref,
    vec_ref,
    w1t_ref,
    w2_ref,
    w3_ref,
    out_ref,
    grad_ref,
    first_ref,
    own_ref,
    away_ref,
    pack_ref,
    vec_out_ref,
    table_ref,
    proj_ref,
    self_pre_ref,
    back_ref,
    dw3_ref,
    dw2_ref,
    dw1_ref,
    sums_ref,
    turned_ref,
):
    step = pl.program_id(0)
    last = pl.num_programs(0) - 1
    rows, width = fresh_ref.shape
    slots, _, edge_width = edge_ref.shape
    block = slots * rows
    table_rows = table_ref.shape[0]
    own_t = w1t_ref[:, :width]
    nbr_t = w1t_ref[:, width : 2 * width]
    feat_t = w1t_ref[:, 2 * width :]

    def vector(i):
        return vec_ref[V_EDGE + i : V_EDGE + i + 1, :edge_width]

    @pl.when(step == 0)
    def _():
        table_ref[:rows] = fresh_ref[...]
        table_ref[rows:] = incoming_ref[...]
        proj_ref[...] = dot_nt(table_ref[...], nbr_t).astype(BF16)
        self_pre_ref[...] = dot_nt(fresh_ref[...], own_t) + vector(0)
        for ref in (back_ref, dw3_ref, dw2_ref, dw1_ref, sums_ref, first_ref):
            ref[...] = jnp.zeros_like(ref)
        turned_ref[0] = feat_t.T
        turned_ref[1] = w2_ref[...].T
        turned_ref[2] = w3_ref[...].T

    def flat(values):
        return values.reshape(block, edge_width)

    def deep(values):
        return values.reshape(slots, rows, edge_width)

    onehot = edge_onehot(pos_ref, table_rows)
    features = flat(edge_ref[...])
    pre1 = dot_nn(features, turned_ref[0]) + dot_nn(onehot, proj_ref[...])
    pre1 = deep(pre1) + self_pre_ref[...][None]
    act1, slope1 = gelu_pair(flat(pre1))
    act1 = act1.astype(BF16)
    pre2 = dot_nn(act1, w2_ref[...]) + vector(1)
    act2, slope2 = gelu_pair(pre2)
    act2 = act2.astype(BF16)
    mixed3 = features.astype(F32) + (dot_nn(act2, w3_ref[...]) + vector(2))
    xhat, scale = norm_parts(mixed3)
    gain = vector(3)
    slot = lax.broadcasted_iota(jnp.int32, (slots, rows, edge_width), 0) + step * slots
    valid = count_ref[...][None, :, :edge_width] > slot.astype(F32)
    out_ref[...] = jnp.where(valid, deep(xhat * gain + vector(4)), 0.0).astype(BF16)
    upstream = flat(jnp.where(valid, cot_ref[...].astype(F32), 0.0))
    sums_ref[3] += jnp.sum(deep(upstream * xhat), axis=0)
    sums_ref[4] += jnp.sum(deep(upstream), axis=0)
    grad_mixed = norm_back(xhat, scale, gain, upstream)
    grad_delta = grad_mixed.astype(BF16)
    dw3_ref[...] += dot_tn(act2, grad_delta)
    sums_ref[2] += jnp.sum(deep(grad_delta.astype(F32)), axis=0)
    grad2 = (dot_nn(grad_delta, turned_ref[2]) * slope2).astype(BF16)
    dw2_ref[...] += dot_tn(act1, grad2)
    sums_ref[1] += jnp.sum(deep(grad2.astype(F32)), axis=0)
    grad1 = (dot_nn(grad2, turned_ref[1]) * slope1).astype(BF16)
    dw1_ref[...] += dot_tn(grad1, features)
    first_ref[...] += jnp.sum(deep(grad1.astype(F32)), axis=0)
    back_ref[...] += dot_tn(onehot, grad1)
    grad_ref[...] = deep(grad_mixed + dot_nn(grad1, feat_t))

    @pl.when(step == last)
    def _():
        first = first_ref[...]
        back = back_ref[...]
        own_ref[...] = back[:rows]
        away_ref[...] = back[rows:].astype(BF16)
        first_high, first_rest = split_low(first)
        back_high, back_rest = split_low(back)
        own_grad = dot_tn(first_high, fresh_ref[...]) + dot_tn(first_rest, fresh_ref[...])
        nbr_grad = dot_tn(back_high, table_ref[...]) + dot_tn(back_rest, table_ref[...])
        pack_ref[:edge_width, :] = own_grad.astype(BF16)
        pack_ref[edge_width : 2 * edge_width, :] = nbr_grad.astype(BF16)
        pad = jnp.zeros((edge_width, width // 2 - edge_width), BF16)
        third = [dw1_ref[...].astype(BF16), pad, dw2_ref[...].astype(BF16), pad]
        pack_ref[2 * edge_width : 3 * edge_width, :] = jnp.concatenate(third, axis=1)
        fourth = [dw3_ref[...].astype(BF16), pad, jnp.zeros((edge_width, width // 2), BF16)]
        pack_ref[3 * edge_width :, :] = jnp.concatenate(fourth, axis=1)
        vec_out_ref[...] = jnp.zeros_like(vec_out_ref)
        vec_out_ref[0:1, :edge_width] = jnp.sum(first, axis=0, keepdims=True)
        for i in range(1, 5):
            vec_out_ref[i : i + 1, :edge_width] = jnp.sum(sums_ref[i], axis=0, keepdims=True)


def feed_kernel(
    cot_ref,
    first_ref,
    own_ref,
    arrived_ref,
    asked_ref,
    count_ref,
    vec_ref,
    w1t_ref,
    mixed1_ref,
    mixed2_ref,
    slope_ref,
    act_sum_ref,
    expand_ref,
    contract_ref,
    w3_ref,
    edge_vec_ref,
    pack_ref,
    copies_ref,
    spread_ref,
    grad_mixed1_ref,
):
    rows, width = cot_ref.shape
    hidden = expand_ref.shape[1]
    own_t = w1t_ref[:, :width]
    nbr_t = w1t_ref[:, width : 2 * width]
    counts = count_ref[...]

    def vector(i):
        return vec_ref[i : i + 1, :]

    def total(values):
        return jnp.sum(values.astype(F32), axis=0, keepdims=True)

    back = own_ref[...] + dot_nn(asked_onehot(asked_ref, rows), arrived_ref[...])
    grad_fresh = (
        cot_ref[...].astype(F32)
        + dot_split(dot_nn, first_ref[...], own_t)
        + dot_split(dot_nn, back, nbr_t)
    )
    xhat2, scale2 = norm_parts(mixed2_ref[...])
    grad_mixed2 = norm_back(xhat2, scale2, vector(V_N2G), grad_fresh)
    grad_contracted = grad_mixed2.astype(BF16)
    for p in range(copies_ref.shape[0]):
        copies_ref[p] = grad_contracted
    grad_updated = grad_mixed2
    for c in range(hidden // width):
        cols = slice(c * width, (c + 1) * width)
        pre = dot_nt(grad_contracted, contract_ref[cols, :]) * slope_ref[:, cols]
        grad_updated = grad_updated + dot_nt(pre.astype(BF16), expand_ref[:, cols])
    xhat1, scale1 = norm_parts(mixed1_ref[...])
    grad_mixed1 = norm_back(xhat1, scale1, vector(V_N1G), grad_updated)
    grad_mixed1_ref[...] = grad_mixed1
    grad_message = (grad_mixed1 / counts).astype(BF16)
    spread_ref[...] = dot_nt(grad_message, w3_ref[...])
    pack_ref[:width, :] = dot_split(dot_tn, act_sum_ref[...], grad_message).astype(BF16)
    vectors = [
        total(counts * grad_message.astype(F32)),
        total(grad_updated * xhat1),
        total(grad_updated),
        total(grad_fresh * xhat2),
        total(grad_fresh),
        edge_vec_ref[...],
    ]
    vectors = jnp.concatenate(vectors, axis=0)
    vectors = jnp.concatenate(
        [vectors, jnp.zeros((pack_ref.shape[0] - width - vectors.shape[0], width), F32)], axis=0
    )
    pack_ref[width:, :] = vectors.astype(BF16)


def feed_weight_kernel(core_ref, low_ref, grad_ref, expand_ref, bias_ref, contract_ref, *refs, more):
    sums_in = refs[:4] if more else None
    expand_out_ref, contract_out_ref, bias_out_ref, last_bias_ref = refs[-6:-2]
    low_turned_ref, grad_turned_ref = refs[-2:]
    del core_ref
    chunk = pl.program_id(0)
    ones = jnp.ones((8, low_ref.shape[0]), F32).astype(BF16)

    @pl.when(chunk == 0)
    def _():
        low_turned_ref[...] = low_ref[...].T
        grad_turned_ref[...] = grad_ref[...].T

    act, slope = gelu_pair(dot_nn(low_ref[...], expand_ref[...]) + bias_ref[0:1, :])
    act = act.astype(BF16)
    pre = (dot_nt(grad_ref[...], contract_ref[...]) * slope).astype(BF16)
    expanded = dot_nn(low_turned_ref[...], pre)
    contracted = dot_nn(grad_turned_ref[...], act).T
    sums = dot_nn(ones, pre)
    if more:
        expanded = expanded + sums_in[0][...]
        contracted = contracted + sums_in[1][...]
        sums = sums + sums_in[2][...]
    expand_out_ref[...] = expanded
    contract_out_ref[...] = contracted
    bias_out_ref[...] = sums

    @pl.when(chunk == 0)
    def _():
        last = dot_nn(ones, grad_ref[...])
        last_bias_ref[...] = last + sums_in[3][...] if more else last


def message_kernel(
    core_ref,
    edge_ref,
    pos_ref,
    act1_ref,
    slope1_ref,
    slope2_ref,
    partial_ref,
    spread_ref,
    table_ref,
    w1_ref,
    w2_ref,
    edge_pack_ref,
    feed_pack_ref,
    grad_ref,
    first_ref,
    own_ref,
    away_ref,
    send_ref,
    keep_ref,
    joint_ref,
    dw2_ref,
    bias2_ref,
    w2_turned_ref,
    w1_turned_ref,
):
    step = pl.program_id(0)
    last = pl.num_programs(0) - 1
    slots, rows, edge_width = edge_ref.shape
    width = act1_ref.shape[1]
    block = slots * rows
    table_rows = table_ref.shape[0]

    @pl.when(step == 0)
    def _():
        for ref in (joint_ref, dw2_ref, bias2_ref, first_ref):
            ref[...] = jnp.zeros_like(ref)
        w2_turned_ref[...] = w2_ref[...].T
        w1_turned_ref[...] = w1_ref[2 * width :].T

    spread = spread_ref[...]
    grad2 = []
    bias2 = bias2_ref[...]
    for k in range(slots):
        part = (spread * slope2_ref[pl.ds(k * rows, rows), :].astype(F32)).astype(BF16)
        bias2 = bias2 + part.astype(F32)
        grad2.append(part)
    bias2_ref[...] = bias2
    grad2 = jnp.concatenate(grad2, axis=0)
    dw2_ref[...] += dot_tn(act1_ref[...], grad2)
    grad1 = (dot_nn(grad2, w2_turned_ref[...]) * slope1_ref[...].astype(F32)).astype(BF16)
    first_ref[...] += jnp.sum(grad1.astype(F32).reshape(slots, rows, width), axis=0)
    onehot = edge_onehot(pos_ref, table_rows)
    features = edge_ref[...].reshape(block, edge_width)
    joint_ref[...] += dot_tn(jnp.concatenate([onehot, features], axis=1), grad1)
    grad_ref[...] = partial_ref[...] + dot_nn(grad1, w1_turned_ref[...]).reshape(
        slots, rows, edge_width
    )

    @pl.when(step == last)
    def _():
        first = first_ref[...]
        back = joint_ref[:table_rows]
        own_ref[...] = back[:rows]
        away_ref[...] = back[rows:].astype(BF16)
        own_grad = dot_split_right(dot_tn, table_ref[:rows], first).astype(BF16)
        nbr_grad = dot_split_right(dot_tn, table_ref[...], back).astype(BF16)
        vectors = [
            feed_pack_ref[width:].astype(F32),
            jnp.sum(first, axis=0, keepdims=True),
            jnp.sum(bias2_ref[...], axis=0, keepdims=True),
        ]
        lower = [own_grad, nbr_grad, feed_pack_ref[:width]]
        upper = [joint_ref[table_rows:].astype(BF16), dw2_ref[...].astype(BF16), edge_pack_ref[...]]

        def fill(ref, pieces, tail):
            base = 0
            for piece in pieces:
                ref[base : base + piece.shape[0]] = piece
                base += piece.shape[0]
            if base < ref.shape[0]:
                gap = ref.shape[0] - base - sum(v.shape[0] for v in tail)
                rest = jnp.concatenate(tail + [jnp.zeros((gap, width), F32)], axis=0)
                ref[base:] = rest.astype(BF16)

        @pl.when(core_ref[0] == 0)
        def _():
            fill(keep_ref, lower, [])
            fill(send_ref, upper, vectors)

        @pl.when(core_ref[0] != 0)
        def _():
            fill(send_ref, lower, [])
            fill(keep_ref, upper, vectors)


def pair_kernel(y_ref, keep_ref, came_ref, away_ref, out_ref, *, parts, cap):
    peers, total, _ = out_ref.shape
    x_size = lax.axis_size("x")
    z_size = parts // x_size
    riders = z_size * cap
    share = total - riders
    for p in range(peers):
        y, x = divmod(p, x_size)
        part = pl.ds(p * share, share)
        out_ref[p, riders:] = (
            keep_ref[part, :].astype(F32) + came_ref[part, :].astype(F32)
        ).astype(BF16)
        rows = [
            away_ref[pl.ds((z * x_size + x) * cap, cap), :].astype(F32) for z in range(z_size)
        ]
        rows = jnp.where(y_ref[0] == y, jnp.concatenate(rows, axis=0), 0.0)
        out_ref[p, :riders] = rows.astype(BF16)


def plane_kernel(y_ref, came_ref, out_ref, *, cap):
    peers = came_ref.shape[0]
    z_size, total, _ = out_ref.shape
    x_size = lax.axis_size("x")
    riders = x_size * cap
    share = total - riders
    first = z_size * cap
    for z in range(z_size):
        part = pl.ds(first + z * share, share)
        value = came_ref[0, part, :].astype(F32)
        for p in range(1, peers):
            value = value + came_ref[p, part, :].astype(F32)
        out_ref[z, riders:] = value.astype(BF16)
    rows = []
    for x in range(x_size):
        value = came_ref[x, :first].astype(F32)
        for y in range(1, peers // x_size):
            value = jnp.where(y_ref[0] == y, came_ref[y * x_size + x, :first].astype(F32), value)
        rows.append(value)
    for z in range(z_size):
        part = [value[z * cap : (z + 1) * cap] for value in rows]
        out_ref[z, :riders] = jnp.concatenate(part, axis=0).astype(BF16)


def column_kernel(came_ref, copies_ref, returned_ref):
    z_size, total, _ = came_ref.shape
    riders = returned_ref.shape[0] // z_size
    value = came_ref[0, riders:].astype(F32)
    for z in range(1, z_size):
        value = value + came_ref[z, riders:].astype(F32)
    for z in range(z_size):
        copies_ref[z] = value.astype(BF16)
        returned_ref[z * riders : (z + 1) * riders, :] = came_ref[z, :riders]


def node_grad_kernel(grad_ref, first_ref, own_ref, arrived_ref, asked_ref, w1_ref, out_ref):
    rows, width = grad_ref.shape
    back = own_ref[...] + dot_nn(asked_onehot(asked_ref, rows), arrived_ref[...])
    out_ref[...] = (
        grad_ref[...]
        + dot_split(dot_nt, first_ref[...], w1_ref[:width])
        + dot_split(dot_nt, back, w1_ref[width : 2 * width])
    )


def unpack_kernel(core_ref, mine_ref, other_ref, bias_ref, last_bias_ref, *refs):
    (
        message1_ref,
        message1_bias_ref,
        message2_ref,
        message2_bias_ref,
        message3_ref,
        message3_bias_ref,
        gain1_ref,
        shift1_ref,
        expand_bias_ref,
        contract_bias_ref,
        gain2_ref,
        shift2_ref,
        edge1_ref,
        edge1_bias_ref,
        edge2_ref,
        edge2_bias_ref,
        edge3_ref,
        edge3_bias_ref,
        gain3_ref,
        shift3_ref,
    ) = refs
    width = mine_ref.shape[1]
    edge_width = edge2_ref.shape[0]
    half = width // 2
    first_core = core_ref[0] == 0

    def lower(start, stop):
        return jnp.where(first_core, mine_ref[start:stop], other_ref[start:stop]).astype(F32)

    def upper(start, stop):
        return jnp.where(first_core, other_ref[start:stop], mine_ref[start:stop]).astype(F32)

    message1_ref[: 2 * width] = lower(0, 2 * width)
    message3_ref[...] = lower(2 * width, 3 * width)
    message1_ref[2 * width :] = upper(0, edge_width)
    base = edge_width
    message2_ref[...] = upper(base, base + width)
    base = base + width
    edge1_ref[:, :width] = upper(base, base + edge_width)
    edge1_ref[:, width : 2 * width] = upper(base + edge_width, base + 2 * edge_width)
    third = upper(base + 2 * edge_width, base + 3 * edge_width)
    edge1_ref[:, 2 * width :] = third[:, :edge_width]
    edge2_ref[...] = third[:, half : half + edge_width]
    edge3_ref[...] = upper(base + 3 * edge_width, base + 4 * edge_width)[:, :edge_width]
    base = base + 4 * edge_width
    vectors = upper(base, mine_ref.shape[0])
    targets = (message3_bias_ref, gain1_ref, shift1_ref, gain2_ref, shift2_ref)
    for i, ref in enumerate(targets):
        ref[...] = vectors[i]
    targets = (edge1_bias_ref, edge2_bias_ref, edge3_bias_ref, gain3_ref, shift3_ref)
    for i, ref in enumerate(targets):
        ref[...] = vectors[5 + i, :edge_width]
    message1_bias_ref[...] = vectors[16]
    message2_bias_ref[...] = vectors[17]
    expand_bias_ref[...] = bias_ref[0]
    contract_bias_ref[...] = last_bias_ref[0]


def gather_copies(copies, axes):
    return lax.all_to_all(copies, axes, split_axis=0, concat_axis=0, tiled=True)


def copies_of(values, axes):
    return jnp.broadcast_to(values[None], (lax.axis_size(axes), *values.shape))


def exchange(values, parts):
    grouped = values.reshape(parts, values.shape[0] // parts, values.shape[1])
    arrived = lax.all_to_all(grouped, RES, split_axis=0, concat_axis=0, tiled=True)
    return arrived.reshape(values.shape)


def other_core(values):
    return lax.ppermute(values, "core", [(0, 1), (1, 0)])


def whole(shape):
    return pl.BlockSpec(shape, lambda *_: (0,) * len(shape))


def params(mebibytes):
    return pltpu.CompilerParams(vmem_limit_bytes=mebibytes * MIB)


def cost(microseconds):
    return pl.CostEstimate(
        flops=int(microseconds * 1.15e9),
        bytes_accessed=int(microseconds * 3.69e6),
        transcendentals=0,
    )


def body(
    node_states,
    edge_states,
    neighbour_index,
    edge_mask,
    node_cotangent,
    edge_cotangent,
    message_weight1,
    message_bias1,
    message_weight2,
    message_bias2,
    message_weight3,
    message_bias3,
    norm1_gain,
    norm1_shift,
    expand_weight,
    expand_bias,
    contract_weight,
    contract_bias,
    norm2_gain,
    norm2_shift,
    edge_weight1,
    edge_bias1,
    edge_weight2,
    edge_bias2,
    edge_weight3,
    edge_bias3,
    norm3_gain,
    norm3_shift,
):
    self_rows = node_states[0]
    rows, width = self_rows.shape
    slots = neighbour_index.shape[2]
    edge_width = edge_states.shape[3]
    hidden = expand_weight.shape[1]
    edges = rows * slots
    parts = lax.axis_size(RES)
    cap = ROW_CAP
    table_rows = rows + parts * cap
    side = lax.axis_size(SIDE)
    steps = STEPS
    block_slots = slots // steps
    block = block_slots * rows
    pairs = block // LANES

    everyone = gather_copies(copies_of(self_rows, RES), RES).reshape(parts * rows, width)
    core = lax.axis_index("core").astype(jnp.int32).reshape(1)
    me = lax.axis_index(RES).astype(jnp.int32).reshape(1)
    edge_rows = edge_states[0].transpose(1, 0, 2)
    edge_cot = edge_cotangent[0].transpose(1, 0, 2)
    slot_index = neighbour_index.transpose(2, 0, 1)
    slot_mask = edge_mask.transpose(2, 0, 1)
    edge_w1t = edge_weight1.T
    wide = (
        message_bias1,
        message_bias2,
        message_bias3,
        norm1_gain,
        norm1_shift,
        contract_bias,
        norm2_gain,
        norm2_shift,
        expand_bias,
    )
    narrow = (edge_bias1, edge_bias2, edge_bias3, norm3_gain, norm3_shift)
    vmem = pl.BlockSpec(memory_space=pltpu.VMEM)

    def shape(dims, kind):
        return jax.ShapeDtypeStruct(dims, kind)

    pos, select, ids, counts, vectors, bias_row = pl.pallas_call(
        functools.partial(
            prepare_kernel, parts=parts, cap=cap, steps=steps, wide=len(wide), narrow=len(narrow)
        ),
        out_shape=(
            shape((steps, LANES, pairs), jnp.int32),
            shape((parts * rows, table_rows), BF16),
            shape((parts, cap), jnp.int32),
            shape((rows, width), F32),
            shape((V_ROWS, width), F32),
            shape((1, hidden), F32),
        ),
        in_specs=[pl.BlockSpec(memory_space=pltpu.SMEM)] + [vmem] * (2 + len(wide) + len(narrow)),
        out_specs=(vmem,) * 6,
        compiler_params=params(56),
        cost_estimate=cost(6),
        name="prepare",
    )(me, slot_index, slot_mask, *wide, *narrow)
    ids, everyone = lax.optimization_barrier((ids, everyone))
    asked = lax.all_to_all(ids, RES, split_axis=0, concat_axis=0, tiled=True)

    edge_spec = pl.BlockSpec((block_slots, rows, edge_width), lambda i: (i, 0, 0))
    flat_spec = pl.BlockSpec((block, width), lambda i: (i, 0))
    pos_spec = pl.BlockSpec((1, LANES, pairs), lambda i: (i, 0, 0))
    any_spec = pl.BlockSpec(memory_space=pl.ANY)
    node_spec = whole((rows, width))
    away_spec = whole((parts * cap, width))

    (
        act1,
        slope1,
        slope2,
        fresh,
        table,
        mixed1,
        mixed2,
        low,
        slope_e,
        act_sum,
    ) = pl.pallas_call(
        node_kernel,
        grid=(steps,),
        in_specs=[
            edge_spec,
            pos_spec,
            whole((parts * rows, table_rows)),
            whole((parts * rows, width)),
            node_spec,
            node_spec,
            whole((V_ROWS, width)),
            whole(message_weight1.shape),
            whole((width, width)),
            whole((width, width)),
            any_spec,
            any_spec,
        ],
        out_specs=[
            flat_spec,
            flat_spec,
            flat_spec,
            node_spec,
            whole((table_rows, width)),
            node_spec,
            node_spec,
            node_spec,
            whole((rows, hidden)),
            node_spec,
        ],
        out_shape=[
            shape((edges, width), BF16),
            shape((edges, width), BF16),
            shape((edges, width), BF16),
            shape((rows, width), BF16),
            shape((table_rows, width), BF16),
            shape((rows, width), F32),
            shape((rows, width), F32),
            shape((rows, width), BF16),
            shape((rows, hidden), F32),
            shape((rows, width), F32),
        ],
        scratch_shapes=[
            pltpu.VMEM((table_rows, width), BF16),
            pltpu.VMEM((rows, width), F32),
            pltpu.VMEM((width, hidden), BF16),
            pltpu.VMEM((hidden, width), BF16),
            pltpu.SemaphoreType.DMA((2,)),
        ],
        compiler_params=params(56),
        cost_estimate=cost(18),
        name="node_forward",
    )(
        edge_rows,
        pos,
        select,
        everyone,
        self_rows,
        counts,
        vectors,
        message_weight1,
        message_weight2,
        message_weight3,
        expand_weight,
        contract_weight,
    )
    outgoing = pl.pallas_call(
        pick_kernel,
        in_specs=[vmem] * 2,
        out_specs=vmem,
        out_shape=shape((parts * cap, width), BF16),
        compiler_params=params(56),
        cost_estimate=cost(1),
        name="pick",
    )(asked, fresh)
    incoming = exchange(outgoing, parts)
    low_all = lax.all_gather(low, BY_CORE, axis=0, tiled=True)

    edge_pack_rows = 4 * edge_width
    edge_out, grad_partial, edge_first, edge_own, edge_away, edge_pack, edge_vec = pl.pallas_call(
        edge_kernel,
        grid=(steps,),
        in_specs=[
            edge_spec,
            edge_spec,
            pos_spec,
            node_spec,
            away_spec,
            node_spec,
            whole((V_ROWS, width)),
            whole(edge_w1t.shape),
            whole((edge_width, edge_width)),
            whole((edge_width, edge_width)),
        ],
        out_specs=[
            edge_spec,
            edge_spec,
            whole((rows, edge_width)),
            whole((rows, edge_width)),
            whole((parts * cap, edge_width)),
            whole((edge_pack_rows, width)),
            whole((8, width)),
        ],
        out_shape=[
            shape((slots, rows, edge_width), BF16),
            shape((slots, rows, edge_width), F32),
            shape((rows, edge_width), F32),
            shape((rows, edge_width), F32),
            shape((parts * cap, edge_width), BF16),
            shape((edge_pack_rows, width), BF16),
            shape((8, width), F32),
        ],
        scratch_shapes=[
            pltpu.VMEM((table_rows, width), BF16),
            pltpu.VMEM((table_rows, edge_width), BF16),
            pltpu.VMEM((rows, edge_width), F32),
            pltpu.VMEM((table_rows, edge_width), F32),
            pltpu.VMEM((edge_width, edge_width), F32),
            pltpu.VMEM((edge_width, edge_width), F32),
            pltpu.VMEM((edge_width, edge_width), F32),
            pltpu.VMEM((5, rows, edge_width), F32),
            pltpu.VMEM((3, edge_width, edge_width), BF16),
        ],
        compiler_params=params(30),
        cost_estimate=cost(17),
        name="edge_both",
    )(
        edge_rows,
        edge_cot,
        pos,
        fresh,
        incoming,
        counts,
        vectors,
        edge_w1t,
        edge_weight2,
        edge_weight3,
    )
    edge_arrived = exchange(edge_away, parts)

    feed_rows = width + 16
    feed_pack, grad_copies, spread, grad_mixed1 = pl.pallas_call(
        feed_kernel,
        in_specs=[vmem] * 16,
        out_specs=[vmem] * 4,
        out_shape=[
            shape((feed_rows, width), BF16),
            shape((side, rows, width), BF16),
            shape((rows, width), F32),
            shape((rows, width), F32),
        ],
        compiler_params=params(20),
        cost_estimate=cost(5),
        name="feed_backward",
    )(
        node_cotangent[0],
        edge_first,
        edge_own,
        edge_arrived,
        asked,
        counts,
        vectors,
        edge_w1t,
        mixed1,
        mixed2,
        slope_e,
        act_sum,
        expand_weight,
        contract_weight,
        message_weight3,
        edge_vec,
    )
    grad_mine = gather_copies(grad_copies, SIDE).reshape(side * rows, width)

    unit = 16 * side
    half_rows = (3 * width + unit - 1) // unit * unit
    edge_grad, first, own, away, send, keep = pl.pallas_call(
        message_kernel,
        grid=(steps,),
        in_specs=[
            pl.BlockSpec(memory_space=pltpu.SMEM),
            edge_spec,
            pos_spec,
            flat_spec,
            flat_spec,
            flat_spec,
            edge_spec,
            node_spec,
            whole((table_rows, width)),
            whole(message_weight1.shape),
            whole((width, width)),
            whole((edge_pack_rows, width)),
            whole((feed_rows, width)),
        ],
        out_specs=[
            edge_spec,
            node_spec,
            node_spec,
            away_spec,
            whole((half_rows, width)),
            whole((half_rows, width)),
        ],
        out_shape=[
            shape((slots, rows, edge_width), F32),
            shape((rows, width), F32),
            shape((rows, width), F32),
            shape((parts * cap, width), BF16),
            shape((half_rows, width), BF16),
            shape((half_rows, width), BF16),
        ],
        scratch_shapes=[
            pltpu.VMEM((table_rows + edge_width, width), F32),
            pltpu.VMEM((width, width), F32),
            pltpu.VMEM((rows, width), F32),
            pltpu.VMEM((width, width), BF16),
            pltpu.VMEM((width, edge_width), BF16),
        ],
        compiler_params=params(40),
        cost_estimate=cost(14),
        name="message_backward",
    )(
        core,
        edge_rows,
        pos,
        act1,
        slope1,
        slope2,
        grad_partial,
        spread,
        table,
        message_weight1,
        message_weight2,
        edge_pack,
        feed_pack,
    )
    came = other_core(send)
    came, low_all = lax.optimization_barrier((came, low_all))
    y_size = lax.axis_size("y")
    x_size = lax.axis_size("x")
    z_size = lax.axis_size("z")
    my_y = lax.axis_index("y").astype(jnp.int32).reshape(1)
    peers = y_size * x_size
    smem = pl.BlockSpec(memory_space=pltpu.SMEM)
    payload = pl.pallas_call(
        functools.partial(pair_kernel, parts=parts, cap=cap),
        in_specs=[smem] + [vmem] * 3,
        out_specs=vmem,
        out_shape=shape((peers, half_rows // peers + z_size * cap, width), BF16),
        compiler_params=params(20),
        cost_estimate=cost(3),
        name="pair_sum",
    )(my_y, keep, came, away)
    _, grad_mine = lax.optimization_barrier((payload, grad_mine))
    grad_other = other_core(grad_mine)
    arrived = lax.all_to_all(payload, PLANE, split_axis=0, concat_axis=0, tiled=True)
    def feed_weights(grad_values, near, at, block_rows, sums):
        units = 256
        blocks = side * rows // block_rows

        def low_block(c, core):
            return ((core[0] if near else 1 - core[0]) * blocks + at, 0)

        sum_specs = [
            pl.BlockSpec((width, units), lambda c, core: (0, c)),
            pl.BlockSpec((units, width), lambda c, core: (c, 0)),
            pl.BlockSpec((8, units), lambda c, core: (0, c)),
            whole((8, width)),
        ]
        return pl.pallas_call(
            functools.partial(feed_weight_kernel, more=bool(sums)),
            grid_spec=pltpu.PrefetchScalarGridSpec(
                num_scalar_prefetch=1,
                grid=(hidden // units,),
                in_specs=[
                    pl.BlockSpec((block_rows, width), low_block),
                    pl.BlockSpec((block_rows, width), lambda c, core: (at, 0)),
                    sum_specs[0],
                    pl.BlockSpec((1, units), lambda c, core: (0, c)),
                    sum_specs[1],
                    *(sum_specs if sums else []),
                ],
                out_specs=sum_specs,
                scratch_shapes=[
                    pltpu.VMEM((width, block_rows), BF16),
                    pltpu.VMEM((width, block_rows), BF16),
                ],
            ),
            out_shape=[
                shape((width, hidden), F32),
                shape((hidden, width), F32),
                shape((8, hidden), F32),
                shape((8, width), F32),
            ],
            compiler_params=params(56),
            cost_estimate=cost(17),
            name="feed_weights_near" if near else "feed_weights_far",
        )(core, low_all, grad_values, expand_weight, bias_row, contract_weight, *sums)

    def feed_side(grad_values, near, sums):
        block_rows = min(side * rows, 1024)
        for at in range(side * rows // block_rows):
            sums = tuple(feed_weights(grad_values, near, at, block_rows, sums))
        return sums

    sums = feed_side(grad_mine, True, ())
    arrived, *sums = lax.optimization_barrier((arrived, *sums))
    payload = pl.pallas_call(
        functools.partial(plane_kernel, cap=cap),
        in_specs=[smem, vmem],
        out_specs=vmem,
        out_shape=shape((z_size, half_rows // side + x_size * cap, width), BF16),
        compiler_params=params(16),
        cost_estimate=cost(3),
        name="plane_sum",
    )(my_y, arrived)
    arrived = lax.all_to_all(payload, "z", split_axis=0, concat_axis=0, tiled=True)
    copies, returned = pl.pallas_call(
        column_kernel,
        in_specs=[vmem],
        out_specs=[vmem] * 2,
        out_shape=[
            shape((z_size, half_rows // side, width), BF16),
            shape((parts * cap, width), BF16),
        ],
        compiler_params=params(8),
        cost_estimate=cost(1),
        name="column_sum",
    )(arrived)
    column = lax.all_to_all(copies, "z", split_axis=0, concat_axis=0, tiled=True)
    column, grad_other, *sums = lax.optimization_barrier((column, grad_other, *sums))
    column = copies_of(column.reshape(half_rows // peers, width), PLANE)
    mine = gather_copies(column, PLANE).reshape(half_rows, width)
    sums = feed_side(grad_other, False, tuple(sums))
    mine, *sums = lax.optimization_barrier((mine, *sums))
    grad_expand, grad_contract, expand_bias_sum, contract_bias_sum = sums
    other = other_core(mine)
    node_grad = pl.pallas_call(
        node_grad_kernel,
        in_specs=[vmem] * 6,
        out_specs=vmem,
        out_shape=shape((rows, width), F32),
        compiler_params=params(12),
        cost_estimate=cost(3),
        name="node_gradient",
    )(grad_mixed1, first, own, returned, asked, message_weight1)

    vec = shape((width,), F32)
    thin = shape((edge_width,), F32)
    square = shape((width, width), F32)
    small = shape((edge_width, edge_width), F32)
    (
        grad_message1,
        grad_mb1,
        grad_message2,
        grad_mb2,
        grad_message3,
        grad_mb3,
        grad_n1g,
        grad_n1s,
        grad_eb,
        grad_cb,
        grad_n2g,
        grad_n2s,
        grad_edge1_t,
        grad_eb1,
        grad_edge2,
        grad_eb2,
        grad_edge3,
        grad_eb3,
        grad_n3g,
        grad_n3s,
    ) = pl.pallas_call(
        unpack_kernel,
        in_specs=[smem] + [vmem] * 4,
        out_specs=[vmem] * 20,
        out_shape=[
            shape(message_weight1.shape, F32),
            vec,
            square,
            vec,
            square,
            vec,
            vec,
            vec,
            shape((hidden,), F32),
            vec,
            vec,
            vec,
            shape(edge_w1t.shape, F32),
            thin,
            small,
            thin,
            small,
            thin,
            thin,
            thin,
        ],
        compiler_params=params(24),
        cost_estimate=cost(4),
        name="unpack",
    )(core, mine, other, expand_bias_sum, contract_bias_sum)
    return (
        fresh[None],
        edge_out.transpose(1, 0, 2)[None],
        node_grad[None],
        edge_grad.transpose(1, 0, 2)[None],
        grad_message1,
        grad_mb1,
        grad_message2,
        grad_mb2,
        grad_message3,
        grad_mb3,
        grad_n1g,
        grad_n1s,
        grad_expand,
        grad_eb,
        grad_contract,
        grad_cb,
        grad_n2g,
        grad_n2s,
        grad_edge1_t.T,
        grad_eb1,
        grad_edge2,
        grad_eb2,
        grad_edge3,
        grad_eb3,
        grad_n3g,
        grad_n3s,
    )


def solution(mesh):
    batch, res = mesh.shape["batch"], mesh.shape["res"]
    x_size = 1 << ((res.bit_length() - 1) // 2)
    sizes = (batch // CORES, CORES, res // x_size, x_size)
    fine = jax.sharding.Mesh(mesh.devices.reshape(sizes), ALL)
    row_spec = P(("y", "core"), RES, None)
    edge_spec = P(("y", "core"), RES, None, None)
    return jax.shard_map(
        body,
        mesh=fine,
        in_specs=(row_spec, edge_spec, row_spec, row_spec, row_spec, edge_spec) + (P(),) * 22,
        out_specs=(row_spec, edge_spec, row_spec, edge_spec) + (P(),) * 22,
        check_vma=False,
    )
```

```python
import functools
import math

import jax
import jax.numpy as jnp
from jax import lax
from jax.experimental import pallas as pl
from jax.experimental.pallas import tpu as pltpu
from jax.sharding import PartitionSpec as P

ROW_CAP = 8
CORES = 2
RES = ("z", "x")
PLANE = ("y", "x")
SIDE = ("y", "z", "x")
ALL = ("y", "core", "z", "x")
EPSILON = 1e-05
LANES = 128
MIB = 1024 * 1024
STEPS = 3
F32 = jnp.float32
BF16 = jnp.bfloat16

V_MB1, V_MB2, V_MB3, V_N1G, V_N1S, V_CB, V_N2G, V_N2S, V_EB = range(9)
V_EDGE = 12
V_ROWS = 24


def dot_nn(left, right):
    return lax.dot_general(left, right, (((1,), (0,)), ((), ())), preferred_element_type=F32)


def dot_nt(left, right):
    return lax.dot_general(left, right, (((1,), (1,)), ((), ())), preferred_element_type=F32)


def dot_tn(left, right):
    return lax.dot_general(left, right, (((0,), (0,)), ((), ())), preferred_element_type=F32)


def split_low(values):
    high = values.astype(BF16)
    return high, (values - high.astype(F32)).astype(BF16)


def dot_split(dot, left, right):
    high, rest = split_low(left)
    return dot(high, right) + dot(rest, right)


def dot_split_right(dot, left, right):
    high, rest = split_low(right)
    return dot(left, high) + dot(left, rest)


def gelu_pair(v):
    e = jnp.exp2((v * v) * (-0.5 * math.log2(math.e)))
    phi_sum = 0.5 + 0.5 * lax.erf(v * math.sqrt(0.5))
    return v * phi_sum, phi_sum + (v * (1.0 / math.sqrt(2.0 * math.pi))) * e


def norm_parts(values):
    average = jnp.mean(values, axis=-1, keepdims=True)
    centred = values - average
    variance = jnp.mean(centred * centred, axis=-1, keepdims=True)
    scale = lax.rsqrt(variance + EPSILON)
    return centred * scale, scale


def norm_back(xhat, scale, gain, upstream):
    w = upstream * gain
    mean_w = jnp.mean(w, axis=-1, keepdims=True)
    mean_wx = jnp.mean(w * xhat, axis=-1, keepdims=True)
    return (w - mean_w - xhat * mean_wx) * scale


def edge_onehot(pos_ref, table_rows):
    pairs = pos_ref.shape[2]
    lane = lax.broadcasted_iota(jnp.int32, (LANES, table_rows), 1)
    return jnp.concatenate(
        [(pos_ref[0, :, p : p + 1] == lane).astype(F32).astype(BF16) for p in range(pairs)], axis=0
    )


def prepare_kernel(me_ref, idx_ref, mask_ref, *refs, parts, cap, steps, wide, narrow):
    wide_refs = refs[:wide]
    narrow_refs = refs[wide : wide + narrow]
    pos_ref, select_ref, ids_ref, count_ref, vec_ref, expand_bias_ref = refs[wide + narrow :]
    rows, width = count_ref.shape
    total = rows * parts
    table = rows + parts * cap
    me = me_ref[0]
    pair_rows = idx_ref.shape[0] // 2
    named = [
        jnp.concatenate([idx_ref[2 * j], idx_ref[2 * j + 1]], axis=1) for j in range(pair_rows)
    ]
    residue = lax.broadcasted_iota(jnp.int32, (total, LANES), 0)
    owner = residue // rows
    within = residue - owner * rows
    hits = jnp.zeros((total, LANES), F32)
    for j in range(pair_rows):
        hits = jnp.where(named[j] == residue, 1.0, hits)
    hit = jnp.max(hits, axis=1, keepdims=True)
    own = owner == me
    wanted = jnp.where(own, 0.0, jnp.broadcast_to(hit, (total, LANES)))
    low_row = lax.broadcasted_iota(jnp.int32, (rows, rows), 0)
    low_col = lax.broadcasted_iota(jnp.int32, (rows, rows), 1)
    lower = (low_col <= low_row).astype(F32).astype(BF16)
    wanted_low = wanted.astype(BF16)
    place = jnp.concatenate(
        [dot_nn(lower, wanted_low[o * rows : (o + 1) * rows]) for o in range(parts)], axis=0
    )
    place = jnp.clip(place - 1.0, 0.0, cap - 1.0)
    pos = jnp.where(own, within.astype(F32), (rows + owner * cap).astype(F32) + place)
    picked = [
        jnp.sum(jnp.where(named[j] == residue, pos, 0.0), axis=0, keepdims=True)
        for j in range(pair_rows)
    ]
    picked.append(jnp.zeros((LANES - pair_rows, LANES), F32))
    turned = jnp.concatenate(picked, axis=0).T.astype(jnp.int32)
    per = pair_rows // steps
    for s in range(steps):
        pos_ref[s] = turned[:, s * per : (s + 1) * per]
    lane = lax.broadcasted_iota(jnp.int32, (total, table), 1).astype(F32)
    live = jnp.where(own, 1.0, wanted)
    chosen = jnp.where(lane == pos[:, :1], jnp.broadcast_to(live[:, :1], (total, table)), 0.0)
    select_ref[...] = chosen.astype(BF16)
    asked_row = jnp.broadcast_to(within[:, :1].astype(F32), (total, parts * cap))
    ids = jnp.sum(chosen[:, rows:] * asked_row, axis=0, keepdims=True)
    ids = ids.astype(jnp.int32)
    for o in range(parts):
        ids_ref[o : o + 1, :] = ids[:, o * cap : (o + 1) * cap]
    count = mask_ref[0]
    for k in range(1, mask_ref.shape[0]):
        count = count + mask_ref[k]
    count = jnp.concatenate([count.astype(F32), jnp.zeros((7, rows), F32)], axis=0)
    count_ref[...] = dot_tn(count.astype(BF16), jnp.ones((8, width), F32).astype(BF16))
    expand_bias_ref[...] = wide_refs[-1][...].astype(F32).reshape(expand_bias_ref.shape)
    vec_ref[...] = jnp.zeros_like(vec_ref)
    at = 0
    for ref in wide_refs:
        for c in range(ref.shape[0] // width):
            part = ref[c * width : (c + 1) * width]
            vec_ref[at : at + 1, :] = part.astype(F32).reshape(1, width)
            at += 1
    for ref in narrow_refs:
        vec_ref[at : at + 1, : ref.shape[0]] = ref[...].astype(F32).reshape(1, ref.shape[0])
        at += 1


def node_kernel(
    edge_ref,
    pos_ref,
    select_ref,
    all_ref,
    self_ref,
    count_ref,
    vec_ref,
    w1_ref,
    w2_ref,
    w3_ref,
    expand_hbm,
    contract_hbm,
    act1_ref,
    slope1_ref,
    slope2_ref,
    fresh_ref,
    table_ref,
    mixed1_ref,
    mixed2_ref,
    low_ref,
    slope_e_ref,
    act_sum_ref,
    proj_ref,
    self_pre_ref,
    expand_ref,
    contract_ref,
    sems,
):
    step = pl.program_id(0)
    last = pl.num_programs(0) - 1
    rows, width = self_ref.shape
    slots = edge_ref.shape[0]
    edge_width = edge_ref.shape[2]
    table_rows = table_ref.shape[0]
    expand_copy = pltpu.make_async_copy(expand_hbm, expand_ref, sems.at[0])
    contract_copy = pltpu.make_async_copy(contract_hbm, contract_ref, sems.at[1])

    @pl.when(step == 0)
    def _():
        expand_copy.start()
        contract_copy.start()
        table = dot_tn(select_ref[...], all_ref[...]).astype(BF16)
        table_ref[...] = table
        proj_ref[...] = dot_nn(table, w1_ref[width : 2 * width]).astype(BF16)
        self_pre_ref[...] = (
            dot_nn(self_ref[...], w1_ref[:width]) + vec_ref[V_MB1 : V_MB1 + 1, :]
        )
        act_sum_ref[...] = jnp.zeros_like(act_sum_ref)

    onehot = edge_onehot(pos_ref, table_rows)
    features = edge_ref[...].reshape(slots * rows, edge_width)
    pre1 = dot_nn(features, w1_ref[2 * width :]) + dot_nn(onehot, proj_ref[...])
    self_pre = self_pre_ref[...]
    act1 = []
    for k in range(slots):
        part = pl.ds(k * rows, rows)
        act, slope = gelu_pair(pre1[k * rows : (k + 1) * rows] + self_pre)
        act = act.astype(BF16)
        act1.append(act)
        act1_ref[part, :] = act
        slope1_ref[part, :] = slope.astype(BF16)
    pre2 = dot_nn(jnp.concatenate(act1, axis=0), w2_ref[...])
    bias2 = vec_ref[V_MB2 : V_MB2 + 1, :]
    act_sum = act_sum_ref[...]
    counts = count_ref[...]
    for k in range(slots):
        act, slope = gelu_pair(pre2[k * rows : (k + 1) * rows] + bias2)
        valid = counts > (step * slots + k).astype(F32)
        act_sum = act_sum + jnp.where(valid, act.astype(BF16).astype(F32), 0.0)
        slope2_ref[pl.ds(k * rows, rows), :] = jnp.where(valid, slope, 0.0).astype(BF16)
    act_sum_ref[...] = act_sum

    @pl.when(step == last)
    def _():
        summed = dot_split(dot_nn, act_sum_ref[...], w3_ref[...])
        summed = summed + counts * vec_ref[V_MB3 : V_MB3 + 1, :]
        mixed1 = self_ref[...].astype(F32) + summed / counts
        mixed1_ref[...] = mixed1
        xhat1, _ = norm_parts(mixed1)
        updated = xhat1 * vec_ref[V_N1G : V_N1G + 1, :] + vec_ref[V_N1S : V_N1S + 1, :]
        low = updated.astype(BF16)
        low_ref[...] = low
        expand_copy.wait()
        contract_copy.wait()
        mixed2 = updated + vec_ref[V_CB : V_CB + 1, :]
        for c in range(expand_ref.shape[1] // width):
            cols = slice(c * width, (c + 1) * width)
            pre = dot_nn(low, expand_ref[:, cols]) + vec_ref[V_EB + c : V_EB + c + 1, :]
            act, slope = gelu_pair(pre)
            act = act.astype(BF16)
            slope_e_ref[:, cols] = slope
            mixed2 = mixed2 + dot_nn(act, contract_ref[cols, :])
        mixed2_ref[...] = mixed2
        xhat2, _ = norm_parts(mixed2)
        fresh = (xhat2 * vec_ref[V_N2G : V_N2G + 1, :] + vec_ref[V_N2S : V_N2S + 1, :]).astype(BF16)
        fresh_ref[...] = fresh


def asked_onehot(asked_ref, rows):
    parts = asked_ref.shape[0]
    asked = jnp.concatenate([asked_ref[o : o + 1, :] for o in range(parts)], axis=1)
    row = lax.broadcasted_iota(jnp.int32, (rows, asked.shape[1]), 0)
    return (asked == row).astype(F32).astype(BF16)


def pick_kernel(asked_ref, fresh_ref, out_ref):
    out_ref[...] = dot_tn(asked_onehot(asked_ref, fresh_ref.shape[0]), fresh_ref[...]).astype(BF16)


def edge_kernel(
    edge_ref,
    cot_ref,
    pos_ref,
    fresh_ref,
    incoming_ref,
    count_ref,
    vec_ref,
    w1t_ref,
    w2_ref,
    w3_ref,
    out_ref,
    grad_ref,
    first_ref,
    own_ref,
    away_ref,
    pack_ref,
    vec_out_ref,
    table_ref,
    proj_ref,
    self_pre_ref,
    back_ref,
    dw3_ref,
    dw2_ref,
    dw1_ref,
    sums_ref,
    turned_ref,
):
    step = pl.program_id(0)
    last = pl.num_programs(0) - 1
    rows, width = fresh_ref.shape
    slots, _, edge_width = edge_ref.shape
    block = slots * rows
    table_rows = table_ref.shape[0]
    own_t = w1t_ref[:, :width]
    nbr_t = w1t_ref[:, width : 2 * width]
    feat_t = w1t_ref[:, 2 * width :]

    def vector(i):
        return vec_ref[V_EDGE + i : V_EDGE + i + 1, :edge_width]

    @pl.when(step == 0)
    def _():
        table_ref[:rows] = fresh_ref[...]
        table_ref[rows:] = incoming_ref[...]
        proj_ref[...] = dot_nt(table_ref[...], nbr_t).astype(BF16)
        self_pre_ref[...] = dot_nt(fresh_ref[...], own_t) + vector(0)
        for ref in (back_ref, dw3_ref, dw2_ref, dw1_ref, sums_ref, first_ref):
            ref[...] = jnp.zeros_like(ref)
        turned_ref[0] = feat_t.T
        turned_ref[1] = w2_ref[...].T
        turned_ref[2] = w3_ref[...].T

    def flat(values):
        return values.reshape(block, edge_width)

    def deep(values):
        return values.reshape(slots, rows, edge_width)

    onehot = edge_onehot(pos_ref, table_rows)
    features = flat(edge_ref[...])
    pre1 = dot_nn(features, turned_ref[0]) + dot_nn(onehot, proj_ref[...])
    pre1 = deep(pre1) + self_pre_ref[...][None]
    act1, slope1 = gelu_pair(flat(pre1))
    act1 = act1.astype(BF16)
    pre2 = dot_nn(act1, w2_ref[...]) + vector(1)
    act2, slope2 = gelu_pair(pre2)
    act2 = act2.astype(BF16)
    mixed3 = features.astype(F32) + (dot_nn(act2, w3_ref[...]) + vector(2))
    xhat, scale = norm_parts(mixed3)
    gain = vector(3)
    slot = lax.broadcasted_iota(jnp.int32, (slots, rows, edge_width), 0) + step * slots
    valid = count_ref[...][None, :, :edge_width] > slot.astype(F32)
    out_ref[...] = jnp.where(valid, deep(xhat * gain + vector(4)), 0.0).astype(BF16)
    upstream = flat(jnp.where(valid, cot_ref[...].astype(F32), 0.0))
    sums_ref[3] += jnp.sum(deep(upstream * xhat), axis=0)
    sums_ref[4] += jnp.sum(deep(upstream), axis=0)
    grad_mixed = norm_back(xhat, scale, gain, upstream)
    grad_delta = grad_mixed.astype(BF16)
    dw3_ref[...] += dot_tn(act2, grad_delta)
    sums_ref[2] += jnp.sum(deep(grad_delta.astype(F32)), axis=0)
    grad2 = (dot_nn(grad_delta, turned_ref[2]) * slope2).astype(BF16)
    dw2_ref[...] += dot_tn(act1, grad2)
    sums_ref[1] += jnp.sum(deep(grad2.astype(F32)), axis=0)
    grad1 = (dot_nn(grad2, turned_ref[1]) * slope1).astype(BF16)
    dw1_ref[...] += dot_tn(grad1, features)
    first_ref[...] += jnp.sum(deep(grad1.astype(F32)), axis=0)
    back_ref[...] += dot_tn(onehot, grad1)
    grad_ref[...] = deep(grad_mixed + dot_nn(grad1, feat_t))

    @pl.when(step == last)
    def _():
        first = first_ref[...]
        back = back_ref[...]
        own_ref[...] = back[:rows]
        away_ref[...] = back[rows:].astype(BF16)
        first_high, first_rest = split_low(first)
        back_high, back_rest = split_low(back)
        own_grad = dot_tn(first_high, fresh_ref[...]) + dot_tn(first_rest, fresh_ref[...])
        nbr_grad = dot_tn(back_high, table_ref[...]) + dot_tn(back_rest, table_ref[...])
        pack_ref[:edge_width, :] = own_grad.astype(BF16)
        pack_ref[edge_width : 2 * edge_width, :] = nbr_grad.astype(BF16)
        pad = jnp.zeros((edge_width, width // 2 - edge_width), BF16)
        third = [dw1_ref[...].astype(BF16), pad, dw2_ref[...].astype(BF16), pad]
        pack_ref[2 * edge_width : 3 * edge_width, :] = jnp.concatenate(third, axis=1)
        fourth = [dw3_ref[...].astype(BF16), pad, jnp.zeros((edge_width, width // 2), BF16)]
        pack_ref[3 * edge_width :, :] = jnp.concatenate(fourth, axis=1)
        vec_out_ref[...] = jnp.zeros_like(vec_out_ref)
        vec_out_ref[0:1, :edge_width] = jnp.sum(first, axis=0, keepdims=True)
        for i in range(1, 5):
            vec_out_ref[i : i + 1, :edge_width] = jnp.sum(sums_ref[i], axis=0, keepdims=True)


def feed_kernel(
    cot_ref,
    first_ref,
    own_ref,
    arrived_ref,
    asked_ref,
    count_ref,
    vec_ref,
    w1t_ref,
    mixed1_ref,
    mixed2_ref,
    slope_ref,
    act_sum_ref,
    expand_hbm,
    contract_hbm,
    w3_ref,
    edge_vec_ref,
    pack_ref,
    copies_ref,
    spread_ref,
    grad_mixed1_ref,
    expand_ref,
    contract_ref,
    sems,
):
    rows, width = cot_ref.shape
    hidden = expand_ref.shape[1]
    own_t = w1t_ref[:, :width]
    nbr_t = w1t_ref[:, width : 2 * width]
    counts = count_ref[...]
    copies = []
    for c in range(hidden // width):
        rows_part, cols_part = pl.ds(c * width, width), pl.ds(c * width, width)
        copies.append(
            (
                pltpu.make_async_copy(
                    contract_hbm.at[rows_part, :], contract_ref.at[rows_part, :], sems.at[2 * c]
                ),
                pltpu.make_async_copy(
                    expand_hbm.at[:, cols_part], expand_ref.at[:, cols_part], sems.at[2 * c + 1]
                ),
            )
        )
    for pair in copies:
        for copy in pair:
            copy.start()

    def vector(i):
        return vec_ref[i : i + 1, :]

    def total(values):
        return jnp.sum(values.astype(F32), axis=0, keepdims=True)

    back = own_ref[...] + dot_nn(asked_onehot(asked_ref, rows), arrived_ref[...])
    grad_fresh = (
        cot_ref[...].astype(F32)
        + dot_split(dot_nn, first_ref[...], own_t)
        + dot_split(dot_nn, back, nbr_t)
    )
    xhat2, scale2 = norm_parts(mixed2_ref[...])
    grad_mixed2 = norm_back(xhat2, scale2, vector(V_N2G), grad_fresh)
    grad_contracted = grad_mixed2.astype(BF16)
    for p in range(copies_ref.shape[0]):
        copies_ref[p] = grad_contracted
    grad_updated = grad_mixed2
    for c in range(hidden // width):
        cols = slice(c * width, (c + 1) * width)
        copies[c][0].wait()
        pre = dot_nt(grad_contracted, contract_ref[cols, :]) * slope_ref[:, cols]
        copies[c][1].wait()
        grad_updated = grad_updated + dot_nt(pre.astype(BF16), expand_ref[:, cols])
    xhat1, scale1 = norm_parts(mixed1_ref[...])
    grad_mixed1 = norm_back(xhat1, scale1, vector(V_N1G), grad_updated)
    grad_mixed1_ref[...] = grad_mixed1
    grad_message = (grad_mixed1 / counts).astype(BF16)
    spread_ref[...] = dot_nt(grad_message, w3_ref[...])
    pack_ref[:width, :] = dot_split(dot_tn, act_sum_ref[...], grad_message).astype(BF16)
    vectors = [
        total(counts * grad_message.astype(F32)),
        total(grad_updated * xhat1),
        total(grad_updated),
        total(grad_fresh * xhat2),
        total(grad_fresh),
        edge_vec_ref[...],
    ]
    vectors = jnp.concatenate(vectors, axis=0)
    vectors = jnp.concatenate(
        [vectors, jnp.zeros((pack_ref.shape[0] - width - vectors.shape[0], width), F32)], axis=0
    )
    pack_ref[width:, :] = vectors.astype(BF16)


def feed_weight_kernel(low_ref, grad_ref, expand_ref, bias_ref, contract_ref, *refs, more):
    sums_in = refs[:4] if more else None
    expand_out_ref, contract_out_ref, bias_out_ref, last_bias_ref = refs[-6:-2]
    low_turned_ref, grad_turned_ref = refs[-2:]
    chunk = pl.program_id(0)
    ones = jnp.ones((8, low_ref.shape[0]), F32).astype(BF16)

    @pl.when(chunk == 0)
    def _():
        low_turned_ref[...] = low_ref[...].T
        grad_turned_ref[...] = grad_ref[...].T

    act, slope = gelu_pair(dot_nn(low_ref[...], expand_ref[...]) + bias_ref[0:1, :])
    act = act.astype(BF16)
    pre = (dot_nt(grad_ref[...], contract_ref[...]) * slope).astype(BF16)
    expanded = dot_nn(low_turned_ref[...], pre)
    contracted = dot_nn(grad_turned_ref[...], act).T
    sums = dot_nn(ones, pre)
    if more:
        expanded = expanded + sums_in[0][...]
        contracted = contracted + sums_in[1][...]
        sums = sums + sums_in[2][...]
    expand_out_ref[...] = expanded
    contract_out_ref[...] = contracted
    bias_out_ref[...] = sums

    @pl.when(chunk == 0)
    def _():
        last = dot_nn(ones, grad_ref[...])
        last_bias_ref[...] = last + sums_in[3][...] if more else last


def message_kernel(
    core_ref,
    edge_ref,
    pos_ref,
    act1_ref,
    slope1_ref,
    slope2_ref,
    partial_ref,
    spread_ref,
    table_ref,
    w1_a_ref,
    w1_b_ref,
    w1_c_ref,
    w2_ref,
    edge_pack_ref,
    feed_pack_ref,
    grad_ref,
    first_ref,
    own_ref,
    away_ref,
    send_ref,
    keep_ref,
    joint_ref,
    dw2_ref,
    bias2_ref,
    w2_turned_ref,
    w1_turned_ref,
):
    step = pl.program_id(0)
    last = pl.num_programs(0) - 1
    slots, rows, edge_width = edge_ref.shape
    width = act1_ref.shape[1]
    block = slots * rows
    table_rows = table_ref.shape[0]

    @pl.when(step == 0)
    def _():
        for ref in (joint_ref, dw2_ref, bias2_ref, first_ref):
            ref[...] = jnp.zeros_like(ref)
        w2_turned_ref[...] = w2_ref[...].T
        w1_parts = [ref[...] for ref in (w1_a_ref, w1_b_ref, w1_c_ref)]
        w1_turned_ref[...] = jnp.concatenate(w1_parts, axis=0).T

    spread = spread_ref[...]
    grad2 = []
    bias2 = bias2_ref[...]
    for k in range(slots):
        part = (spread * slope2_ref[pl.ds(k * rows, rows), :].astype(F32)).astype(BF16)
        bias2 = bias2 + part.astype(F32)
        grad2.append(part)
    bias2_ref[...] = bias2
    grad2 = jnp.concatenate(grad2, axis=0)
    dw2_ref[...] += dot_tn(act1_ref[...], grad2)
    grad1 = (dot_nn(grad2, w2_turned_ref[...]) * slope1_ref[...].astype(F32)).astype(BF16)
    first_ref[...] += jnp.sum(grad1.astype(F32).reshape(slots, rows, width), axis=0)
    onehot = edge_onehot(pos_ref, table_rows)
    features = edge_ref[...].reshape(block, edge_width)
    joint_ref[...] += dot_tn(jnp.concatenate([onehot, features], axis=1), grad1)
    grad_ref[...] = partial_ref[...] + dot_nn(grad1, w1_turned_ref[...]).reshape(
        slots, rows, edge_width
    )

    @pl.when(step == last)
    def _():
        first = first_ref[...]
        back = joint_ref[:table_rows]
        own_ref[...] = back[:rows]
        away_ref[...] = back[rows:].astype(BF16)
        own_grad = dot_split_right(dot_tn, table_ref[:rows], first).astype(BF16)
        nbr_grad = dot_split_right(dot_tn, table_ref[...], back).astype(BF16)
        vectors = [
            feed_pack_ref[width:].astype(F32),
            jnp.sum(first, axis=0, keepdims=True),
            jnp.sum(bias2_ref[...], axis=0, keepdims=True),
        ]
        lower = [own_grad, nbr_grad, feed_pack_ref[:width]]
        upper = [joint_ref[table_rows:].astype(BF16), dw2_ref[...].astype(BF16), edge_pack_ref[...]]

        def fill(ref, pieces, tail):
            base = 0
            for piece in pieces:
                ref[base : base + piece.shape[0]] = piece
                base += piece.shape[0]
            if base < ref.shape[0]:
                gap = ref.shape[0] - base - sum(v.shape[0] for v in tail)
                rest = jnp.concatenate(tail + [jnp.zeros((gap, width), F32)], axis=0)
                ref[base:] = rest.astype(BF16)

        @pl.when(core_ref[0] == 0)
        def _():
            fill(keep_ref, lower, [])
            fill(send_ref, upper, vectors)

        @pl.when(core_ref[0] != 0)
        def _():
            fill(send_ref, lower, [])
            fill(keep_ref, upper, vectors)


def pair_kernel(y_ref, keep_ref, came_ref, away_ref, out_ref, *, parts, cap):
    peers, total, _ = out_ref.shape
    x_size = lax.axis_size("x")
    z_size = parts // x_size
    riders = z_size * cap
    share = total - riders
    for p in range(peers):
        y, x = divmod(p, x_size)
        part = pl.ds(p * share, share)
        out_ref[p, riders:] = (
            keep_ref[part, :].astype(F32) + came_ref[part, :].astype(F32)
        ).astype(BF16)
        rows = [
            away_ref[pl.ds((z * x_size + x) * cap, cap), :].astype(F32) for z in range(z_size)
        ]
        rows = jnp.where(y_ref[0] == y, jnp.concatenate(rows, axis=0), 0.0)
        out_ref[p, :riders] = rows.astype(BF16)


def plane_kernel(y_ref, came_ref, out_ref, *, cap):
    peers = came_ref.shape[0]
    z_size, total, _ = out_ref.shape
    x_size = lax.axis_size("x")
    riders = x_size * cap
    share = total - riders
    first = z_size * cap
    for z in range(z_size):
        part = pl.ds(first + z * share, share)
        value = came_ref[0, part, :].astype(F32)
        for p in range(1, peers):
            value = value + came_ref[p, part, :].astype(F32)
        out_ref[z, riders:] = value.astype(BF16)
    rows = []
    for x in range(x_size):
        value = came_ref[x, :first].astype(F32)
        for y in range(1, peers // x_size):
            value = jnp.where(y_ref[0] == y, came_ref[y * x_size + x, :first].astype(F32), value)
        rows.append(value)
    for z in range(z_size):
        part = [value[z * cap : (z + 1) * cap] for value in rows]
        out_ref[z, :riders] = jnp.concatenate(part, axis=0).astype(BF16)


def column_kernel(came_ref, copies_ref, returned_ref):
    z_size, total, _ = came_ref.shape
    riders = returned_ref.shape[0] // z_size
    value = came_ref[0, riders:].astype(F32)
    for z in range(1, z_size):
        value = value + came_ref[z, riders:].astype(F32)
    for z in range(z_size):
        copies_ref[z] = value.astype(BF16)
        returned_ref[z * riders : (z + 1) * riders, :] = came_ref[z, :riders]


def node_grad_kernel(grad_ref, first_ref, own_ref, arrived_ref, asked_ref, w1_ref, out_ref):
    rows, width = grad_ref.shape
    back = own_ref[...] + dot_nn(asked_onehot(asked_ref, rows), arrived_ref[...])
    out_ref[...] = (
        grad_ref[...]
        + dot_split(dot_nt, first_ref[...], w1_ref[:width])
        + dot_split(dot_nt, back, w1_ref[width : 2 * width])
    )


def unpack_kernel(core_ref, mine_ref, other_ref, bias_ref, last_bias_ref, *refs):
    (
        message1_ref,
        message1_bias_ref,
        message2_ref,
        message2_bias_ref,
        message3_ref,
        message3_bias_ref,
        gain1_ref,
        shift1_ref,
        expand_bias_ref,
        contract_bias_ref,
        gain2_ref,
        shift2_ref,
        edge1_ref,
        edge1_bias_ref,
        edge2_ref,
        edge2_bias_ref,
        edge3_ref,
        edge3_bias_ref,
        gain3_ref,
        shift3_ref,
    ) = refs
    width = mine_ref.shape[1]
    edge_width = edge2_ref.shape[0]
    half = width // 2
    first_core = core_ref[0] == 0

    def lower(start, stop):
        return jnp.where(first_core, mine_ref[start:stop], other_ref[start:stop]).astype(F32)

    def upper(start, stop):
        return jnp.where(first_core, other_ref[start:stop], mine_ref[start:stop]).astype(F32)

    message1_ref[: 2 * width] = lower(0, 2 * width)
    message3_ref[...] = lower(2 * width, 3 * width)
    message1_ref[2 * width :] = upper(0, edge_width)
    base = edge_width
    message2_ref[...] = upper(base, base + width)
    base = base + width
    edge1_ref[:, :width] = upper(base, base + edge_width)
    edge1_ref[:, width : 2 * width] = upper(base + edge_width, base + 2 * edge_width)
    third = upper(base + 2 * edge_width, base + 3 * edge_width)
    edge1_ref[:, 2 * width :] = third[:, :edge_width]
    edge2_ref[...] = third[:, half : half + edge_width]
    edge3_ref[...] = upper(base + 3 * edge_width, base + 4 * edge_width)[:, :edge_width]
    base = base + 4 * edge_width
    vectors = upper(base, mine_ref.shape[0])
    targets = (message3_bias_ref, gain1_ref, shift1_ref, gain2_ref, shift2_ref)
    for i, ref in enumerate(targets):
        ref[...] = vectors[i]
    targets = (edge1_bias_ref, edge2_bias_ref, edge3_bias_ref, gain3_ref, shift3_ref)
    for i, ref in enumerate(targets):
        ref[...] = vectors[5 + i, :edge_width]
    message1_bias_ref[...] = vectors[16]
    message2_bias_ref[...] = vectors[17]
    expand_bias_ref[...] = bias_ref[0]
    contract_bias_ref[...] = last_bias_ref[0]


def gather_copies(copies, axes):
    return lax.all_to_all(copies, axes, split_axis=0, concat_axis=0, tiled=True)


def copies_of(values, axes):
    return jnp.broadcast_to(values[None], (lax.axis_size(axes), *values.shape))


def exchange(values, parts):
    grouped = values.reshape(parts, values.shape[0] // parts, values.shape[1])
    arrived = lax.all_to_all(grouped, RES, split_axis=0, concat_axis=0, tiled=True)
    return arrived.reshape(values.shape)


def other_core(values):
    return lax.ppermute(values, "core", [(0, 1), (1, 0)])


def whole(shape):
    return pl.BlockSpec(shape, lambda *_: (0,) * len(shape))


def params(mebibytes):
    return pltpu.CompilerParams(vmem_limit_bytes=mebibytes * MIB)


def cost(microseconds):
    return pl.CostEstimate(
        flops=int(microseconds * 1.15e9),
        bytes_accessed=int(microseconds * 3.69e6),
        transcendentals=0,
    )


def body(
    node_states,
    edge_states,
    neighbour_index,
    edge_mask,
    node_cotangent,
    edge_cotangent,
    message_weight1,
    message_bias1,
    message_weight2,
    message_bias2,
    message_weight3,
    message_bias3,
    norm1_gain,
    norm1_shift,
    expand_weight,
    expand_bias,
    contract_weight,
    contract_bias,
    norm2_gain,
    norm2_shift,
    edge_weight1,
    edge_bias1,
    edge_weight2,
    edge_bias2,
    edge_weight3,
    edge_bias3,
    norm3_gain,
    norm3_shift,
):
    self_rows = node_states[0]
    rows, width = self_rows.shape
    slots = neighbour_index.shape[2]
    edge_width = edge_states.shape[3]
    hidden = expand_weight.shape[1]
    edges = rows * slots
    parts = lax.axis_size(RES)
    cap = ROW_CAP
    table_rows = rows + parts * cap
    side = lax.axis_size(SIDE)
    steps = STEPS
    block_slots = slots // steps
    block = block_slots * rows
    pairs = block // LANES

    everyone = gather_copies(copies_of(self_rows, RES), RES).reshape(parts * rows, width)
    core = lax.axis_index("core").astype(jnp.int32).reshape(1)
    me = lax.axis_index(RES).astype(jnp.int32).reshape(1)
    edge_rows = edge_states[0].transpose(1, 0, 2)
    edge_cot = edge_cotangent[0].transpose(1, 0, 2)
    slot_index = neighbour_index.transpose(2, 0, 1)
    slot_mask = edge_mask.transpose(2, 0, 1)
    edge_w1t = edge_weight1.T
    wide = (
        message_bias1,
        message_bias2,
        message_bias3,
        norm1_gain,
        norm1_shift,
        contract_bias,
        norm2_gain,
        norm2_shift,
        expand_bias,
    )
    narrow = (edge_bias1, edge_bias2, edge_bias3, norm3_gain, norm3_shift)
    vmem = pl.BlockSpec(memory_space=pltpu.VMEM)

    def shape(dims, kind):
        return jax.ShapeDtypeStruct(dims, kind)

    pos, select, ids, counts, vectors, bias_row = pl.pallas_call(
        functools.partial(
            prepare_kernel, parts=parts, cap=cap, steps=steps, wide=len(wide), narrow=len(narrow)
        ),
        out_shape=(
            shape((steps, LANES, pairs), jnp.int32),
            shape((parts * rows, table_rows), BF16),
            shape((parts, cap), jnp.int32),
            shape((rows, width), F32),
            shape((V_ROWS, width), F32),
            shape((1, hidden), F32),
        ),
        in_specs=[pl.BlockSpec(memory_space=pltpu.SMEM)] + [vmem] * (2 + len(wide) + len(narrow)),
        out_specs=(vmem,) * 6,
        compiler_params=params(56),
        cost_estimate=cost(6),
        name="prepare",
    )(me, slot_index, slot_mask, *wide, *narrow)
    ids, everyone = lax.optimization_barrier((ids, everyone))
    asked = lax.all_to_all(ids, RES, split_axis=0, concat_axis=0, tiled=True)

    edge_spec = pl.BlockSpec((block_slots, rows, edge_width), lambda i: (i, 0, 0))
    flat_spec = pl.BlockSpec((block, width), lambda i: (i, 0))
    pos_spec = pl.BlockSpec((1, LANES, pairs), lambda i: (i, 0, 0))
    any_spec = pl.BlockSpec(memory_space=pl.ANY)
    node_spec = whole((rows, width))
    away_spec = whole((parts * cap, width))

    (
        act1,
        slope1,
        slope2,
        fresh,
        table,
        mixed1,
        mixed2,
        low,
        slope_e,
        act_sum,
    ) = pl.pallas_call(
        node_kernel,
        grid=(steps,),
        in_specs=[
            edge_spec,
            pos_spec,
            whole((parts * rows, table_rows)),
            whole((parts * rows, width)),
            node_spec,
            node_spec,
            whole((V_ROWS, width)),
            whole(message_weight1.shape),
            whole((width, width)),
            whole((width, width)),
            any_spec,
            any_spec,
        ],
        out_specs=[
            flat_spec,
            flat_spec,
            flat_spec,
            node_spec,
            whole((table_rows, width)),
            node_spec,
            node_spec,
            node_spec,
            whole((rows, hidden)),
            node_spec,
        ],
        out_shape=[
            shape((edges, width), BF16),
            shape((edges, width), BF16),
            shape((edges, width), BF16),
            shape((rows, width), BF16),
            shape((table_rows, width), BF16),
            shape((rows, width), F32),
            shape((rows, width), F32),
            shape((rows, width), BF16),
            shape((rows, hidden), F32),
            shape((rows, width), F32),
        ],
        scratch_shapes=[
            pltpu.VMEM((table_rows, width), BF16),
            pltpu.VMEM((rows, width), F32),
            pltpu.VMEM((width, hidden), BF16),
            pltpu.VMEM((hidden, width), BF16),
            pltpu.SemaphoreType.DMA((2,)),
        ],
        compiler_params=params(56),
        cost_estimate=cost(18),
        name="node_forward",
    )(
        edge_rows,
        pos,
        select,
        everyone,
        self_rows,
        counts,
        vectors,
        message_weight1,
        message_weight2,
        message_weight3,
        expand_weight,
        contract_weight,
    )
    outgoing = pl.pallas_call(
        pick_kernel,
        in_specs=[vmem] * 2,
        out_specs=vmem,
        out_shape=shape((parts * cap, width), BF16),
        compiler_params=params(8),
        cost_estimate=cost(1),
        name="pick",
    )(asked, fresh)
    incoming = exchange(outgoing, parts)
    low_mine = lax.all_gather(low, SIDE, axis=0, tiled=True)

    edge_pack_rows = 4 * edge_width
    edge_out, grad_partial, edge_first, edge_own, edge_away, edge_pack, edge_vec = pl.pallas_call(
        edge_kernel,
        grid=(steps,),
        in_specs=[
            edge_spec,
            edge_spec,
            pos_spec,
            node_spec,
            away_spec,
            node_spec,
            whole((V_ROWS, width)),
            whole(edge_w1t.shape),
            whole((edge_width, edge_width)),
            whole((edge_width, edge_width)),
        ],
        out_specs=[
            edge_spec,
            edge_spec,
            whole((rows, edge_width)),
            whole((rows, edge_width)),
            whole((parts * cap, edge_width)),
            whole((edge_pack_rows, width)),
            whole((8, width)),
        ],
        out_shape=[
            shape((slots, rows, edge_width), BF16),
            shape((slots, rows, edge_width), F32),
            shape((rows, edge_width), F32),
            shape((rows, edge_width), F32),
            shape((parts * cap, edge_width), BF16),
            shape((edge_pack_rows, width), BF16),
            shape((8, width), F32),
        ],
        scratch_shapes=[
            pltpu.VMEM((table_rows, width), BF16),
            pltpu.VMEM((table_rows, edge_width), BF16),
            pltpu.VMEM((rows, edge_width), F32),
            pltpu.VMEM((table_rows, edge_width), F32),
            pltpu.VMEM((edge_width, edge_width), F32),
            pltpu.VMEM((edge_width, edge_width), F32),
            pltpu.VMEM((edge_width, edge_width), F32),
            pltpu.VMEM((5, rows, edge_width), F32),
            pltpu.VMEM((3, edge_width, edge_width), BF16),
        ],
        compiler_params=params(56),
        cost_estimate=cost(17),
        name="edge_both",
    )(
        edge_rows,
        edge_cot,
        pos,
        fresh,
        incoming,
        counts,
        vectors,
        edge_w1t,
        edge_weight2,
        edge_weight3,
    )
    edge_arrived = exchange(edge_away, parts)

    feed_rows = width + 16
    feed_pack, grad_copies, spread, grad_mixed1 = pl.pallas_call(
        feed_kernel,
        in_specs=[vmem] * 12 + [any_spec] * 2 + [vmem] * 2,
        out_specs=[vmem] * 4,
        out_shape=[
            shape((feed_rows, width), BF16),
            shape((side, rows, width), BF16),
            shape((rows, width), F32),
            shape((rows, width), F32),
        ],
        scratch_shapes=[
            pltpu.VMEM((width, hidden), BF16),
            pltpu.VMEM((hidden, width), BF16),
            pltpu.SemaphoreType.DMA((2 * hidden // width,)),
        ],
        compiler_params=params(56),
        cost_estimate=cost(6),
        name="feed_backward",
    )(
        node_cotangent[0],
        edge_first,
        edge_own,
        edge_arrived,
        asked,
        counts,
        vectors,
        edge_w1t,
        mixed1,
        mixed2,
        slope_e,
        act_sum,
        expand_weight,
        contract_weight,
        message_weight3,
        edge_vec,
    )
    grad_mine = gather_copies(grad_copies, SIDE).reshape(side * rows, width)

    unit = 16 * side
    half_rows = (3 * width + unit - 1) // unit * unit
    third = edge_width // 3
    edge_grad, first, own, away, send, keep = pl.pallas_call(
        message_kernel,
        grid=(steps,),
        in_specs=[
            pl.BlockSpec(memory_space=pltpu.SMEM),
            edge_spec,
            pos_spec,
            flat_spec,
            flat_spec,
            flat_spec,
            edge_spec,
            node_spec,
            whole((table_rows, width)),
            *[
                pl.BlockSpec((third, width), lambda i, p=p: (2 * width // third + p, 0))
                for p in range(3)
            ],
            whole((width, width)),
            whole((edge_pack_rows, width)),
            whole((feed_rows, width)),
        ],
        out_specs=[
            edge_spec,
            node_spec,
            node_spec,
            away_spec,
            whole((half_rows, width)),
            whole((half_rows, width)),
        ],
        out_shape=[
            shape((slots, rows, edge_width), F32),
            shape((rows, width), F32),
            shape((rows, width), F32),
            shape((parts * cap, width), BF16),
            shape((half_rows, width), BF16),
            shape((half_rows, width), BF16),
        ],
        scratch_shapes=[
            pltpu.VMEM((table_rows + edge_width, width), F32),
            pltpu.VMEM((width, width), F32),
            pltpu.VMEM((rows, width), F32),
            pltpu.VMEM((width, width), BF16),
            pltpu.VMEM((width, edge_width), BF16),
        ],
        compiler_params=params(56),
        cost_estimate=cost(16),
        name="message_backward",
    )(
        core,
        edge_rows,
        pos,
        act1,
        slope1,
        slope2,
        grad_partial,
        spread,
        table,
        message_weight1,
        message_weight1,
        message_weight1,
        message_weight2,
        edge_pack,
        feed_pack,
    )
    send, low_mine = lax.optimization_barrier((send, low_mine))
    came = other_core(send)
    y_size = lax.axis_size("y")
    x_size = lax.axis_size("x")
    z_size = lax.axis_size("z")
    my_y = lax.axis_index("y").astype(jnp.int32).reshape(1)
    peers = y_size * x_size
    smem = pl.BlockSpec(memory_space=pltpu.SMEM)
    payload = pl.pallas_call(
        functools.partial(pair_kernel, parts=parts, cap=cap),
        in_specs=[smem] + [vmem] * 3,
        out_specs=vmem,
        out_shape=shape((peers, half_rows // peers + z_size * cap, width), BF16),
        compiler_params=params(20),
        cost_estimate=cost(3),
        name="pair_sum",
    )(my_y, keep, came, away)
    _, grad_mine, low_mine = lax.optimization_barrier((payload, grad_mine, low_mine))
    grad_other = other_core(grad_mine)
    low_other = other_core(low_mine)
    arrived = lax.all_to_all(payload, PLANE, split_axis=0, concat_axis=0, tiled=True)
    def feed_weights(low_values, grad_values, at, block_rows, sums):
        units = 256
        row_block = pl.BlockSpec((block_rows, width), lambda c: (at, 0))
        sum_specs = [
            pl.BlockSpec((width, units), lambda c: (0, c)),
            pl.BlockSpec((units, width), lambda c: (c, 0)),
            pl.BlockSpec((8, units), lambda c: (0, c)),
            whole((8, width)),
        ]
        return pl.pallas_call(
            functools.partial(feed_weight_kernel, more=bool(sums)),
            grid=(hidden // units,),
            in_specs=[
                row_block,
                row_block,
                sum_specs[0],
                pl.BlockSpec((1, units), lambda c: (0, c)),
                sum_specs[1],
                *(sum_specs if sums else []),
            ],
            out_specs=sum_specs,
            scratch_shapes=[
                pltpu.VMEM((width, block_rows), BF16),
                pltpu.VMEM((width, block_rows), BF16),
            ],
            out_shape=[
                shape((width, hidden), F32),
                shape((hidden, width), F32),
                shape((8, hidden), F32),
                shape((8, width), F32),
            ],
            compiler_params=params(56),
            cost_estimate=cost(17),
            name="feed_weights_more" if sums else "feed_weights",
        )(low_values, grad_values, expand_weight, bias_row, contract_weight, *sums)

    def feed_side(low_values, grad_values, sums):
        block_rows = min(side * rows, 1024)
        for at in range(side * rows // block_rows):
            sums = tuple(feed_weights(low_values, grad_values, at, block_rows, sums))
        return sums

    sums = feed_side(low_mine, grad_mine, ())
    arrived, *sums = lax.optimization_barrier((arrived, *sums))
    payload = pl.pallas_call(
        functools.partial(plane_kernel, cap=cap),
        in_specs=[smem, vmem],
        out_specs=vmem,
        out_shape=shape((z_size, half_rows // side + x_size * cap, width), BF16),
        compiler_params=params(16),
        cost_estimate=cost(3),
        name="plane_sum",
    )(my_y, arrived)
    arrived = lax.all_to_all(payload, "z", split_axis=0, concat_axis=0, tiled=True)
    copies, returned = pl.pallas_call(
        column_kernel,
        in_specs=[vmem],
        out_specs=[vmem] * 2,
        out_shape=[
            shape((z_size, half_rows // side, width), BF16),
            shape((parts * cap, width), BF16),
        ],
        compiler_params=params(8),
        cost_estimate=cost(1),
        name="column_sum",
    )(arrived)
    column = lax.all_to_all(copies, "z", split_axis=0, concat_axis=0, tiled=True)
    column, grad_other, low_other, *sums = lax.optimization_barrier(
        (column, grad_other, low_other, *sums)
    )
    column = copies_of(column.reshape(half_rows // peers, width), PLANE)
    mine = gather_copies(column, PLANE).reshape(half_rows, width)
    sums = feed_side(low_other, grad_other, tuple(sums))
    mine, *sums = lax.optimization_barrier((mine, *sums))
    grad_expand, grad_contract, expand_bias_sum, contract_bias_sum = sums
    other = other_core(mine)
    node_grad = pl.pallas_call(
        node_grad_kernel,
        in_specs=[vmem] * 6,
        out_specs=vmem,
        out_shape=shape((rows, width), F32),
        compiler_params=params(12),
        cost_estimate=cost(3),
        name="node_gradient",
    )(grad_mixed1, first, own, returned, asked, message_weight1)

    vec = shape((width,), F32)
    thin = shape((edge_width,), F32)
    square = shape((width, width), F32)
    small = shape((edge_width, edge_width), F32)
    (
        grad_message1,
        grad_mb1,
        grad_message2,
        grad_mb2,
        grad_message3,
        grad_mb3,
        grad_n1g,
        grad_n1s,
        grad_eb,
        grad_cb,
        grad_n2g,
        grad_n2s,
        grad_edge1_t,
        grad_eb1,
        grad_edge2,
        grad_eb2,
        grad_edge3,
        grad_eb3,
        grad_n3g,
        grad_n3s,
    ) = pl.pallas_call(
        unpack_kernel,
        in_specs=[smem] + [vmem] * 4,
        out_specs=[vmem] * 20,
        out_shape=[
            shape(message_weight1.shape, F32),
            vec,
            square,
            vec,
            square,
            vec,
            vec,
            vec,
            shape((hidden,), F32),
            vec,
            vec,
            vec,
            shape(edge_w1t.shape, F32),
            thin,
            small,
            thin,
            small,
            thin,
            thin,
            thin,
        ],
        compiler_params=params(24),
        cost_estimate=cost(4),
        name="unpack",
    )(core, mine, other, expand_bias_sum, contract_bias_sum)
    return (
        fresh[None],
        edge_out.transpose(1, 0, 2)[None],
        node_grad[None],
        edge_grad.transpose(1, 0, 2)[None],
        grad_message1,
        grad_mb1,
        grad_message2,
        grad_mb2,
        grad_message3,
        grad_mb3,
        grad_n1g,
        grad_n1s,
        grad_expand,
        grad_eb,
        grad_contract,
        grad_cb,
        grad_n2g,
        grad_n2s,
        grad_edge1_t.T,
        grad_eb1,
        grad_edge2,
        grad_eb2,
        grad_edge3,
        grad_eb3,
        grad_n3g,
        grad_n3s,
    )


def solution(mesh):
    batch, res = mesh.shape["batch"], mesh.shape["res"]
    x_size = 1 << ((res.bit_length() - 1) // 2)
    sizes = (batch // CORES, CORES, res // x_size, x_size)
    fine = jax.sharding.Mesh(mesh.devices.reshape(sizes), ALL)
    row_spec = P(("y", "core"), RES, None)
    edge_spec = P(("y", "core"), RES, None, None)
    return jax.shard_map(
        body,
        mesh=fine,
        in_specs=(row_spec, edge_spec, row_spec, row_spec, row_spec, edge_spec) + (P(),) * 22,
        out_specs=(row_spec, edge_spec, row_spec, edge_spec) + (P(),) * 22,
        check_vma=False,
    )
```

```python
import functools
import math

import jax
import jax.numpy as jnp
from jax import lax
from jax.experimental import pallas as pl
from jax.experimental.pallas import tpu as pltpu
from jax.sharding import PartitionSpec as P

ROW_CAP = 8
CORES = 2
RES = ("z", "x")
PLANE = ("y", "x")
SIDE = ("y", "z", "x")
ALL = ("y", "core", "z", "x")
EPSILON = 1e-05
LANES = 128
MIB = 1024 * 1024
STEPS = 3
EARLY_ROWS = 48
F32 = jnp.float32
BF16 = jnp.bfloat16

V_MB1, V_MB2, V_MB3, V_N1G, V_N1S, V_CB, V_N2G, V_N2S, V_EB = range(9)
V_EDGE = 12
V_ROWS = 24


def dot_nn(left, right):
    return lax.dot_general(left, right, (((1,), (0,)), ((), ())), preferred_element_type=F32)


def dot_nt(left, right):
    return lax.dot_general(left, right, (((1,), (1,)), ((), ())), preferred_element_type=F32)


def dot_tn(left, right):
    return lax.dot_general(left, right, (((0,), (0,)), ((), ())), preferred_element_type=F32)


def split_low(values):
    high = values.astype(BF16)
    return high, (values - high.astype(F32)).astype(BF16)


def dot_split(dot, left, right):
    high, rest = split_low(left)
    return dot(high, right) + dot(rest, right)


def dot_split_right(dot, left, right):
    high, rest = split_low(right)
    return dot(left, high) + dot(left, rest)


def gelu_pair(v):
    e = jnp.exp2((v * v) * (-0.5 * math.log2(math.e)))
    phi_sum = 0.5 + 0.5 * lax.erf(v * math.sqrt(0.5))
    return v * phi_sum, phi_sum + (v * (1.0 / math.sqrt(2.0 * math.pi))) * e


def norm_parts(values):
    average = jnp.mean(values, axis=-1, keepdims=True)
    centred = values - average
    variance = jnp.mean(centred * centred, axis=-1, keepdims=True)
    scale = lax.rsqrt(variance + EPSILON)
    return centred * scale, scale


def norm_back(xhat, scale, gain, upstream):
    w = upstream * gain
    mean_w = jnp.mean(w, axis=-1, keepdims=True)
    mean_wx = jnp.mean(w * xhat, axis=-1, keepdims=True)
    return (w - mean_w - xhat * mean_wx) * scale


def edge_onehot(pos_ref, table_rows):
    pairs = pos_ref.shape[2]
    lane = lax.broadcasted_iota(jnp.int32, (LANES, table_rows), 1)
    return jnp.concatenate(
        [(pos_ref[0, :, p : p + 1] == lane).astype(F32).astype(BF16) for p in range(pairs)], axis=0
    )


def prepare_kernel(me_ref, idx_ref, mask_ref, *refs, parts, cap, steps, wide, narrow):
    wide_refs = refs[:wide]
    narrow_refs = refs[wide : wide + narrow]
    pos_ref, select_ref, ids_ref, count_ref, vec_ref, expand_bias_ref = refs[wide + narrow :]
    rows, width = count_ref.shape
    total = rows * parts
    table = rows + parts * cap
    me = me_ref[0]
    pair_rows = idx_ref.shape[0] // 2
    named = [
        jnp.concatenate([idx_ref[2 * j], idx_ref[2 * j + 1]], axis=1) for j in range(pair_rows)
    ]
    residue = lax.broadcasted_iota(jnp.int32, (total, LANES), 0)
    owner = residue // rows
    within = residue - owner * rows
    hits = jnp.zeros((total, LANES), F32)
    for j in range(pair_rows):
        hits = jnp.where(named[j] == residue, 1.0, hits)
    hit = jnp.max(hits, axis=1, keepdims=True)
    own = owner == me
    wanted = jnp.where(own, 0.0, jnp.broadcast_to(hit, (total, LANES)))
    low_row = lax.broadcasted_iota(jnp.int32, (rows, rows), 0)
    low_col = lax.broadcasted_iota(jnp.int32, (rows, rows), 1)
    lower = (low_col <= low_row).astype(F32).astype(BF16)
    wanted_low = wanted.astype(BF16)
    place = jnp.concatenate(
        [dot_nn(lower, wanted_low[o * rows : (o + 1) * rows]) for o in range(parts)], axis=0
    )
    place = jnp.clip(place - 1.0, 0.0, cap - 1.0)
    pos = jnp.where(own, within.astype(F32), (rows + owner * cap).astype(F32) + place)
    picked = [
        jnp.sum(jnp.where(named[j] == residue, pos, 0.0), axis=0, keepdims=True)
        for j in range(pair_rows)
    ]
    picked.append(jnp.zeros((LANES - pair_rows, LANES), F32))
    turned = jnp.concatenate(picked, axis=0).T.astype(jnp.int32)
    per = pair_rows // steps
    for s in range(steps):
        pos_ref[s] = turned[:, s * per : (s + 1) * per]
    lane = lax.broadcasted_iota(jnp.int32, (total, table), 1).astype(F32)
    live = jnp.where(own, 1.0, wanted)
    chosen = jnp.where(lane == pos[:, :1], jnp.broadcast_to(live[:, :1], (total, table)), 0.0)
    select_ref[...] = chosen.astype(BF16)
    asked_row = jnp.broadcast_to(within[:, :1].astype(F32), (total, parts * cap))
    ids = jnp.sum(chosen[:, rows:] * asked_row, axis=0, keepdims=True)
    ids = ids.astype(jnp.int32)
    for o in range(parts):
        ids_ref[o : o + 1, :] = ids[:, o * cap : (o + 1) * cap]
    count = mask_ref[0]
    for k in range(1, mask_ref.shape[0]):
        count = count + mask_ref[k]
    count = jnp.concatenate([count.astype(F32), jnp.zeros((7, rows), F32)], axis=0)
    count_ref[...] = dot_tn(count.astype(BF16), jnp.ones((8, width), F32).astype(BF16))
    expand_bias_ref[...] = wide_refs[-1][...].astype(F32).reshape(expand_bias_ref.shape)
    vec_ref[...] = jnp.zeros_like(vec_ref)
    at = 0
    for ref in wide_refs:
        for c in range(ref.shape[0] // width):
            part = ref[c * width : (c + 1) * width]
            vec_ref[at : at + 1, :] = part.astype(F32).reshape(1, width)
            at += 1
    for ref in narrow_refs:
        vec_ref[at : at + 1, : ref.shape[0]] = ref[...].astype(F32).reshape(1, ref.shape[0])
        at += 1


def node_kernel(
    edge_ref,
    pos_ref,
    select_ref,
    all_ref,
    self_ref,
    count_ref,
    vec_ref,
    w1_ref,
    w2_ref,
    w3_ref,
    expand_hbm,
    contract_hbm,
    act1_ref,
    slope1_ref,
    slope2_ref,
    fresh_ref,
    table_ref,
    mixed1_ref,
    mixed2_ref,
    low_ref,
    low_late_ref,
    slope_e_ref,
    act_sum_ref,
    proj_ref,
    self_pre_ref,
    expand_ref,
    contract_ref,
    sems,
):
    step = pl.program_id(0)
    last = pl.num_programs(0) - 1
    rows, width = self_ref.shape
    slots = edge_ref.shape[0]
    edge_width = edge_ref.shape[2]
    table_rows = table_ref.shape[0]
    expand_copy = pltpu.make_async_copy(expand_hbm, expand_ref, sems.at[0])
    contract_copy = pltpu.make_async_copy(contract_hbm, contract_ref, sems.at[1])

    @pl.when(step == 0)
    def _():
        expand_copy.start()
        contract_copy.start()
        table = dot_tn(select_ref[...], all_ref[...]).astype(BF16)
        table_ref[...] = table
        proj_ref[...] = dot_nn(table, w1_ref[width : 2 * width]).astype(BF16)
        self_pre_ref[...] = (
            dot_nn(self_ref[...], w1_ref[:width]) + vec_ref[V_MB1 : V_MB1 + 1, :]
        )
        act_sum_ref[...] = jnp.zeros_like(act_sum_ref)

    onehot = edge_onehot(pos_ref, table_rows)
    features = edge_ref[...].reshape(slots * rows, edge_width)
    pre1 = dot_nn(features, w1_ref[2 * width :]) + dot_nn(onehot, proj_ref[...])
    self_pre = self_pre_ref[...]
    act1 = []
    for k in range(slots):
        part = pl.ds(k * rows, rows)
        act, slope = gelu_pair(pre1[k * rows : (k + 1) * rows] + self_pre)
        act = act.astype(BF16)
        act1.append(act)
        act1_ref[part, :] = act
        slope1_ref[part, :] = slope.astype(BF16)
    pre2 = dot_nn(jnp.concatenate(act1, axis=0), w2_ref[...])
    bias2 = vec_ref[V_MB2 : V_MB2 + 1, :]
    act_sum = act_sum_ref[...]
    counts = count_ref[...]
    for k in range(slots):
        act, slope = gelu_pair(pre2[k * rows : (k + 1) * rows] + bias2)
        valid = counts > (step * slots + k).astype(F32)
        act_sum = act_sum + jnp.where(valid, act.astype(BF16).astype(F32), 0.0)
        slope2_ref[pl.ds(k * rows, rows), :] = jnp.where(valid, slope, 0.0).astype(BF16)
    act_sum_ref[...] = act_sum

    @pl.when(step == last)
    def _():
        summed = dot_split(dot_nn, act_sum_ref[...], w3_ref[...])
        summed = summed + counts * vec_ref[V_MB3 : V_MB3 + 1, :]
        mixed1 = self_ref[...].astype(F32) + summed / counts
        mixed1_ref[...] = mixed1
        xhat1, _ = norm_parts(mixed1)
        updated = xhat1 * vec_ref[V_N1G : V_N1G + 1, :] + vec_ref[V_N1S : V_N1S + 1, :]
        low = updated.astype(BF16)
        for p in range(low_ref.shape[0]):
            low_ref[p] = low[: low_ref.shape[1]]
        low_late_ref[...] = low[low_ref.shape[1] :]
        expand_copy.wait()
        contract_copy.wait()
        mixed2 = updated + vec_ref[V_CB : V_CB + 1, :]
        for c in range(expand_ref.shape[1] // width):
            cols = slice(c * width, (c + 1) * width)
            pre = dot_nn(low, expand_ref[:, cols]) + vec_ref[V_EB + c : V_EB + c + 1, :]
            act, slope = gelu_pair(pre)
            act = act.astype(BF16)
            slope_e_ref[:, cols] = slope
            mixed2 = mixed2 + dot_nn(act, contract_ref[cols, :])
        mixed2_ref[...] = mixed2
        xhat2, _ = norm_parts(mixed2)
        fresh = (xhat2 * vec_ref[V_N2G : V_N2G + 1, :] + vec_ref[V_N2S : V_N2S + 1, :]).astype(BF16)
        fresh_ref[...] = fresh


def asked_onehot(asked_ref, rows):
    parts = asked_ref.shape[0]
    asked = jnp.concatenate([asked_ref[o : o + 1, :] for o in range(parts)], axis=1)
    row = lax.broadcasted_iota(jnp.int32, (rows, asked.shape[1]), 0)
    return (asked == row).astype(F32).astype(BF16)


def pick_kernel(asked_ref, fresh_ref, out_ref):
    out_ref[...] = dot_tn(asked_onehot(asked_ref, fresh_ref.shape[0]), fresh_ref[...]).astype(BF16)


def edge_kernel(
    edge_ref,
    cot_ref,
    pos_ref,
    fresh_ref,
    incoming_ref,
    count_ref,
    vec_ref,
    w1t_ref,
    w2_ref,
    w3_ref,
    out_ref,
    grad_ref,
    first_ref,
    own_ref,
    away_ref,
    pack_ref,
    vec_out_ref,
    table_ref,
    proj_ref,
    self_pre_ref,
    back_ref,
    dw3_ref,
    dw2_ref,
    dw1_ref,
    sums_ref,
    turned_ref,
):
    step = pl.program_id(0)
    last = pl.num_programs(0) - 1
    rows, width = fresh_ref.shape
    slots, _, edge_width = edge_ref.shape
    block = slots * rows
    table_rows = table_ref.shape[0]
    own_t = w1t_ref[:, :width]
    nbr_t = w1t_ref[:, width : 2 * width]
    feat_t = w1t_ref[:, 2 * width :]

    def vector(i):
        return vec_ref[V_EDGE + i : V_EDGE + i + 1, :edge_width]

    @pl.when(step == 0)
    def _():
        table_ref[:rows] = fresh_ref[...]
        table_ref[rows:] = incoming_ref[...]
        proj_ref[...] = dot_nt(table_ref[...], nbr_t).astype(BF16)
        self_pre_ref[...] = dot_nt(fresh_ref[...], own_t) + vector(0)
        for ref in (back_ref, dw3_ref, dw2_ref, dw1_ref, sums_ref, first_ref):
            ref[...] = jnp.zeros_like(ref)
        turned_ref[0] = feat_t.T
        turned_ref[1] = w2_ref[...].T
        turned_ref[2] = w3_ref[...].T

    def flat(values):
        return values.reshape(block, edge_width)

    def deep(values):
        return values.reshape(slots, rows, edge_width)

    onehot = edge_onehot(pos_ref, table_rows)
    features = flat(edge_ref[...])
    pre1 = dot_nn(features, turned_ref[0]) + dot_nn(onehot, proj_ref[...])
    pre1 = deep(pre1) + self_pre_ref[...][None]
    act1, slope1 = gelu_pair(flat(pre1))
    act1 = act1.astype(BF16)
    pre2 = dot_nn(act1, w2_ref[...]) + vector(1)
    act2, slope2 = gelu_pair(pre2)
    act2 = act2.astype(BF16)
    mixed3 = features.astype(F32) + (dot_nn(act2, w3_ref[...]) + vector(2))
    xhat, scale = norm_parts(mixed3)
    gain = vector(3)
    slot = lax.broadcasted_iota(jnp.int32, (slots, rows, edge_width), 0) + step * slots
    valid = count_ref[...][None, :, :edge_width] > slot.astype(F32)
    out_ref[...] = jnp.where(valid, deep(xhat * gain + vector(4)), 0.0).astype(BF16)
    upstream = flat(jnp.where(valid, cot_ref[...].astype(F32), 0.0))
    sums_ref[3] += jnp.sum(deep(upstream * xhat), axis=0)
    sums_ref[4] += jnp.sum(deep(upstream), axis=0)
    grad_mixed = norm_back(xhat, scale, gain, upstream)
    grad_delta = grad_mixed.astype(BF16)
    dw3_ref[...] += dot_tn(act2, grad_delta)
    sums_ref[2] += jnp.sum(deep(grad_delta.astype(F32)), axis=0)
    grad2 = (dot_nn(grad_delta, turned_ref[2]) * slope2).astype(BF16)
    dw2_ref[...] += dot_tn(act1, grad2)
    sums_ref[1] += jnp.sum(deep(grad2.astype(F32)), axis=0)
    grad1 = (dot_nn(grad2, turned_ref[1]) * slope1).astype(BF16)
    dw1_ref[...] += dot_tn(grad1, features)
    first_ref[...] += jnp.sum(deep(grad1.astype(F32)), axis=0)
    back_ref[...] += dot_tn(onehot, grad1)
    grad_ref[...] = deep(grad_mixed + dot_nn(grad1, feat_t))

    @pl.when(step == last)
    def _():
        first = first_ref[...]
        back = back_ref[...]
        own_ref[...] = back[:rows]
        away_ref[...] = back[rows:].astype(BF16)
        first_high, first_rest = split_low(first)
        back_high, back_rest = split_low(back)
        own_grad = dot_tn(first_high, fresh_ref[...]) + dot_tn(first_rest, fresh_ref[...])
        nbr_grad = dot_tn(back_high, table_ref[...]) + dot_tn(back_rest, table_ref[...])
        pack_ref[:edge_width, :] = own_grad.astype(BF16)
        pack_ref[edge_width : 2 * edge_width, :] = nbr_grad.astype(BF16)
        pad = jnp.zeros((edge_width, width // 2 - edge_width), BF16)
        third = [dw1_ref[...].astype(BF16), pad, dw2_ref[...].astype(BF16), pad]
        pack_ref[2 * edge_width : 3 * edge_width, :] = jnp.concatenate(third, axis=1)
        fourth = [dw3_ref[...].astype(BF16), pad, jnp.zeros((edge_width, width // 2), BF16)]
        pack_ref[3 * edge_width :, :] = jnp.concatenate(fourth, axis=1)
        vec_out_ref[...] = jnp.zeros_like(vec_out_ref)
        vec_out_ref[0:1, :edge_width] = jnp.sum(first, axis=0, keepdims=True)
        for i in range(1, 5):
            vec_out_ref[i : i + 1, :edge_width] = jnp.sum(sums_ref[i], axis=0, keepdims=True)


def feed_kernel(
    cot_ref,
    first_ref,
    own_ref,
    arrived_ref,
    asked_ref,
    count_ref,
    vec_ref,
    w1t_ref,
    mixed1_ref,
    mixed2_ref,
    slope_ref,
    act_sum_ref,
    expand_hbm,
    contract_hbm,
    w3_ref,
    edge_vec_ref,
    low_late_ref,
    pack_ref,
    copies_ref,
    spread_ref,
    grad_mixed1_ref,
    expand_ref,
    contract_ref,
    sems,
):
    rows, width = cot_ref.shape
    hidden = expand_ref.shape[1]
    own_t = w1t_ref[:, :width]
    nbr_t = w1t_ref[:, width : 2 * width]
    counts = count_ref[...]
    copies = []
    for c in range(hidden // width):
        rows_part, cols_part = pl.ds(c * width, width), pl.ds(c * width, width)
        copies.append(
            (
                pltpu.make_async_copy(
                    contract_hbm.at[rows_part, :], contract_ref.at[rows_part, :], sems.at[2 * c]
                ),
                pltpu.make_async_copy(
                    expand_hbm.at[:, cols_part], expand_ref.at[:, cols_part], sems.at[2 * c + 1]
                ),
            )
        )
    for pair in copies:
        for copy in pair:
            copy.start()

    def vector(i):
        return vec_ref[i : i + 1, :]

    def total(values):
        return jnp.sum(values.astype(F32), axis=0, keepdims=True)

    back = own_ref[...] + dot_nn(asked_onehot(asked_ref, rows), arrived_ref[...])
    grad_fresh = (
        cot_ref[...].astype(F32)
        + dot_split(dot_nn, first_ref[...], own_t)
        + dot_split(dot_nn, back, nbr_t)
    )
    xhat2, scale2 = norm_parts(mixed2_ref[...])
    grad_mixed2 = norm_back(xhat2, scale2, vector(V_N2G), grad_fresh)
    grad_contracted = grad_mixed2.astype(BF16)
    for p in range(copies_ref.shape[0]):
        copies_ref[p, :rows] = grad_contracted
        copies_ref[p, rows:] = low_late_ref[...]
    grad_updated = grad_mixed2
    for c in range(hidden // width):
        cols = slice(c * width, (c + 1) * width)
        copies[c][0].wait()
        pre = dot_nt(grad_contracted, contract_ref[cols, :]) * slope_ref[:, cols]
        copies[c][1].wait()
        grad_updated = grad_updated + dot_nt(pre.astype(BF16), expand_ref[:, cols])
    xhat1, scale1 = norm_parts(mixed1_ref[...])
    grad_mixed1 = norm_back(xhat1, scale1, vector(V_N1G), grad_updated)
    grad_mixed1_ref[...] = grad_mixed1
    grad_message = (grad_mixed1 / counts).astype(BF16)
    spread_ref[...] = dot_nt(grad_message, w3_ref[...])
    pack_ref[:width, :] = dot_split(dot_tn, act_sum_ref[...], grad_message).astype(BF16)
    vectors = [
        total(counts * grad_message.astype(F32)),
        total(grad_updated * xhat1),
        total(grad_updated),
        total(grad_fresh * xhat2),
        total(grad_fresh),
        edge_vec_ref[...],
    ]
    vectors = jnp.concatenate(vectors, axis=0)
    vectors = jnp.concatenate(
        [vectors, jnp.zeros((pack_ref.shape[0] - width - vectors.shape[0], width), F32)], axis=0
    )
    pack_ref[width:, :] = vectors.astype(BF16)


def feed_weight_kernel(early_ref, late_ref, expand_ref, bias_ref, contract_ref, *refs, more):
    sums_in = refs[:4] if more else None
    expand_out_ref, contract_out_ref, bias_out_ref, last_bias_ref = refs[-8:-4]
    low_ref, grad_ref, low_turned_ref, grad_turned_ref = refs[-4:]
    early = early_ref.shape[1]
    each = (early + late_ref.shape[1]) // 2
    chunk = pl.program_id(1)
    ones = jnp.ones((8, low_ref.shape[0]), F32).astype(BF16)

    @pl.when(chunk == 0)
    def _():
        for p in range(early_ref.shape[0]):
            low_ref[p * each : p * each + early] = early_ref[p]
            low_ref[p * each + early : (p + 1) * each] = late_ref[p, each:]
            grad_ref[p * each : (p + 1) * each] = late_ref[p, :each]
        low_turned_ref[...] = low_ref[...].T
        grad_turned_ref[...] = grad_ref[...].T

    act, slope = gelu_pair(dot_nn(low_ref[...], expand_ref[...]) + bias_ref[0:1, :])
    act = act.astype(BF16)
    pre = (dot_nt(grad_ref[...], contract_ref[...]) * slope).astype(BF16)
    expanded = dot_nn(low_turned_ref[...], pre)
    contracted = dot_nn(grad_turned_ref[...], act).T
    sums = dot_nn(ones, pre)
    if more:
        expanded = expanded + sums_in[0][...]
        contracted = contracted + sums_in[1][...]
        sums = sums + sums_in[2][...]
    expand_out_ref[...] = expanded
    contract_out_ref[...] = contracted
    bias_out_ref[...] = sums

    @pl.when(chunk == 0)
    def _():
        last = dot_nn(ones, grad_ref[...])
        last_bias_ref[...] = last + sums_in[3][...] if more else last


def message_kernel(
    core_ref,
    edge_ref,
    pos_ref,
    act1_ref,
    slope1_ref,
    slope2_ref,
    partial_ref,
    spread_ref,
    table_ref,
    w1_a_ref,
    w1_b_ref,
    w1_c_ref,
    w2_ref,
    edge_pack_ref,
    feed_pack_ref,
    grad_ref,
    first_ref,
    own_ref,
    away_ref,
    send_ref,
    keep_ref,
    joint_ref,
    dw2_ref,
    bias2_ref,
    w2_turned_ref,
    w1_turned_ref,
):
    step = pl.program_id(0)
    last = pl.num_programs(0) - 1
    slots, rows, edge_width = edge_ref.shape
    width = act1_ref.shape[1]
    block = slots * rows
    table_rows = table_ref.shape[0]

    @pl.when(step == 0)
    def _():
        for ref in (joint_ref, dw2_ref, bias2_ref, first_ref):
            ref[...] = jnp.zeros_like(ref)
        w2_turned_ref[...] = w2_ref[...].T
        w1_parts = [ref[...] for ref in (w1_a_ref, w1_b_ref, w1_c_ref)]
        w1_turned_ref[...] = jnp.concatenate(w1_parts, axis=0).T

    spread = spread_ref[...]
    grad2 = []
    bias2 = bias2_ref[...]
    for k in range(slots):
        part = (spread * slope2_ref[pl.ds(k * rows, rows), :].astype(F32)).astype(BF16)
        bias2 = bias2 + part.astype(F32)
        grad2.append(part)
    bias2_ref[...] = bias2
    grad2 = jnp.concatenate(grad2, axis=0)
    dw2_ref[...] += dot_tn(act1_ref[...], grad2)
    grad1 = (dot_nn(grad2, w2_turned_ref[...]) * slope1_ref[...].astype(F32)).astype(BF16)
    first_ref[...] += jnp.sum(grad1.astype(F32).reshape(slots, rows, width), axis=0)
    onehot = edge_onehot(pos_ref, table_rows)
    features = edge_ref[...].reshape(block, edge_width)
    joint_ref[...] += dot_tn(jnp.concatenate([onehot, features], axis=1), grad1)
    grad_ref[...] = partial_ref[...] + dot_nn(grad1, w1_turned_ref[...]).reshape(
        slots, rows, edge_width
    )

    @pl.when(step == last)
    def _():
        first = first_ref[...]
        back = joint_ref[:table_rows]
        own_ref[...] = back[:rows]
        away_ref[...] = back[rows:].astype(BF16)
        own_grad = dot_split_right(dot_tn, table_ref[:rows], first).astype(BF16)
        nbr_grad = dot_split_right(dot_tn, table_ref[...], back).astype(BF16)
        vectors = [
            feed_pack_ref[width:].astype(F32),
            jnp.sum(first, axis=0, keepdims=True),
            jnp.sum(bias2_ref[...], axis=0, keepdims=True),
        ]
        lower = [own_grad, nbr_grad, feed_pack_ref[:width]]
        upper = [joint_ref[table_rows:].astype(BF16), dw2_ref[...].astype(BF16), edge_pack_ref[...]]

        def fill(ref, pieces, tail):
            base = 0
            for piece in pieces:
                ref[base : base + piece.shape[0]] = piece
                base += piece.shape[0]
            if base < ref.shape[0]:
                gap = ref.shape[0] - base - sum(v.shape[0] for v in tail)
                rest = jnp.concatenate(tail + [jnp.zeros((gap, width), F32)], axis=0)
                ref[base:] = rest.astype(BF16)

        @pl.when(core_ref[0] == 0)
        def _():
            fill(keep_ref, lower, [])
            fill(send_ref, upper, vectors)

        @pl.when(core_ref[0] != 0)
        def _():
            fill(send_ref, lower, [])
            fill(keep_ref, upper, vectors)


def wrapped(value, size):
    value = jnp.where(value >= size, value - size, value)
    return jnp.where(value < 0, value + size, value)


def pick_of(index, values):
    result = values[0]
    for i in range(1, len(values)):
        result = jnp.where(index == i, values[i], result)
    return result


def pair_kernel(y_ref, x_ref, keep_ref, came_ref, away_ref, *out_refs, parts, cap):
    y_size = lax.axis_size("y")
    x_size = lax.axis_size("x")
    z_size = parts // x_size
    riders = z_size * cap
    share = keep_ref.shape[0] // len(out_refs)
    away = away_ref[...].astype(F32)
    for e, out_ref in enumerate(out_refs):
        dy, dx = divmod(e, x_size)
        x = wrapped(x_ref[0] + dx, x_size)
        device = wrapped(y_ref[0] + dy, y_size) * x_size + x
        part = pl.ds(pl.multiple_of(device * share, 16), share)
        at = out_ref.shape[0] - share
        out_ref[at:] = (keep_ref[part, :].astype(F32) + came_ref[part, :].astype(F32)).astype(BF16)
        if at:
            rows = []
            for to in range(x_size):
                owners = [(z * x_size + to) * cap for z in range(z_size)]
                rows.append(jnp.concatenate([away[o : o + cap] for o in owners], axis=0))
            out_ref[:riders] = pick_of(x, rows).astype(BF16)


def plane_kernel(x_ref, z_ref, *refs, peers, cap):
    came_refs, out_refs = refs[:peers], refs[peers:]
    x_size = lax.axis_size("x")
    z_size = len(out_refs)
    riders = x_size * cap
    share = out_refs[0].shape[0] - riders
    first = z_size * cap
    rows = []
    for source in range(x_size):
        pieces = [ref[:first].astype(F32) for ref in came_refs[:x_size]]
        rows.append(pick_of(wrapped(x_ref[0] - source, x_size), pieces))
    for dz, out_ref in enumerate(out_refs):
        z = wrapped(z_ref[0] + dz, z_size)
        value = jnp.zeros((share, out_ref.shape[1]), F32)
        for e, ref in enumerate(came_refs):
            start = z * share + (first if e < x_size else 0)
            value = value + ref[pl.ds(pl.multiple_of(start, 16), share), :].astype(F32)
        out_ref[riders:] = value.astype(BF16)
        part = [
            pick_of(z, [value[i * cap : (i + 1) * cap] for i in range(z_size)]) for value in rows
        ]
        out_ref[:riders] = jnp.concatenate(part, axis=0).astype(BF16)


def column_kernel(z_ref, *refs):
    came_refs, total_ref, returned_ref = refs[:-2], refs[-2], refs[-1]
    z_size = len(came_refs)
    riders = returned_ref.shape[0] // z_size
    value = jnp.zeros(total_ref.shape, F32)
    for dz, ref in enumerate(came_refs):
        value = value + ref[riders:].astype(F32)
        start = wrapped(z_ref[0] - dz, z_size) * riders
        returned_ref[pl.ds(pl.multiple_of(start, 16), riders), :] = ref[:riders]
    total_ref[...] = value.astype(BF16)


def stack_kernel(z_ref, *refs):
    came_refs, out_ref = refs[:-1], refs[-1]
    share = came_refs[0].shape[0]
    for dz, ref in enumerate(came_refs):
        start = wrapped(z_ref[0] - dz, len(came_refs)) * share
        out_ref[pl.ds(pl.multiple_of(start, 16), share), :] = ref[...]


def node_grad_kernel(grad_ref, first_ref, own_ref, arrived_ref, asked_ref, w1_ref, out_ref):
    rows, width = grad_ref.shape
    back = own_ref[...] + dot_nn(asked_onehot(asked_ref, rows), arrived_ref[...])
    out_ref[...] = (
        grad_ref[...]
        + dot_split(dot_nt, first_ref[...], w1_ref[:width])
        + dot_split(dot_nt, back, w1_ref[width : 2 * width])
    )


def unpack_kernel(core_ref, y_ref, x_ref, *refs, peers):
    mine_refs, other_refs, refs = refs[:peers], refs[peers : 2 * peers], refs[2 * peers :]
    bias_ref, last_bias_ref = refs[:2]
    mine_ref, other_ref = refs[-2:]
    refs = refs[2:-2]
    x_size = lax.axis_size("x")
    share = mine_refs[0].shape[0]
    for e in range(peers):
        dy, dx = divmod(e, x_size)
        device = wrapped(y_ref[0] - dy, peers // x_size) * x_size + wrapped(x_ref[0] - dx, x_size)
        part = pl.ds(pl.multiple_of(device * share, 16), share)
        mine_ref[part, :] = mine_refs[e][...]
        other_ref[part, :] = other_refs[e][...]
    (
        message1_ref,
        message1_bias_ref,
        message2_ref,
        message2_bias_ref,
        message3_ref,
        message3_bias_ref,
        gain1_ref,
        shift1_ref,
        expand_bias_ref,
        contract_bias_ref,
        gain2_ref,
        shift2_ref,
        edge1_ref,
        edge1_bias_ref,
        edge2_ref,
        edge2_bias_ref,
        edge3_ref,
        edge3_bias_ref,
        gain3_ref,
        shift3_ref,
    ) = refs
    width = mine_ref.shape[1]
    edge_width = edge2_ref.shape[0]
    half = width // 2
    first_core = core_ref[0] == 0

    def lower(start, stop):
        return jnp.where(first_core, mine_ref[start:stop], other_ref[start:stop]).astype(F32)

    def upper(start, stop):
        return jnp.where(first_core, other_ref[start:stop], mine_ref[start:stop]).astype(F32)

    message1_ref[: 2 * width] = lower(0, 2 * width)
    message3_ref[...] = lower(2 * width, 3 * width)
    message1_ref[2 * width :] = upper(0, edge_width)
    base = edge_width
    message2_ref[...] = upper(base, base + width)
    base = base + width
    edge1_ref[:, :width] = upper(base, base + edge_width)
    edge1_ref[:, width : 2 * width] = upper(base + edge_width, base + 2 * edge_width)
    third = upper(base + 2 * edge_width, base + 3 * edge_width)
    edge1_ref[:, 2 * width :] = third[:, :edge_width]
    edge2_ref[...] = third[:, half : half + edge_width]
    edge3_ref[...] = upper(base + 3 * edge_width, base + 4 * edge_width)[:, :edge_width]
    base = base + 4 * edge_width
    vectors = upper(base, mine_ref.shape[0])
    targets = (message3_bias_ref, gain1_ref, shift1_ref, gain2_ref, shift2_ref)
    for i, ref in enumerate(targets):
        ref[...] = vectors[i]
    targets = (edge1_bias_ref, edge2_bias_ref, edge3_bias_ref, gain3_ref, shift3_ref)
    for i, ref in enumerate(targets):
        ref[...] = vectors[5 + i, :edge_width]
    message1_bias_ref[...] = vectors[16]
    message2_bias_ref[...] = vectors[17]
    expand_bias_ref[...] = bias_ref[0]
    contract_bias_ref[...] = last_bias_ref[0]


def gather_copies(copies, axes):
    return lax.all_to_all(copies, axes, split_axis=0, concat_axis=0, tiled=True)


def copies_of(values, axes):
    return jnp.broadcast_to(values[None], (lax.axis_size(axes), *values.shape))


def exchange(values, parts):
    grouped = values.reshape(parts, values.shape[0] // parts, values.shape[1])
    arrived = lax.all_to_all(grouped, RES, split_axis=0, concat_axis=0, tiled=True)
    return arrived.reshape(values.shape)


def move(values, dy=0, dz=0, dx=0):
    sizes = [lax.axis_size(axis) for axis in SIDE]
    pairs = []
    for i in range(math.prod(sizes)):
        rest, x = divmod(i, sizes[2])
        y, z = divmod(rest, sizes[1])
        to_y, to_z, to_x = (y + dy) % sizes[0], (z + dz) % sizes[1], (x + dx) % sizes[2]
        pairs.append((i, (to_y * sizes[1] + to_z) * sizes[2] + to_x))
    return lax.ppermute(values, SIDE, pairs)


def other_core(values):
    return lax.ppermute(values, "core", [(0, 1), (1, 0)])


def whole(shape):
    return pl.BlockSpec(shape, lambda *_: (0,) * len(shape))


def params(mebibytes):
    return pltpu.CompilerParams(vmem_limit_bytes=mebibytes * MIB)


def cost(microseconds):
    return pl.CostEstimate(
        flops=int(microseconds * 1.15e9),
        bytes_accessed=int(microseconds * 3.69e6),
        transcendentals=0,
    )


def body(
    node_states,
    edge_states,
    neighbour_index,
    edge_mask,
    node_cotangent,
    edge_cotangent,
    message_weight1,
    message_bias1,
    message_weight2,
    message_bias2,
    message_weight3,
    message_bias3,
    norm1_gain,
    norm1_shift,
    expand_weight,
    expand_bias,
    contract_weight,
    contract_bias,
    norm2_gain,
    norm2_shift,
    edge_weight1,
    edge_bias1,
    edge_weight2,
    edge_bias2,
    edge_weight3,
    edge_bias3,
    norm3_gain,
    norm3_shift,
):
    self_rows = node_states[0]
    rows, width = self_rows.shape
    slots = neighbour_index.shape[2]
    edge_width = edge_states.shape[3]
    hidden = expand_weight.shape[1]
    edges = rows * slots
    parts = lax.axis_size(RES)
    cap = ROW_CAP
    table_rows = rows + parts * cap
    side = lax.axis_size(SIDE)
    steps = STEPS
    block_slots = slots // steps
    block = block_slots * rows
    pairs = block // LANES

    everyone = gather_copies(copies_of(self_rows, RES), RES).reshape(parts * rows, width)
    core = lax.axis_index("core").astype(jnp.int32).reshape(1)
    me = lax.axis_index(RES).astype(jnp.int32).reshape(1)
    edge_rows = edge_states[0].transpose(1, 0, 2)
    edge_cot = edge_cotangent[0].transpose(1, 0, 2)
    slot_index = neighbour_index.transpose(2, 0, 1)
    slot_mask = edge_mask.transpose(2, 0, 1)
    edge_w1t = edge_weight1.T
    wide = (
        message_bias1,
        message_bias2,
        message_bias3,
        norm1_gain,
        norm1_shift,
        contract_bias,
        norm2_gain,
        norm2_shift,
        expand_bias,
    )
    narrow = (edge_bias1, edge_bias2, edge_bias3, norm3_gain, norm3_shift)
    vmem = pl.BlockSpec(memory_space=pltpu.VMEM)

    def shape(dims, kind):
        return jax.ShapeDtypeStruct(dims, kind)

    pos, select, ids, counts, vectors, bias_row = pl.pallas_call(
        functools.partial(
            prepare_kernel, parts=parts, cap=cap, steps=steps, wide=len(wide), narrow=len(narrow)
        ),
        out_shape=(
            shape((steps, LANES, pairs), jnp.int32),
            shape((parts * rows, table_rows), BF16),
            shape((parts, cap), jnp.int32),
            shape((rows, width), F32),
            shape((V_ROWS, width), F32),
            shape((1, hidden), F32),
        ),
        in_specs=[pl.BlockSpec(memory_space=pltpu.SMEM)] + [vmem] * (2 + len(wide) + len(narrow)),
        out_specs=(vmem,) * 6,
        compiler_params=params(56),
        cost_estimate=cost(6),
        name="prepare",
    )(me, slot_index, slot_mask, *wide, *narrow)
    ids, everyone = lax.optimization_barrier((ids, everyone))
    asked = lax.all_to_all(ids, RES, split_axis=0, concat_axis=0, tiled=True)

    edge_spec = pl.BlockSpec((block_slots, rows, edge_width), lambda i: (i, 0, 0))
    flat_spec = pl.BlockSpec((block, width), lambda i: (i, 0))
    pos_spec = pl.BlockSpec((1, LANES, pairs), lambda i: (i, 0, 0))
    any_spec = pl.BlockSpec(memory_space=pl.ANY)
    node_spec = whole((rows, width))
    away_spec = whole((parts * cap, width))

    (
        act1,
        slope1,
        slope2,
        fresh,
        table,
        mixed1,
        mixed2,
        low,
        low_late,
        slope_e,
        act_sum,
    ) = pl.pallas_call(
        node_kernel,
        grid=(steps,),
        in_specs=[
            edge_spec,
            pos_spec,
            whole((parts * rows, table_rows)),
            whole((parts * rows, width)),
            node_spec,
            node_spec,
            whole((V_ROWS, width)),
            whole(message_weight1.shape),
            whole((width, width)),
            whole((width, width)),
            any_spec,
            any_spec,
        ],
        out_specs=[
            flat_spec,
            flat_spec,
            flat_spec,
            node_spec,
            whole((table_rows, width)),
            node_spec,
            node_spec,
            whole((side, EARLY_ROWS, width)),
            whole((rows - EARLY_ROWS, width)),
            whole((rows, hidden)),
            node_spec,
        ],
        out_shape=[
            shape((edges, width), BF16),
            shape((edges, width), BF16),
            shape((edges, width), BF16),
            shape((rows, width), BF16),
            shape((table_rows, width), BF16),
            shape((rows, width), F32),
            shape((rows, width), F32),
            shape((side, EARLY_ROWS, width), BF16),
            shape((rows - EARLY_ROWS, width), BF16),
            shape((rows, hidden), F32),
            shape((rows, width), F32),
        ],
        scratch_shapes=[
            pltpu.VMEM((table_rows, width), BF16),
            pltpu.VMEM((rows, width), F32),
            pltpu.VMEM((width, hidden), BF16),
            pltpu.VMEM((hidden, width), BF16),
            pltpu.SemaphoreType.DMA((2,)),
        ],
        compiler_params=params(56),
        cost_estimate=cost(26),
        name="node_forward",
    )(
        edge_rows,
        pos,
        select,
        everyone,
        self_rows,
        counts,
        vectors,
        message_weight1,
        message_weight2,
        message_weight3,
        expand_weight,
        contract_weight,
    )
    outgoing = pl.pallas_call(
        pick_kernel,
        in_specs=[vmem] * 2,
        out_specs=vmem,
        out_shape=shape((parts * cap, width), BF16),
        compiler_params=params(8),
        cost_estimate=cost(1),
        name="pick",
    )(asked, fresh)
    incoming = exchange(outgoing, parts)
    low_mine = gather_copies(low, SIDE)

    edge_pack_rows = 4 * edge_width
    edge_out, grad_partial, edge_first, edge_own, edge_away, edge_pack, edge_vec = pl.pallas_call(
        edge_kernel,
        grid=(steps,),
        in_specs=[
            edge_spec,
            edge_spec,
            pos_spec,
            node_spec,
            away_spec,
            node_spec,
            whole((V_ROWS, width)),
            whole(edge_w1t.shape),
            whole((edge_width, edge_width)),
            whole((edge_width, edge_width)),
        ],
        out_specs=[
            edge_spec,
            edge_spec,
            whole((rows, edge_width)),
            whole((rows, edge_width)),
            whole((parts * cap, edge_width)),
            whole((edge_pack_rows, width)),
            whole((8, width)),
        ],
        out_shape=[
            shape((slots, rows, edge_width), BF16),
            shape((slots, rows, edge_width), F32),
            shape((rows, edge_width), F32),
            shape((rows, edge_width), F32),
            shape((parts * cap, edge_width), BF16),
            shape((edge_pack_rows, width), BF16),
            shape((8, width), F32),
        ],
        scratch_shapes=[
            pltpu.VMEM((table_rows, width), BF16),
            pltpu.VMEM((table_rows, edge_width), BF16),
            pltpu.VMEM((rows, edge_width), F32),
            pltpu.VMEM((table_rows, edge_width), F32),
            pltpu.VMEM((edge_width, edge_width), F32),
            pltpu.VMEM((edge_width, edge_width), F32),
            pltpu.VMEM((edge_width, edge_width), F32),
            pltpu.VMEM((5, rows, edge_width), F32),
            pltpu.VMEM((3, edge_width, edge_width), BF16),
        ],
        compiler_params=params(56),
        cost_estimate=cost(1),
        name="edge_both",
    )(
        edge_rows,
        edge_cot,
        pos,
        fresh,
        incoming,
        counts,
        vectors,
        edge_w1t,
        edge_weight2,
        edge_weight3,
    )
    edge_away, low_mine = lax.optimization_barrier((edge_away, low_mine))
    edge_arrived = exchange(edge_away, parts)

    feed_rows = width + 16
    feed_pack, grad_copies, spread, grad_mixed1 = pl.pallas_call(
        feed_kernel,
        in_specs=[vmem] * 12 + [any_spec] * 2 + [vmem] * 3,
        out_specs=[vmem] * 4,
        out_shape=[
            shape((feed_rows, width), BF16),
            shape((side, 2 * rows - EARLY_ROWS, width), BF16),
            shape((rows, width), F32),
            shape((rows, width), F32),
        ],
        scratch_shapes=[
            pltpu.VMEM((width, hidden), BF16),
            pltpu.VMEM((hidden, width), BF16),
            pltpu.SemaphoreType.DMA((2 * hidden // width,)),
        ],
        compiler_params=params(56),
        cost_estimate=cost(7),
        name="feed_backward",
    )(
        node_cotangent[0],
        edge_first,
        edge_own,
        edge_arrived,
        asked,
        counts,
        vectors,
        edge_w1t,
        mixed1,
        mixed2,
        slope_e,
        act_sum,
        expand_weight,
        contract_weight,
        message_weight3,
        edge_vec,
        low_late,
    )
    grad_mine = gather_copies(grad_copies, SIDE)

    unit = 16 * side
    half_rows = (3 * width + unit - 1) // unit * unit
    third = edge_width // 3
    edge_grad, first, own, away, send, keep = pl.pallas_call(
        message_kernel,
        grid=(steps,),
        in_specs=[
            pl.BlockSpec(memory_space=pltpu.SMEM),
            edge_spec,
            pos_spec,
            flat_spec,
            flat_spec,
            flat_spec,
            edge_spec,
            node_spec,
            whole((table_rows, width)),
            *[
                pl.BlockSpec((third, width), lambda i, p=p: (2 * width // third + p, 0))
                for p in range(3)
            ],
            whole((width, width)),
            whole((edge_pack_rows, width)),
            whole((feed_rows, width)),
        ],
        out_specs=[
            edge_spec,
            node_spec,
            node_spec,
            away_spec,
            whole((half_rows, width)),
            whole((half_rows, width)),
        ],
        out_shape=[
            shape((slots, rows, edge_width), F32),
            shape((rows, width), F32),
            shape((rows, width), F32),
            shape((parts * cap, width), BF16),
            shape((half_rows, width), BF16),
            shape((half_rows, width), BF16),
        ],
        scratch_shapes=[
            pltpu.VMEM((table_rows + edge_width, width), F32),
            pltpu.VMEM((width, width), F32),
            pltpu.VMEM((rows, width), F32),
            pltpu.VMEM((width, width), BF16),
            pltpu.VMEM((width, edge_width), BF16),
        ],
        compiler_params=params(56),
        cost_estimate=cost(14),
        name="message_backward",
    )(
        core,
        edge_rows,
        pos,
        act1,
        slope1,
        slope2,
        grad_partial,
        spread,
        table,
        message_weight1,
        message_weight1,
        message_weight1,
        message_weight2,
        edge_pack,
        feed_pack,
    )
    came = other_core(send)
    y_size = lax.axis_size("y")
    x_size = lax.axis_size("x")
    z_size = lax.axis_size("z")
    my_y = lax.axis_index("y").astype(jnp.int32).reshape(1)
    peers = y_size * x_size
    smem = pl.BlockSpec(memory_space=pltpu.SMEM)
    my_x = lax.axis_index("x").astype(jnp.int32).reshape(1)
    my_z = lax.axis_index("z").astype(jnp.int32).reshape(1)
    share = half_rows // peers
    steps_of = [divmod(e, x_size) for e in range(peers)]
    pieces = pl.pallas_call(
        functools.partial(pair_kernel, parts=parts, cap=cap),
        in_specs=[smem] * 2 + [vmem] * 3,
        out_specs=[vmem] * peers,
        out_shape=[
            shape((share if dy else share + z_size * cap, width), BF16) for dy, _ in steps_of
        ],
        compiler_params=params(20),
        cost_estimate=cost(3),
        name="pair_sum",
    )(my_y, my_x, keep, came, away)
    _, grad_mine, low_mine = lax.optimization_barrier((pieces[0], grad_mine, low_mine))

    def over_plane(values):
        came = [values[0]]
        for value, (dy, dx) in zip(values[1:], steps_of[1:]):
            came.append(move(value, dy=dy, dx=dx))
        return came

    def over_z(values):
        return [values[0]] + [move(value, dz=d) for d, value in enumerate(values[1:], start=1)]

    arrived = over_plane(pieces)
    grad_other = other_core(grad_mine)
    low_other = other_core(low_mine)

    def feed_weights(early, late, sums):
        units = 256
        block_rows = early.shape[0] * rows
        sum_specs = [
            pl.BlockSpec((width, units), lambda _, c: (0, c)),
            pl.BlockSpec((units, width), lambda _, c: (c, 0)),
            pl.BlockSpec((8, units), lambda _, c: (0, c)),
            whole((8, width)),
        ]
        return pl.pallas_call(
            functools.partial(feed_weight_kernel, more=bool(sums)),
            grid=(1, hidden // units),
            in_specs=[
                whole(early.shape),
                whole(late.shape),
                sum_specs[0],
                pl.BlockSpec((1, units), lambda _, c: (0, c)),
                sum_specs[1],
                *(sum_specs if sums else []),
            ],
            out_specs=sum_specs,
            out_shape=[
                shape((width, hidden), F32),
                shape((hidden, width), F32),
                shape((8, hidden), F32),
                shape((8, width), F32),
            ],
            scratch_shapes=[
                pltpu.VMEM((block_rows, width), BF16),
                pltpu.VMEM((block_rows, width), BF16),
                pltpu.VMEM((width, block_rows), BF16),
                pltpu.VMEM((width, block_rows), BF16),
            ],
            compiler_params=params(56),
            cost_estimate=cost(12),
            name="feed_weights_more" if sums else "feed_weights",
        )(early, late, expand_weight, bias_row, contract_weight, *sums)

    def feed_side(early, late, sums):
        group = min(side, 16)
        for at in range(0, side, group):
            sums = tuple(feed_weights(early[at : at + group], late[at : at + group], sums))
        return sums

    sums = feed_side(low_mine, grad_mine, ())
    arrived, sums = lax.optimization_barrier((arrived, sums))
    pieces = pl.pallas_call(
        functools.partial(plane_kernel, peers=peers, cap=cap),
        in_specs=[smem] * 2 + [vmem] * peers,
        out_specs=[vmem] * z_size,
        out_shape=[shape((half_rows // side + x_size * cap, width), BF16)] * z_size,
        compiler_params=params(16),
        cost_estimate=cost(3),
        name="plane_sum",
    )(my_x, my_z, *arrived)
    total, returned = pl.pallas_call(
        column_kernel,
        in_specs=[smem] + [vmem] * z_size,
        out_specs=[vmem] * 2,
        out_shape=[
            shape((half_rows // side, width), BF16),
            shape((parts * cap, width), BF16),
        ],
        compiler_params=params(8),
        cost_estimate=cost(1),
        name="column_sum",
    )(my_z, *over_z(pieces))
    column = pl.pallas_call(
        stack_kernel,
        in_specs=[smem] + [vmem] * z_size,
        out_specs=vmem,
        out_shape=shape((share, width), BF16),
        compiler_params=params(8),
        cost_estimate=cost(1),
        name="stack",
    )(my_z, *over_z([total] * z_size))
    _, grad_other, low_other, sums = lax.optimization_barrier((column, grad_other, low_other, sums))
    mine = over_plane([column] * peers)
    other_first = other_core(column)
    sums = feed_side(low_other, grad_other, tuple(sums))
    mine, other_first, sums = lax.optimization_barrier((mine, other_first, sums))
    grad_expand, grad_contract, expand_bias_sum, contract_bias_sum = sums
    other = [other_first] + [other_core(value) for value in mine[1:]]
    node_grad = pl.pallas_call(
        node_grad_kernel,
        in_specs=[vmem] * 6,
        out_specs=vmem,
        out_shape=shape((rows, width), F32),
        compiler_params=params(12),
        cost_estimate=cost(3),
        name="node_gradient",
    )(grad_mixed1, first, own, returned, asked, message_weight1)

    vec = shape((width,), F32)
    thin = shape((edge_width,), F32)
    square = shape((width, width), F32)
    small = shape((edge_width, edge_width), F32)
    (
        grad_message1,
        grad_mb1,
        grad_message2,
        grad_mb2,
        grad_message3,
        grad_mb3,
        grad_n1g,
        grad_n1s,
        grad_eb,
        grad_cb,
        grad_n2g,
        grad_n2s,
        grad_edge1_t,
        grad_eb1,
        grad_edge2,
        grad_eb2,
        grad_edge3,
        grad_eb3,
        grad_n3g,
        grad_n3s,
    ) = pl.pallas_call(
        functools.partial(unpack_kernel, peers=peers),
        in_specs=[smem] * 3 + [vmem] * (2 * peers + 2),
        out_specs=[vmem] * 20,
        out_shape=[
            shape(message_weight1.shape, F32),
            vec,
            square,
            vec,
            square,
            vec,
            vec,
            vec,
            shape((hidden,), F32),
            vec,
            vec,
            vec,
            shape(edge_w1t.shape, F32),
            thin,
            small,
            thin,
            small,
            thin,
            thin,
            thin,
        ],
        scratch_shapes=[pltpu.VMEM((half_rows, width), BF16)] * 2,
        compiler_params=params(24),
        cost_estimate=cost(4),
        name="unpack",
    )(core, my_y, my_x, *mine, *other, expand_bias_sum, contract_bias_sum)
    return (
        fresh[None],
        edge_out.transpose(1, 0, 2)[None],
        node_grad[None],
        edge_grad.transpose(1, 0, 2)[None],
        grad_message1,
        grad_mb1,
        grad_message2,
        grad_mb2,
        grad_message3,
        grad_mb3,
        grad_n1g,
        grad_n1s,
        grad_expand,
        grad_eb,
        grad_contract,
        grad_cb,
        grad_n2g,
        grad_n2s,
        grad_edge1_t.T,
        grad_eb1,
        grad_edge2,
        grad_eb2,
        grad_edge3,
        grad_eb3,
        grad_n3g,
        grad_n3s,
    )


def solution(mesh):
    batch, res = mesh.shape["batch"], mesh.shape["res"]
    x_size = 1 << ((res.bit_length() - 1) // 2)
    sizes = (batch // CORES, CORES, res // x_size, x_size)
    fine = jax.sharding.Mesh(mesh.devices.reshape(sizes), ALL)
    row_spec = P(("y", "core"), RES, None)
    edge_spec = P(("y", "core"), RES, None, None)
    return jax.shard_map(
        body,
        mesh=fine,
        in_specs=(row_spec, edge_spec, row_spec, row_spec, row_spec, edge_spec) + (P(),) * 22,
        out_specs=(row_spec, edge_spec, row_spec, edge_spec) + (P(),) * 22,
        check_vma=False,
    )
```

```python
import functools
import math

import jax
import jax.numpy as jnp
from jax import lax
from jax.experimental import pallas as pl
from jax.experimental.pallas import tpu as pltpu
from jax.sharding import PartitionSpec as P

ROW_CAP = 8
CORES = 2
RES = ("z", "x")
PLANE = ("y", "x")
SIDE = ("y", "z", "x")
BY_COLUMN = ("y", "x", "z")
ALL = ("y", "core", "z", "x")
EPSILON = 1e-05
LANES = 128
MIB = 1024 * 1024
STEPS = 3
F32 = jnp.float32
BF16 = jnp.bfloat16

V_MB1, V_MB2, V_MB3, V_N1G, V_N1S, V_CB, V_N2G, V_N2S, V_EB = range(9)
V_EDGE = 12
V_ROWS = 24


def dot_nn(left, right):
    return lax.dot_general(left, right, (((1,), (0,)), ((), ())), preferred_element_type=F32)


def dot_nt(left, right):
    return lax.dot_general(left, right, (((1,), (1,)), ((), ())), preferred_element_type=F32)


def dot_tn(left, right):
    return lax.dot_general(left, right, (((0,), (0,)), ((), ())), preferred_element_type=F32)


def split_low(values):
    high = values.astype(BF16)
    return high, (values - high.astype(F32)).astype(BF16)


def dot_split(dot, left, right):
    high, rest = split_low(left)
    return dot(high, right) + dot(rest, right)


def dot_split_right(dot, left, right):
    high, rest = split_low(right)
    return dot(left, high) + dot(left, rest)


def gelu_pair(v):
    e = jnp.exp2((v * v) * (-0.5 * math.log2(math.e)))
    phi_sum = 0.5 + 0.5 * lax.erf(v * math.sqrt(0.5))
    return v * phi_sum, phi_sum + (v * (1.0 / math.sqrt(2.0 * math.pi))) * e


def norm_parts(values):
    average = jnp.mean(values, axis=-1, keepdims=True)
    centred = values - average
    variance = jnp.mean(centred * centred, axis=-1, keepdims=True)
    scale = lax.rsqrt(variance + EPSILON)
    return centred * scale, scale


def norm_back(xhat, scale, gain, upstream):
    w = upstream * gain
    mean_w = jnp.mean(w, axis=-1, keepdims=True)
    mean_wx = jnp.mean(w * xhat, axis=-1, keepdims=True)
    return (w - mean_w - xhat * mean_wx) * scale


def edge_onehot(pos_ref, table_rows):
    pairs = pos_ref.shape[2]
    lane = lax.broadcasted_iota(jnp.int32, (LANES, table_rows), 1)
    return jnp.concatenate(
        [(pos_ref[0, :, p : p + 1] == lane).astype(F32).astype(BF16) for p in range(pairs)], axis=0
    )


def prepare_kernel(me_ref, idx_ref, mask_ref, *refs, parts, cap, steps, wide, narrow):
    wide_refs = refs[:wide]
    narrow_refs = refs[wide : wide + narrow]
    pos_ref, select_ref, ids_ref, count_ref, vec_ref, expand_bias_ref = refs[wide + narrow :]
    rows, width = count_ref.shape
    total = rows * parts
    table = rows + parts * cap
    me = me_ref[0]
    pair_rows = idx_ref.shape[0] // 2
    named = [
        jnp.concatenate([idx_ref[2 * j], idx_ref[2 * j + 1]], axis=1) for j in range(pair_rows)
    ]
    residue = lax.broadcasted_iota(jnp.int32, (total, LANES), 0)
    owner = residue // rows
    within = residue - owner * rows
    hits = jnp.zeros((total, LANES), F32)
    for j in range(pair_rows):
        hits = jnp.where(named[j] == residue, 1.0, hits)
    hit = jnp.max(hits, axis=1, keepdims=True)
    own = owner == me
    wanted = jnp.where(own, 0.0, jnp.broadcast_to(hit, (total, LANES)))
    low_row = lax.broadcasted_iota(jnp.int32, (rows, rows), 0)
    low_col = lax.broadcasted_iota(jnp.int32, (rows, rows), 1)
    lower = (low_col <= low_row).astype(F32).astype(BF16)
    wanted_low = wanted.astype(BF16)
    place = jnp.concatenate(
        [dot_nn(lower, wanted_low[o * rows : (o + 1) * rows]) for o in range(parts)], axis=0
    )
    place = jnp.clip(place - 1.0, 0.0, cap - 1.0)
    pos = jnp.where(own, within.astype(F32), (rows + owner * cap).astype(F32) + place)
    picked = [
        jnp.sum(jnp.where(named[j] == residue, pos, 0.0), axis=0, keepdims=True)
        for j in range(pair_rows)
    ]
    picked.append(jnp.zeros((LANES - pair_rows, LANES), F32))
    turned = jnp.concatenate(picked, axis=0).T.astype(jnp.int32)
    per = pair_rows // steps
    for s in range(steps):
        pos_ref[s] = turned[:, s * per : (s + 1) * per]
    lane = lax.broadcasted_iota(jnp.int32, (total, table), 1).astype(F32)
    live = jnp.where(own, 1.0, wanted)
    chosen = jnp.where(lane == pos[:, :1], jnp.broadcast_to(live[:, :1], (total, table)), 0.0)
    select_ref[...] = chosen.astype(BF16)
    asked_row = jnp.broadcast_to(within[:, :1].astype(F32), (total, parts * cap))
    ids = jnp.sum(chosen[:, rows:] * asked_row, axis=0, keepdims=True)
    ids = ids.astype(jnp.int32)
    for o in range(parts):
        ids_ref[o : o + 1, :] = ids[:, o * cap : (o + 1) * cap]
    count = mask_ref[0]
    for k in range(1, mask_ref.shape[0]):
        count = count + mask_ref[k]
    count = jnp.concatenate([count.astype(F32), jnp.zeros((7, rows), F32)], axis=0)
    count_ref[...] = dot_tn(count.astype(BF16), jnp.ones((8, width), F32).astype(BF16))
    expand_bias_ref[...] = wide_refs[-1][...].astype(F32).reshape(expand_bias_ref.shape)
    vec_ref[...] = jnp.zeros_like(vec_ref)
    at = 0
    for ref in wide_refs:
        for c in range(ref.shape[0] // width):
            part = ref[c * width : (c + 1) * width]
            vec_ref[at : at + 1, :] = part.astype(F32).reshape(1, width)
            at += 1
    for ref in narrow_refs:
        vec_ref[at : at + 1, : ref.shape[0]] = ref[...].astype(F32).reshape(1, ref.shape[0])
        at += 1


def node_kernel(
    edge_ref,
    pos_ref,
    select_ref,
    all_ref,
    self_ref,
    count_ref,
    vec_ref,
    w1_ref,
    w2_ref,
    w3_ref,
    expand_hbm,
    contract_hbm,
    act1_ref,
    slope1_ref,
    slope2_ref,
    fresh_ref,
    table_ref,
    mixed1_ref,
    mixed2_ref,
    low_ref,
    slope_e_ref,
    act_sum_ref,
    proj_ref,
    self_pre_ref,
    expand_ref,
    contract_ref,
    sems,
):
    step = pl.program_id(0)
    last = pl.num_programs(0) - 1
    rows, width = self_ref.shape
    slots = edge_ref.shape[0]
    edge_width = edge_ref.shape[2]
    table_rows = table_ref.shape[0]
    expand_copy = pltpu.make_async_copy(expand_hbm, expand_ref, sems.at[0])
    contract_copy = pltpu.make_async_copy(contract_hbm, contract_ref, sems.at[1])

    @pl.when(step == 0)
    def _():
        expand_copy.start()
        contract_copy.start()
        table = dot_tn(select_ref[...], all_ref[...]).astype(BF16)
        table_ref[...] = table
        proj_ref[...] = dot_nn(table, w1_ref[width : 2 * width]).astype(BF16)
        self_pre_ref[...] = (
            dot_nn(self_ref[...], w1_ref[:width]) + vec_ref[V_MB1 : V_MB1 + 1, :]
        )
        act_sum_ref[...] = jnp.zeros_like(act_sum_ref)

    onehot = edge_onehot(pos_ref, table_rows)
    features = edge_ref[...].reshape(slots * rows, edge_width)
    pre1 = dot_nn(features, w1_ref[2 * width :]) + dot_nn(onehot, proj_ref[...])
    self_pre = self_pre_ref[...]
    act1 = []
    for k in range(slots):
        part = pl.ds(k * rows, rows)
        act, slope = gelu_pair(pre1[k * rows : (k + 1) * rows] + self_pre)
        act = act.astype(BF16)
        act1.append(act)
        act1_ref[part, :] = act
        slope1_ref[part, :] = slope.astype(BF16)
    pre2 = dot_nn(jnp.concatenate(act1, axis=0), w2_ref[...])
    bias2 = vec_ref[V_MB2 : V_MB2 + 1, :]
    act_sum = act_sum_ref[...]
    counts = count_ref[...]
    for k in range(slots):
        act, slope = gelu_pair(pre2[k * rows : (k + 1) * rows] + bias2)
        valid = counts > (step * slots + k).astype(F32)
        act_sum = act_sum + jnp.where(valid, act.astype(BF16).astype(F32), 0.0)
        slope2_ref[pl.ds(k * rows, rows), :] = jnp.where(valid, slope, 0.0).astype(BF16)
    act_sum_ref[...] = act_sum

    @pl.when(step == last)
    def _():
        summed = dot_split(dot_nn, act_sum_ref[...], w3_ref[...])
        summed = summed + counts * vec_ref[V_MB3 : V_MB3 + 1, :]
        mixed1 = self_ref[...].astype(F32) + summed / counts
        mixed1_ref[...] = mixed1
        xhat1, _ = norm_parts(mixed1)
        updated = xhat1 * vec_ref[V_N1G : V_N1G + 1, :] + vec_ref[V_N1S : V_N1S + 1, :]
        low = updated.astype(BF16)
        low_ref[...] = low
        expand_copy.wait()
        contract_copy.wait()
        mixed2 = updated + vec_ref[V_CB : V_CB + 1, :]
        for c in range(expand_ref.shape[1] // width):
            cols = slice(c * width, (c + 1) * width)
            pre = dot_nn(low, expand_ref[:, cols]) + vec_ref[V_EB + c : V_EB + c + 1, :]
            act, slope = gelu_pair(pre)
            act = act.astype(BF16)
            slope_e_ref[:, cols] = slope
            mixed2 = mixed2 + dot_nn(act, contract_ref[cols, :])
        mixed2_ref[...] = mixed2
        xhat2, _ = norm_parts(mixed2)
        fresh = (xhat2 * vec_ref[V_N2G : V_N2G + 1, :] + vec_ref[V_N2S : V_N2S + 1, :]).astype(BF16)
        fresh_ref[...] = fresh


def asked_onehot(asked_ref, rows):
    parts = asked_ref.shape[0]
    asked = jnp.concatenate([asked_ref[o : o + 1, :] for o in range(parts)], axis=1)
    row = lax.broadcasted_iota(jnp.int32, (rows, asked.shape[1]), 0)
    return (asked == row).astype(F32).astype(BF16)


def pick_kernel(asked_ref, fresh_ref, out_ref):
    out_ref[...] = dot_tn(asked_onehot(asked_ref, fresh_ref.shape[0]), fresh_ref[...]).astype(BF16)


def edge_kernel(
    edge_ref,
    cot_ref,
    pos_ref,
    fresh_ref,
    incoming_ref,
    count_ref,
    vec_ref,
    w1t_ref,
    w2_ref,
    w3_ref,
    out_ref,
    grad_ref,
    first_ref,
    own_ref,
    away_ref,
    pack_ref,
    vec_out_ref,
    table_ref,
    proj_ref,
    self_pre_ref,
    back_ref,
    dw3_ref,
    dw2_ref,
    dw1_ref,
    sums_ref,
    turned_ref,
):
    step = pl.program_id(0)
    last = pl.num_programs(0) - 1
    rows, width = fresh_ref.shape
    slots, _, edge_width = edge_ref.shape
    block = slots * rows
    table_rows = table_ref.shape[0]
    own_t = w1t_ref[:, :width]
    nbr_t = w1t_ref[:, width : 2 * width]
    feat_t = w1t_ref[:, 2 * width :]

    def vector(i):
        return vec_ref[V_EDGE + i : V_EDGE + i + 1, :edge_width]

    @pl.when(step == 0)
    def _():
        table_ref[:rows] = fresh_ref[...]
        table_ref[rows:] = incoming_ref[...]
        proj_ref[...] = dot_nt(table_ref[...], nbr_t).astype(BF16)
        self_pre_ref[...] = dot_nt(fresh_ref[...], own_t) + vector(0)
        for ref in (back_ref, dw3_ref, dw2_ref, dw1_ref, sums_ref, first_ref):
            ref[...] = jnp.zeros_like(ref)
        turned_ref[0] = feat_t.T
        turned_ref[1] = w2_ref[...].T
        turned_ref[2] = w3_ref[...].T

    def flat(values):
        return values.reshape(block, edge_width)

    def deep(values):
        return values.reshape(slots, rows, edge_width)

    onehot = edge_onehot(pos_ref, table_rows)
    features = flat(edge_ref[...])
    pre1 = dot_nn(features, turned_ref[0]) + dot_nn(onehot, proj_ref[...])
    pre1 = deep(pre1) + self_pre_ref[...][None]
    act1, slope1 = gelu_pair(flat(pre1))
    act1 = act1.astype(BF16)
    pre2 = dot_nn(act1, w2_ref[...]) + vector(1)
    act2, slope2 = gelu_pair(pre2)
    act2 = act2.astype(BF16)
    mixed3 = features.astype(F32) + (dot_nn(act2, w3_ref[...]) + vector(2))
    xhat, scale = norm_parts(mixed3)
    gain = vector(3)
    slot = lax.broadcasted_iota(jnp.int32, (slots, rows, edge_width), 0) + step * slots
    valid = count_ref[...][None, :, :edge_width] > slot.astype(F32)
    out_ref[...] = jnp.where(valid, deep(xhat * gain + vector(4)), 0.0).astype(BF16)
    upstream = flat(jnp.where(valid, cot_ref[...].astype(F32), 0.0))
    sums_ref[3] += jnp.sum(deep(upstream * xhat), axis=0)
    sums_ref[4] += jnp.sum(deep(upstream), axis=0)
    grad_mixed = norm_back(xhat, scale, gain, upstream)
    grad_delta = grad_mixed.astype(BF16)
    dw3_ref[...] += dot_tn(act2, grad_delta)
    sums_ref[2] += jnp.sum(deep(grad_delta.astype(F32)), axis=0)
    grad2 = (dot_nn(grad_delta, turned_ref[2]) * slope2).astype(BF16)
    dw2_ref[...] += dot_tn(act1, grad2)
    sums_ref[1] += jnp.sum(deep(grad2.astype(F32)), axis=0)
    grad1 = (dot_nn(grad2, turned_ref[1]) * slope1).astype(BF16)
    dw1_ref[...] += dot_tn(grad1, features)
    first_ref[...] += jnp.sum(deep(grad1.astype(F32)), axis=0)
    back_ref[...] += dot_tn(onehot, grad1)
    grad_ref[...] = deep(grad_mixed + dot_nn(grad1, feat_t))

    @pl.when(step == last)
    def _():
        first = first_ref[...]
        back = back_ref[...]
        own_ref[...] = back[:rows]
        away_ref[...] = back[rows:].astype(BF16)
        first_high, first_rest = split_low(first)
        back_high, back_rest = split_low(back)
        own_grad = dot_tn(first_high, fresh_ref[...]) + dot_tn(first_rest, fresh_ref[...])
        nbr_grad = dot_tn(back_high, table_ref[...]) + dot_tn(back_rest, table_ref[...])
        pack_ref[:edge_width, :] = own_grad.astype(BF16)
        pack_ref[edge_width : 2 * edge_width, :] = nbr_grad.astype(BF16)
        pad = jnp.zeros((edge_width, width // 2 - edge_width), BF16)
        third = [dw1_ref[...].astype(BF16), pad, dw2_ref[...].astype(BF16), pad]
        pack_ref[2 * edge_width : 3 * edge_width, :] = jnp.concatenate(third, axis=1)
        fourth = [dw3_ref[...].astype(BF16), pad, jnp.zeros((edge_width, width // 2), BF16)]
        pack_ref[3 * edge_width :, :] = jnp.concatenate(fourth, axis=1)
        vec_out_ref[...] = jnp.zeros_like(vec_out_ref)
        vec_out_ref[0:1, :edge_width] = jnp.sum(first, axis=0, keepdims=True)
        for i in range(1, 5):
            vec_out_ref[i : i + 1, :edge_width] = jnp.sum(sums_ref[i], axis=0, keepdims=True)


def feed_kernel(
    cot_ref,
    first_ref,
    own_ref,
    arrived_ref,
    asked_ref,
    count_ref,
    vec_ref,
    w1t_ref,
    mixed1_ref,
    mixed2_ref,
    slope_ref,
    act_sum_ref,
    expand_hbm,
    contract_hbm,
    w3_ref,
    edge_vec_ref,
    pack_ref,
    copies_ref,
    spread_ref,
    grad_mixed1_ref,
    expand_ref,
    contract_ref,
    sems,
):
    rows, width = cot_ref.shape
    hidden = expand_ref.shape[1]
    own_t = w1t_ref[:, :width]
    nbr_t = w1t_ref[:, width : 2 * width]
    counts = count_ref[...]
    copies = []
    for c in range(hidden // width):
        rows_part, cols_part = pl.ds(c * width, width), pl.ds(c * width, width)
        copies.append(
            (
                pltpu.make_async_copy(
                    contract_hbm.at[rows_part, :], contract_ref.at[rows_part, :], sems.at[2 * c]
                ),
                pltpu.make_async_copy(
                    expand_hbm.at[:, cols_part], expand_ref.at[:, cols_part], sems.at[2 * c + 1]
                ),
            )
        )
    for pair in copies:
        for copy in pair:
            copy.start()

    def vector(i):
        return vec_ref[i : i + 1, :]

    def total(values):
        return jnp.sum(values.astype(F32), axis=0, keepdims=True)

    back = own_ref[...] + dot_nn(asked_onehot(asked_ref, rows), arrived_ref[...])
    grad_fresh = (
        cot_ref[...].astype(F32)
        + dot_split(dot_nn, first_ref[...], own_t)
        + dot_split(dot_nn, back, nbr_t)
    )
    xhat2, scale2 = norm_parts(mixed2_ref[...])
    grad_mixed2 = norm_back(xhat2, scale2, vector(V_N2G), grad_fresh)
    grad_contracted = grad_mixed2.astype(BF16)
    for p in range(copies_ref.shape[0]):
        copies_ref[p] = grad_contracted
    grad_updated = grad_mixed2
    for c in range(hidden // width):
        cols = slice(c * width, (c + 1) * width)
        copies[c][0].wait()
        pre = dot_nt(grad_contracted, contract_ref[cols, :]) * slope_ref[:, cols]
        copies[c][1].wait()
        grad_updated = grad_updated + dot_nt(pre.astype(BF16), expand_ref[:, cols])
    xhat1, scale1 = norm_parts(mixed1_ref[...])
    grad_mixed1 = norm_back(xhat1, scale1, vector(V_N1G), grad_updated)
    grad_mixed1_ref[...] = grad_mixed1
    grad_message = (grad_mixed1 / counts).astype(BF16)
    spread_ref[...] = dot_nt(grad_message, w3_ref[...])
    pack_ref[:width, :] = dot_split(dot_tn, act_sum_ref[...], grad_message).astype(BF16)
    vectors = [
        total(counts * grad_message.astype(F32)),
        total(grad_updated * xhat1),
        total(grad_updated),
        total(grad_fresh * xhat2),
        total(grad_fresh),
        edge_vec_ref[...],
    ]
    vectors = jnp.concatenate(vectors, axis=0)
    vectors = jnp.concatenate(
        [vectors, jnp.zeros((pack_ref.shape[0] - width - vectors.shape[0], width), F32)], axis=0
    )
    pack_ref[width:, :] = vectors.astype(BF16)


def feed_weight_kernel(low_ref, grad_ref, expand_ref, bias_ref, contract_ref, *refs, more):
    sums_in = refs[:4] if more else None
    expand_out_ref, contract_out_ref, bias_out_ref, last_bias_ref = refs[-6:-2]
    low_turned_ref, grad_turned_ref = refs[-2:]
    chunk = pl.program_id(0)
    ones = jnp.ones((8, low_ref.shape[0]), F32).astype(BF16)

    @pl.when(chunk == 0)
    def _():
        low_turned_ref[...] = low_ref[...].T
        grad_turned_ref[...] = grad_ref[...].T

    act, slope = gelu_pair(dot_nn(low_ref[...], expand_ref[...]) + bias_ref[0:1, :])
    act = act.astype(BF16)
    pre = (dot_nt(grad_ref[...], contract_ref[...]) * slope).astype(BF16)
    expanded = dot_nn(low_turned_ref[...], pre)
    contracted = dot_nn(grad_turned_ref[...], act).T
    sums = dot_nn(ones, pre)
    if more:
        expanded = expanded + sums_in[0][...]
        contracted = contracted + sums_in[1][...]
        sums = sums + sums_in[2][...]
    expand_out_ref[...] = expanded
    contract_out_ref[...] = contracted
    bias_out_ref[...] = sums

    @pl.when(chunk == 0)
    def _():
        last = dot_nn(ones, grad_ref[...])
        last_bias_ref[...] = last + sums_in[3][...] if more else last


def message_kernel(
    core_ref,
    edge_ref,
    pos_ref,
    act1_ref,
    slope1_ref,
    slope2_ref,
    partial_ref,
    spread_ref,
    table_ref,
    w1_a_ref,
    w1_b_ref,
    w1_c_ref,
    w2_ref,
    edge_pack_ref,
    feed_pack_ref,
    grad_ref,
    first_ref,
    own_ref,
    away_ref,
    send_ref,
    keep_ref,
    joint_ref,
    dw2_ref,
    bias2_ref,
    w2_turned_ref,
    w1_turned_ref,
):
    step = pl.program_id(0)
    last = pl.num_programs(0) - 1
    slots, rows, edge_width = edge_ref.shape
    width = act1_ref.shape[1]
    block = slots * rows
    table_rows = table_ref.shape[0]

    @pl.when(step == 0)
    def _():
        for ref in (joint_ref, dw2_ref, bias2_ref, first_ref):
            ref[...] = jnp.zeros_like(ref)
        w2_turned_ref[...] = w2_ref[...].T
        w1_parts = [ref[...] for ref in (w1_a_ref, w1_b_ref, w1_c_ref)]
        w1_turned_ref[...] = jnp.concatenate(w1_parts, axis=0).T

    spread = spread_ref[...]
    grad2 = []
    bias2 = bias2_ref[...]
    for k in range(slots):
        part = (spread * slope2_ref[pl.ds(k * rows, rows), :].astype(F32)).astype(BF16)
        bias2 = bias2 + part.astype(F32)
        grad2.append(part)
    bias2_ref[...] = bias2
    grad2 = jnp.concatenate(grad2, axis=0)
    dw2_ref[...] += dot_tn(act1_ref[...], grad2)
    grad1 = (dot_nn(grad2, w2_turned_ref[...]) * slope1_ref[...].astype(F32)).astype(BF16)
    first_ref[...] += jnp.sum(grad1.astype(F32).reshape(slots, rows, width), axis=0)
    onehot = edge_onehot(pos_ref, table_rows)
    features = edge_ref[...].reshape(block, edge_width)
    joint_ref[...] += dot_tn(jnp.concatenate([onehot, features], axis=1), grad1)
    grad_ref[...] = partial_ref[...] + dot_nn(grad1, w1_turned_ref[...]).reshape(
        slots, rows, edge_width
    )

    @pl.when(step == last)
    def _():
        first = first_ref[...]
        back = joint_ref[:table_rows]
        own_ref[...] = back[:rows]
        away_ref[...] = back[rows:].astype(BF16)
        own_grad = dot_split_right(dot_tn, table_ref[:rows], first).astype(BF16)
        nbr_grad = dot_split_right(dot_tn, table_ref[...], back).astype(BF16)
        vectors = [
            feed_pack_ref[width:].astype(F32),
            jnp.sum(first, axis=0, keepdims=True),
            jnp.sum(bias2_ref[...], axis=0, keepdims=True),
        ]
        lower = [own_grad, nbr_grad, feed_pack_ref[:width]]
        upper = [joint_ref[table_rows:].astype(BF16), dw2_ref[...].astype(BF16), edge_pack_ref[...]]

        def fill(ref, pieces, tail):
            base = 0
            for piece in pieces:
                ref[base : base + piece.shape[0]] = piece
                base += piece.shape[0]
            if base < ref.shape[0]:
                gap = ref.shape[0] - base - sum(v.shape[0] for v in tail)
                rest = jnp.concatenate(tail + [jnp.zeros((gap, width), F32)], axis=0)
                ref[base:] = rest.astype(BF16)

        @pl.when(core_ref[0] == 0)
        def _():
            fill(keep_ref, lower, [])
            fill(send_ref, upper, vectors)

        @pl.when(core_ref[0] != 0)
        def _():
            fill(send_ref, lower, [])
            fill(keep_ref, upper, vectors)


def wrapped(value, size):
    value = jnp.where(value >= size, value - size, value)
    return jnp.where(value < 0, value + size, value)


def pick_of(index, values):
    result = values[0]
    for i in range(1, len(values)):
        result = jnp.where(index == i, values[i], result)
    return result


def pair_kernel(y_ref, x_ref, keep_ref, came_ref, away_ref, *out_refs, parts, cap):
    y_size = lax.axis_size("y")
    x_size = lax.axis_size("x")
    z_size = parts // x_size
    riders = z_size * cap
    share = keep_ref.shape[0] // len(out_refs)
    away = away_ref[...].astype(F32)
    for e, out_ref in enumerate(out_refs):
        dy, dx = divmod(e, x_size)
        x = wrapped(x_ref[0] + dx, x_size)
        device = wrapped(y_ref[0] + dy, y_size) * x_size + x
        part = pl.ds(pl.multiple_of(device * share, 16), share)
        at = out_ref.shape[0] - share
        out_ref[at:] = (keep_ref[part, :].astype(F32) + came_ref[part, :].astype(F32)).astype(BF16)
        if at:
            rows = []
            for to in range(x_size):
                owners = [(z * x_size + to) * cap for z in range(z_size)]
                rows.append(jnp.concatenate([away[o : o + cap] for o in owners], axis=0))
            out_ref[:riders] = pick_of(x, rows).astype(BF16)


def plane_kernel(x_ref, z_ref, *refs, peers, cap):
    came_refs, out_refs = refs[:peers], refs[peers:]
    x_size = lax.axis_size("x")
    z_size = len(out_refs)
    riders = x_size * cap
    share = out_refs[0].shape[0] - riders
    first = z_size * cap
    rows = []
    for source in range(x_size):
        pieces = [ref[:first].astype(F32) for ref in came_refs[:x_size]]
        rows.append(pick_of(wrapped(x_ref[0] - source, x_size), pieces))
    for dz, out_ref in enumerate(out_refs):
        z = wrapped(z_ref[0] + dz, z_size)
        value = jnp.zeros((share, out_ref.shape[1]), F32)
        for e, ref in enumerate(came_refs):
            start = z * share + (first if e < x_size else 0)
            value = value + ref[pl.ds(pl.multiple_of(start, 16), share), :].astype(F32)
        out_ref[riders:] = value.astype(BF16)
        part = [
            pick_of(z, [value[i * cap : (i + 1) * cap] for i in range(z_size)]) for value in rows
        ]
        out_ref[:riders] = jnp.concatenate(part, axis=0).astype(BF16)


def column_kernel(z_ref, *refs):
    came_refs, total_ref, returned_ref = refs[:-2], refs[-2], refs[-1]
    z_size = len(came_refs)
    riders = returned_ref.shape[0] // z_size
    value = jnp.zeros(total_ref.shape, F32)
    for dz, ref in enumerate(came_refs):
        value = value + ref[riders:].astype(F32)
        start = wrapped(z_ref[0] - dz, z_size) * riders
        returned_ref[pl.ds(pl.multiple_of(start, 16), riders), :] = ref[:riders]
    total_ref[...] = value.astype(BF16)


def plane_stack_kernel(y_ref, x_ref, *refs):
    came_refs, out_ref = refs[:-1], refs[-1]
    x_size = lax.axis_size("x")
    share = came_refs[0].shape[0]
    for e, ref in enumerate(came_refs):
        dy, dx = divmod(e, x_size)
        y = wrapped(y_ref[0] - dy, len(came_refs) // x_size)
        start = (y * x_size + wrapped(x_ref[0] - dx, x_size)) * share
        out_ref[pl.ds(pl.multiple_of(start, 16), share), :] = ref[...]


def stack_kernel(z_ref, *refs):
    came_refs, out_ref = refs[:-1], refs[-1]
    share = came_refs[0].shape[0]
    for dz, ref in enumerate(came_refs):
        start = wrapped(z_ref[0] - dz, len(came_refs)) * share
        out_ref[pl.ds(pl.multiple_of(start, 16), share), :] = ref[...]


def node_grad_kernel(grad_ref, first_ref, own_ref, arrived_ref, asked_ref, w1_ref, out_ref):
    rows, width = grad_ref.shape
    back = own_ref[...] + dot_nn(asked_onehot(asked_ref, rows), arrived_ref[...])
    out_ref[...] = (
        grad_ref[...]
        + dot_split(dot_nt, first_ref[...], w1_ref[:width])
        + dot_split(dot_nt, back, w1_ref[width : 2 * width])
    )


def unpack_kernel(core_ref, y_ref, x_ref, *refs, peers):
    mine_refs, other_refs, refs = refs[:peers], refs[peers : 2 * peers], refs[2 * peers :]
    bias_ref, last_bias_ref = refs[:2]
    mine_ref, other_ref = refs[-2:]
    refs = refs[2:-2]
    x_size = lax.axis_size("x")
    share = mine_refs[0].shape[0]
    for e in range(peers):
        dy, dx = divmod(e, x_size)
        device = wrapped(y_ref[0] - dy, peers // x_size) * x_size + wrapped(x_ref[0] - dx, x_size)
        part = pl.ds(pl.multiple_of(device * share, 16), share)
        mine_ref[part, :] = mine_refs[e][...]
        other_ref[part, :] = other_refs[e][...]
    (
        message1_ref,
        message1_bias_ref,
        message2_ref,
        message2_bias_ref,
        message3_ref,
        message3_bias_ref,
        gain1_ref,
        shift1_ref,
        expand_bias_ref,
        contract_bias_ref,
        gain2_ref,
        shift2_ref,
        edge1_ref,
        edge1_bias_ref,
        edge2_ref,
        edge2_bias_ref,
        edge3_ref,
        edge3_bias_ref,
        gain3_ref,
        shift3_ref,
    ) = refs
    width = mine_ref.shape[1]
    edge_width = edge2_ref.shape[0]
    half = width // 2
    first_core = core_ref[0] == 0

    def lower(start, stop):
        return jnp.where(first_core, mine_ref[start:stop], other_ref[start:stop]).astype(F32)

    def upper(start, stop):
        return jnp.where(first_core, other_ref[start:stop], mine_ref[start:stop]).astype(F32)

    message1_ref[: 2 * width] = lower(0, 2 * width)
    message3_ref[...] = lower(2 * width, 3 * width)
    message1_ref[2 * width :] = upper(0, edge_width)
    base = edge_width
    message2_ref[...] = upper(base, base + width)
    base = base + width
    edge1_ref[:, :width] = upper(base, base + edge_width)
    edge1_ref[:, width : 2 * width] = upper(base + edge_width, base + 2 * edge_width)
    third = upper(base + 2 * edge_width, base + 3 * edge_width)
    edge1_ref[:, 2 * width :] = third[:, :edge_width]
    edge2_ref[...] = third[:, half : half + edge_width]
    edge3_ref[...] = upper(base + 3 * edge_width, base + 4 * edge_width)[:, :edge_width]
    base = base + 4 * edge_width
    vectors = upper(base, mine_ref.shape[0])
    targets = (message3_bias_ref, gain1_ref, shift1_ref, gain2_ref, shift2_ref)
    for i, ref in enumerate(targets):
        ref[...] = vectors[i]
    targets = (edge1_bias_ref, edge2_bias_ref, edge3_bias_ref, gain3_ref, shift3_ref)
    for i, ref in enumerate(targets):
        ref[...] = vectors[5 + i, :edge_width]
    message1_bias_ref[...] = vectors[16]
    message2_bias_ref[...] = vectors[17]
    expand_bias_ref[...] = bias_ref[0]
    contract_bias_ref[...] = last_bias_ref[0]


def gather_copies(copies, axes):
    return lax.all_to_all(copies, axes, split_axis=0, concat_axis=0, tiled=True)


def copies_of(values, axes):
    return jnp.broadcast_to(values[None], (lax.axis_size(axes), *values.shape))


def exchange(values, parts):
    grouped = values.reshape(parts, values.shape[0] // parts, values.shape[1])
    arrived = lax.all_to_all(grouped, RES, split_axis=0, concat_axis=0, tiled=True)
    return arrived.reshape(values.shape)


def move(values, dy=0, dz=0, dx=0):
    sizes = [lax.axis_size(axis) for axis in SIDE]
    pairs = []
    for i in range(math.prod(sizes)):
        rest, x = divmod(i, sizes[2])
        y, z = divmod(rest, sizes[1])
        to_y, to_z, to_x = (y + dy) % sizes[0], (z + dz) % sizes[1], (x + dx) % sizes[2]
        pairs.append((i, (to_y * sizes[1] + to_z) * sizes[2] + to_x))
    return lax.ppermute(values, SIDE, pairs)


def other_core(values):
    return lax.ppermute(values, "core", [(0, 1), (1, 0)])


def whole(shape):
    return pl.BlockSpec(shape, lambda *_: (0,) * len(shape))


def params(mebibytes):
    return pltpu.CompilerParams(vmem_limit_bytes=mebibytes * MIB)


def cost(microseconds):
    return pl.CostEstimate(
        flops=int(microseconds * 1.15e9),
        bytes_accessed=int(microseconds * 3.69e6),
        transcendentals=0,
    )


def body(
    node_states,
    edge_states,
    neighbour_index,
    edge_mask,
    node_cotangent,
    edge_cotangent,
    message_weight1,
    message_bias1,
    message_weight2,
    message_bias2,
    message_weight3,
    message_bias3,
    norm1_gain,
    norm1_shift,
    expand_weight,
    expand_bias,
    contract_weight,
    contract_bias,
    norm2_gain,
    norm2_shift,
    edge_weight1,
    edge_bias1,
    edge_weight2,
    edge_bias2,
    edge_weight3,
    edge_bias3,
    norm3_gain,
    norm3_shift,
):
    self_rows = node_states[0]
    rows, width = self_rows.shape
    slots = neighbour_index.shape[2]
    edge_width = edge_states.shape[3]
    hidden = expand_weight.shape[1]
    edges = rows * slots
    parts = lax.axis_size(RES)
    cap = ROW_CAP
    table_rows = rows + parts * cap
    side = lax.axis_size(SIDE)
    steps = STEPS
    block_slots = slots // steps
    block = block_slots * rows
    pairs = block // LANES

    everyone = gather_copies(copies_of(self_rows, RES), RES).reshape(parts * rows, width)
    core = lax.axis_index("core").astype(jnp.int32).reshape(1)
    me = lax.axis_index(RES).astype(jnp.int32).reshape(1)
    edge_rows = edge_states[0].transpose(1, 0, 2)
    edge_cot = edge_cotangent[0].transpose(1, 0, 2)
    slot_index = neighbour_index.transpose(2, 0, 1)
    slot_mask = edge_mask.transpose(2, 0, 1)
    edge_w1t = edge_weight1.T
    wide = (
        message_bias1,
        message_bias2,
        message_bias3,
        norm1_gain,
        norm1_shift,
        contract_bias,
        norm2_gain,
        norm2_shift,
        expand_bias,
    )
    narrow = (edge_bias1, edge_bias2, edge_bias3, norm3_gain, norm3_shift)
    vmem = pl.BlockSpec(memory_space=pltpu.VMEM)

    def shape(dims, kind):
        return jax.ShapeDtypeStruct(dims, kind)

    pos, select, ids, counts, vectors, bias_row = pl.pallas_call(
        functools.partial(
            prepare_kernel, parts=parts, cap=cap, steps=steps, wide=len(wide), narrow=len(narrow)
        ),
        out_shape=(
            shape((steps, LANES, pairs), jnp.int32),
            shape((parts * rows, table_rows), BF16),
            shape((parts, cap), jnp.int32),
            shape((rows, width), F32),
            shape((V_ROWS, width), F32),
            shape((1, hidden), F32),
        ),
        in_specs=[pl.BlockSpec(memory_space=pltpu.SMEM)] + [vmem] * (2 + len(wide) + len(narrow)),
        out_specs=(vmem,) * 6,
        compiler_params=params(56),
        cost_estimate=cost(6),
        name="prepare",
    )(me, slot_index, slot_mask, *wide, *narrow)
    ids, everyone = lax.optimization_barrier((ids, everyone))
    asked = lax.all_to_all(ids, RES, split_axis=0, concat_axis=0, tiled=True)

    edge_spec = pl.BlockSpec((block_slots, rows, edge_width), lambda i: (i, 0, 0))
    flat_spec = pl.BlockSpec((block, width), lambda i: (i, 0))
    pos_spec = pl.BlockSpec((1, LANES, pairs), lambda i: (i, 0, 0))
    any_spec = pl.BlockSpec(memory_space=pl.ANY)
    node_spec = whole((rows, width))
    away_spec = whole((parts * cap, width))

    (
        act1,
        slope1,
        slope2,
        fresh,
        table,
        mixed1,
        mixed2,
        low,
        slope_e,
        act_sum,
    ) = pl.pallas_call(
        node_kernel,
        grid=(steps,),
        in_specs=[
            edge_spec,
            pos_spec,
            whole((parts * rows, table_rows)),
            whole((parts * rows, width)),
            node_spec,
            node_spec,
            whole((V_ROWS, width)),
            whole(message_weight1.shape),
            whole((width, width)),
            whole((width, width)),
            any_spec,
            any_spec,
        ],
        out_specs=[
            flat_spec,
            flat_spec,
            flat_spec,
            node_spec,
            whole((table_rows, width)),
            node_spec,
            node_spec,
            node_spec,
            whole((rows, hidden)),
            node_spec,
        ],
        out_shape=[
            shape((edges, width), BF16),
            shape((edges, width), BF16),
            shape((edges, width), BF16),
            shape((rows, width), BF16),
            shape((table_rows, width), BF16),
            shape((rows, width), F32),
            shape((rows, width), F32),
            shape((rows, width), BF16),
            shape((rows, hidden), F32),
            shape((rows, width), F32),
        ],
        scratch_shapes=[
            pltpu.VMEM((table_rows, width), BF16),
            pltpu.VMEM((rows, width), F32),
            pltpu.VMEM((width, hidden), BF16),
            pltpu.VMEM((hidden, width), BF16),
            pltpu.SemaphoreType.DMA((2,)),
        ],
        compiler_params=params(56),
        cost_estimate=cost(26),
        name="node_forward",
    )(
        edge_rows,
        pos,
        select,
        everyone,
        self_rows,
        counts,
        vectors,
        message_weight1,
        message_weight2,
        message_weight3,
        expand_weight,
        contract_weight,
    )
    outgoing = pl.pallas_call(
        pick_kernel,
        in_specs=[vmem] * 2,
        out_specs=vmem,
        out_shape=shape((parts * cap, width), BF16),
        compiler_params=params(8),
        cost_estimate=cost(1),
        name="pick",
    )(asked, fresh)
    y_size = lax.axis_size("y")
    x_size = lax.axis_size("x")
    z_size = lax.axis_size("z")
    peers = y_size * x_size
    my_y = lax.axis_index("y").astype(jnp.int32).reshape(1)
    my_x = lax.axis_index("x").astype(jnp.int32).reshape(1)
    my_z = lax.axis_index("z").astype(jnp.int32).reshape(1)
    smem = pl.BlockSpec(memory_space=pltpu.SMEM)
    steps_of = [divmod(e, x_size) for e in range(peers)]

    def over_plane(values):
        came = [values[0]]
        for value, (dy, dx) in zip(values[1:], steps_of[1:]):
            came.append(move(value, dy=dy, dx=dx))
        return came

    def over_z(values):
        return [values[0]] + [move(value, dz=d) for d, value in enumerate(values[1:], start=1)]

    def stack_z(values):
        came = over_z([values] * z_size)
        return pl.pallas_call(
            stack_kernel,
            in_specs=[smem] + [vmem] * z_size,
            out_specs=vmem,
            out_shape=shape((z_size * values.shape[0], width), BF16),
            compiler_params=params(8),
            cost_estimate=cost(1),
            name="stack",
        )(my_z, *came)

    outgoing, low = lax.optimization_barrier((outgoing, low))
    incoming = exchange(outgoing, parts)
    low_column = stack_z(low)

    edge_pack_rows = 4 * edge_width
    edge_out, grad_partial, edge_first, edge_own, edge_away, edge_pack, edge_vec = pl.pallas_call(
        edge_kernel,
        grid=(steps,),
        in_specs=[
            edge_spec,
            edge_spec,
            pos_spec,
            node_spec,
            away_spec,
            node_spec,
            whole((V_ROWS, width)),
            whole(edge_w1t.shape),
            whole((edge_width, edge_width)),
            whole((edge_width, edge_width)),
        ],
        out_specs=[
            edge_spec,
            edge_spec,
            whole((rows, edge_width)),
            whole((rows, edge_width)),
            whole((parts * cap, edge_width)),
            whole((edge_pack_rows, width)),
            whole((8, width)),
        ],
        out_shape=[
            shape((slots, rows, edge_width), BF16),
            shape((slots, rows, edge_width), F32),
            shape((rows, edge_width), F32),
            shape((rows, edge_width), F32),
            shape((parts * cap, edge_width), BF16),
            shape((edge_pack_rows, width), BF16),
            shape((8, width), F32),
        ],
        scratch_shapes=[
            pltpu.VMEM((table_rows, width), BF16),
            pltpu.VMEM((table_rows, edge_width), BF16),
            pltpu.VMEM((rows, edge_width), F32),
            pltpu.VMEM((table_rows, edge_width), F32),
            pltpu.VMEM((edge_width, edge_width), F32),
            pltpu.VMEM((edge_width, edge_width), F32),
            pltpu.VMEM((edge_width, edge_width), F32),
            pltpu.VMEM((5, rows, edge_width), F32),
            pltpu.VMEM((3, edge_width, edge_width), BF16),
        ],
        compiler_params=params(56),
        cost_estimate=cost(1),
        name="edge_both",
    )(
        edge_rows,
        edge_cot,
        pos,
        fresh,
        incoming,
        counts,
        vectors,
        edge_w1t,
        edge_weight2,
        edge_weight3,
    )
    edge_away, low_column = lax.optimization_barrier((edge_away, low_column))
    edge_arrived = exchange(edge_away, parts)
    low_pieces = over_plane([low_column] * peers)

    feed_rows = width + 16
    feed_pack, grad_copies, spread, grad_mixed1 = pl.pallas_call(
        feed_kernel,
        in_specs=[vmem] * 12 + [any_spec] * 2 + [vmem] * 2,
        out_specs=[vmem] * 4,
        out_shape=[
            shape((feed_rows, width), BF16),
            shape((side, rows, width), BF16),
            shape((rows, width), F32),
            shape((rows, width), F32),
        ],
        scratch_shapes=[
            pltpu.VMEM((width, hidden), BF16),
            pltpu.VMEM((hidden, width), BF16),
            pltpu.SemaphoreType.DMA((2 * hidden // width,)),
        ],
        compiler_params=params(56),
        cost_estimate=cost(7),
        name="feed_backward",
    )(
        node_cotangent[0],
        edge_first,
        edge_own,
        edge_arrived,
        asked,
        counts,
        vectors,
        edge_w1t,
        mixed1,
        mixed2,
        slope_e,
        act_sum,
        expand_weight,
        contract_weight,
        message_weight3,
        edge_vec,
    )
    grad_mine = gather_copies(grad_copies, BY_COLUMN).reshape(side * rows, width)
    spread, low_pieces = lax.optimization_barrier((spread, low_pieces))

    unit = 16 * side
    half_rows = (3 * width + unit - 1) // unit * unit
    third = edge_width // 3
    edge_grad, first, own, away, send, keep = pl.pallas_call(
        message_kernel,
        grid=(steps,),
        in_specs=[
            pl.BlockSpec(memory_space=pltpu.SMEM),
            edge_spec,
            pos_spec,
            flat_spec,
            flat_spec,
            flat_spec,
            edge_spec,
            node_spec,
            whole((table_rows, width)),
            *[
                pl.BlockSpec((third, width), lambda i, p=p: (2 * width // third + p, 0))
                for p in range(3)
            ],
            whole((width, width)),
            whole((edge_pack_rows, width)),
            whole((feed_rows, width)),
        ],
        out_specs=[
            edge_spec,
            node_spec,
            node_spec,
            away_spec,
            whole((half_rows, width)),
            whole((half_rows, width)),
        ],
        out_shape=[
            shape((slots, rows, edge_width), F32),
            shape((rows, width), F32),
            shape((rows, width), F32),
            shape((parts * cap, width), BF16),
            shape((half_rows, width), BF16),
            shape((half_rows, width), BF16),
        ],
        scratch_shapes=[
            pltpu.VMEM((table_rows + edge_width, width), F32),
            pltpu.VMEM((width, width), F32),
            pltpu.VMEM((rows, width), F32),
            pltpu.VMEM((width, width), BF16),
            pltpu.VMEM((width, edge_width), BF16),
        ],
        compiler_params=params(56),
        cost_estimate=cost(14),
        name="message_backward",
    )(
        core,
        edge_rows,
        pos,
        act1,
        slope1,
        slope2,
        grad_partial,
        spread,
        table,
        message_weight1,
        message_weight1,
        message_weight1,
        message_weight2,
        edge_pack,
        feed_pack,
    )
    came = other_core(send)
    share = half_rows // peers
    pieces = pl.pallas_call(
        functools.partial(pair_kernel, parts=parts, cap=cap),
        in_specs=[smem] * 2 + [vmem] * 3,
        out_specs=[vmem] * peers,
        out_shape=[
            shape((share if dy else share + z_size * cap, width), BF16) for dy, _ in steps_of
        ],
        compiler_params=params(20),
        cost_estimate=cost(3),
        name="pair_sum",
    )(my_y, my_x, keep, came, away)
    _, grad_mine, low_pieces = lax.optimization_barrier((pieces[0], grad_mine, low_pieces))
    low_mine = pl.pallas_call(
        plane_stack_kernel,
        in_specs=[smem] * 2 + [vmem] * peers,
        out_specs=vmem,
        out_shape=shape((side * rows, width), BF16),
        compiler_params=params(max(8, side * rows // 256)),
        cost_estimate=cost(1),
        name="plane_stack",
    )(my_y, my_x, *low_pieces)

    arrived = over_plane(pieces)
    grad_other = other_core(grad_mine)
    low_other = other_core(low_mine)

    def feed_weights(low_values, grad_values, at, block_rows, sums):
        units = 256
        row_block = pl.BlockSpec((block_rows, width), lambda c: (at, 0))
        sum_specs = [
            pl.BlockSpec((width, units), lambda c: (0, c)),
            pl.BlockSpec((units, width), lambda c: (c, 0)),
            pl.BlockSpec((8, units), lambda c: (0, c)),
            whole((8, width)),
        ]
        return pl.pallas_call(
            functools.partial(feed_weight_kernel, more=bool(sums)),
            grid=(hidden // units,),
            in_specs=[
                row_block,
                row_block,
                sum_specs[0],
                pl.BlockSpec((1, units), lambda c: (0, c)),
                sum_specs[1],
                *(sum_specs if sums else []),
            ],
            out_specs=sum_specs,
            scratch_shapes=[
                pltpu.VMEM((width, block_rows), BF16),
                pltpu.VMEM((width, block_rows), BF16),
            ],
            out_shape=[
                shape((width, hidden), F32),
                shape((hidden, width), F32),
                shape((8, hidden), F32),
                shape((8, width), F32),
            ],
            compiler_params=params(56),
            cost_estimate=cost(17),
            name="feed_weights_more" if sums else "feed_weights",
        )(low_values, grad_values, expand_weight, bias_row, contract_weight, *sums)

    def feed_side(low_values, grad_values, sums):
        block_rows = min(side * rows, 1024)
        for at in range(side * rows // block_rows):
            sums = tuple(feed_weights(low_values, grad_values, at, block_rows, sums))
        return sums

    sums = feed_side(low_mine, grad_mine, ())
    arrived, sums = lax.optimization_barrier((arrived, sums))
    pieces = pl.pallas_call(
        functools.partial(plane_kernel, peers=peers, cap=cap),
        in_specs=[smem] * 2 + [vmem] * peers,
        out_specs=[vmem] * z_size,
        out_shape=[shape((half_rows // side + x_size * cap, width), BF16)] * z_size,
        compiler_params=params(16),
        cost_estimate=cost(3),
        name="plane_sum",
    )(my_x, my_z, *arrived)
    total, returned = pl.pallas_call(
        column_kernel,
        in_specs=[smem] + [vmem] * z_size,
        out_specs=[vmem] * 2,
        out_shape=[
            shape((half_rows // side, width), BF16),
            shape((parts * cap, width), BF16),
        ],
        compiler_params=params(8),
        cost_estimate=cost(1),
        name="column_sum",
    )(my_z, *over_z(pieces))
    column = stack_z(total)
    _, grad_other, low_other, sums = lax.optimization_barrier((column, grad_other, low_other, sums))
    mine = over_plane([column] * peers)
    other_first = other_core(column)
    sums = feed_side(low_other, grad_other, tuple(sums))
    mine, other_first, sums = lax.optimization_barrier((mine, other_first, sums))
    grad_expand, grad_contract, expand_bias_sum, contract_bias_sum = sums
    other = [other_first] + [other_core(value) for value in mine[1:]]
    node_grad = pl.pallas_call(
        node_grad_kernel,
        in_specs=[vmem] * 6,
        out_specs=vmem,
        out_shape=shape((rows, width), F32),
        compiler_params=params(12),
        cost_estimate=cost(3),
        name="node_gradient",
    )(grad_mixed1, first, own, returned, asked, message_weight1)

    vec = shape((width,), F32)
    thin = shape((edge_width,), F32)
    square = shape((width, width), F32)
    small = shape((edge_width, edge_width), F32)
    (
        grad_message1,
        grad_mb1,
        grad_message2,
        grad_mb2,
        grad_message3,
        grad_mb3,
        grad_n1g,
        grad_n1s,
        grad_eb,
        grad_cb,
        grad_n2g,
        grad_n2s,
        grad_edge1_t,
        grad_eb1,
        grad_edge2,
        grad_eb2,
        grad_edge3,
        grad_eb3,
        grad_n3g,
        grad_n3s,
    ) = pl.pallas_call(
        functools.partial(unpack_kernel, peers=peers),
        in_specs=[smem] * 3 + [vmem] * (2 * peers + 2),
        out_specs=[vmem] * 20,
        out_shape=[
            shape(message_weight1.shape, F32),
            vec,
            square,
            vec,
            square,
            vec,
            vec,
            vec,
            shape((hidden,), F32),
            vec,
            vec,
            vec,
            shape(edge_w1t.shape, F32),
            thin,
            small,
            thin,
            small,
            thin,
            thin,
            thin,
        ],
        scratch_shapes=[pltpu.VMEM((half_rows, width), BF16)] * 2,
        compiler_params=params(24),
        cost_estimate=cost(4),
        name="unpack",
    )(core, my_y, my_x, *mine, *other, expand_bias_sum, contract_bias_sum)
    return (
        fresh[None],
        edge_out.transpose(1, 0, 2)[None],
        node_grad[None],
        edge_grad.transpose(1, 0, 2)[None],
        grad_message1,
        grad_mb1,
        grad_message2,
        grad_mb2,
        grad_message3,
        grad_mb3,
        grad_n1g,
        grad_n1s,
        grad_expand,
        grad_eb,
        grad_contract,
        grad_cb,
        grad_n2g,
        grad_n2s,
        grad_edge1_t.T,
        grad_eb1,
        grad_edge2,
        grad_eb2,
        grad_edge3,
        grad_eb3,
        grad_n3g,
        grad_n3s,
    )


def solution(mesh):
    batch, res = mesh.shape["batch"], mesh.shape["res"]
    x_size = 1 << ((res.bit_length() - 1) // 2)
    sizes = (batch // CORES, CORES, res // x_size, x_size)
    fine = jax.sharding.Mesh(mesh.devices.reshape(sizes), ALL)
    row_spec = P(("y", "core"), RES, None)
    edge_spec = P(("y", "core"), RES, None, None)
    return jax.shard_map(
        body,
        mesh=fine,
        in_specs=(row_spec, edge_spec, row_spec, row_spec, row_spec, edge_spec) + (P(),) * 22,
        out_specs=(row_spec, edge_spec, row_spec, edge_spec) + (P(),) * 22,
        check_vma=False,
    )
```

```python
import functools
import math

import jax
import jax.numpy as jnp
from jax import lax
from jax.experimental import pallas as pl
from jax.experimental.pallas import tpu as pltpu
from jax.sharding import PartitionSpec as P

ROW_CAP = 8
CORES = 2
RES = ("z", "x")
PLANE = ("y", "x")
SIDE = ("y", "z", "x")
BY_COLUMN = ("y", "x", "z")
ALL = ("y", "core", "z", "x")
EPSILON = 1e-05
LANES = 128
MIB = 1024 * 1024
STEPS = 3
F32 = jnp.float32
BF16 = jnp.bfloat16

V_MB1, V_MB2, V_MB3, V_N1G, V_N1S, V_CB, V_N2G, V_N2S, V_EB = range(9)
V_EDGE = 12
V_ROWS = 24


def dot_nn(left, right):
    return lax.dot_general(left, right, (((1,), (0,)), ((), ())), preferred_element_type=F32)


def dot_nt(left, right):
    return lax.dot_general(left, right, (((1,), (1,)), ((), ())), preferred_element_type=F32)


def dot_tn(left, right):
    return lax.dot_general(left, right, (((0,), (0,)), ((), ())), preferred_element_type=F32)


def split_low(values):
    high = values.astype(BF16)
    return high, (values - high.astype(F32)).astype(BF16)


def dot_split(dot, left, right):
    high, rest = split_low(left)
    return dot(high, right) + dot(rest, right)


def dot_split_right(dot, left, right):
    high, rest = split_low(right)
    return dot(left, high) + dot(left, rest)


def gelu_pair(v):
    e = jnp.exp2((v * v) * (-0.5 * math.log2(math.e)))
    phi_sum = 0.5 + 0.5 * lax.erf(v * math.sqrt(0.5))
    return v * phi_sum, phi_sum + (v * (1.0 / math.sqrt(2.0 * math.pi))) * e


def norm_parts(values):
    average = jnp.mean(values, axis=-1, keepdims=True)
    centred = values - average
    variance = jnp.mean(centred * centred, axis=-1, keepdims=True)
    scale = lax.rsqrt(variance + EPSILON)
    return centred * scale, scale


def norm_back(xhat, scale, gain, upstream):
    w = upstream * gain
    mean_w = jnp.mean(w, axis=-1, keepdims=True)
    mean_wx = jnp.mean(w * xhat, axis=-1, keepdims=True)
    return (w - mean_w - xhat * mean_wx) * scale


def edge_onehot(pos_ref, table_rows):
    pairs = pos_ref.shape[2]
    lane = lax.broadcasted_iota(jnp.int32, (LANES, table_rows), 1)
    return jnp.concatenate(
        [(pos_ref[0, :, p : p + 1] == lane).astype(F32).astype(BF16) for p in range(pairs)], axis=0
    )


def prepare_kernel(me_ref, idx_ref, mask_ref, *refs, parts, cap, steps, wide, narrow):
    wide_refs = refs[:wide]
    narrow_refs = refs[wide : wide + narrow]
    pos_ref, select_ref, ids_ref, count_ref, vec_ref, expand_bias_ref = refs[wide + narrow :]
    rows, width = count_ref.shape
    total = rows * parts
    table = rows + parts * cap
    me = me_ref[0]
    pair_rows = idx_ref.shape[0] // 2
    named = [
        jnp.concatenate([idx_ref[2 * j], idx_ref[2 * j + 1]], axis=1) for j in range(pair_rows)
    ]
    residue = lax.broadcasted_iota(jnp.int32, (total, LANES), 0)
    owner = residue // rows
    within = residue - owner * rows
    hits = jnp.zeros((total, LANES), F32)
    for j in range(pair_rows):
        hits = jnp.where(named[j] == residue, 1.0, hits)
    hit = jnp.max(hits, axis=1, keepdims=True)
    own = owner == me
    wanted = jnp.where(own, 0.0, jnp.broadcast_to(hit, (total, LANES)))
    low_row = lax.broadcasted_iota(jnp.int32, (rows, rows), 0)
    low_col = lax.broadcasted_iota(jnp.int32, (rows, rows), 1)
    lower = (low_col <= low_row).astype(F32).astype(BF16)
    wanted_low = wanted.astype(BF16)
    place = jnp.concatenate(
        [dot_nn(lower, wanted_low[o * rows : (o + 1) * rows]) for o in range(parts)], axis=0
    )
    place = jnp.clip(place - 1.0, 0.0, cap - 1.0)
    pos = jnp.where(own, within.astype(F32), (rows + owner * cap).astype(F32) + place)
    picked = [
        jnp.sum(jnp.where(named[j] == residue, pos, 0.0), axis=0, keepdims=True)
        for j in range(pair_rows)
    ]
    picked.append(jnp.zeros((LANES - pair_rows, LANES), F32))
    turned = jnp.concatenate(picked, axis=0).T.astype(jnp.int32)
    per = pair_rows // steps
    for s in range(steps):
        pos_ref[s] = turned[:, s * per : (s + 1) * per]
    lane = lax.broadcasted_iota(jnp.int32, (total, table), 1).astype(F32)
    live = jnp.where(own, 1.0, wanted)
    chosen = jnp.where(lane == pos[:, :1], jnp.broadcast_to(live[:, :1], (total, table)), 0.0)
    select_ref[...] = chosen.astype(BF16)
    asked_row = jnp.broadcast_to(within[:, :1].astype(F32), (total, parts * cap))
    ids = jnp.sum(chosen[:, rows:] * asked_row, axis=0, keepdims=True)
    ids = ids.astype(jnp.int32)
    for o in range(parts):
        ids_ref[o : o + 1, :] = ids[:, o * cap : (o + 1) * cap]
    count = mask_ref[0]
    for k in range(1, mask_ref.shape[0]):
        count = count + mask_ref[k]
    count = jnp.concatenate([count.astype(F32), jnp.zeros((7, rows), F32)], axis=0)
    count_ref[...] = dot_tn(count.astype(BF16), jnp.ones((8, width), F32).astype(BF16))
    expand_bias_ref[...] = wide_refs[-1][...].astype(F32).reshape(expand_bias_ref.shape)
    vec_ref[...] = jnp.zeros_like(vec_ref)
    at = 0
    for ref in wide_refs:
        for c in range(ref.shape[0] // width):
            part = ref[c * width : (c + 1) * width]
            vec_ref[at : at + 1, :] = part.astype(F32).reshape(1, width)
            at += 1
    for ref in narrow_refs:
        vec_ref[at : at + 1, : ref.shape[0]] = ref[...].astype(F32).reshape(1, ref.shape[0])
        at += 1


def node_kernel(
    edge_ref,
    pos_ref,
    select_ref,
    all_ref,
    self_ref,
    count_ref,
    vec_ref,
    w1_ref,
    w2_ref,
    w3_ref,
    expand_hbm,
    contract_hbm,
    act1_ref,
    slope1_ref,
    slope2_ref,
    fresh_ref,
    table_ref,
    mixed1_ref,
    mixed2_ref,
    low_ref,
    slope_e_ref,
    act_sum_ref,
    proj_ref,
    self_pre_ref,
    expand_ref,
    contract_ref,
    sems,
):
    step = pl.program_id(0)
    last = pl.num_programs(0) - 1
    rows, width = self_ref.shape
    slots = edge_ref.shape[0]
    edge_width = edge_ref.shape[2]
    table_rows = table_ref.shape[0]
    expand_copy = pltpu.make_async_copy(expand_hbm, expand_ref, sems.at[0])
    contract_copy = pltpu.make_async_copy(contract_hbm, contract_ref, sems.at[1])

    @pl.when(step == 0)
    def _():
        expand_copy.start()
        contract_copy.start()
        table = dot_tn(select_ref[...], all_ref[...]).astype(BF16)
        table_ref[...] = table
        proj_ref[...] = dot_nn(table, w1_ref[width : 2 * width]).astype(BF16)
        self_pre_ref[...] = (
            dot_nn(self_ref[...], w1_ref[:width]) + vec_ref[V_MB1 : V_MB1 + 1, :]
        )
        act_sum_ref[...] = jnp.zeros_like(act_sum_ref)

    onehot = edge_onehot(pos_ref, table_rows)
    features = edge_ref[...].reshape(slots * rows, edge_width)
    pre1 = dot_nn(features, w1_ref[2 * width :]) + dot_nn(onehot, proj_ref[...])
    self_pre = self_pre_ref[...]
    act1 = []
    for k in range(slots):
        part = pl.ds(k * rows, rows)
        act, slope = gelu_pair(pre1[k * rows : (k + 1) * rows] + self_pre)
        act = act.astype(BF16)
        act1.append(act)
        act1_ref[part, :] = act
        slope1_ref[part, :] = slope.astype(BF16)
    pre2 = dot_nn(jnp.concatenate(act1, axis=0), w2_ref[...])
    bias2 = vec_ref[V_MB2 : V_MB2 + 1, :]
    act_sum = act_sum_ref[...]
    counts = count_ref[...]
    for k in range(slots):
        act, slope = gelu_pair(pre2[k * rows : (k + 1) * rows] + bias2)
        valid = counts > (step * slots + k).astype(F32)
        act_sum = act_sum + jnp.where(valid, act.astype(BF16).astype(F32), 0.0)
        slope2_ref[pl.ds(k * rows, rows), :] = jnp.where(valid, slope, 0.0).astype(BF16)
    act_sum_ref[...] = act_sum

    @pl.when(step == last)
    def _():
        summed = dot_split(dot_nn, act_sum_ref[...], w3_ref[...])
        summed = summed + counts * vec_ref[V_MB3 : V_MB3 + 1, :]
        mixed1 = self_ref[...].astype(F32) + summed / counts
        mixed1_ref[...] = mixed1
        xhat1, _ = norm_parts(mixed1)
        updated = xhat1 * vec_ref[V_N1G : V_N1G + 1, :] + vec_ref[V_N1S : V_N1S + 1, :]
        low = updated.astype(BF16)
        low_ref[...] = low
        expand_copy.wait()
        contract_copy.wait()
        mixed2 = updated + vec_ref[V_CB : V_CB + 1, :]
        for c in range(expand_ref.shape[1] // width):
            cols = slice(c * width, (c + 1) * width)
            pre = dot_nn(low, expand_ref[:, cols]) + vec_ref[V_EB + c : V_EB + c + 1, :]
            act, slope = gelu_pair(pre)
            act = act.astype(BF16)
            slope_e_ref[:, cols] = slope
            mixed2 = mixed2 + dot_nn(act, contract_ref[cols, :])
        mixed2_ref[...] = mixed2
        xhat2, _ = norm_parts(mixed2)
        fresh = (xhat2 * vec_ref[V_N2G : V_N2G + 1, :] + vec_ref[V_N2S : V_N2S + 1, :]).astype(BF16)
        fresh_ref[...] = fresh


def asked_onehot(asked_ref, rows):
    parts = asked_ref.shape[0]
    asked = jnp.concatenate([asked_ref[o : o + 1, :] for o in range(parts)], axis=1)
    row = lax.broadcasted_iota(jnp.int32, (rows, asked.shape[1]), 0)
    return (asked == row).astype(F32).astype(BF16)


def pick_kernel(asked_ref, fresh_ref, out_ref):
    out_ref[...] = dot_tn(asked_onehot(asked_ref, fresh_ref.shape[0]), fresh_ref[...]).astype(BF16)


def edge_kernel(
    edge_ref,
    cot_ref,
    pos_ref,
    fresh_ref,
    incoming_ref,
    count_ref,
    vec_ref,
    w1t_ref,
    w2_ref,
    w3_ref,
    out_ref,
    grad_ref,
    first_ref,
    own_ref,
    away_ref,
    pack_ref,
    vec_out_ref,
    table_ref,
    proj_ref,
    self_pre_ref,
    back_ref,
    dw3_ref,
    dw2_ref,
    dw1_ref,
    sums_ref,
    turned_ref,
):
    step = pl.program_id(0)
    last = pl.num_programs(0) - 1
    rows, width = fresh_ref.shape
    slots, _, edge_width = edge_ref.shape
    block = slots * rows
    table_rows = table_ref.shape[0]
    own_t = w1t_ref[:, :width]
    nbr_t = w1t_ref[:, width : 2 * width]
    feat_t = w1t_ref[:, 2 * width :]

    def vector(i):
        return vec_ref[V_EDGE + i : V_EDGE + i + 1, :edge_width]

    @pl.when(step == 0)
    def _():
        table_ref[:rows] = fresh_ref[...]
        table_ref[rows:] = incoming_ref[...]
        proj_ref[...] = dot_nt(table_ref[...], nbr_t).astype(BF16)
        self_pre_ref[...] = dot_nt(fresh_ref[...], own_t) + vector(0)
        for ref in (back_ref, dw3_ref, dw2_ref, dw1_ref, sums_ref, first_ref):
            ref[...] = jnp.zeros_like(ref)
        turned_ref[0] = feat_t.T
        turned_ref[1] = w2_ref[...].T
        turned_ref[2] = w3_ref[...].T

    def flat(values):
        return values.reshape(block, edge_width)

    def deep(values):
        return values.reshape(slots, rows, edge_width)

    onehot = edge_onehot(pos_ref, table_rows)
    features = flat(edge_ref[...])
    pre1 = dot_nn(features, turned_ref[0]) + dot_nn(onehot, proj_ref[...])
    pre1 = deep(pre1) + self_pre_ref[...][None]
    act1, slope1 = gelu_pair(flat(pre1))
    act1 = act1.astype(BF16)
    pre2 = dot_nn(act1, w2_ref[...]) + vector(1)
    act2, slope2 = gelu_pair(pre2)
    act2 = act2.astype(BF16)
    mixed3 = features.astype(F32) + (dot_nn(act2, w3_ref[...]) + vector(2))
    xhat, scale = norm_parts(mixed3)
    gain = vector(3)
    slot = lax.broadcasted_iota(jnp.int32, (slots, rows, edge_width), 0) + step * slots
    valid = count_ref[...][None, :, :edge_width] > slot.astype(F32)
    out_ref[...] = jnp.where(valid, deep(xhat * gain + vector(4)), 0.0).astype(BF16)
    upstream = flat(jnp.where(valid, cot_ref[...].astype(F32), 0.0))
    sums_ref[3] += jnp.sum(deep(upstream * xhat), axis=0)
    sums_ref[4] += jnp.sum(deep(upstream), axis=0)
    grad_mixed = norm_back(xhat, scale, gain, upstream)
    grad_delta = grad_mixed.astype(BF16)
    dw3_ref[...] += dot_tn(act2, grad_delta)
    sums_ref[2] += jnp.sum(deep(grad_delta.astype(F32)), axis=0)
    grad2 = (dot_nn(grad_delta, turned_ref[2]) * slope2).astype(BF16)
    dw2_ref[...] += dot_tn(act1, grad2)
    sums_ref[1] += jnp.sum(deep(grad2.astype(F32)), axis=0)
    grad1 = (dot_nn(grad2, turned_ref[1]) * slope1).astype(BF16)
    dw1_ref[...] += dot_tn(grad1, features)
    first_ref[...] += jnp.sum(deep(grad1.astype(F32)), axis=0)
    back_ref[...] += dot_tn(onehot, grad1)
    grad_ref[...] = deep(grad_mixed + dot_nn(grad1, feat_t))

    @pl.when(step == last)
    def _():
        first = first_ref[...]
        back = back_ref[...]
        own_ref[...] = back[:rows]
        away_ref[...] = back[rows:].astype(BF16)
        first_high, first_rest = split_low(first)
        back_high, back_rest = split_low(back)
        own_grad = dot_tn(first_high, fresh_ref[...]) + dot_tn(first_rest, fresh_ref[...])
        nbr_grad = dot_tn(back_high, table_ref[...]) + dot_tn(back_rest, table_ref[...])
        pack_ref[:edge_width, :] = own_grad.astype(BF16)
        pack_ref[edge_width : 2 * edge_width, :] = nbr_grad.astype(BF16)
        pad = jnp.zeros((edge_width, width // 2 - edge_width), BF16)
        third = [dw1_ref[...].astype(BF16), pad, dw2_ref[...].astype(BF16), pad]
        pack_ref[2 * edge_width : 3 * edge_width, :] = jnp.concatenate(third, axis=1)
        fourth = [dw3_ref[...].astype(BF16), pad, jnp.zeros((edge_width, width // 2), BF16)]
        pack_ref[3 * edge_width :, :] = jnp.concatenate(fourth, axis=1)
        vec_out_ref[...] = jnp.zeros_like(vec_out_ref)
        vec_out_ref[0:1, :edge_width] = jnp.sum(first, axis=0, keepdims=True)
        for i in range(1, 5):
            vec_out_ref[i : i + 1, :edge_width] = jnp.sum(sums_ref[i], axis=0, keepdims=True)


def feed_kernel(
    cot_ref,
    first_ref,
    own_ref,
    arrived_ref,
    asked_ref,
    count_ref,
    vec_ref,
    w1t_ref,
    mixed1_ref,
    mixed2_ref,
    slope_ref,
    act_sum_ref,
    expand_hbm,
    contract_hbm,
    w3_ref,
    edge_vec_ref,
    pack_ref,
    copies_ref,
    spread_ref,
    grad_mixed1_ref,
    expand_ref,
    contract_ref,
    sems,
):
    rows, width = cot_ref.shape
    hidden = expand_ref.shape[1]
    own_t = w1t_ref[:, :width]
    nbr_t = w1t_ref[:, width : 2 * width]
    counts = count_ref[...]
    copies = []
    for c in range(hidden // width):
        rows_part, cols_part = pl.ds(c * width, width), pl.ds(c * width, width)
        copies.append(
            (
                pltpu.make_async_copy(
                    contract_hbm.at[rows_part, :], contract_ref.at[rows_part, :], sems.at[2 * c]
                ),
                pltpu.make_async_copy(
                    expand_hbm.at[:, cols_part], expand_ref.at[:, cols_part], sems.at[2 * c + 1]
                ),
            )
        )
    for pair in copies:
        for copy in pair:
            copy.start()

    def vector(i):
        return vec_ref[i : i + 1, :]

    def total(values):
        return jnp.sum(values.astype(F32), axis=0, keepdims=True)

    back = own_ref[...] + dot_nn(asked_onehot(asked_ref, rows), arrived_ref[...])
    grad_fresh = (
        cot_ref[...].astype(F32)
        + dot_split(dot_nn, first_ref[...], own_t)
        + dot_split(dot_nn, back, nbr_t)
    )
    xhat2, scale2 = norm_parts(mixed2_ref[...])
    grad_mixed2 = norm_back(xhat2, scale2, vector(V_N2G), grad_fresh)
    grad_contracted = grad_mixed2.astype(BF16)
    for p in range(copies_ref.shape[0]):
        copies_ref[p] = grad_contracted
    grad_updated = grad_mixed2
    for c in range(hidden // width):
        cols = slice(c * width, (c + 1) * width)
        copies[c][0].wait()
        pre = dot_nt(grad_contracted, contract_ref[cols, :]) * slope_ref[:, cols]
        copies[c][1].wait()
        grad_updated = grad_updated + dot_nt(pre.astype(BF16), expand_ref[:, cols])
    xhat1, scale1 = norm_parts(mixed1_ref[...])
    grad_mixed1 = norm_back(xhat1, scale1, vector(V_N1G), grad_updated)
    grad_mixed1_ref[...] = grad_mixed1
    grad_message = (grad_mixed1 / counts).astype(BF16)
    spread_ref[...] = dot_nt(grad_message, w3_ref[...])
    pack_ref[:width, :] = dot_split(dot_tn, act_sum_ref[...], grad_message).astype(BF16)
    vectors = [
        total(counts * grad_message.astype(F32)),
        total(grad_updated * xhat1),
        total(grad_updated),
        total(grad_fresh * xhat2),
        total(grad_fresh),
        edge_vec_ref[...],
    ]
    vectors = jnp.concatenate(vectors, axis=0)
    vectors = jnp.concatenate(
        [vectors, jnp.zeros((pack_ref.shape[0] - width - vectors.shape[0], width), F32)], axis=0
    )
    pack_ref[width:, :] = vectors.astype(BF16)


def feed_weight_kernel(
    low_ref, grad_ref, expand_ref, bias_ref, contract_ref, *refs, more, last
):
    sums_in = refs[:3] if more else None
    outputs = refs[-6:-2] if last else refs[-5:-2]
    expand_out_ref, contract_out_ref, bias_out_ref = outputs[:3]
    low_turned_ref, grad_turned_ref = refs[-2:]
    ones = jnp.ones((8, low_ref.shape[0]), F32).astype(BF16)

    @pl.when(pl.program_id(0) == 0)
    def _():
        low_turned_ref[...] = low_ref[...].T
        grad_turned_ref[...] = grad_ref[...].T
        if last:
            outputs[3][...] = dot_nn(ones, grad_ref[...])

    act, slope = gelu_pair(dot_nn(low_ref[...], expand_ref[...]) + bias_ref[0:1, :])
    act = act.astype(BF16)
    pre = (dot_nt(grad_ref[...], contract_ref[...]) * slope).astype(BF16)
    expanded = dot_nn(low_turned_ref[...], pre)
    contracted = dot_nn(grad_turned_ref[...], act).T
    sums = dot_nn(ones, pre)
    if more:
        expanded = expanded + sums_in[0][...]
        contracted = contracted + sums_in[1][...]
        sums = sums + sums_in[2][...]
    expand_out_ref[...] = expanded
    contract_out_ref[...] = contracted
    bias_out_ref[...] = sums


def message_kernel(
    core_ref,
    edge_ref,
    pos_ref,
    act1_ref,
    slope1_ref,
    slope2_ref,
    partial_ref,
    spread_ref,
    table_ref,
    w1_a_ref,
    w1_b_ref,
    w1_c_ref,
    w2_ref,
    edge_pack_ref,
    feed_pack_ref,
    grad_ref,
    first_ref,
    own_ref,
    away_ref,
    send_ref,
    keep_ref,
    joint_ref,
    dw2_ref,
    bias2_ref,
    w2_turned_ref,
    w1_turned_ref,
):
    step = pl.program_id(0)
    last = pl.num_programs(0) - 1
    slots, rows, edge_width = edge_ref.shape
    width = act1_ref.shape[1]
    block = slots * rows
    table_rows = table_ref.shape[0]

    @pl.when(step == 0)
    def _():
        for ref in (joint_ref, dw2_ref, bias2_ref, first_ref):
            ref[...] = jnp.zeros_like(ref)
        w2_turned_ref[...] = w2_ref[...].T
        w1_parts = [ref[...] for ref in (w1_a_ref, w1_b_ref, w1_c_ref)]
        w1_turned_ref[...] = jnp.concatenate(w1_parts, axis=0).T

    spread = spread_ref[...]
    grad2 = []
    bias2 = bias2_ref[...]
    for k in range(slots):
        part = (spread * slope2_ref[pl.ds(k * rows, rows), :].astype(F32)).astype(BF16)
        bias2 = bias2 + part.astype(F32)
        grad2.append(part)
    bias2_ref[...] = bias2
    grad2 = jnp.concatenate(grad2, axis=0)
    dw2_ref[...] += dot_tn(act1_ref[...], grad2)
    grad1 = (dot_nn(grad2, w2_turned_ref[...]) * slope1_ref[...].astype(F32)).astype(BF16)
    first_ref[...] += jnp.sum(grad1.astype(F32).reshape(slots, rows, width), axis=0)
    onehot = edge_onehot(pos_ref, table_rows)
    features = edge_ref[...].reshape(block, edge_width)
    joint_ref[...] += dot_tn(jnp.concatenate([onehot, features], axis=1), grad1)
    grad_ref[...] = partial_ref[...] + dot_nn(grad1, w1_turned_ref[...]).reshape(
        slots, rows, edge_width
    )

    @pl.when(step == last)
    def _():
        first = first_ref[...]
        back = joint_ref[:table_rows]
        own_ref[...] = back[:rows]
        away_ref[...] = back[rows:].astype(BF16)
        own_grad = dot_split_right(dot_tn, table_ref[:rows], first).astype(BF16)
        nbr_grad = dot_split_right(dot_tn, table_ref[...], back).astype(BF16)
        vectors = [
            feed_pack_ref[width:].astype(F32),
            jnp.sum(first, axis=0, keepdims=True),
            jnp.sum(bias2_ref[...], axis=0, keepdims=True),
        ]
        lower = [own_grad, nbr_grad, feed_pack_ref[:width]]
        upper = [joint_ref[table_rows:].astype(BF16), dw2_ref[...].astype(BF16), edge_pack_ref[...]]

        def fill(ref, pieces, tail):
            base = 0
            for piece in pieces:
                ref[base : base + piece.shape[0]] = piece
                base += piece.shape[0]
            if base < ref.shape[0]:
                gap = ref.shape[0] - base - sum(v.shape[0] for v in tail)
                rest = jnp.concatenate(tail + [jnp.zeros((gap, width), F32)], axis=0)
                ref[base:] = rest.astype(BF16)

        @pl.when(core_ref[0] == 0)
        def _():
            fill(keep_ref, lower, [])
            fill(send_ref, upper, vectors)

        @pl.when(core_ref[0] != 0)
        def _():
            fill(send_ref, lower, [])
            fill(keep_ref, upper, vectors)


def wrapped(value, size):
    value = jnp.where(value >= size, value - size, value)
    return jnp.where(value < 0, value + size, value)


def pick_of(index, values):
    result = values[0]
    for i in range(1, len(values)):
        result = jnp.where(index == i, values[i], result)
    return result


def pair_kernel(y_ref, x_ref, keep_ref, came_ref, away_ref, *out_refs, parts, cap):
    y_size = lax.axis_size("y")
    x_size = lax.axis_size("x")
    z_size = parts // x_size
    riders = z_size * cap
    share = keep_ref.shape[0] // len(out_refs)
    away = away_ref[...].astype(F32)
    for e, out_ref in enumerate(out_refs):
        dy, dx = divmod(e, x_size)
        x = wrapped(x_ref[0] + dx, x_size)
        device = wrapped(y_ref[0] + dy, y_size) * x_size + x
        part = pl.ds(pl.multiple_of(device * share, 16), share)
        at = out_ref.shape[0] - share
        out_ref[at:] = (keep_ref[part, :].astype(F32) + came_ref[part, :].astype(F32)).astype(BF16)
        if at:
            rows = []
            for to in range(x_size):
                owners = [(z * x_size + to) * cap for z in range(z_size)]
                rows.append(jnp.concatenate([away[o : o + cap] for o in owners], axis=0))
            out_ref[:riders] = pick_of(x, rows).astype(BF16)


def plane_kernel(x_ref, z_ref, *refs, peers, cap):
    came_refs, out_refs = refs[:peers], refs[peers:]
    x_size = lax.axis_size("x")
    z_size = len(out_refs)
    riders = x_size * cap
    share = out_refs[0].shape[0] - riders
    first = z_size * cap
    rows = []
    for source in range(x_size):
        pieces = [ref[:first].astype(F32) for ref in came_refs[:x_size]]
        rows.append(pick_of(wrapped(x_ref[0] - source, x_size), pieces))
    for dz, out_ref in enumerate(out_refs):
        z = wrapped(z_ref[0] + dz, z_size)
        value = jnp.zeros((share, out_ref.shape[1]), F32)
        for e, ref in enumerate(came_refs):
            start = z * share + (first if e < x_size else 0)
            value = value + ref[pl.ds(pl.multiple_of(start, 16), share), :].astype(F32)
        out_ref[riders:] = value.astype(BF16)
        part = [
            pick_of(z, [value[i * cap : (i + 1) * cap] for i in range(z_size)]) for value in rows
        ]
        out_ref[:riders] = jnp.concatenate(part, axis=0).astype(BF16)


def column_kernel(z_ref, *refs):
    came_refs, total_ref, returned_ref = refs[:-2], refs[-2], refs[-1]
    z_size = len(came_refs)
    riders = returned_ref.shape[0] // z_size
    value = jnp.zeros(total_ref.shape, F32)
    for dz, ref in enumerate(came_refs):
        value = value + ref[riders:].astype(F32)
        start = wrapped(z_ref[0] - dz, z_size) * riders
        returned_ref[pl.ds(pl.multiple_of(start, 16), riders), :] = ref[:riders]
    total_ref[...] = value.astype(BF16)


def plane_stack_kernel(y_ref, x_ref, *refs):
    came_refs, out_ref = refs[:-1], refs[-1]
    x_size = lax.axis_size("x")
    share = came_refs[0].shape[0]
    for e, ref in enumerate(came_refs):
        dy, dx = divmod(e, x_size)
        y = wrapped(y_ref[0] - dy, len(came_refs) // x_size)
        start = (y * x_size + wrapped(x_ref[0] - dx, x_size)) * share
        out_ref[pl.ds(pl.multiple_of(start, 16), share), :] = ref[...]


def stack_kernel(z_ref, *refs):
    came_refs, out_ref = refs[:-1], refs[-1]
    share = came_refs[0].shape[0]
    for dz, ref in enumerate(came_refs):
        start = wrapped(z_ref[0] - dz, len(came_refs)) * share
        out_ref[pl.ds(pl.multiple_of(start, 16), share), :] = ref[...]


def node_grad_kernel(grad_ref, first_ref, own_ref, arrived_ref, asked_ref, w1_ref, out_ref):
    rows, width = grad_ref.shape
    back = own_ref[...] + dot_nn(asked_onehot(asked_ref, rows), arrived_ref[...])
    out_ref[...] = (
        grad_ref[...]
        + dot_split(dot_nt, first_ref[...], w1_ref[:width])
        + dot_split(dot_nt, back, w1_ref[width : 2 * width])
    )


def unpack_kernel(core_ref, y_ref, x_ref, *refs, peers, lasts):
    mine_refs, other_refs, refs = refs[:peers], refs[peers : 2 * peers], refs[2 * peers :]
    bias_ref, last_bias_refs = refs[0], refs[1 : 1 + lasts]
    mine_ref, other_ref = refs[-2:]
    refs = refs[1 + lasts : -2]
    x_size = lax.axis_size("x")
    share = mine_refs[0].shape[0]
    for e in range(peers):
        dy, dx = divmod(e, x_size)
        device = wrapped(y_ref[0] - dy, peers // x_size) * x_size + wrapped(x_ref[0] - dx, x_size)
        part = pl.ds(pl.multiple_of(device * share, 16), share)
        mine_ref[part, :] = mine_refs[e][...]
        other_ref[part, :] = other_refs[e][...]
    (
        message1_ref,
        message1_bias_ref,
        message2_ref,
        message2_bias_ref,
        message3_ref,
        message3_bias_ref,
        gain1_ref,
        shift1_ref,
        expand_bias_ref,
        contract_bias_ref,
        gain2_ref,
        shift2_ref,
        edge1_ref,
        edge1_bias_ref,
        edge2_ref,
        edge2_bias_ref,
        edge3_ref,
        edge3_bias_ref,
        gain3_ref,
        shift3_ref,
    ) = refs
    width = mine_ref.shape[1]
    edge_width = edge2_ref.shape[0]
    half = width // 2
    first_core = core_ref[0] == 0

    def lower(start, stop):
        return jnp.where(first_core, mine_ref[start:stop], other_ref[start:stop]).astype(F32)

    def upper(start, stop):
        return jnp.where(first_core, other_ref[start:stop], mine_ref[start:stop]).astype(F32)

    message1_ref[: 2 * width] = lower(0, 2 * width)
    message3_ref[...] = lower(2 * width, 3 * width)
    message1_ref[2 * width :] = upper(0, edge_width)
    base = edge_width
    message2_ref[...] = upper(base, base + width)
    base = base + width
    edge1_ref[:, :width] = upper(base, base + edge_width)
    edge1_ref[:, width : 2 * width] = upper(base + edge_width, base + 2 * edge_width)
    third = upper(base + 2 * edge_width, base + 3 * edge_width)
    edge1_ref[:, 2 * width :] = third[:, :edge_width]
    edge2_ref[...] = third[:, half : half + edge_width]
    edge3_ref[...] = upper(base + 3 * edge_width, base + 4 * edge_width)[:, :edge_width]
    base = base + 4 * edge_width
    vectors = upper(base, mine_ref.shape[0])
    targets = (message3_bias_ref, gain1_ref, shift1_ref, gain2_ref, shift2_ref)
    for i, ref in enumerate(targets):
        ref[...] = vectors[i]
    targets = (edge1_bias_ref, edge2_bias_ref, edge3_bias_ref, gain3_ref, shift3_ref)
    for i, ref in enumerate(targets):
        ref[...] = vectors[5 + i, :edge_width]
    message1_bias_ref[...] = vectors[16]
    message2_bias_ref[...] = vectors[17]
    expand_bias_ref[...] = bias_ref[0]
    contract_bias = last_bias_refs[0][0]
    for ref in last_bias_refs[1:]:
        contract_bias = contract_bias + ref[0]
    contract_bias_ref[...] = contract_bias


def gather_copies(copies, axes):
    return lax.all_to_all(copies, axes, split_axis=0, concat_axis=0, tiled=True)


def copies_of(values, axes):
    return jnp.broadcast_to(values[None], (lax.axis_size(axes), *values.shape))


def exchange(values, parts):
    grouped = values.reshape(parts, values.shape[0] // parts, values.shape[1])
    arrived = lax.all_to_all(grouped, RES, split_axis=0, concat_axis=0, tiled=True)
    return arrived.reshape(values.shape)


def move(values, dy=0, dz=0, dx=0):
    sizes = [lax.axis_size(axis) for axis in SIDE]
    pairs = []
    for i in range(math.prod(sizes)):
        rest, x = divmod(i, sizes[2])
        y, z = divmod(rest, sizes[1])
        to_y, to_z, to_x = (y + dy) % sizes[0], (z + dz) % sizes[1], (x + dx) % sizes[2]
        pairs.append((i, (to_y * sizes[1] + to_z) * sizes[2] + to_x))
    return lax.ppermute(values, SIDE, pairs)


def other_core(values):
    return lax.ppermute(values, "core", [(0, 1), (1, 0)])


def whole(shape):
    return pl.BlockSpec(shape, lambda *_: (0,) * len(shape))


def params(mebibytes):
    return pltpu.CompilerParams(vmem_limit_bytes=mebibytes * MIB)


def cost(microseconds):
    return pl.CostEstimate(
        flops=int(microseconds * 1.15e9),
        bytes_accessed=int(microseconds * 3.69e6),
        transcendentals=0,
    )


def body(
    node_states,
    edge_states,
    neighbour_index,
    edge_mask,
    node_cotangent,
    edge_cotangent,
    message_weight1,
    message_bias1,
    message_weight2,
    message_bias2,
    message_weight3,
    message_bias3,
    norm1_gain,
    norm1_shift,
    expand_weight,
    expand_bias,
    contract_weight,
    contract_bias,
    norm2_gain,
    norm2_shift,
    edge_weight1,
    edge_bias1,
    edge_weight2,
    edge_bias2,
    edge_weight3,
    edge_bias3,
    norm3_gain,
    norm3_shift,
):
    self_rows = node_states[0]
    rows, width = self_rows.shape
    slots = neighbour_index.shape[2]
    edge_width = edge_states.shape[3]
    hidden = expand_weight.shape[1]
    edges = rows * slots
    parts = lax.axis_size(RES)
    cap = ROW_CAP
    table_rows = rows + parts * cap
    side = lax.axis_size(SIDE)
    steps = STEPS
    block_slots = slots // steps
    block = block_slots * rows
    pairs = block // LANES

    everyone = gather_copies(copies_of(self_rows, RES), RES).reshape(parts * rows, width)
    core = lax.axis_index("core").astype(jnp.int32).reshape(1)
    me = lax.axis_index(RES).astype(jnp.int32).reshape(1)
    edge_rows = edge_states[0].transpose(1, 0, 2)
    edge_cot = edge_cotangent[0].transpose(1, 0, 2)
    slot_index = neighbour_index.transpose(2, 0, 1)
    slot_mask = edge_mask.transpose(2, 0, 1)
    edge_w1t = edge_weight1.T
    wide = (
        message_bias1,
        message_bias2,
        message_bias3,
        norm1_gain,
        norm1_shift,
        contract_bias,
        norm2_gain,
        norm2_shift,
        expand_bias,
    )
    narrow = (edge_bias1, edge_bias2, edge_bias3, norm3_gain, norm3_shift)
    vmem = pl.BlockSpec(memory_space=pltpu.VMEM)

    def shape(dims, kind):
        return jax.ShapeDtypeStruct(dims, kind)

    pos, select, ids, counts, vectors, bias_row = pl.pallas_call(
        functools.partial(
            prepare_kernel, parts=parts, cap=cap, steps=steps, wide=len(wide), narrow=len(narrow)
        ),
        out_shape=(
            shape((steps, LANES, pairs), jnp.int32),
            shape((parts * rows, table_rows), BF16),
            shape((parts, cap), jnp.int32),
            shape((rows, width), F32),
            shape((V_ROWS, width), F32),
            shape((1, hidden), F32),
        ),
        in_specs=[pl.BlockSpec(memory_space=pltpu.SMEM)] + [vmem] * (2 + len(wide) + len(narrow)),
        out_specs=(vmem,) * 6,
        compiler_params=params(56),
        cost_estimate=cost(6),
        name="prepare",
    )(me, slot_index, slot_mask, *wide, *narrow)
    ids, everyone = lax.optimization_barrier((ids, everyone))
    asked = lax.all_to_all(ids, RES, split_axis=0, concat_axis=0, tiled=True)

    edge_spec = pl.BlockSpec((block_slots, rows, edge_width), lambda i: (i, 0, 0))
    flat_spec = pl.BlockSpec((block, width), lambda i: (i, 0))
    pos_spec = pl.BlockSpec((1, LANES, pairs), lambda i: (i, 0, 0))
    any_spec = pl.BlockSpec(memory_space=pl.ANY)
    node_spec = whole((rows, width))
    away_spec = whole((parts * cap, width))

    (
        act1,
        slope1,
        slope2,
        fresh,
        table,
        mixed1,
        mixed2,
        low,
        slope_e,
        act_sum,
    ) = pl.pallas_call(
        node_kernel,
        grid=(steps,),
        in_specs=[
            edge_spec,
            pos_spec,
            whole((parts * rows, table_rows)),
            whole((parts * rows, width)),
            node_spec,
            node_spec,
            whole((V_ROWS, width)),
            whole(message_weight1.shape),
            whole((width, width)),
            whole((width, width)),
            any_spec,
            any_spec,
        ],
        out_specs=[
            flat_spec,
            flat_spec,
            flat_spec,
            node_spec,
            whole((table_rows, width)),
            node_spec,
            node_spec,
            node_spec,
            whole((rows, hidden)),
            node_spec,
        ],
        out_shape=[
            shape((edges, width), BF16),
            shape((edges, width), BF16),
            shape((edges, width), BF16),
            shape((rows, width), BF16),
            shape((table_rows, width), BF16),
            shape((rows, width), F32),
            shape((rows, width), F32),
            shape((rows, width), BF16),
            shape((rows, hidden), F32),
            shape((rows, width), F32),
        ],
        scratch_shapes=[
            pltpu.VMEM((table_rows, width), BF16),
            pltpu.VMEM((rows, width), F32),
            pltpu.VMEM((width, hidden), BF16),
            pltpu.VMEM((hidden, width), BF16),
            pltpu.SemaphoreType.DMA((2,)),
        ],
        compiler_params=params(56),
        cost_estimate=cost(26),
        name="node_forward",
    )(
        edge_rows,
        pos,
        select,
        everyone,
        self_rows,
        counts,
        vectors,
        message_weight1,
        message_weight2,
        message_weight3,
        expand_weight,
        contract_weight,
    )
    outgoing = pl.pallas_call(
        pick_kernel,
        in_specs=[vmem] * 2,
        out_specs=vmem,
        out_shape=shape((parts * cap, width), BF16),
        compiler_params=params(8),
        cost_estimate=cost(1),
        name="pick",
    )(asked, fresh)
    y_size = lax.axis_size("y")
    x_size = lax.axis_size("x")
    z_size = lax.axis_size("z")
    peers = y_size * x_size
    my_y = lax.axis_index("y").astype(jnp.int32).reshape(1)
    my_x = lax.axis_index("x").astype(jnp.int32).reshape(1)
    my_z = lax.axis_index("z").astype(jnp.int32).reshape(1)
    smem = pl.BlockSpec(memory_space=pltpu.SMEM)
    steps_of = [divmod(e, x_size) for e in range(peers)]

    def over_plane(values):
        came = [values[0]]
        for value, (dy, dx) in zip(values[1:], steps_of[1:]):
            came.append(move(value, dy=dy, dx=dx))
        return came

    def over_z(values):
        return [values[0]] + [move(value, dz=d) for d, value in enumerate(values[1:], start=1)]

    def stack_z(came):
        return pl.pallas_call(
            stack_kernel,
            in_specs=[smem] + [vmem] * z_size,
            out_specs=vmem,
            out_shape=shape((z_size * came[0].shape[0], width), BF16),
            compiler_params=params(8),
            cost_estimate=cost(1),
            name="stack",
        )(my_z, *came)

    outgoing, low = lax.optimization_barrier((outgoing, low))
    incoming = exchange(outgoing, parts)
    low_column = stack_z(over_z([low] * z_size))

    edge_pack_rows = 4 * edge_width
    edge_out, grad_partial, edge_first, edge_own, edge_away, edge_pack, edge_vec = pl.pallas_call(
        edge_kernel,
        grid=(steps,),
        in_specs=[
            edge_spec,
            edge_spec,
            pos_spec,
            node_spec,
            away_spec,
            node_spec,
            whole((V_ROWS, width)),
            whole(edge_w1t.shape),
            whole((edge_width, edge_width)),
            whole((edge_width, edge_width)),
        ],
        out_specs=[
            edge_spec,
            edge_spec,
            whole((rows, edge_width)),
            whole((rows, edge_width)),
            whole((parts * cap, edge_width)),
            whole((edge_pack_rows, width)),
            whole((8, width)),
        ],
        out_shape=[
            shape((slots, rows, edge_width), BF16),
            shape((slots, rows, edge_width), F32),
            shape((rows, edge_width), F32),
            shape((rows, edge_width), F32),
            shape((parts * cap, edge_width), BF16),
            shape((edge_pack_rows, width), BF16),
            shape((8, width), F32),
        ],
        scratch_shapes=[
            pltpu.VMEM((table_rows, width), BF16),
            pltpu.VMEM((table_rows, edge_width), BF16),
            pltpu.VMEM((rows, edge_width), F32),
            pltpu.VMEM((table_rows, edge_width), F32),
            pltpu.VMEM((edge_width, edge_width), F32),
            pltpu.VMEM((edge_width, edge_width), F32),
            pltpu.VMEM((edge_width, edge_width), F32),
            pltpu.VMEM((5, rows, edge_width), F32),
            pltpu.VMEM((3, edge_width, edge_width), BF16),
        ],
        compiler_params=params(56),
        cost_estimate=cost(6),
        name="edge_both",
    )(
        edge_rows,
        edge_cot,
        pos,
        fresh,
        incoming,
        counts,
        vectors,
        edge_w1t,
        edge_weight2,
        edge_weight3,
    )
    edge_away, low_column = lax.optimization_barrier((edge_away, low_column))
    edge_arrived = exchange(edge_away, parts)
    low_pieces = over_plane([low_column] * peers)

    feed_rows = width + 16
    feed_pack, grad_copies, spread, grad_mixed1 = pl.pallas_call(
        feed_kernel,
        in_specs=[vmem] * 12 + [any_spec] * 2 + [vmem] * 2,
        out_specs=[vmem] * 4,
        out_shape=[
            shape((feed_rows, width), BF16),
            shape((side, rows, width), BF16),
            shape((rows, width), F32),
            shape((rows, width), F32),
        ],
        scratch_shapes=[
            pltpu.VMEM((width, hidden), BF16),
            pltpu.VMEM((hidden, width), BF16),
            pltpu.SemaphoreType.DMA((2 * hidden // width,)),
        ],
        compiler_params=params(56),
        cost_estimate=cost(7),
        name="feed_backward",
    )(
        node_cotangent[0],
        edge_first,
        edge_own,
        edge_arrived,
        asked,
        counts,
        vectors,
        edge_w1t,
        mixed1,
        mixed2,
        slope_e,
        act_sum,
        expand_weight,
        contract_weight,
        message_weight3,
        edge_vec,
    )
    grad_mine = gather_copies(grad_copies, BY_COLUMN).reshape(side * rows, width)
    spread, low_pieces = lax.optimization_barrier((spread, low_pieces))

    unit = 16 * side
    half_rows = (3 * width + unit - 1) // unit * unit
    third = edge_width // 3
    edge_grad, first, own, away, send, keep = pl.pallas_call(
        message_kernel,
        grid=(steps,),
        in_specs=[
            pl.BlockSpec(memory_space=pltpu.SMEM),
            edge_spec,
            pos_spec,
            flat_spec,
            flat_spec,
            flat_spec,
            edge_spec,
            node_spec,
            whole((table_rows, width)),
            *[
                pl.BlockSpec((third, width), lambda i, p=p: (2 * width // third + p, 0))
                for p in range(3)
            ],
            whole((width, width)),
            whole((edge_pack_rows, width)),
            whole((feed_rows, width)),
        ],
        out_specs=[
            edge_spec,
            node_spec,
            node_spec,
            away_spec,
            whole((half_rows, width)),
            whole((half_rows, width)),
        ],
        out_shape=[
            shape((slots, rows, edge_width), F32),
            shape((rows, width), F32),
            shape((rows, width), F32),
            shape((parts * cap, width), BF16),
            shape((half_rows, width), BF16),
            shape((half_rows, width), BF16),
        ],
        scratch_shapes=[
            pltpu.VMEM((table_rows + edge_width, width), F32),
            pltpu.VMEM((width, width), F32),
            pltpu.VMEM((rows, width), F32),
            pltpu.VMEM((width, width), BF16),
            pltpu.VMEM((width, edge_width), BF16),
        ],
        compiler_params=params(56),
        cost_estimate=cost(14),
        name="message_backward",
    )(
        core,
        edge_rows,
        pos,
        act1,
        slope1,
        slope2,
        grad_partial,
        spread,
        table,
        message_weight1,
        message_weight1,
        message_weight1,
        message_weight2,
        edge_pack,
        feed_pack,
    )
    came = other_core(send)
    share = half_rows // peers
    pieces = pl.pallas_call(
        functools.partial(pair_kernel, parts=parts, cap=cap),
        in_specs=[smem] * 2 + [vmem] * 3,
        out_specs=[vmem] * peers,
        out_shape=[
            shape((share if dy else share + z_size * cap, width), BF16) for dy, _ in steps_of
        ],
        compiler_params=params(20),
        cost_estimate=cost(3),
        name="pair_sum",
    )(my_y, my_x, keep, came, away)
    _, grad_mine, low_pieces = lax.optimization_barrier((pieces[0], grad_mine, low_pieces))
    low_mine = pl.pallas_call(
        plane_stack_kernel,
        in_specs=[smem] * 2 + [vmem] * peers,
        out_specs=vmem,
        out_shape=shape((side * rows, width), BF16),
        compiler_params=params(max(8, side * rows // 256)),
        cost_estimate=cost(1),
        name="plane_stack",
    )(my_y, my_x, *low_pieces)

    arrived = over_plane(pieces)
    grad_other = other_core(grad_mine)
    low_other = other_core(low_mine)

    units = 256
    chunks = hidden // units
    last_biases = []

    def feed_weights(low_values, grad_values, at, block_rows, part, sums, more):
        start, stop = part
        last = start == 0
        row_block = pl.BlockSpec((block_rows, width), lambda c: (at, 0))
        sum_specs = [
            pl.BlockSpec((width, units), lambda c: (0, start + c)),
            pl.BlockSpec((units, width), lambda c: (start + c, 0)),
            pl.BlockSpec((8, units), lambda c: (0, start + c)),
        ]
        results = pl.pallas_call(
            functools.partial(feed_weight_kernel, more=more, last=last),
            grid=(stop - start,),
            in_specs=[
                row_block,
                row_block,
                sum_specs[0],
                pl.BlockSpec((1, units), lambda c: (0, start + c)),
                sum_specs[1],
                *(sum_specs if more else [any_spec] * len(sums)),
            ],
            out_specs=sum_specs + ([whole((8, width))] if last else []),
            scratch_shapes=[
                pltpu.VMEM((width, block_rows), BF16),
                pltpu.VMEM((width, block_rows), BF16),
            ],
            out_shape=[
                shape((width, hidden), F32),
                shape((hidden, width), F32),
                shape((8, hidden), F32),
            ]
            + ([shape((8, width), F32)] if last else []),
            input_output_aliases={5 + i: i for i in range(len(sums))},
            compiler_params=params(56),
            cost_estimate=cost(2 * (stop - start) + 1),
            name="feed_weights_more" if more else "feed_weights",
        )(low_values, grad_values, expand_weight, bias_row, contract_weight, *sums)
        last_biases.extend(results[3:])
        return tuple(results[:3])

    def feed_side(low_values, grad_values, part, sums, more):
        block_rows = min(side * rows, 1024)
        for at in range(side * rows // block_rows):
            sums = feed_weights(low_values, grad_values, at, block_rows, part, sums, more or at > 0)
        return sums

    most, rest = (0, chunks - 2), (chunks - 2, chunks)
    sums = feed_side(low_mine, grad_mine, most, (), False)
    arrived, sums = lax.optimization_barrier((arrived, sums))
    pieces = pl.pallas_call(
        functools.partial(plane_kernel, peers=peers, cap=cap),
        in_specs=[smem] * 2 + [vmem] * peers,
        out_specs=[vmem] * z_size,
        out_shape=[shape((half_rows // side + x_size * cap, width), BF16)] * z_size,
        compiler_params=params(16),
        cost_estimate=cost(3),
        name="plane_sum",
    )(my_x, my_z, *arrived)
    _, sums = lax.optimization_barrier((pieces[0], sums))
    sums = feed_side(low_mine, grad_mine, rest, sums, False)
    arrived, sums = lax.optimization_barrier((over_z(pieces), sums))
    total, returned = pl.pallas_call(
        column_kernel,
        in_specs=[smem] + [vmem] * z_size,
        out_specs=[vmem] * 2,
        out_shape=[
            shape((half_rows // side, width), BF16),
            shape((parts * cap, width), BF16),
        ],
        compiler_params=params(8),
        cost_estimate=cost(1),
        name="column_sum",
    )(my_z, *arrived)
    arrived = over_z([total] * z_size)
    _, grad_other, low_other, sums = lax.optimization_barrier((total, grad_other, low_other, sums))
    sums = feed_side(low_other, grad_other, rest, sums, True)
    arrived, sums = lax.optimization_barrier((arrived, sums))
    column = stack_z(arrived)
    _, grad_other, low_other, sums = lax.optimization_barrier((column, grad_other, low_other, sums))
    mine = over_plane([column] * peers)
    other_first = other_core(column)
    sums = feed_side(low_other, grad_other, most, sums, True)
    mine, other_first, sums = lax.optimization_barrier((mine, other_first, sums))
    grad_expand, grad_contract, expand_bias_sum = sums
    other = [other_first] + [other_core(value) for value in mine[1:]]
    node_grad = pl.pallas_call(
        node_grad_kernel,
        in_specs=[vmem] * 6,
        out_specs=vmem,
        out_shape=shape((rows, width), F32),
        compiler_params=params(12),
        cost_estimate=cost(3),
        name="node_gradient",
    )(grad_mixed1, first, own, returned, asked, message_weight1)

    vec = shape((width,), F32)
    thin = shape((edge_width,), F32)
    square = shape((width, width), F32)
    small = shape((edge_width, edge_width), F32)
    (
        grad_message1,
        grad_mb1,
        grad_message2,
        grad_mb2,
        grad_message3,
        grad_mb3,
        grad_n1g,
        grad_n1s,
        grad_eb,
        grad_cb,
        grad_n2g,
        grad_n2s,
        grad_edge1_t,
        grad_eb1,
        grad_edge2,
        grad_eb2,
        grad_edge3,
        grad_eb3,
        grad_n3g,
        grad_n3s,
    ) = pl.pallas_call(
        functools.partial(unpack_kernel, peers=peers, lasts=len(last_biases)),
        in_specs=[smem] * 3 + [vmem] * (2 * peers + 1 + len(last_biases)),
        out_specs=[vmem] * 20,
        out_shape=[
            shape(message_weight1.shape, F32),
            vec,
            square,
            vec,
            square,
            vec,
            vec,
            vec,
            shape((hidden,), F32),
            vec,
            vec,
            vec,
            shape(edge_w1t.shape, F32),
            thin,
            small,
            thin,
            small,
            thin,
            thin,
            thin,
        ],
        scratch_shapes=[pltpu.VMEM((half_rows, width), BF16)] * 2,
        compiler_params=params(24),
        cost_estimate=cost(4),
        name="unpack",
    )(core, my_y, my_x, *mine, *other, expand_bias_sum, *last_biases)
    return (
        fresh[None],
        edge_out.transpose(1, 0, 2)[None],
        node_grad[None],
        edge_grad.transpose(1, 0, 2)[None],
        grad_message1,
        grad_mb1,
        grad_message2,
        grad_mb2,
        grad_message3,
        grad_mb3,
        grad_n1g,
        grad_n1s,
        grad_expand,
        grad_eb,
        grad_contract,
        grad_cb,
        grad_n2g,
        grad_n2s,
        grad_edge1_t.T,
        grad_eb1,
        grad_edge2,
        grad_eb2,
        grad_edge3,
        grad_eb3,
        grad_n3g,
        grad_n3s,
    )


def solution(mesh):
    batch, res = mesh.shape["batch"], mesh.shape["res"]
    x_size = 1 << ((res.bit_length() - 1) // 2)
    sizes = (batch // CORES, CORES, res // x_size, x_size)
    fine = jax.sharding.Mesh(mesh.devices.reshape(sizes), ALL)
    row_spec = P(("y", "core"), RES, None)
    edge_spec = P(("y", "core"), RES, None, None)
    return jax.shard_map(
        body,
        mesh=fine,
        in_specs=(row_spec, edge_spec, row_spec, row_spec, row_spec, edge_spec) + (P(),) * 22,
        out_specs=(row_spec, edge_spec, row_spec, edge_spec) + (P(),) * 22,
        check_vma=False,
    )
```

```python
import functools
import math

import jax
import jax.numpy as jnp
from jax import lax
from jax.experimental import pallas as pl
from jax.experimental.pallas import tpu as pltpu
from jax.sharding import PartitionSpec as P

ROW_CAP = 8
CORES = 2
RES = ("z", "x")
PLANE = ("y", "x")
SIDE = ("y", "z", "x")
BY_COLUMN = ("y", "x", "z")
ALL = ("y", "core", "z", "x")
EPSILON = 1e-05
LANES = 128
MIB = 1024 * 1024
STEPS = 3
F32 = jnp.float32
BF16 = jnp.bfloat16

V_MB1, V_MB2, V_MB3, V_N1G, V_N1S, V_CB, V_N2G, V_N2S, V_EB = range(9)
V_EDGE = 12
V_ROWS = 24


def dot_nn(left, right):
    return lax.dot_general(left, right, (((1,), (0,)), ((), ())), preferred_element_type=F32)


def dot_nt(left, right):
    return lax.dot_general(left, right, (((1,), (1,)), ((), ())), preferred_element_type=F32)


def dot_tn(left, right):
    return lax.dot_general(left, right, (((0,), (0,)), ((), ())), preferred_element_type=F32)


def split_low(values):
    high = values.astype(BF16)
    return high, (values - high.astype(F32)).astype(BF16)


def dot_split(dot, left, right):
    high, rest = split_low(left)
    return dot(high, right) + dot(rest, right)


def dot_split_right(dot, left, right):
    high, rest = split_low(right)
    return dot(left, high) + dot(left, rest)


def gelu_pair(v):
    e = jnp.exp2((v * v) * (-0.5 * math.log2(math.e)))
    phi_sum = 0.5 + 0.5 * lax.erf(v * math.sqrt(0.5))
    return v * phi_sum, phi_sum + (v * (1.0 / math.sqrt(2.0 * math.pi))) * e


def norm_parts(values):
    average = jnp.mean(values, axis=-1, keepdims=True)
    centred = values - average
    variance = jnp.mean(centred * centred, axis=-1, keepdims=True)
    scale = lax.rsqrt(variance + EPSILON)
    return centred * scale, scale


def norm_back(xhat, scale, gain, upstream):
    w = upstream * gain
    mean_w = jnp.mean(w, axis=-1, keepdims=True)
    mean_wx = jnp.mean(w * xhat, axis=-1, keepdims=True)
    return (w - mean_w - xhat * mean_wx) * scale


def edge_onehot(pos_ref, table_rows):
    pairs = pos_ref.shape[2]
    lane = lax.broadcasted_iota(jnp.int32, (LANES, table_rows), 1)
    return jnp.concatenate(
        [(pos_ref[0, :, p : p + 1] == lane).astype(F32).astype(BF16) for p in range(pairs)], axis=0
    )


def prepare_kernel(me_ref, idx_ref, mask_ref, *refs, parts, cap, steps, wide, narrow):
    wide_refs = refs[:wide]
    narrow_refs = refs[wide : wide + narrow]
    pos_ref, select_ref, ids_ref, count_ref, vec_ref, expand_bias_ref = refs[wide + narrow :]
    rows, width = count_ref.shape
    total = rows * parts
    table = rows + parts * cap
    me = me_ref[0]
    pair_rows = idx_ref.shape[0] // 2
    named = [
        jnp.concatenate([idx_ref[2 * j], idx_ref[2 * j + 1]], axis=1) for j in range(pair_rows)
    ]
    residue = lax.broadcasted_iota(jnp.int32, (total, LANES), 0)
    owner = residue // rows
    within = residue - owner * rows
    hits = jnp.zeros((total, LANES), F32)
    for j in range(pair_rows):
        hits = jnp.where(named[j] == residue, 1.0, hits)
    hit = jnp.max(hits, axis=1, keepdims=True)
    own = owner == me
    wanted = jnp.where(own, 0.0, jnp.broadcast_to(hit, (total, LANES)))
    low_row = lax.broadcasted_iota(jnp.int32, (rows, rows), 0)
    low_col = lax.broadcasted_iota(jnp.int32, (rows, rows), 1)
    lower = (low_col <= low_row).astype(F32).astype(BF16)
    wanted_low = wanted.astype(BF16)
    place = jnp.concatenate(
        [dot_nn(lower, wanted_low[o * rows : (o + 1) * rows]) for o in range(parts)], axis=0
    )
    place = jnp.clip(place - 1.0, 0.0, cap - 1.0)
    pos = jnp.where(own, within.astype(F32), (rows + owner * cap).astype(F32) + place)
    picked = [
        jnp.sum(jnp.where(named[j] == residue, pos, 0.0), axis=0, keepdims=True)
        for j in range(pair_rows)
    ]
    picked.append(jnp.zeros((LANES - pair_rows, LANES), F32))
    turned = jnp.concatenate(picked, axis=0).T.astype(jnp.int32)
    per = pair_rows // steps
    for s in range(steps):
        pos_ref[s] = turned[:, s * per : (s + 1) * per]
    lane = lax.broadcasted_iota(jnp.int32, (total, table), 1).astype(F32)
    live = jnp.where(own, 1.0, wanted)
    chosen = jnp.where(lane == pos[:, :1], jnp.broadcast_to(live[:, :1], (total, table)), 0.0)
    select_ref[...] = chosen.astype(BF16)
    asked_row = jnp.broadcast_to(within[:, :1].astype(F32), (total, parts * cap))
    ids = jnp.sum(chosen[:, rows:] * asked_row, axis=0, keepdims=True)
    ids = ids.astype(jnp.int32)
    for o in range(parts):
        ids_ref[o : o + 1, :] = ids[:, o * cap : (o + 1) * cap]
    count = mask_ref[0]
    for k in range(1, mask_ref.shape[0]):
        count = count + mask_ref[k]
    count = jnp.concatenate([count.astype(F32), jnp.zeros((7, rows), F32)], axis=0)
    count_ref[...] = dot_tn(count.astype(BF16), jnp.ones((8, width), F32).astype(BF16))
    expand_bias_ref[...] = wide_refs[-1][...].astype(F32).reshape(expand_bias_ref.shape)
    vec_ref[...] = jnp.zeros_like(vec_ref)
    at = 0
    for ref in wide_refs:
        for c in range(ref.shape[0] // width):
            part = ref[c * width : (c + 1) * width]
            vec_ref[at : at + 1, :] = part.astype(F32).reshape(1, width)
            at += 1
    for ref in narrow_refs:
        vec_ref[at : at + 1, : ref.shape[0]] = ref[...].astype(F32).reshape(1, ref.shape[0])
        at += 1


def node_kernel(
    edge_ref,
    pos_ref,
    select_ref,
    all_ref,
    self_ref,
    count_ref,
    vec_ref,
    w1_ref,
    w2_ref,
    w3_ref,
    expand_hbm,
    contract_hbm,
    act1_ref,
    slope1_ref,
    slope2_ref,
    fresh_ref,
    table_ref,
    mixed1_ref,
    mixed2_ref,
    low_ref,
    slope_e_ref,
    act_sum_ref,
    proj_ref,
    self_pre_ref,
    expand_ref,
    contract_ref,
    sems,
):
    step = pl.program_id(0)
    last = pl.num_programs(0) - 1
    rows, width = self_ref.shape
    slots = edge_ref.shape[0]
    edge_width = edge_ref.shape[2]
    table_rows = table_ref.shape[0]
    expand_copy = pltpu.make_async_copy(expand_hbm, expand_ref, sems.at[0])
    contract_copy = pltpu.make_async_copy(contract_hbm, contract_ref, sems.at[1])

    @pl.when(step == 0)
    def _():
        expand_copy.start()
        contract_copy.start()
        table = dot_tn(select_ref[...], all_ref[...]).astype(BF16)
        table_ref[...] = table
        proj_ref[...] = dot_nn(table, w1_ref[width : 2 * width]).astype(BF16)
        self_pre_ref[...] = (
            dot_nn(self_ref[...], w1_ref[:width]) + vec_ref[V_MB1 : V_MB1 + 1, :]
        )
        act_sum_ref[...] = jnp.zeros_like(act_sum_ref)

    onehot = edge_onehot(pos_ref, table_rows)
    features = edge_ref[...].reshape(slots * rows, edge_width)
    pre1 = dot_nn(features, w1_ref[2 * width :]) + dot_nn(onehot, proj_ref[...])
    self_pre = self_pre_ref[...]
    act1 = []
    for k in range(slots):
        part = pl.ds(k * rows, rows)
        act, slope = gelu_pair(pre1[k * rows : (k + 1) * rows] + self_pre)
        act = act.astype(BF16)
        act1.append(act)
        act1_ref[part, :] = act
        slope1_ref[part, :] = slope.astype(BF16)
    pre2 = dot_nn(jnp.concatenate(act1, axis=0), w2_ref[...])
    bias2 = vec_ref[V_MB2 : V_MB2 + 1, :]
    act_sum = act_sum_ref[...]
    counts = count_ref[...]
    for k in range(slots):
        act, slope = gelu_pair(pre2[k * rows : (k + 1) * rows] + bias2)
        valid = counts > (step * slots + k).astype(F32)
        act_sum = act_sum + jnp.where(valid, act.astype(BF16).astype(F32), 0.0)
        slope2_ref[pl.ds(k * rows, rows), :] = jnp.where(valid, slope, 0.0).astype(BF16)
    act_sum_ref[...] = act_sum

    @pl.when(step == last)
    def _():
        summed = dot_split(dot_nn, act_sum_ref[...], w3_ref[...])
        summed = summed + counts * vec_ref[V_MB3 : V_MB3 + 1, :]
        mixed1 = self_ref[...].astype(F32) + summed / counts
        mixed1_ref[...] = mixed1
        xhat1, _ = norm_parts(mixed1)
        updated = xhat1 * vec_ref[V_N1G : V_N1G + 1, :] + vec_ref[V_N1S : V_N1S + 1, :]
        low = updated.astype(BF16)
        low_ref[...] = low
        expand_copy.wait()
        contract_copy.wait()
        mixed2 = updated + vec_ref[V_CB : V_CB + 1, :]
        for c in range(expand_ref.shape[1] // width):
            cols = slice(c * width, (c + 1) * width)
            pre = dot_nn(low, expand_ref[:, cols]) + vec_ref[V_EB + c : V_EB + c + 1, :]
            act, slope = gelu_pair(pre)
            act = act.astype(BF16)
            slope_e_ref[:, cols] = slope
            mixed2 = mixed2 + dot_nn(act, contract_ref[cols, :])
        mixed2_ref[...] = mixed2
        xhat2, _ = norm_parts(mixed2)
        fresh = (xhat2 * vec_ref[V_N2G : V_N2G + 1, :] + vec_ref[V_N2S : V_N2S + 1, :]).astype(BF16)
        fresh_ref[...] = fresh


def asked_onehot(asked_ref, rows):
    parts = asked_ref.shape[0]
    asked = jnp.concatenate([asked_ref[o : o + 1, :] for o in range(parts)], axis=1)
    row = lax.broadcasted_iota(jnp.int32, (rows, asked.shape[1]), 0)
    return (asked == row).astype(F32).astype(BF16)


def pick_kernel(asked_ref, fresh_ref, out_ref):
    out_ref[...] = dot_tn(asked_onehot(asked_ref, fresh_ref.shape[0]), fresh_ref[...]).astype(BF16)


def edge_kernel(
    edge_ref,
    cot_ref,
    pos_ref,
    fresh_ref,
    incoming_ref,
    count_ref,
    vec_ref,
    w1t_ref,
    w2_ref,
    w3_ref,
    out_ref,
    grad_ref,
    first_ref,
    own_ref,
    away_ref,
    pack_ref,
    vec_out_ref,
    table_ref,
    proj_ref,
    self_pre_ref,
    back_ref,
    dw3_ref,
    dw2_ref,
    dw1_ref,
    sums_ref,
    turned_ref,
):
    step = pl.program_id(0)
    last = pl.num_programs(0) - 1
    rows, width = fresh_ref.shape
    slots, _, edge_width = edge_ref.shape
    block = slots * rows
    table_rows = table_ref.shape[0]
    own_t = w1t_ref[:, :width]
    nbr_t = w1t_ref[:, width : 2 * width]
    feat_t = w1t_ref[:, 2 * width :]

    def vector(i):
        return vec_ref[V_EDGE + i : V_EDGE + i + 1, :edge_width]

    @pl.when(step == 0)
    def _():
        table_ref[:rows] = fresh_ref[...]
        table_ref[rows:] = incoming_ref[...]
        proj_ref[...] = dot_nt(table_ref[...], nbr_t).astype(BF16)
        self_pre_ref[...] = dot_nt(fresh_ref[...], own_t) + vector(0)
        for ref in (back_ref, dw3_ref, dw2_ref, dw1_ref, sums_ref, first_ref):
            ref[...] = jnp.zeros_like(ref)
        turned_ref[0] = feat_t.T
        turned_ref[1] = w2_ref[...].T
        turned_ref[2] = w3_ref[...].T

    def flat(values):
        return values.reshape(block, edge_width)

    def deep(values):
        return values.reshape(slots, rows, edge_width)

    onehot = edge_onehot(pos_ref, table_rows)
    features = flat(edge_ref[...])
    pre1 = dot_nn(features, turned_ref[0]) + dot_nn(onehot, proj_ref[...])
    pre1 = deep(pre1) + self_pre_ref[...][None]
    act1, slope1 = gelu_pair(flat(pre1))
    act1 = act1.astype(BF16)
    pre2 = dot_nn(act1, w2_ref[...]) + vector(1)
    act2, slope2 = gelu_pair(pre2)
    act2 = act2.astype(BF16)
    mixed3 = features.astype(F32) + (dot_nn(act2, w3_ref[...]) + vector(2))
    xhat, scale = norm_parts(mixed3)
    gain = vector(3)
    slot = lax.broadcasted_iota(jnp.int32, (slots, rows, edge_width), 0) + step * slots
    valid = count_ref[...][None, :, :edge_width] > slot.astype(F32)
    out_ref[...] = jnp.where(valid, deep(xhat * gain + vector(4)), 0.0).astype(BF16)
    upstream = flat(jnp.where(valid, cot_ref[...].astype(F32), 0.0))
    sums_ref[3] += jnp.sum(deep(upstream * xhat), axis=0)
    sums_ref[4] += jnp.sum(deep(upstream), axis=0)
    grad_mixed = norm_back(xhat, scale, gain, upstream)
    grad_delta = grad_mixed.astype(BF16)
    dw3_ref[...] += dot_tn(act2, grad_delta)
    sums_ref[2] += jnp.sum(deep(grad_delta.astype(F32)), axis=0)
    grad2 = (dot_nn(grad_delta, turned_ref[2]) * slope2).astype(BF16)
    dw2_ref[...] += dot_tn(act1, grad2)
    sums_ref[1] += jnp.sum(deep(grad2.astype(F32)), axis=0)
    grad1 = (dot_nn(grad2, turned_ref[1]) * slope1).astype(BF16)
    dw1_ref[...] += dot_tn(grad1, features)
    first_ref[...] += jnp.sum(deep(grad1.astype(F32)), axis=0)
    back_ref[...] += dot_tn(onehot, grad1)
    grad_ref[...] = deep(grad_mixed + dot_nn(grad1, feat_t))

    @pl.when(step == last)
    def _():
        first = first_ref[...]
        back = back_ref[...]
        own_ref[...] = back[:rows]
        away_ref[...] = back[rows:].astype(BF16)
        first_high, first_rest = split_low(first)
        back_high, back_rest = split_low(back)
        own_grad = dot_tn(first_high, fresh_ref[...]) + dot_tn(first_rest, fresh_ref[...])
        nbr_grad = dot_tn(back_high, table_ref[...]) + dot_tn(back_rest, table_ref[...])
        pack_ref[:edge_width, :] = own_grad.astype(BF16)
        pack_ref[edge_width : 2 * edge_width, :] = nbr_grad.astype(BF16)
        pad = jnp.zeros((edge_width, width // 2 - edge_width), BF16)
        third = [dw1_ref[...].astype(BF16), pad, dw2_ref[...].astype(BF16), pad]
        pack_ref[2 * edge_width : 3 * edge_width, :] = jnp.concatenate(third, axis=1)
        fourth = [dw3_ref[...].astype(BF16), pad, jnp.zeros((edge_width, width // 2), BF16)]
        pack_ref[3 * edge_width :, :] = jnp.concatenate(fourth, axis=1)
        vec_out_ref[...] = jnp.zeros_like(vec_out_ref)
        vec_out_ref[0:1, :edge_width] = jnp.sum(first, axis=0, keepdims=True)
        for i in range(1, 5):
            vec_out_ref[i : i + 1, :edge_width] = jnp.sum(sums_ref[i], axis=0, keepdims=True)


def feed_kernel(
    cot_ref,
    first_ref,
    own_ref,
    arrived_ref,
    asked_ref,
    count_ref,
    vec_ref,
    w1t_ref,
    mixed1_ref,
    mixed2_ref,
    slope_ref,
    act_sum_ref,
    expand_hbm,
    contract_hbm,
    w3_ref,
    edge_vec_ref,
    pack_ref,
    copies_ref,
    spread_ref,
    grad_mixed1_ref,
    expand_ref,
    contract_ref,
    sems,
):
    rows, width = cot_ref.shape
    hidden = expand_ref.shape[1]
    own_t = w1t_ref[:, :width]
    nbr_t = w1t_ref[:, width : 2 * width]
    counts = count_ref[...]
    copies = []
    for c in range(hidden // width):
        rows_part, cols_part = pl.ds(c * width, width), pl.ds(c * width, width)
        copies.append(
            (
                pltpu.make_async_copy(
                    contract_hbm.at[rows_part, :], contract_ref.at[rows_part, :], sems.at[2 * c]
                ),
                pltpu.make_async_copy(
                    expand_hbm.at[:, cols_part], expand_ref.at[:, cols_part], sems.at[2 * c + 1]
                ),
            )
        )
    for pair in copies:
        for copy in pair:
            copy.start()

    def vector(i):
        return vec_ref[i : i + 1, :]

    def total(values):
        return jnp.sum(values.astype(F32), axis=0, keepdims=True)

    back = own_ref[...] + dot_nn(asked_onehot(asked_ref, rows), arrived_ref[...])
    grad_fresh = (
        cot_ref[...].astype(F32)
        + dot_split(dot_nn, first_ref[...], own_t)
        + dot_split(dot_nn, back, nbr_t)
    )
    xhat2, scale2 = norm_parts(mixed2_ref[...])
    grad_mixed2 = norm_back(xhat2, scale2, vector(V_N2G), grad_fresh)
    grad_contracted = grad_mixed2.astype(BF16)
    for p in range(copies_ref.shape[0]):
        copies_ref[p] = grad_contracted
    grad_updated = grad_mixed2
    for c in range(hidden // width):
        cols = slice(c * width, (c + 1) * width)
        copies[c][0].wait()
        pre = dot_nt(grad_contracted, contract_ref[cols, :]) * slope_ref[:, cols]
        copies[c][1].wait()
        grad_updated = grad_updated + dot_nt(pre.astype(BF16), expand_ref[:, cols])
    xhat1, scale1 = norm_parts(mixed1_ref[...])
    grad_mixed1 = norm_back(xhat1, scale1, vector(V_N1G), grad_updated)
    grad_mixed1_ref[...] = grad_mixed1
    grad_message = (grad_mixed1 / counts).astype(BF16)
    spread_ref[...] = dot_nt(grad_message, w3_ref[...])
    pack_ref[:width, :] = dot_split(dot_tn, act_sum_ref[...], grad_message).astype(BF16)
    vectors = [
        total(counts * grad_message.astype(F32)),
        total(grad_updated * xhat1),
        total(grad_updated),
        total(grad_fresh * xhat2),
        total(grad_fresh),
        edge_vec_ref[...],
    ]
    vectors = jnp.concatenate(vectors, axis=0)
    vectors = jnp.concatenate(
        [vectors, jnp.zeros((pack_ref.shape[0] - width - vectors.shape[0], width), F32)], axis=0
    )
    pack_ref[width:, :] = vectors.astype(BF16)


def feed_weight_kernel(
    low_ref, grad_ref, expand_ref, bias_ref, contract_ref, *refs, more, last
):
    sums_in = refs[:3] if more else None
    outputs = refs[-6:-2] if last else refs[-5:-2]
    expand_out_ref, contract_out_ref, bias_out_ref = outputs[:3]
    low_turned_ref, grad_turned_ref = refs[-2:]
    ones = jnp.ones((8, low_ref.shape[0]), F32).astype(BF16)

    @pl.when(pl.program_id(0) == 0)
    def _():
        low_turned_ref[...] = low_ref[...].T
        grad_turned_ref[...] = grad_ref[...].T
        if last:
            outputs[3][...] = dot_nn(ones, grad_ref[...])

    act, slope = gelu_pair(dot_nn(low_ref[...], expand_ref[...]) + bias_ref[0:1, :])
    act = act.astype(BF16)
    pre = (dot_nt(grad_ref[...], contract_ref[...]) * slope).astype(BF16)
    expanded = dot_nn(low_turned_ref[...], pre)
    contracted = dot_nn(grad_turned_ref[...], act).T
    sums = dot_nn(ones, pre)
    if more:
        expanded = expanded + sums_in[0][...]
        contracted = contracted + sums_in[1][...]
        sums = sums + sums_in[2][...]
    expand_out_ref[...] = expanded
    contract_out_ref[...] = contracted
    bias_out_ref[...] = sums


def message_kernel(
    core_ref,
    edge_ref,
    pos_ref,
    act1_ref,
    slope1_ref,
    slope2_ref,
    partial_ref,
    spread_ref,
    table_ref,
    w1_a_ref,
    w1_b_ref,
    w1_c_ref,
    w2_ref,
    edge_pack_ref,
    feed_pack_ref,
    grad_ref,
    first_ref,
    own_ref,
    away_ref,
    send_ref,
    keep_ref,
    joint_ref,
    dw2_ref,
    bias2_ref,
    w2_turned_ref,
    w1_turned_ref,
):
    step = pl.program_id(0)
    last = pl.num_programs(0) - 1
    slots, rows, edge_width = edge_ref.shape
    width = act1_ref.shape[1]
    block = slots * rows
    table_rows = table_ref.shape[0]

    @pl.when(step == 0)
    def _():
        for ref in (joint_ref, dw2_ref, bias2_ref, first_ref):
            ref[...] = jnp.zeros_like(ref)
        w2_turned_ref[...] = w2_ref[...].T
        w1_parts = [ref[...] for ref in (w1_a_ref, w1_b_ref, w1_c_ref)]
        w1_turned_ref[...] = jnp.concatenate(w1_parts, axis=0).T

    spread = spread_ref[...]
    grad2 = []
    bias2 = bias2_ref[...]
    for k in range(slots):
        part = (spread * slope2_ref[pl.ds(k * rows, rows), :].astype(F32)).astype(BF16)
        bias2 = bias2 + part.astype(F32)
        grad2.append(part)
    bias2_ref[...] = bias2
    grad2 = jnp.concatenate(grad2, axis=0)
    dw2_ref[...] += dot_tn(act1_ref[...], grad2)
    grad1 = (dot_nn(grad2, w2_turned_ref[...]) * slope1_ref[...].astype(F32)).astype(BF16)
    first_ref[...] += jnp.sum(grad1.astype(F32).reshape(slots, rows, width), axis=0)
    onehot = edge_onehot(pos_ref, table_rows)
    features = edge_ref[...].reshape(block, edge_width)
    joint_ref[...] += dot_tn(jnp.concatenate([onehot, features], axis=1), grad1)
    grad_ref[...] = partial_ref[...] + dot_nn(grad1, w1_turned_ref[...]).reshape(
        slots, rows, edge_width
    )

    @pl.when(step == last)
    def _():
        first = first_ref[...]
        back = joint_ref[:table_rows]
        own_ref[...] = back[:rows]
        away_ref[...] = back[rows:].astype(BF16)
        own_grad = dot_split_right(dot_tn, table_ref[:rows], first).astype(BF16)
        nbr_grad = dot_split_right(dot_tn, table_ref[...], back).astype(BF16)
        vectors = [
            feed_pack_ref[width:].astype(F32),
            jnp.sum(first, axis=0, keepdims=True),
            jnp.sum(bias2_ref[...], axis=0, keepdims=True),
        ]
        lower = [own_grad, nbr_grad, feed_pack_ref[:width]]
        upper = [joint_ref[table_rows:].astype(BF16), dw2_ref[...].astype(BF16), edge_pack_ref[...]]

        def fill(ref, pieces, tail):
            base = 0
            for piece in pieces:
                ref[base : base + piece.shape[0]] = piece
                base += piece.shape[0]
            if base < ref.shape[0]:
                gap = ref.shape[0] - base - sum(v.shape[0] for v in tail)
                rest = jnp.concatenate(tail + [jnp.zeros((gap, width), F32)], axis=0)
                ref[base:] = rest.astype(BF16)

        @pl.when(core_ref[0] == 0)
        def _():
            fill(keep_ref, lower, [])
            fill(send_ref, upper, vectors)

        @pl.when(core_ref[0] != 0)
        def _():
            fill(send_ref, lower, [])
            fill(keep_ref, upper, vectors)


def wrapped(value, size):
    value = jnp.where(value >= size, value - size, value)
    return jnp.where(value < 0, value + size, value)


def pick_of(index, values):
    result = values[0]
    for i in range(1, len(values)):
        result = jnp.where(index == i, values[i], result)
    return result


def hold_kernel(keep_ref, away_ref, keep_out_ref, away_out_ref):
    keep_out_ref[...] = keep_ref[...]
    away_out_ref[...] = away_ref[...]


def pair_kernel(y_ref, x_ref, keep_ref, came_ref, away_ref, *out_refs, parts, cap):
    y_size = lax.axis_size("y")
    x_size = lax.axis_size("x")
    z_size = parts // x_size
    riders = z_size * cap
    share = keep_ref.shape[0] // len(out_refs)
    away = away_ref[...].astype(F32)
    for e, out_ref in enumerate(out_refs):
        dy, dx = divmod(e, x_size)
        x = wrapped(x_ref[0] + dx, x_size)
        device = wrapped(y_ref[0] + dy, y_size) * x_size + x
        part = pl.ds(pl.multiple_of(device * share, 16), share)
        at = out_ref.shape[0] - share
        out_ref[at:] = (keep_ref[part, :].astype(F32) + came_ref[part, :].astype(F32)).astype(BF16)
        if at:
            rows = []
            for to in range(x_size):
                owners = [(z * x_size + to) * cap for z in range(z_size)]
                rows.append(jnp.concatenate([away[o : o + cap] for o in owners], axis=0))
            out_ref[:riders] = pick_of(x, rows).astype(BF16)


def plane_kernel(x_ref, z_ref, *refs, peers, cap):
    came_refs, out_refs = refs[:peers], refs[peers:]
    x_size = lax.axis_size("x")
    z_size = len(out_refs)
    riders = x_size * cap
    share = out_refs[0].shape[0] - riders
    first = z_size * cap
    rows = []
    for source in range(x_size):
        pieces = [ref[:first].astype(F32) for ref in came_refs[:x_size]]
        rows.append(pick_of(wrapped(x_ref[0] - source, x_size), pieces))
    for dz, out_ref in enumerate(out_refs):
        z = wrapped(z_ref[0] + dz, z_size)
        value = jnp.zeros((share, out_ref.shape[1]), F32)
        for e, ref in enumerate(came_refs):
            start = z * share + (first if e < x_size else 0)
            value = value + ref[pl.ds(pl.multiple_of(start, 16), share), :].astype(F32)
        out_ref[riders:] = value.astype(BF16)
        part = [
            pick_of(z, [value[i * cap : (i + 1) * cap] for i in range(z_size)]) for value in rows
        ]
        out_ref[:riders] = jnp.concatenate(part, axis=0).astype(BF16)


def column_kernel(z_ref, *refs):
    came_refs, total_ref, returned_ref = refs[:-2], refs[-2], refs[-1]
    z_size = len(came_refs)
    riders = returned_ref.shape[0] // z_size
    value = jnp.zeros(total_ref.shape, F32)
    for dz, ref in enumerate(came_refs):
        value = value + ref[riders:].astype(F32)
        start = wrapped(z_ref[0] - dz, z_size) * riders
        returned_ref[pl.ds(pl.multiple_of(start, 16), riders), :] = ref[:riders]
    total_ref[...] = value.astype(BF16)


def plane_stack_kernel(y_ref, x_ref, *refs):
    came_refs, out_ref = refs[:-1], refs[-1]
    x_size = lax.axis_size("x")
    share = came_refs[0].shape[0]
    for e, ref in enumerate(came_refs):
        dy, dx = divmod(e, x_size)
        y = wrapped(y_ref[0] - dy, len(came_refs) // x_size)
        start = (y * x_size + wrapped(x_ref[0] - dx, x_size)) * share
        out_ref[pl.ds(pl.multiple_of(start, 16), share), :] = ref[...]


def stack_kernel(z_ref, *refs):
    came_refs, out_ref = refs[:-1], refs[-1]
    share = came_refs[0].shape[0]
    for dz, ref in enumerate(came_refs):
        start = wrapped(z_ref[0] - dz, len(came_refs)) * share
        out_ref[pl.ds(pl.multiple_of(start, 16), share), :] = ref[...]


def node_grad_kernel(grad_ref, first_ref, own_ref, arrived_ref, asked_ref, w1_ref, out_ref):
    rows, width = grad_ref.shape
    back = own_ref[...] + dot_nn(asked_onehot(asked_ref, rows), arrived_ref[...])
    out_ref[...] = (
        grad_ref[...]
        + dot_split(dot_nt, first_ref[...], w1_ref[:width])
        + dot_split(dot_nt, back, w1_ref[width : 2 * width])
    )


def unpack_kernel(core_ref, y_ref, x_ref, *refs, peers, lasts):
    mine_refs, other_refs, refs = refs[:peers], refs[peers : 2 * peers], refs[2 * peers :]
    bias_ref, last_bias_refs = refs[0], refs[1 : 1 + lasts]
    mine_ref, other_ref = refs[-2:]
    refs = refs[1 + lasts : -2]
    x_size = lax.axis_size("x")
    share = mine_refs[0].shape[0]
    for e in range(peers):
        dy, dx = divmod(e, x_size)
        device = wrapped(y_ref[0] - dy, peers // x_size) * x_size + wrapped(x_ref[0] - dx, x_size)
        part = pl.ds(pl.multiple_of(device * share, 16), share)
        mine_ref[part, :] = mine_refs[e][...]
        other_ref[part, :] = other_refs[e][...]
    (
        message1_ref,
        message1_bias_ref,
        message2_ref,
        message2_bias_ref,
        message3_ref,
        message3_bias_ref,
        gain1_ref,
        shift1_ref,
        expand_bias_ref,
        contract_bias_ref,
        gain2_ref,
        shift2_ref,
        edge1_ref,
        edge1_bias_ref,
        edge2_ref,
        edge2_bias_ref,
        edge3_ref,
        edge3_bias_ref,
        gain3_ref,
        shift3_ref,
    ) = refs
    width = mine_ref.shape[1]
    edge_width = edge2_ref.shape[0]
    half = width // 2
    first_core = core_ref[0] == 0

    def lower(start, stop):
        return jnp.where(first_core, mine_ref[start:stop], other_ref[start:stop]).astype(F32)

    def upper(start, stop):
        return jnp.where(first_core, other_ref[start:stop], mine_ref[start:stop]).astype(F32)

    message1_ref[: 2 * width] = lower(0, 2 * width)
    message3_ref[...] = lower(2 * width, 3 * width)
    message1_ref[2 * width :] = upper(0, edge_width)
    base = edge_width
    message2_ref[...] = upper(base, base + width)
    base = base + width
    edge1_ref[:, :width] = upper(base, base + edge_width)
    edge1_ref[:, width : 2 * width] = upper(base + edge_width, base + 2 * edge_width)
    third = upper(base + 2 * edge_width, base + 3 * edge_width)
    edge1_ref[:, 2 * width :] = third[:, :edge_width]
    edge2_ref[...] = third[:, half : half + edge_width]
    edge3_ref[...] = upper(base + 3 * edge_width, base + 4 * edge_width)[:, :edge_width]
    base = base + 4 * edge_width
    vectors = upper(base, mine_ref.shape[0])
    targets = (message3_bias_ref, gain1_ref, shift1_ref, gain2_ref, shift2_ref)
    for i, ref in enumerate(targets):
        ref[...] = vectors[i]
    targets = (edge1_bias_ref, edge2_bias_ref, edge3_bias_ref, gain3_ref, shift3_ref)
    for i, ref in enumerate(targets):
        ref[...] = vectors[5 + i, :edge_width]
    message1_bias_ref[...] = vectors[16]
    message2_bias_ref[...] = vectors[17]
    expand_bias_ref[...] = bias_ref[0]
    contract_bias = last_bias_refs[0][0]
    for ref in last_bias_refs[1:]:
        contract_bias = contract_bias + ref[0]
    contract_bias_ref[...] = contract_bias


def gather_copies(copies, axes):
    return lax.all_to_all(copies, axes, split_axis=0, concat_axis=0, tiled=True)


def copies_of(values, axes):
    return jnp.broadcast_to(values[None], (lax.axis_size(axes), *values.shape))


def exchange(values, parts):
    grouped = values.reshape(parts, values.shape[0] // parts, values.shape[1])
    arrived = lax.all_to_all(grouped, RES, split_axis=0, concat_axis=0, tiled=True)
    return arrived.reshape(values.shape)


def move(values, dy=0, dz=0, dx=0):
    sizes = [lax.axis_size(axis) for axis in SIDE]
    pairs = []
    for i in range(math.prod(sizes)):
        rest, x = divmod(i, sizes[2])
        y, z = divmod(rest, sizes[1])
        to_y, to_z, to_x = (y + dy) % sizes[0], (z + dz) % sizes[1], (x + dx) % sizes[2]
        pairs.append((i, (to_y * sizes[1] + to_z) * sizes[2] + to_x))
    return lax.ppermute(values, SIDE, pairs)


def other_core(values):
    return lax.ppermute(values, "core", [(0, 1), (1, 0)])


def whole(shape):
    return pl.BlockSpec(shape, lambda *_: (0,) * len(shape))


def params(mebibytes):
    return pltpu.CompilerParams(vmem_limit_bytes=mebibytes * MIB)


def cost(microseconds):
    return pl.CostEstimate(
        flops=int(microseconds * 1.15e9),
        bytes_accessed=int(microseconds * 3.69e6),
        transcendentals=0,
    )


def body(
    node_states,
    edge_states,
    neighbour_index,
    edge_mask,
    node_cotangent,
    edge_cotangent,
    message_weight1,
    message_bias1,
    message_weight2,
    message_bias2,
    message_weight3,
    message_bias3,
    norm1_gain,
    norm1_shift,
    expand_weight,
    expand_bias,
    contract_weight,
    contract_bias,
    norm2_gain,
    norm2_shift,
    edge_weight1,
    edge_bias1,
    edge_weight2,
    edge_bias2,
    edge_weight3,
    edge_bias3,
    norm3_gain,
    norm3_shift,
):
    self_rows = node_states[0]
    rows, width = self_rows.shape
    slots = neighbour_index.shape[2]
    edge_width = edge_states.shape[3]
    hidden = expand_weight.shape[1]
    edges = rows * slots
    parts = lax.axis_size(RES)
    cap = ROW_CAP
    table_rows = rows + parts * cap
    side = lax.axis_size(SIDE)
    steps = STEPS
    block_slots = slots // steps
    block = block_slots * rows
    pairs = block // LANES

    everyone = gather_copies(copies_of(self_rows, RES), RES).reshape(parts * rows, width)
    core = lax.axis_index("core").astype(jnp.int32).reshape(1)
    me = lax.axis_index(RES).astype(jnp.int32).reshape(1)
    edge_rows = edge_states[0].transpose(1, 0, 2)
    edge_cot = edge_cotangent[0].transpose(1, 0, 2)
    slot_index = neighbour_index.transpose(2, 0, 1)
    slot_mask = edge_mask.transpose(2, 0, 1)
    edge_w1t = edge_weight1.T
    wide = (
        message_bias1,
        message_bias2,
        message_bias3,
        norm1_gain,
        norm1_shift,
        contract_bias,
        norm2_gain,
        norm2_shift,
        expand_bias,
    )
    narrow = (edge_bias1, edge_bias2, edge_bias3, norm3_gain, norm3_shift)
    vmem = pl.BlockSpec(memory_space=pltpu.VMEM)

    def shape(dims, kind):
        return jax.ShapeDtypeStruct(dims, kind)

    pos, select, ids, counts, vectors, bias_row = pl.pallas_call(
        functools.partial(
            prepare_kernel, parts=parts, cap=cap, steps=steps, wide=len(wide), narrow=len(narrow)
        ),
        out_shape=(
            shape((steps, LANES, pairs), jnp.int32),
            shape((parts * rows, table_rows), BF16),
            shape((parts, cap), jnp.int32),
            shape((rows, width), F32),
            shape((V_ROWS, width), F32),
            shape((1, hidden), F32),
        ),
        in_specs=[pl.BlockSpec(memory_space=pltpu.SMEM)] + [vmem] * (2 + len(wide) + len(narrow)),
        out_specs=(vmem,) * 6,
        compiler_params=params(56),
        cost_estimate=cost(6),
        name="prepare",
    )(me, slot_index, slot_mask, *wide, *narrow)
    ids, everyone = lax.optimization_barrier((ids, everyone))
    asked = lax.all_to_all(ids, RES, split_axis=0, concat_axis=0, tiled=True)

    edge_spec = pl.BlockSpec((block_slots, rows, edge_width), lambda i: (i, 0, 0))
    flat_spec = pl.BlockSpec((block, width), lambda i: (i, 0))
    pos_spec = pl.BlockSpec((1, LANES, pairs), lambda i: (i, 0, 0))
    any_spec = pl.BlockSpec(memory_space=pl.ANY)
    node_spec = whole((rows, width))
    away_spec = whole((parts * cap, width))

    (
        act1,
        slope1,
        slope2,
        fresh,
        table,
        mixed1,
        mixed2,
        low,
        slope_e,
        act_sum,
    ) = pl.pallas_call(
        node_kernel,
        grid=(steps,),
        in_specs=[
            edge_spec,
            pos_spec,
            whole((parts * rows, table_rows)),
            whole((parts * rows, width)),
            node_spec,
            node_spec,
            whole((V_ROWS, width)),
            whole(message_weight1.shape),
            whole((width, width)),
            whole((width, width)),
            any_spec,
            any_spec,
        ],
        out_specs=[
            flat_spec,
            flat_spec,
            flat_spec,
            node_spec,
            whole((table_rows, width)),
            node_spec,
            node_spec,
            node_spec,
            whole((rows, hidden)),
            node_spec,
        ],
        out_shape=[
            shape((edges, width), BF16),
            shape((edges, width), BF16),
            shape((edges, width), BF16),
            shape((rows, width), BF16),
            shape((table_rows, width), BF16),
            shape((rows, width), F32),
            shape((rows, width), F32),
            shape((rows, width), BF16),
            shape((rows, hidden), F32),
            shape((rows, width), F32),
        ],
        scratch_shapes=[
            pltpu.VMEM((table_rows, width), BF16),
            pltpu.VMEM((rows, width), F32),
            pltpu.VMEM((width, hidden), BF16),
            pltpu.VMEM((hidden, width), BF16),
            pltpu.SemaphoreType.DMA((2,)),
        ],
        compiler_params=params(56),
        cost_estimate=cost(26),
        name="node_forward",
    )(
        edge_rows,
        pos,
        select,
        everyone,
        self_rows,
        counts,
        vectors,
        message_weight1,
        message_weight2,
        message_weight3,
        expand_weight,
        contract_weight,
    )
    outgoing = pl.pallas_call(
        pick_kernel,
        in_specs=[vmem] * 2,
        out_specs=vmem,
        out_shape=shape((parts * cap, width), BF16),
        compiler_params=params(8),
        cost_estimate=cost(1),
        name="pick",
    )(asked, fresh)
    y_size = lax.axis_size("y")
    x_size = lax.axis_size("x")
    z_size = lax.axis_size("z")
    peers = y_size * x_size
    my_y = lax.axis_index("y").astype(jnp.int32).reshape(1)
    my_x = lax.axis_index("x").astype(jnp.int32).reshape(1)
    my_z = lax.axis_index("z").astype(jnp.int32).reshape(1)
    smem = pl.BlockSpec(memory_space=pltpu.SMEM)
    steps_of = [divmod(e, x_size) for e in range(peers)]

    def over_plane(values):
        came = [values[0]]
        for value, (dy, dx) in zip(values[1:], steps_of[1:]):
            came.append(move(value, dy=dy, dx=dx))
        return came

    def over_z(values):
        return [values[0]] + [move(value, dz=d) for d, value in enumerate(values[1:], start=1)]

    def stack_z(came):
        return pl.pallas_call(
            stack_kernel,
            in_specs=[smem] + [vmem] * z_size,
            out_specs=vmem,
            out_shape=shape((z_size * came[0].shape[0], width), BF16),
            compiler_params=params(8),
            cost_estimate=cost(1),
            name="stack",
        )(my_z, *came)

    outgoing, low = lax.optimization_barrier((outgoing, low))
    incoming = exchange(outgoing, parts)
    low_column = stack_z(over_z([low] * z_size))

    edge_pack_rows = 4 * edge_width
    edge_out, grad_partial, edge_first, edge_own, edge_away, edge_pack, edge_vec = pl.pallas_call(
        edge_kernel,
        grid=(steps,),
        in_specs=[
            edge_spec,
            edge_spec,
            pos_spec,
            node_spec,
            away_spec,
            node_spec,
            whole((V_ROWS, width)),
            whole(edge_w1t.shape),
            whole((edge_width, edge_width)),
            whole((edge_width, edge_width)),
        ],
        out_specs=[
            edge_spec,
            edge_spec,
            whole((rows, edge_width)),
            whole((rows, edge_width)),
            whole((parts * cap, edge_width)),
            whole((edge_pack_rows, width)),
            whole((8, width)),
        ],
        out_shape=[
            shape((slots, rows, edge_width), BF16),
            shape((slots, rows, edge_width), F32),
            shape((rows, edge_width), F32),
            shape((rows, edge_width), F32),
            shape((parts * cap, edge_width), BF16),
            shape((edge_pack_rows, width), BF16),
            shape((8, width), F32),
        ],
        scratch_shapes=[
            pltpu.VMEM((table_rows, width), BF16),
            pltpu.VMEM((table_rows, edge_width), BF16),
            pltpu.VMEM((rows, edge_width), F32),
            pltpu.VMEM((table_rows, edge_width), F32),
            pltpu.VMEM((edge_width, edge_width), F32),
            pltpu.VMEM((edge_width, edge_width), F32),
            pltpu.VMEM((edge_width, edge_width), F32),
            pltpu.VMEM((5, rows, edge_width), F32),
            pltpu.VMEM((3, edge_width, edge_width), BF16),
        ],
        compiler_params=params(56),
        cost_estimate=cost(10),
        name="edge_both",
    )(
        edge_rows,
        edge_cot,
        pos,
        fresh,
        incoming,
        counts,
        vectors,
        edge_w1t,
        edge_weight2,
        edge_weight3,
    )
    edge_away, low_column = lax.optimization_barrier((edge_away, low_column))
    edge_arrived = exchange(edge_away, parts)
    low_pieces = over_plane([low_column] * peers)

    feed_rows = width + 16
    feed_pack, grad_copies, spread, grad_mixed1 = pl.pallas_call(
        feed_kernel,
        in_specs=[vmem] * 12 + [any_spec] * 2 + [vmem] * 2,
        out_specs=[vmem] * 4,
        out_shape=[
            shape((feed_rows, width), BF16),
            shape((side, rows, width), BF16),
            shape((rows, width), F32),
            shape((rows, width), F32),
        ],
        scratch_shapes=[
            pltpu.VMEM((width, hidden), BF16),
            pltpu.VMEM((hidden, width), BF16),
            pltpu.SemaphoreType.DMA((2 * hidden // width,)),
        ],
        compiler_params=params(56),
        cost_estimate=cost(7),
        name="feed_backward",
    )(
        node_cotangent[0],
        edge_first,
        edge_own,
        edge_arrived,
        asked,
        counts,
        vectors,
        edge_w1t,
        mixed1,
        mixed2,
        slope_e,
        act_sum,
        expand_weight,
        contract_weight,
        message_weight3,
        edge_vec,
    )
    grad_mine = gather_copies(grad_copies, BY_COLUMN).reshape(side * rows, width)
    spread, low_pieces = lax.optimization_barrier((spread, low_pieces))

    unit = 16 * side
    half_rows = (3 * width + unit - 1) // unit * unit
    third = edge_width // 3
    edge_grad, first, own, away, send, keep = pl.pallas_call(
        message_kernel,
        grid=(steps,),
        in_specs=[
            pl.BlockSpec(memory_space=pltpu.SMEM),
            edge_spec,
            pos_spec,
            flat_spec,
            flat_spec,
            flat_spec,
            edge_spec,
            node_spec,
            whole((table_rows, width)),
            *[
                pl.BlockSpec((third, width), lambda i, p=p: (2 * width // third + p, 0))
                for p in range(3)
            ],
            whole((width, width)),
            whole((edge_pack_rows, width)),
            whole((feed_rows, width)),
        ],
        out_specs=[
            edge_spec,
            node_spec,
            node_spec,
            away_spec,
            whole((half_rows, width)),
            whole((half_rows, width)),
        ],
        out_shape=[
            shape((slots, rows, edge_width), F32),
            shape((rows, width), F32),
            shape((rows, width), F32),
            shape((parts * cap, width), BF16),
            shape((half_rows, width), BF16),
            shape((half_rows, width), BF16),
        ],
        scratch_shapes=[
            pltpu.VMEM((table_rows + edge_width, width), F32),
            pltpu.VMEM((width, width), F32),
            pltpu.VMEM((rows, width), F32),
            pltpu.VMEM((width, width), BF16),
            pltpu.VMEM((width, edge_width), BF16),
        ],
        compiler_params=params(56),
        cost_estimate=cost(14),
        name="message_backward",
    )(
        core,
        edge_rows,
        pos,
        act1,
        slope1,
        slope2,
        grad_partial,
        spread,
        table,
        message_weight1,
        message_weight1,
        message_weight1,
        message_weight2,
        edge_pack,
        feed_pack,
    )
    came = other_core(send)
    keep, away = pl.pallas_call(
        hold_kernel,
        in_specs=[vmem] * 2,
        out_specs=[vmem] * 2,
        out_shape=[shape(keep.shape, BF16), shape(away.shape, BF16)],
        compiler_params=params(12),
        cost_estimate=cost(2),
        name="hold",
    )(keep, away)
    share = half_rows // peers
    pieces = pl.pallas_call(
        functools.partial(pair_kernel, parts=parts, cap=cap),
        in_specs=[smem] * 2 + [vmem] * 3,
        out_specs=[vmem] * peers,
        out_shape=[
            shape((share if dy else share + z_size * cap, width), BF16) for dy, _ in steps_of
        ],
        compiler_params=params(20),
        cost_estimate=cost(3),
        name="pair_sum",
    )(my_y, my_x, keep, came, away)
    _, grad_mine, low_pieces = lax.optimization_barrier((pieces[0], grad_mine, low_pieces))
    low_mine = pl.pallas_call(
        plane_stack_kernel,
        in_specs=[smem] * 2 + [vmem] * peers,
        out_specs=vmem,
        out_shape=shape((side * rows, width), BF16),
        compiler_params=params(max(8, side * rows // 256)),
        cost_estimate=cost(1),
        name="plane_stack",
    )(my_y, my_x, *low_pieces)

    arrived = over_plane(pieces)
    grad_other = other_core(grad_mine)
    low_other = other_core(low_mine)

    units = 256
    chunks = hidden // units
    last_biases = []

    def feed_weights(low_values, grad_values, at, block_rows, part, sums, more):
        start, stop = part
        last = start == 0
        row_block = pl.BlockSpec((block_rows, width), lambda c: (at, 0))
        sum_specs = [
            pl.BlockSpec((width, units), lambda c: (0, start + c)),
            pl.BlockSpec((units, width), lambda c: (start + c, 0)),
            pl.BlockSpec((8, units), lambda c: (0, start + c)),
        ]
        results = pl.pallas_call(
            functools.partial(feed_weight_kernel, more=more, last=last),
            grid=(stop - start,),
            in_specs=[
                row_block,
                row_block,
                sum_specs[0],
                pl.BlockSpec((1, units), lambda c: (0, start + c)),
                sum_specs[1],
                *(sum_specs if more else [any_spec] * len(sums)),
            ],
            out_specs=sum_specs + ([whole((8, width))] if last else []),
            scratch_shapes=[
                pltpu.VMEM((width, block_rows), BF16),
                pltpu.VMEM((width, block_rows), BF16),
            ],
            out_shape=[
                shape((width, hidden), F32),
                shape((hidden, width), F32),
                shape((8, hidden), F32),
            ]
            + ([shape((8, width), F32)] if last else []),
            input_output_aliases={5 + i: i for i in range(len(sums))},
            compiler_params=params(56),
            cost_estimate=cost(2 * (stop - start) + 1),
            name="feed_weights_more" if more else "feed_weights",
        )(low_values, grad_values, expand_weight, bias_row, contract_weight, *sums)
        last_biases.extend(results[3:])
        return tuple(results[:3])

    def feed_side(low_values, grad_values, part, sums, more):
        block_rows = min(side * rows, 1024)
        for at in range(side * rows // block_rows):
            sums = feed_weights(low_values, grad_values, at, block_rows, part, sums, more or at > 0)
        return sums

    most, rest = (0, chunks - 2), (chunks - 2, chunks)
    sums = feed_side(low_mine, grad_mine, most, (), False)
    arrived, sums = lax.optimization_barrier((arrived, sums))
    pieces = pl.pallas_call(
        functools.partial(plane_kernel, peers=peers, cap=cap),
        in_specs=[smem] * 2 + [vmem] * peers,
        out_specs=[vmem] * z_size,
        out_shape=[shape((half_rows // side + x_size * cap, width), BF16)] * z_size,
        compiler_params=params(16),
        cost_estimate=cost(3),
        name="plane_sum",
    )(my_x, my_z, *arrived)
    _, sums = lax.optimization_barrier((pieces[0], sums))
    sums = feed_side(low_mine, grad_mine, rest, sums, False)
    arrived, sums = lax.optimization_barrier((over_z(pieces), sums))
    total, returned = pl.pallas_call(
        column_kernel,
        in_specs=[smem] + [vmem] * z_size,
        out_specs=[vmem] * 2,
        out_shape=[
            shape((half_rows // side, width), BF16),
            shape((parts * cap, width), BF16),
        ],
        compiler_params=params(8),
        cost_estimate=cost(1),
        name="column_sum",
    )(my_z, *arrived)
    arrived = over_z([total] * z_size)
    _, grad_other, low_other, sums = lax.optimization_barrier((total, grad_other, low_other, sums))
    sums = feed_side(low_other, grad_other, rest, sums, True)
    arrived, sums = lax.optimization_barrier((arrived, sums))
    column = stack_z(arrived)
    _, grad_other, low_other, sums = lax.optimization_barrier((column, grad_other, low_other, sums))
    mine = over_plane([column] * peers)
    other_first = other_core(column)
    sums = feed_side(low_other, grad_other, most, sums, True)
    mine, other_first, sums = lax.optimization_barrier((mine, other_first, sums))
    grad_expand, grad_contract, expand_bias_sum = sums
    other = [other_first] + [other_core(value) for value in mine[1:]]
    node_grad = pl.pallas_call(
        node_grad_kernel,
        in_specs=[vmem] * 6,
        out_specs=vmem,
        out_shape=shape((rows, width), F32),
        compiler_params=params(12),
        cost_estimate=cost(3),
        name="node_gradient",
    )(grad_mixed1, first, own, returned, asked, message_weight1)

    vec = shape((width,), F32)
    thin = shape((edge_width,), F32)
    square = shape((width, width), F32)
    small = shape((edge_width, edge_width), F32)
    (
        grad_message1,
        grad_mb1,
        grad_message2,
        grad_mb2,
        grad_message3,
        grad_mb3,
        grad_n1g,
        grad_n1s,
        grad_eb,
        grad_cb,
        grad_n2g,
        grad_n2s,
        grad_edge1_t,
        grad_eb1,
        grad_edge2,
        grad_eb2,
        grad_edge3,
        grad_eb3,
        grad_n3g,
        grad_n3s,
    ) = pl.pallas_call(
        functools.partial(unpack_kernel, peers=peers, lasts=len(last_biases)),
        in_specs=[smem] * 3 + [vmem] * (2 * peers + 1 + len(last_biases)),
        out_specs=[vmem] * 20,
        out_shape=[
            shape(message_weight1.shape, F32),
            vec,
            square,
            vec,
            square,
            vec,
            vec,
            vec,
            shape((hidden,), F32),
            vec,
            vec,
            vec,
            shape(edge_w1t.shape, F32),
            thin,
            small,
            thin,
            small,
            thin,
            thin,
            thin,
        ],
        scratch_shapes=[pltpu.VMEM((half_rows, width), BF16)] * 2,
        compiler_params=params(24),
        cost_estimate=cost(4),
        name="unpack",
    )(core, my_y, my_x, *mine, *other, expand_bias_sum, *last_biases)
    return (
        fresh[None],
        edge_out.transpose(1, 0, 2)[None],
        node_grad[None],
        edge_grad.transpose(1, 0, 2)[None],
        grad_message1,
        grad_mb1,
        grad_message2,
        grad_mb2,
        grad_message3,
        grad_mb3,
        grad_n1g,
        grad_n1s,
        grad_expand,
        grad_eb,
        grad_contract,
        grad_cb,
        grad_n2g,
        grad_n2s,
        grad_edge1_t.T,
        grad_eb1,
        grad_edge2,
        grad_eb2,
        grad_edge3,
        grad_eb3,
        grad_n3g,
        grad_n3s,
    )


def solution(mesh):
    batch, res = mesh.shape["batch"], mesh.shape["res"]
    x_size = 1 << ((res.bit_length() - 1) // 2)
    sizes = (batch // CORES, CORES, res // x_size, x_size)
    fine = jax.sharding.Mesh(mesh.devices.reshape(sizes), ALL)
    row_spec = P(("y", "core"), RES, None)
    edge_spec = P(("y", "core"), RES, None, None)
    return jax.shard_map(
        body,
        mesh=fine,
        in_specs=(row_spec, edge_spec, row_spec, row_spec, row_spec, edge_spec) + (P(),) * 22,
        out_specs=(row_spec, edge_spec, row_spec, edge_spec) + (P(),) * 22,
        check_vma=False,
    )
```

```python
import functools
import math

import jax
import jax.numpy as jnp
from jax import lax
from jax.experimental import pallas as pl
from jax.experimental.pallas import tpu as pltpu
from jax.sharding import PartitionSpec as P

ROW_CAP = 8
CORES = 2
RES = ("z", "x")
PLANE = ("y", "x")
SIDE = ("y", "z", "x")
BY_COLUMN = ("y", "x", "z")
ALL = ("y", "core", "z", "x")
EPSILON = 1e-05
LANES = 128
MIB = 1024 * 1024
STEPS = 3
F32 = jnp.float32
BF16 = jnp.bfloat16

V_MB1, V_MB2, V_MB3, V_N1G, V_N1S, V_CB, V_N2G, V_N2S, V_EB = range(9)
V_EDGE = 12
V_ROWS = 24


def dot_nn(left, right):
    return lax.dot_general(left, right, (((1,), (0,)), ((), ())), preferred_element_type=F32)


def dot_nt(left, right):
    return lax.dot_general(left, right, (((1,), (1,)), ((), ())), preferred_element_type=F32)


def dot_tn(left, right):
    return lax.dot_general(left, right, (((0,), (0,)), ((), ())), preferred_element_type=F32)


def split_low(values):
    high = values.astype(BF16)
    return high, (values - high.astype(F32)).astype(BF16)


def dot_split(dot, left, right):
    high, rest = split_low(left)
    return dot(high, right) + dot(rest, right)


def dot_split_right(dot, left, right):
    high, rest = split_low(right)
    return dot(left, high) + dot(left, rest)


def gelu_pair(v):
    e = jnp.exp2((v * v) * (-0.5 * math.log2(math.e)))
    phi_sum = 0.5 + 0.5 * lax.erf(v * math.sqrt(0.5))
    return v * phi_sum, phi_sum + (v * (1.0 / math.sqrt(2.0 * math.pi))) * e


def norm_parts(values):
    average = jnp.mean(values, axis=-1, keepdims=True)
    centred = values - average
    variance = jnp.mean(centred * centred, axis=-1, keepdims=True)
    scale = lax.rsqrt(variance + EPSILON)
    return centred * scale, scale


def norm_back(xhat, scale, gain, upstream):
    w = upstream * gain
    mean_w = jnp.mean(w, axis=-1, keepdims=True)
    mean_wx = jnp.mean(w * xhat, axis=-1, keepdims=True)
    return (w - mean_w - xhat * mean_wx) * scale


def edge_onehot(pos_ref, table_rows):
    pairs = pos_ref.shape[2]
    lane = lax.broadcasted_iota(jnp.int32, (LANES, table_rows), 1)
    return jnp.concatenate(
        [(pos_ref[0, :, p : p + 1] == lane).astype(F32).astype(BF16) for p in range(pairs)], axis=0
    )


def prepare_kernel(me_ref, idx_ref, mask_ref, *refs, parts, cap, steps, wide, narrow):
    wide_refs = refs[:wide]
    narrow_refs = refs[wide : wide + narrow]
    pos_ref, select_ref, ids_ref, count_ref, vec_ref, expand_bias_ref = refs[wide + narrow :]
    rows, width = count_ref.shape
    total = rows * parts
    table = rows + parts * cap
    me = me_ref[0]
    pair_rows = idx_ref.shape[0] // 2
    named = [
        jnp.concatenate([idx_ref[2 * j], idx_ref[2 * j + 1]], axis=1) for j in range(pair_rows)
    ]
    residue = lax.broadcasted_iota(jnp.int32, (total, LANES), 0)
    owner = residue // rows
    within = residue - owner * rows
    hits = jnp.zeros((total, LANES), F32)
    for j in range(pair_rows):
        hits = jnp.where(named[j] == residue, 1.0, hits)
    hit = jnp.max(hits, axis=1, keepdims=True)
    own = owner == me
    wanted = jnp.where(own, 0.0, jnp.broadcast_to(hit, (total, LANES)))
    low_row = lax.broadcasted_iota(jnp.int32, (rows, rows), 0)
    low_col = lax.broadcasted_iota(jnp.int32, (rows, rows), 1)
    lower = (low_col <= low_row).astype(F32).astype(BF16)
    wanted_low = wanted.astype(BF16)
    place = jnp.concatenate(
        [dot_nn(lower, wanted_low[o * rows : (o + 1) * rows]) for o in range(parts)], axis=0
    )
    place = jnp.clip(place - 1.0, 0.0, cap - 1.0)
    pos = jnp.where(own, within.astype(F32), (rows + owner * cap).astype(F32) + place)
    picked = [
        jnp.sum(jnp.where(named[j] == residue, pos, 0.0), axis=0, keepdims=True)
        for j in range(pair_rows)
    ]
    picked.append(jnp.zeros((LANES - pair_rows, LANES), F32))
    turned = jnp.concatenate(picked, axis=0).T.astype(jnp.int32)
    per = pair_rows // steps
    for s in range(steps):
        pos_ref[s] = turned[:, s * per : (s + 1) * per]
    lane = lax.broadcasted_iota(jnp.int32, (total, table), 1).astype(F32)
    live = jnp.where(own, 1.0, wanted)
    chosen = jnp.where(lane == pos[:, :1], jnp.broadcast_to(live[:, :1], (total, table)), 0.0)
    select_ref[...] = chosen.astype(BF16)
    asked_row = jnp.broadcast_to(within[:, :1].astype(F32), (total, parts * cap))
    ids = jnp.sum(chosen[:, rows:] * asked_row, axis=0, keepdims=True)
    ids = ids.astype(jnp.int32)
    for o in range(parts):
        ids_ref[o : o + 1, :] = ids[:, o * cap : (o + 1) * cap]
    count = mask_ref[0]
    for k in range(1, mask_ref.shape[0]):
        count = count + mask_ref[k]
    count = jnp.concatenate([count.astype(F32), jnp.zeros((7, rows), F32)], axis=0)
    count_ref[...] = dot_tn(count.astype(BF16), jnp.ones((8, width), F32).astype(BF16))
    expand_bias_ref[...] = wide_refs[-1][...].astype(F32).reshape(expand_bias_ref.shape)
    vec_ref[...] = jnp.zeros_like(vec_ref)
    at = 0
    for ref in wide_refs:
        for c in range(ref.shape[0] // width):
            part = ref[c * width : (c + 1) * width]
            vec_ref[at : at + 1, :] = part.astype(F32).reshape(1, width)
            at += 1
    for ref in narrow_refs:
        vec_ref[at : at + 1, : ref.shape[0]] = ref[...].astype(F32).reshape(1, ref.shape[0])
        at += 1


def node_kernel(
    edge_ref,
    pos_ref,
    select_ref,
    all_ref,
    self_ref,
    count_ref,
    vec_ref,
    w1_ref,
    w2_ref,
    w3_ref,
    expand_hbm,
    contract_hbm,
    act1_ref,
    slope1_ref,
    slope2_ref,
    fresh_ref,
    table_ref,
    mixed1_ref,
    mixed2_ref,
    low_ref,
    slope_e_ref,
    act_sum_ref,
    proj_ref,
    self_pre_ref,
    expand_ref,
    contract_ref,
    sems,
):
    step = pl.program_id(0)
    last = pl.num_programs(0) - 1
    rows, width = self_ref.shape
    slots = edge_ref.shape[0]
    edge_width = edge_ref.shape[2]
    table_rows = table_ref.shape[0]
    expand_copy = pltpu.make_async_copy(expand_hbm, expand_ref, sems.at[0])
    contract_copy = pltpu.make_async_copy(contract_hbm, contract_ref, sems.at[1])

    @pl.when(step == 0)
    def _():
        expand_copy.start()
        contract_copy.start()
        table = dot_tn(select_ref[...], all_ref[...]).astype(BF16)
        table_ref[...] = table
        proj_ref[...] = dot_nn(table, w1_ref[width : 2 * width]).astype(BF16)
        self_pre_ref[...] = (
            dot_nn(self_ref[...], w1_ref[:width]) + vec_ref[V_MB1 : V_MB1 + 1, :]
        )
        act_sum_ref[...] = jnp.zeros_like(act_sum_ref)

    onehot = edge_onehot(pos_ref, table_rows)
    features = edge_ref[...].reshape(slots * rows, edge_width)
    pre1 = dot_nn(features, w1_ref[2 * width :]) + dot_nn(onehot, proj_ref[...])
    self_pre = self_pre_ref[...]
    act1 = []
    for k in range(slots):
        part = pl.ds(k * rows, rows)
        act, slope = gelu_pair(pre1[k * rows : (k + 1) * rows] + self_pre)
        act = act.astype(BF16)
        act1.append(act)
        act1_ref[part, :] = act
        slope1_ref[part, :] = slope.astype(BF16)
    pre2 = dot_nn(jnp.concatenate(act1, axis=0), w2_ref[...])
    bias2 = vec_ref[V_MB2 : V_MB2 + 1, :]
    act_sum = act_sum_ref[...]
    counts = count_ref[...]
    for k in range(slots):
        act, slope = gelu_pair(pre2[k * rows : (k + 1) * rows] + bias2)
        valid = counts > (step * slots + k).astype(F32)
        act_sum = act_sum + jnp.where(valid, act.astype(BF16).astype(F32), 0.0)
        slope2_ref[pl.ds(k * rows, rows), :] = jnp.where(valid, slope, 0.0).astype(BF16)
    act_sum_ref[...] = act_sum

    @pl.when(step == last)
    def _():
        summed = dot_split(dot_nn, act_sum_ref[...], w3_ref[...])
        summed = summed + counts * vec_ref[V_MB3 : V_MB3 + 1, :]
        mixed1 = self_ref[...].astype(F32) + summed / counts
        mixed1_ref[...] = mixed1
        xhat1, _ = norm_parts(mixed1)
        updated = xhat1 * vec_ref[V_N1G : V_N1G + 1, :] + vec_ref[V_N1S : V_N1S + 1, :]
        low = updated.astype(BF16)
        low_ref[...] = low
        expand_copy.wait()
        contract_copy.wait()
        mixed2 = updated + vec_ref[V_CB : V_CB + 1, :]
        for c in range(expand_ref.shape[1] // width):
            cols = slice(c * width, (c + 1) * width)
            pre = dot_nn(low, expand_ref[:, cols]) + vec_ref[V_EB + c : V_EB + c + 1, :]
            act, slope = gelu_pair(pre)
            act = act.astype(BF16)
            slope_e_ref[:, cols] = slope
            mixed2 = mixed2 + dot_nn(act, contract_ref[cols, :])
        mixed2_ref[...] = mixed2
        xhat2, _ = norm_parts(mixed2)
        fresh = (xhat2 * vec_ref[V_N2G : V_N2G + 1, :] + vec_ref[V_N2S : V_N2S + 1, :]).astype(BF16)
        fresh_ref[...] = fresh


def asked_onehot(asked_ref, rows):
    parts = asked_ref.shape[0]
    asked = jnp.concatenate([asked_ref[o : o + 1, :] for o in range(parts)], axis=1)
    row = lax.broadcasted_iota(jnp.int32, (rows, asked.shape[1]), 0)
    return (asked == row).astype(F32).astype(BF16)


def pick_kernel(asked_ref, fresh_ref, out_ref):
    out_ref[...] = dot_tn(asked_onehot(asked_ref, fresh_ref.shape[0]), fresh_ref[...]).astype(BF16)


def edge_kernel(
    edge_ref,
    cot_ref,
    pos_ref,
    fresh_ref,
    incoming_ref,
    count_ref,
    vec_ref,
    w1t_ref,
    w2_ref,
    w3_ref,
    out_ref,
    grad_ref,
    first_ref,
    own_ref,
    away_ref,
    pack_ref,
    vec_out_ref,
    table_ref,
    proj_ref,
    self_pre_ref,
    back_ref,
    dw3_ref,
    dw2_ref,
    dw1_ref,
    sums_ref,
    turned_ref,
):
    step = pl.program_id(0)
    last = pl.num_programs(0) - 1
    rows, width = fresh_ref.shape
    slots, _, edge_width = edge_ref.shape
    block = slots * rows
    table_rows = table_ref.shape[0]
    own_t = w1t_ref[:, :width]
    nbr_t = w1t_ref[:, width : 2 * width]
    feat_t = w1t_ref[:, 2 * width :]

    def vector(i):
        return vec_ref[V_EDGE + i : V_EDGE + i + 1, :edge_width]

    @pl.when(step == 0)
    def _():
        table_ref[:rows] = fresh_ref[...]
        table_ref[rows:] = incoming_ref[...]
        proj_ref[...] = dot_nt(table_ref[...], nbr_t).astype(BF16)
        self_pre_ref[...] = dot_nt(fresh_ref[...], own_t) + vector(0)
        for ref in (back_ref, dw3_ref, dw2_ref, dw1_ref, sums_ref, first_ref):
            ref[...] = jnp.zeros_like(ref)
        turned_ref[0] = feat_t.T
        turned_ref[1] = w2_ref[...].T
        turned_ref[2] = w3_ref[...].T

    def flat(values):
        return values.reshape(block, edge_width)

    def deep(values):
        return values.reshape(slots, rows, edge_width)

    onehot = edge_onehot(pos_ref, table_rows)
    features = flat(edge_ref[...])
    pre1 = dot_nn(features, turned_ref[0]) + dot_nn(onehot, proj_ref[...])
    pre1 = deep(pre1) + self_pre_ref[...][None]
    act1, slope1 = gelu_pair(flat(pre1))
    act1 = act1.astype(BF16)
    pre2 = dot_nn(act1, w2_ref[...]) + vector(1)
    act2, slope2 = gelu_pair(pre2)
    act2 = act2.astype(BF16)
    mixed3 = features.astype(F32) + (dot_nn(act2, w3_ref[...]) + vector(2))
    xhat, scale = norm_parts(mixed3)
    gain = vector(3)
    slot = lax.broadcasted_iota(jnp.int32, (slots, rows, edge_width), 0) + step * slots
    valid = count_ref[...][None, :, :edge_width] > slot.astype(F32)
    out_ref[...] = jnp.where(valid, deep(xhat * gain + vector(4)), 0.0).astype(BF16)
    upstream = flat(jnp.where(valid, cot_ref[...].astype(F32), 0.0))
    sums_ref[3] += jnp.sum(deep(upstream * xhat), axis=0)
    sums_ref[4] += jnp.sum(deep(upstream), axis=0)
    grad_mixed = norm_back(xhat, scale, gain, upstream)
    grad_delta = grad_mixed.astype(BF16)
    dw3_ref[...] += dot_tn(act2, grad_delta)
    sums_ref[2] += jnp.sum(deep(grad_delta.astype(F32)), axis=0)
    grad2 = (dot_nn(grad_delta, turned_ref[2]) * slope2).astype(BF16)
    dw2_ref[...] += dot_tn(act1, grad2)
    sums_ref[1] += jnp.sum(deep(grad2.astype(F32)), axis=0)
    grad1 = (dot_nn(grad2, turned_ref[1]) * slope1).astype(BF16)
    dw1_ref[...] += dot_tn(grad1, features)
    first_ref[...] += jnp.sum(deep(grad1.astype(F32)), axis=0)
    back_ref[...] += dot_tn(onehot, grad1)
    grad_ref[...] = deep(grad_mixed + dot_nn(grad1, feat_t))

    @pl.when(step == last)
    def _():
        first = first_ref[...]
        back = back_ref[...]
        own_ref[...] = back[:rows]
        away_ref[...] = back[rows:].astype(BF16)
        first_high, first_rest = split_low(first)
        back_high, back_rest = split_low(back)
        own_grad = dot_tn(first_high, fresh_ref[...]) + dot_tn(first_rest, fresh_ref[...])
        nbr_grad = dot_tn(back_high, table_ref[...]) + dot_tn(back_rest, table_ref[...])
        pack_ref[:edge_width, :] = own_grad.astype(BF16)
        pack_ref[edge_width : 2 * edge_width, :] = nbr_grad.astype(BF16)
        pad = jnp.zeros((edge_width, width // 2 - edge_width), BF16)
        third = [dw1_ref[...].astype(BF16), pad, dw2_ref[...].astype(BF16), pad]
        pack_ref[2 * edge_width : 3 * edge_width, :] = jnp.concatenate(third, axis=1)
        fourth = [dw3_ref[...].astype(BF16), pad, jnp.zeros((edge_width, width // 2), BF16)]
        pack_ref[3 * edge_width :, :] = jnp.concatenate(fourth, axis=1)
        vec_out_ref[...] = jnp.zeros_like(vec_out_ref)
        vec_out_ref[0:1, :edge_width] = jnp.sum(first, axis=0, keepdims=True)
        for i in range(1, 5):
            vec_out_ref[i : i + 1, :edge_width] = jnp.sum(sums_ref[i], axis=0, keepdims=True)


def feed_kernel(
    cot_ref,
    first_ref,
    own_ref,
    arrived_ref,
    asked_ref,
    count_ref,
    vec_ref,
    w1t_ref,
    mixed1_ref,
    mixed2_ref,
    slope_ref,
    act_sum_ref,
    expand_hbm,
    contract_hbm,
    w3_ref,
    edge_vec_ref,
    pack_ref,
    copies_ref,
    spread_ref,
    grad_mixed1_ref,
    expand_ref,
    contract_ref,
    sems,
):
    rows, width = cot_ref.shape
    hidden = expand_ref.shape[1]
    own_t = w1t_ref[:, :width]
    nbr_t = w1t_ref[:, width : 2 * width]
    counts = count_ref[...]
    copies = []
    for c in range(hidden // width):
        rows_part, cols_part = pl.ds(c * width, width), pl.ds(c * width, width)
        copies.append(
            (
                pltpu.make_async_copy(
                    contract_hbm.at[rows_part, :], contract_ref.at[rows_part, :], sems.at[2 * c]
                ),
                pltpu.make_async_copy(
                    expand_hbm.at[:, cols_part], expand_ref.at[:, cols_part], sems.at[2 * c + 1]
                ),
            )
        )
    for pair in copies:
        for copy in pair:
            copy.start()

    def vector(i):
        return vec_ref[i : i + 1, :]

    def total(values):
        return jnp.sum(values.astype(F32), axis=0, keepdims=True)

    back = own_ref[...] + dot_nn(asked_onehot(asked_ref, rows), arrived_ref[...])
    grad_fresh = (
        cot_ref[...].astype(F32)
        + dot_split(dot_nn, first_ref[...], own_t)
        + dot_split(dot_nn, back, nbr_t)
    )
    xhat2, scale2 = norm_parts(mixed2_ref[...])
    grad_mixed2 = norm_back(xhat2, scale2, vector(V_N2G), grad_fresh)
    grad_contracted = grad_mixed2.astype(BF16)
    for p in range(copies_ref.shape[0]):
        copies_ref[p] = grad_contracted
    grad_updated = grad_mixed2
    for c in range(hidden // width):
        cols = slice(c * width, (c + 1) * width)
        copies[c][0].wait()
        pre = dot_nt(grad_contracted, contract_ref[cols, :]) * slope_ref[:, cols]
        copies[c][1].wait()
        grad_updated = grad_updated + dot_nt(pre.astype(BF16), expand_ref[:, cols])
    xhat1, scale1 = norm_parts(mixed1_ref[...])
    grad_mixed1 = norm_back(xhat1, scale1, vector(V_N1G), grad_updated)
    grad_mixed1_ref[...] = grad_mixed1
    grad_message = (grad_mixed1 / counts).astype(BF16)
    spread_ref[...] = dot_nt(grad_message, w3_ref[...])
    pack_ref[:width, :] = dot_split(dot_tn, act_sum_ref[...], grad_message).astype(BF16)
    vectors = [
        total(counts * grad_message.astype(F32)),
        total(grad_updated * xhat1),
        total(grad_updated),
        total(grad_fresh * xhat2),
        total(grad_fresh),
        edge_vec_ref[...],
    ]
    vectors = jnp.concatenate(vectors, axis=0)
    vectors = jnp.concatenate(
        [vectors, jnp.zeros((pack_ref.shape[0] - width - vectors.shape[0], width), F32)], axis=0
    )
    pack_ref[width:, :] = vectors.astype(BF16)


def feed_weight_kernel(
    low_ref, grad_ref, expand_ref, bias_ref, contract_ref, *refs, more, last
):
    sums_in = refs[:3] if more else None
    outputs = refs[-6:-2] if last else refs[-5:-2]
    expand_out_ref, contract_out_ref, bias_out_ref = outputs[:3]
    low_turned_ref, grad_turned_ref = refs[-2:]
    ones = jnp.ones((8, low_ref.shape[0]), F32).astype(BF16)

    @pl.when(pl.program_id(0) == 0)
    def _():
        low_turned_ref[...] = low_ref[...].T
        grad_turned_ref[...] = grad_ref[...].T
        if last:
            outputs[3][...] = dot_nn(ones, grad_ref[...])

    act, slope = gelu_pair(dot_nn(low_ref[...], expand_ref[...]) + bias_ref[0:1, :])
    act = act.astype(BF16)
    pre = (dot_nt(grad_ref[...], contract_ref[...]) * slope).astype(BF16)
    expanded = dot_nn(low_turned_ref[...], pre)
    contracted = dot_nn(grad_turned_ref[...], act).T
    sums = dot_nn(ones, pre)
    if more:
        expanded = expanded + sums_in[0][...]
        contracted = contracted + sums_in[1][...]
        sums = sums + sums_in[2][...]
    expand_out_ref[...] = expanded
    contract_out_ref[...] = contracted
    bias_out_ref[...] = sums


def message_kernel(
    core_ref,
    edge_ref,
    pos_ref,
    act1_ref,
    slope1_ref,
    slope2_ref,
    partial_ref,
    spread_ref,
    table_ref,
    w1_a_ref,
    w1_b_ref,
    w1_c_ref,
    w2_ref,
    edge_pack_ref,
    feed_pack_ref,
    grad_ref,
    first_ref,
    own_ref,
    away_ref,
    send_ref,
    keep_ref,
    joint_ref,
    dw2_ref,
    bias2_ref,
    w2_turned_ref,
    w1_turned_ref,
):
    step = pl.program_id(0)
    last = pl.num_programs(0) - 1
    slots, rows, edge_width = edge_ref.shape
    width = act1_ref.shape[1]
    block = slots * rows
    table_rows = table_ref.shape[0]

    @pl.when(step == 0)
    def _():
        for ref in (joint_ref, dw2_ref, bias2_ref, first_ref):
            ref[...] = jnp.zeros_like(ref)
        w2_turned_ref[...] = w2_ref[...].T
        w1_parts = [ref[...] for ref in (w1_a_ref, w1_b_ref, w1_c_ref)]
        w1_turned_ref[...] = jnp.concatenate(w1_parts, axis=0).T

    spread = spread_ref[...]
    grad2 = []
    bias2 = bias2_ref[...]
    for k in range(slots):
        part = (spread * slope2_ref[pl.ds(k * rows, rows), :].astype(F32)).astype(BF16)
        bias2 = bias2 + part.astype(F32)
        grad2.append(part)
    bias2_ref[...] = bias2
    grad2 = jnp.concatenate(grad2, axis=0)
    dw2_ref[...] += dot_tn(act1_ref[...], grad2)
    grad1 = (dot_nn(grad2, w2_turned_ref[...]) * slope1_ref[...].astype(F32)).astype(BF16)
    first_ref[...] += jnp.sum(grad1.astype(F32).reshape(slots, rows, width), axis=0)
    onehot = edge_onehot(pos_ref, table_rows)
    features = edge_ref[...].reshape(block, edge_width)
    joint_ref[...] += dot_tn(jnp.concatenate([onehot, features], axis=1), grad1)
    grad_ref[...] = partial_ref[...] + dot_nn(grad1, w1_turned_ref[...]).reshape(
        slots, rows, edge_width
    )

    @pl.when(step == last)
    def _():
        first = first_ref[...]
        back = joint_ref[:table_rows]
        own_ref[...] = back[:rows]
        away_ref[...] = back[rows:].astype(BF16)
        own_grad = dot_split_right(dot_tn, table_ref[:rows], first).astype(BF16)
        nbr_grad = dot_split_right(dot_tn, table_ref[...], back).astype(BF16)
        vectors = [
            feed_pack_ref[width:].astype(F32),
            jnp.sum(first, axis=0, keepdims=True),
            jnp.sum(bias2_ref[...], axis=0, keepdims=True),
        ]
        lower = [own_grad, nbr_grad, feed_pack_ref[:width]]
        upper = [joint_ref[table_rows:].astype(BF16), dw2_ref[...].astype(BF16), edge_pack_ref[...]]

        def fill(ref, pieces, tail):
            base = 0
            for piece in pieces:
                ref[base : base + piece.shape[0]] = piece
                base += piece.shape[0]
            if base < ref.shape[0]:
                gap = ref.shape[0] - base - sum(v.shape[0] for v in tail)
                rest = jnp.concatenate(tail + [jnp.zeros((gap, width), F32)], axis=0)
                ref[base:] = rest.astype(BF16)

        @pl.when(core_ref[0] == 0)
        def _():
            fill(keep_ref, lower, [])
            fill(send_ref, upper, vectors)

        @pl.when(core_ref[0] != 0)
        def _():
            fill(send_ref, lower, [])
            fill(keep_ref, upper, vectors)


def wrapped(value, size):
    value = jnp.where(value >= size, value - size, value)
    return jnp.where(value < 0, value + size, value)


def pick_of(index, values):
    result = values[0]
    for i in range(1, len(values)):
        result = jnp.where(index == i, values[i], result)
    return result


def hold_kernel(keep_ref, away_ref, keep_out_ref, away_out_ref):
    keep_out_ref[...] = keep_ref[...]
    away_out_ref[...] = away_ref[...]


def pair_kernel(y_ref, x_ref, keep_ref, came_ref, away_ref, *out_refs, parts, cap):
    y_size = lax.axis_size("y")
    x_size = lax.axis_size("x")
    z_size = parts // x_size
    riders = z_size * cap
    share = keep_ref.shape[0] // len(out_refs)
    away = away_ref[...].astype(F32)
    for e, out_ref in enumerate(out_refs):
        dy, dx = divmod(e, x_size)
        x = wrapped(x_ref[0] + dx, x_size)
        device = wrapped(y_ref[0] + dy, y_size) * x_size + x
        part = pl.ds(pl.multiple_of(device * share, 16), share)
        at = out_ref.shape[0] - share
        out_ref[at:] = (keep_ref[part, :].astype(F32) + came_ref[part, :].astype(F32)).astype(BF16)
        if at:
            rows = []
            for to in range(x_size):
                owners = [(z * x_size + to) * cap for z in range(z_size)]
                rows.append(jnp.concatenate([away[o : o + cap] for o in owners], axis=0))
            out_ref[:riders] = pick_of(x, rows).astype(BF16)


def plane_kernel(x_ref, z_ref, *refs, peers, cap):
    came_refs, out_refs = refs[:peers], refs[peers:]
    x_size = lax.axis_size("x")
    z_size = len(out_refs)
    riders = x_size * cap
    share = out_refs[0].shape[0] - riders
    first = z_size * cap
    rows = []
    for source in range(x_size):
        pieces = [ref[:first].astype(F32) for ref in came_refs[:x_size]]
        rows.append(pick_of(wrapped(x_ref[0] - source, x_size), pieces))
    for dz, out_ref in enumerate(out_refs):
        z = wrapped(z_ref[0] + dz, z_size)
        value = jnp.zeros((share, out_ref.shape[1]), F32)
        for e, ref in enumerate(came_refs):
            start = z * share + (first if e < x_size else 0)
            value = value + ref[pl.ds(pl.multiple_of(start, 16), share), :].astype(F32)
        out_ref[riders:] = value.astype(BF16)
        part = [
            pick_of(z, [value[i * cap : (i + 1) * cap] for i in range(z_size)]) for value in rows
        ]
        out_ref[:riders] = jnp.concatenate(part, axis=0).astype(BF16)


def column_kernel(z_ref, *refs):
    came_refs, total_ref, returned_ref = refs[:-2], refs[-2], refs[-1]
    z_size = len(came_refs)
    riders = returned_ref.shape[0] // z_size
    value = jnp.zeros(total_ref.shape, F32)
    for dz, ref in enumerate(came_refs):
        value = value + ref[riders:].astype(F32)
        start = wrapped(z_ref[0] - dz, z_size) * riders
        returned_ref[pl.ds(pl.multiple_of(start, 16), riders), :] = ref[:riders]
    total_ref[...] = value.astype(BF16)


def plane_stack_kernel(y_ref, x_ref, *refs):
    came_refs, out_ref = refs[:-1], refs[-1]
    x_size = lax.axis_size("x")
    share = came_refs[0].shape[0]
    for e, ref in enumerate(came_refs):
        dy, dx = divmod(e, x_size)
        y = wrapped(y_ref[0] - dy, len(came_refs) // x_size)
        start = (y * x_size + wrapped(x_ref[0] - dx, x_size)) * share
        out_ref[pl.ds(pl.multiple_of(start, 16), share), :] = ref[...]


def stack_kernel(z_ref, *refs):
    came_refs, out_ref = refs[:-1], refs[-1]
    share = came_refs[0].shape[0]
    for dz, ref in enumerate(came_refs):
        start = wrapped(z_ref[0] - dz, len(came_refs)) * share
        out_ref[pl.ds(pl.multiple_of(start, 16), share), :] = ref[...]


def node_grad_kernel(grad_ref, first_ref, own_ref, arrived_ref, asked_ref, w1_ref, out_ref):
    rows, width = grad_ref.shape
    back = own_ref[...] + dot_nn(asked_onehot(asked_ref, rows), arrived_ref[...])
    out_ref[...] = (
        grad_ref[...]
        + dot_split(dot_nt, first_ref[...], w1_ref[:width])
        + dot_split(dot_nt, back, w1_ref[width : 2 * width])
    )


def unpack_kernel(core_ref, y_ref, x_ref, *refs, peers, lasts):
    mine_refs, other_refs, refs = refs[:peers], refs[peers : 2 * peers], refs[2 * peers :]
    bias_ref, last_bias_refs = refs[0], refs[1 : 1 + lasts]
    mine_ref, other_ref = refs[-2:]
    refs = refs[1 + lasts : -2]
    x_size = lax.axis_size("x")
    share = mine_refs[0].shape[0]
    for e in range(peers):
        dy, dx = divmod(e, x_size)
        device = wrapped(y_ref[0] - dy, peers // x_size) * x_size + wrapped(x_ref[0] - dx, x_size)
        part = pl.ds(pl.multiple_of(device * share, 16), share)
        mine_ref[part, :] = mine_refs[e][...]
        other_ref[part, :] = other_refs[e][...]
    (
        message1_ref,
        message1_bias_ref,
        message2_ref,
        message2_bias_ref,
        message3_ref,
        message3_bias_ref,
        gain1_ref,
        shift1_ref,
        expand_bias_ref,
        contract_bias_ref,
        gain2_ref,
        shift2_ref,
        edge1_ref,
        edge1_bias_ref,
        edge2_ref,
        edge2_bias_ref,
        edge3_ref,
        edge3_bias_ref,
        gain3_ref,
        shift3_ref,
    ) = refs
    width = mine_ref.shape[1]
    edge_width = edge2_ref.shape[0]
    half = width // 2
    first_core = core_ref[0] == 0

    def lower(start, stop):
        return jnp.where(first_core, mine_ref[start:stop], other_ref[start:stop]).astype(F32)

    def upper(start, stop):
        return jnp.where(first_core, other_ref[start:stop], mine_ref[start:stop]).astype(F32)

    message1_ref[: 2 * width] = lower(0, 2 * width)
    message3_ref[...] = lower(2 * width, 3 * width)
    message1_ref[2 * width :] = upper(0, edge_width)
    base = edge_width
    message2_ref[...] = upper(base, base + width)
    base = base + width
    edge1_ref[:, :width] = upper(base, base + edge_width)
    edge1_ref[:, width : 2 * width] = upper(base + edge_width, base + 2 * edge_width)
    third = upper(base + 2 * edge_width, base + 3 * edge_width)
    edge1_ref[:, 2 * width :] = third[:, :edge_width]
    edge2_ref[...] = third[:, half : half + edge_width]
    edge3_ref[...] = upper(base + 3 * edge_width, base + 4 * edge_width)[:, :edge_width]
    base = base + 4 * edge_width
    vectors = upper(base, mine_ref.shape[0])
    targets = (message3_bias_ref, gain1_ref, shift1_ref, gain2_ref, shift2_ref)
    for i, ref in enumerate(targets):
        ref[...] = vectors[i]
    targets = (edge1_bias_ref, edge2_bias_ref, edge3_bias_ref, gain3_ref, shift3_ref)
    for i, ref in enumerate(targets):
        ref[...] = vectors[5 + i, :edge_width]
    message1_bias_ref[...] = vectors[16]
    message2_bias_ref[...] = vectors[17]
    expand_bias_ref[...] = bias_ref[0]
    contract_bias = last_bias_refs[0][0]
    for ref in last_bias_refs[1:]:
        contract_bias = contract_bias + ref[0]
    contract_bias_ref[...] = contract_bias


def gather_copies(copies, axes):
    return lax.all_to_all(copies, axes, split_axis=0, concat_axis=0, tiled=True)


def copies_of(values, axes):
    return jnp.broadcast_to(values[None], (lax.axis_size(axes), *values.shape))


def exchange(values, parts):
    grouped = values.reshape(parts, values.shape[0] // parts, values.shape[1])
    arrived = lax.all_to_all(grouped, RES, split_axis=0, concat_axis=0, tiled=True)
    return arrived.reshape(values.shape)


def move(values, dy=0, dz=0, dx=0):
    sizes = [lax.axis_size(axis) for axis in SIDE]
    pairs = []
    for i in range(math.prod(sizes)):
        rest, x = divmod(i, sizes[2])
        y, z = divmod(rest, sizes[1])
        to_y, to_z, to_x = (y + dy) % sizes[0], (z + dz) % sizes[1], (x + dx) % sizes[2]
        pairs.append((i, (to_y * sizes[1] + to_z) * sizes[2] + to_x))
    return lax.ppermute(values, SIDE, pairs)


def other_core(values):
    return lax.ppermute(values, "core", [(0, 1), (1, 0)])


def whole(shape):
    return pl.BlockSpec(shape, lambda *_: (0,) * len(shape))


def params(mebibytes):
    return pltpu.CompilerParams(vmem_limit_bytes=mebibytes * MIB)


def cost(microseconds):
    return pl.CostEstimate(
        flops=int(microseconds * 1.15e9),
        bytes_accessed=int(microseconds * 3.69e6),
        transcendentals=0,
    )


def body(
    node_states,
    edge_states,
    neighbour_index,
    edge_mask,
    node_cotangent,
    edge_cotangent,
    message_weight1,
    message_bias1,
    message_weight2,
    message_bias2,
    message_weight3,
    message_bias3,
    norm1_gain,
    norm1_shift,
    expand_weight,
    expand_bias,
    contract_weight,
    contract_bias,
    norm2_gain,
    norm2_shift,
    edge_weight1,
    edge_bias1,
    edge_weight2,
    edge_bias2,
    edge_weight3,
    edge_bias3,
    norm3_gain,
    norm3_shift,
):
    self_rows = node_states[0]
    rows, width = self_rows.shape
    slots = neighbour_index.shape[2]
    edge_width = edge_states.shape[3]
    hidden = expand_weight.shape[1]
    edges = rows * slots
    parts = lax.axis_size(RES)
    cap = ROW_CAP
    table_rows = rows + parts * cap
    side = lax.axis_size(SIDE)
    steps = STEPS
    block_slots = slots // steps
    block = block_slots * rows
    pairs = block // LANES

    everyone = gather_copies(copies_of(self_rows, RES), RES).reshape(parts * rows, width)
    core = lax.axis_index("core").astype(jnp.int32).reshape(1)
    me = lax.axis_index(RES).astype(jnp.int32).reshape(1)
    edge_rows = edge_states[0].transpose(1, 0, 2)
    edge_cot = edge_cotangent[0].transpose(1, 0, 2)
    slot_index = neighbour_index.transpose(2, 0, 1)
    slot_mask = edge_mask.transpose(2, 0, 1)
    edge_w1t = edge_weight1.T
    wide = (
        message_bias1,
        message_bias2,
        message_bias3,
        norm1_gain,
        norm1_shift,
        contract_bias,
        norm2_gain,
        norm2_shift,
        expand_bias,
    )
    narrow = (edge_bias1, edge_bias2, edge_bias3, norm3_gain, norm3_shift)
    vmem = pl.BlockSpec(memory_space=pltpu.VMEM)

    def shape(dims, kind):
        return jax.ShapeDtypeStruct(dims, kind)

    pos, select, ids, counts, vectors, bias_row = pl.pallas_call(
        functools.partial(
            prepare_kernel, parts=parts, cap=cap, steps=steps, wide=len(wide), narrow=len(narrow)
        ),
        out_shape=(
            shape((steps, LANES, pairs), jnp.int32),
            shape((parts * rows, table_rows), BF16),
            shape((parts, cap), jnp.int32),
            shape((rows, width), F32),
            shape((V_ROWS, width), F32),
            shape((1, hidden), F32),
        ),
        in_specs=[pl.BlockSpec(memory_space=pltpu.SMEM)] + [vmem] * (2 + len(wide) + len(narrow)),
        out_specs=(vmem,) * 6,
        compiler_params=params(56),
        cost_estimate=cost(6),
        name="prepare",
    )(me, slot_index, slot_mask, *wide, *narrow)
    ids, everyone = lax.optimization_barrier((ids, everyone))
    asked = lax.all_to_all(ids, RES, split_axis=0, concat_axis=0, tiled=True)

    edge_spec = pl.BlockSpec((block_slots, rows, edge_width), lambda i: (i, 0, 0))
    flat_spec = pl.BlockSpec((block, width), lambda i: (i, 0))
    pos_spec = pl.BlockSpec((1, LANES, pairs), lambda i: (i, 0, 0))
    any_spec = pl.BlockSpec(memory_space=pl.ANY)
    node_spec = whole((rows, width))
    away_spec = whole((parts * cap, width))

    (
        act1,
        slope1,
        slope2,
        fresh,
        table,
        mixed1,
        mixed2,
        low,
        slope_e,
        act_sum,
    ) = pl.pallas_call(
        node_kernel,
        grid=(steps,),
        in_specs=[
            edge_spec,
            pos_spec,
            whole((parts * rows, table_rows)),
            whole((parts * rows, width)),
            node_spec,
            node_spec,
            whole((V_ROWS, width)),
            whole(message_weight1.shape),
            whole((width, width)),
            whole((width, width)),
            any_spec,
            any_spec,
        ],
        out_specs=[
            flat_spec,
            flat_spec,
            flat_spec,
            node_spec,
            whole((table_rows, width)),
            node_spec,
            node_spec,
            node_spec,
            whole((rows, hidden)),
            node_spec,
        ],
        out_shape=[
            shape((edges, width), BF16),
            shape((edges, width), BF16),
            shape((edges, width), BF16),
            shape((rows, width), BF16),
            shape((table_rows, width), BF16),
            shape((rows, width), F32),
            shape((rows, width), F32),
            shape((rows, width), BF16),
            shape((rows, hidden), F32),
            shape((rows, width), F32),
        ],
        scratch_shapes=[
            pltpu.VMEM((table_rows, width), BF16),
            pltpu.VMEM((rows, width), F32),
            pltpu.VMEM((width, hidden), BF16),
            pltpu.VMEM((hidden, width), BF16),
            pltpu.SemaphoreType.DMA((2,)),
        ],
        compiler_params=params(56),
        cost_estimate=cost(26),
        name="node_forward",
    )(
        edge_rows,
        pos,
        select,
        everyone,
        self_rows,
        counts,
        vectors,
        message_weight1,
        message_weight2,
        message_weight3,
        expand_weight,
        contract_weight,
    )
    outgoing = pl.pallas_call(
        pick_kernel,
        in_specs=[vmem] * 2,
        out_specs=vmem,
        out_shape=shape((parts * cap, width), BF16),
        compiler_params=params(8),
        cost_estimate=cost(1),
        name="pick",
    )(asked, fresh)
    y_size = lax.axis_size("y")
    x_size = lax.axis_size("x")
    z_size = lax.axis_size("z")
    peers = y_size * x_size
    my_y = lax.axis_index("y").astype(jnp.int32).reshape(1)
    my_x = lax.axis_index("x").astype(jnp.int32).reshape(1)
    my_z = lax.axis_index("z").astype(jnp.int32).reshape(1)
    smem = pl.BlockSpec(memory_space=pltpu.SMEM)
    steps_of = [divmod(e, x_size) for e in range(peers)]

    def over_plane(values):
        came = [values[0]]
        for value, (dy, dx) in zip(values[1:], steps_of[1:]):
            came.append(move(value, dy=dy, dx=dx))
        return came

    def over_z(values):
        return [values[0]] + [move(value, dz=d) for d, value in enumerate(values[1:], start=1)]

    def stack_z(came):
        return pl.pallas_call(
            stack_kernel,
            in_specs=[smem] + [vmem] * z_size,
            out_specs=vmem,
            out_shape=shape((z_size * came[0].shape[0], width), BF16),
            compiler_params=params(8),
            cost_estimate=cost(1),
            name="stack",
        )(my_z, *came)

    outgoing, low = lax.optimization_barrier((outgoing, low))
    incoming = exchange(outgoing, parts)
    low_column = stack_z(over_z([low] * z_size))

    edge_pack_rows = 4 * edge_width
    edge_out, grad_partial, edge_first, edge_own, edge_away, edge_pack, edge_vec = pl.pallas_call(
        edge_kernel,
        grid=(steps,),
        in_specs=[
            edge_spec,
            edge_spec,
            pos_spec,
            node_spec,
            away_spec,
            node_spec,
            whole((V_ROWS, width)),
            whole(edge_w1t.shape),
            whole((edge_width, edge_width)),
            whole((edge_width, edge_width)),
        ],
        out_specs=[
            edge_spec,
            edge_spec,
            whole((rows, edge_width)),
            whole((rows, edge_width)),
            whole((parts * cap, edge_width)),
            whole((edge_pack_rows, width)),
            whole((8, width)),
        ],
        out_shape=[
            shape((slots, rows, edge_width), BF16),
            shape((slots, rows, edge_width), F32),
            shape((rows, edge_width), F32),
            shape((rows, edge_width), F32),
            shape((parts * cap, edge_width), BF16),
            shape((edge_pack_rows, width), BF16),
            shape((8, width), F32),
        ],
        scratch_shapes=[
            pltpu.VMEM((table_rows, width), BF16),
            pltpu.VMEM((table_rows, edge_width), BF16),
            pltpu.VMEM((rows, edge_width), F32),
            pltpu.VMEM((table_rows, edge_width), F32),
            pltpu.VMEM((edge_width, edge_width), F32),
            pltpu.VMEM((edge_width, edge_width), F32),
            pltpu.VMEM((edge_width, edge_width), F32),
            pltpu.VMEM((5, rows, edge_width), F32),
            pltpu.VMEM((3, edge_width, edge_width), BF16),
        ],
        compiler_params=params(56),
        cost_estimate=cost(21),
        name="edge_both",
    )(
        edge_rows,
        edge_cot,
        pos,
        fresh,
        incoming,
        counts,
        vectors,
        edge_w1t,
        edge_weight2,
        edge_weight3,
    )
    edge_away, low_column = lax.optimization_barrier((edge_away, low_column))
    edge_arrived = exchange(edge_away, parts)
    low_pieces = over_plane([low_column] * peers)

    feed_rows = width + 16
    feed_pack, grad_copies, spread, grad_mixed1 = pl.pallas_call(
        feed_kernel,
        in_specs=[vmem] * 12 + [any_spec] * 2 + [vmem] * 2,
        out_specs=[vmem] * 4,
        out_shape=[
            shape((feed_rows, width), BF16),
            shape((side, rows, width), BF16),
            shape((rows, width), F32),
            shape((rows, width), F32),
        ],
        scratch_shapes=[
            pltpu.VMEM((width, hidden), BF16),
            pltpu.VMEM((hidden, width), BF16),
            pltpu.SemaphoreType.DMA((2 * hidden // width,)),
        ],
        compiler_params=params(56),
        cost_estimate=cost(7),
        name="feed_backward",
    )(
        node_cotangent[0],
        edge_first,
        edge_own,
        edge_arrived,
        asked,
        counts,
        vectors,
        edge_w1t,
        mixed1,
        mixed2,
        slope_e,
        act_sum,
        expand_weight,
        contract_weight,
        message_weight3,
        edge_vec,
    )
    grad_mine = gather_copies(grad_copies, BY_COLUMN).reshape(side * rows, width)
    spread, low_pieces = lax.optimization_barrier((spread, low_pieces))

    unit = 16 * side
    half_rows = (3 * width + unit - 1) // unit * unit
    third = edge_width // 3
    edge_grad, first, own, away, send, keep = pl.pallas_call(
        message_kernel,
        grid=(steps,),
        in_specs=[
            pl.BlockSpec(memory_space=pltpu.SMEM),
            edge_spec,
            pos_spec,
            flat_spec,
            flat_spec,
            flat_spec,
            edge_spec,
            node_spec,
            whole((table_rows, width)),
            *[
                pl.BlockSpec((third, width), lambda i, p=p: (2 * width // third + p, 0))
                for p in range(3)
            ],
            whole((width, width)),
            whole((edge_pack_rows, width)),
            whole((feed_rows, width)),
        ],
        out_specs=[
            edge_spec,
            node_spec,
            node_spec,
            away_spec,
            whole((half_rows, width)),
            whole((half_rows, width)),
        ],
        out_shape=[
            shape((slots, rows, edge_width), F32),
            shape((rows, width), F32),
            shape((rows, width), F32),
            shape((parts * cap, width), BF16),
            shape((half_rows, width), BF16),
            shape((half_rows, width), BF16),
        ],
        scratch_shapes=[
            pltpu.VMEM((table_rows + edge_width, width), F32),
            pltpu.VMEM((width, width), F32),
            pltpu.VMEM((rows, width), F32),
            pltpu.VMEM((width, width), BF16),
            pltpu.VMEM((width, edge_width), BF16),
        ],
        compiler_params=params(56),
        cost_estimate=cost(14),
        name="message_backward",
    )(
        core,
        edge_rows,
        pos,
        act1,
        slope1,
        slope2,
        grad_partial,
        spread,
        table,
        message_weight1,
        message_weight1,
        message_weight1,
        message_weight2,
        edge_pack,
        feed_pack,
    )
    came = other_core(send)
    keep, away = pl.pallas_call(
        hold_kernel,
        in_specs=[vmem] * 2,
        out_specs=[vmem] * 2,
        out_shape=[shape(keep.shape, BF16), shape(away.shape, BF16)],
        compiler_params=params(12),
        cost_estimate=cost(2),
        name="hold",
    )(keep, away)
    share = half_rows // peers
    pieces = pl.pallas_call(
        functools.partial(pair_kernel, parts=parts, cap=cap),
        in_specs=[smem] * 2 + [vmem] * 3,
        out_specs=[vmem] * peers,
        out_shape=[
            shape((share if dy else share + z_size * cap, width), BF16) for dy, _ in steps_of
        ],
        compiler_params=params(20),
        cost_estimate=cost(3),
        name="pair_sum",
    )(my_y, my_x, keep, came, away)
    _, grad_mine, low_pieces = lax.optimization_barrier((pieces[0], grad_mine, low_pieces))
    low_mine = pl.pallas_call(
        plane_stack_kernel,
        in_specs=[smem] * 2 + [vmem] * peers,
        out_specs=vmem,
        out_shape=shape((side * rows, width), BF16),
        compiler_params=params(max(8, side * rows // 256)),
        cost_estimate=cost(1),
        name="plane_stack",
    )(my_y, my_x, *low_pieces)

    arrived = over_plane(pieces)
    grad_other = other_core(grad_mine)
    low_other = other_core(low_mine)

    units = 256
    chunks = hidden // units
    last_biases = []

    def feed_weights(low_values, grad_values, at, block_rows, part, sums, more):
        start, stop = part
        last = start == 0
        row_block = pl.BlockSpec((block_rows, width), lambda c: (at, 0))
        sum_specs = [
            pl.BlockSpec((width, units), lambda c: (0, start + c)),
            pl.BlockSpec((units, width), lambda c: (start + c, 0)),
            pl.BlockSpec((8, units), lambda c: (0, start + c)),
        ]
        results = pl.pallas_call(
            functools.partial(feed_weight_kernel, more=more, last=last),
            grid=(stop - start,),
            in_specs=[
                row_block,
                row_block,
                sum_specs[0],
                pl.BlockSpec((1, units), lambda c: (0, start + c)),
                sum_specs[1],
                *(sum_specs if more else [any_spec] * len(sums)),
            ],
            out_specs=sum_specs + ([whole((8, width))] if last else []),
            scratch_shapes=[
                pltpu.VMEM((width, block_rows), BF16),
                pltpu.VMEM((width, block_rows), BF16),
            ],
            out_shape=[
                shape((width, hidden), F32),
                shape((hidden, width), F32),
                shape((8, hidden), F32),
            ]
            + ([shape((8, width), F32)] if last else []),
            input_output_aliases={5 + i: i for i in range(len(sums))},
            compiler_params=params(56),
            cost_estimate=cost(2 * (stop - start) + 1),
            name="feed_weights_more" if more else "feed_weights",
        )(low_values, grad_values, expand_weight, bias_row, contract_weight, *sums)
        last_biases.extend(results[3:])
        return tuple(results[:3])

    def feed_side(low_values, grad_values, part, sums, more):
        block_rows = min(side * rows, 1024)
        for at in range(side * rows // block_rows):
            sums = feed_weights(low_values, grad_values, at, block_rows, part, sums, more or at > 0)
        return sums

    most, rest = (0, chunks - 2), (chunks - 2, chunks)
    sums = feed_side(low_mine, grad_mine, most, (), False)
    arrived, sums = lax.optimization_barrier((arrived, sums))
    pieces = pl.pallas_call(
        functools.partial(plane_kernel, peers=peers, cap=cap),
        in_specs=[smem] * 2 + [vmem] * peers,
        out_specs=[vmem] * z_size,
        out_shape=[shape((half_rows // side + x_size * cap, width), BF16)] * z_size,
        compiler_params=params(16),
        cost_estimate=cost(3),
        name="plane_sum",
    )(my_x, my_z, *arrived)
    _, sums = lax.optimization_barrier((pieces[0], sums))
    sums = feed_side(low_mine, grad_mine, rest, sums, False)
    arrived, sums = lax.optimization_barrier((over_z(pieces), sums))
    total, returned = pl.pallas_call(
        column_kernel,
        in_specs=[smem] + [vmem] * z_size,
        out_specs=[vmem] * 2,
        out_shape=[
            shape((half_rows // side, width), BF16),
            shape((parts * cap, width), BF16),
        ],
        compiler_params=params(8),
        cost_estimate=cost(1),
        name="column_sum",
    )(my_z, *arrived)
    arrived = over_z([total] * z_size)
    _, grad_other, low_other, sums = lax.optimization_barrier((total, grad_other, low_other, sums))
    sums = feed_side(low_other, grad_other, rest, sums, True)
    arrived, sums = lax.optimization_barrier((arrived, sums))
    column = stack_z(arrived)
    _, grad_other, low_other, sums = lax.optimization_barrier((column, grad_other, low_other, sums))
    mine = over_plane([column] * peers)
    other_first = other_core(column)
    sums = feed_side(low_other, grad_other, most, sums, True)
    mine, other_first, sums = lax.optimization_barrier((mine, other_first, sums))
    grad_expand, grad_contract, expand_bias_sum = sums
    other = [other_first] + [other_core(value) for value in mine[1:]]
    node_grad = pl.pallas_call(
        node_grad_kernel,
        in_specs=[vmem] * 6,
        out_specs=vmem,
        out_shape=shape((rows, width), F32),
        compiler_params=params(12),
        cost_estimate=cost(3),
        name="node_gradient",
    )(grad_mixed1, first, own, returned, asked, message_weight1)

    vec = shape((width,), F32)
    thin = shape((edge_width,), F32)
    square = shape((width, width), F32)
    small = shape((edge_width, edge_width), F32)
    (
        grad_message1,
        grad_mb1,
        grad_message2,
        grad_mb2,
        grad_message3,
        grad_mb3,
        grad_n1g,
        grad_n1s,
        grad_eb,
        grad_cb,
        grad_n2g,
        grad_n2s,
        grad_edge1_t,
        grad_eb1,
        grad_edge2,
        grad_eb2,
        grad_edge3,
        grad_eb3,
        grad_n3g,
        grad_n3s,
    ) = pl.pallas_call(
        functools.partial(unpack_kernel, peers=peers, lasts=len(last_biases)),
        in_specs=[smem] * 3 + [vmem] * (2 * peers + 1 + len(last_biases)),
        out_specs=[vmem] * 20,
        out_shape=[
            shape(message_weight1.shape, F32),
            vec,
            square,
            vec,
            square,
            vec,
            vec,
            vec,
            shape((hidden,), F32),
            vec,
            vec,
            vec,
            shape(edge_w1t.shape, F32),
            thin,
            small,
            thin,
            small,
            thin,
            thin,
            thin,
        ],
        scratch_shapes=[pltpu.VMEM((half_rows, width), BF16)] * 2,
        compiler_params=params(24),
        cost_estimate=cost(4),
        name="unpack",
    )(core, my_y, my_x, *mine, *other, expand_bias_sum, *last_biases)
    return (
        fresh[None],
        edge_out.transpose(1, 0, 2)[None],
        node_grad[None],
        edge_grad.transpose(1, 0, 2)[None],
        grad_message1,
        grad_mb1,
        grad_message2,
        grad_mb2,
        grad_message3,
        grad_mb3,
        grad_n1g,
        grad_n1s,
        grad_expand,
        grad_eb,
        grad_contract,
        grad_cb,
        grad_n2g,
        grad_n2s,
        grad_edge1_t.T,
        grad_eb1,
        grad_edge2,
        grad_eb2,
        grad_edge3,
        grad_eb3,
        grad_n3g,
        grad_n3s,
    )


def solution(mesh):
    batch, res = mesh.shape["batch"], mesh.shape["res"]
    x_size = 1 << ((res.bit_length() - 1) // 2)
    sizes = (batch // CORES, CORES, res // x_size, x_size)
    fine = jax.sharding.Mesh(mesh.devices.reshape(sizes), ALL)
    row_spec = P(("y", "core"), RES, None)
    edge_spec = P(("y", "core"), RES, None, None)
    return jax.shard_map(
        body,
        mesh=fine,
        in_specs=(row_spec, edge_spec, row_spec, row_spec, row_spec, edge_spec) + (P(),) * 22,
        out_specs=(row_spec, edge_spec, row_spec, edge_spec) + (P(),) * 22,
        check_vma=False,
    )
```
